32 devices in a mesh: fsdp: 16 (over z, y, x), replica: 2 (over core).
Axes of the slice: x: 2, y: 2, z: 4, core: 2. Of those that a mesh axis runs over, the one named last changes fastest.
Arguments:
- partials: float32 [2, 16384, 128], P('replica', 'fsdp'), may hold values from -6 to 6
- diag_stat: float32 [16384, 128], P('fsdp'), may hold values from 0.8 to 3
- first_stat: float32 [16384, 128], P('fsdp'), may hold values from -0.35 to 0.35
- second_stat: float32 [16384, 128], P('fsdp'), may hold values from -0.35 to 0.35
Outputs:
- update: float32 [16384, 128], P('fsdp')
- diag_next: float32 [16384, 128], P('fsdp')
- first_next: float32 [16384, 128], P('fsdp')
- second_next: float32 [16384, 128], P('fsdp')
The draws below stay inside these ranges and needn't reach their ends.
All inputs are finite; a program needn't handle non-finite values.
Results may differ from the reference program's by a relative error of at most 0.00002.
Values sent between devices are 32-bit elements; how exact they have to be, the bound alone decides.
No kernel may reach another device: no remote copies, remote signals or barrier semaphores. Data moves between devices by JAX's collectives and lax.ppermute only.
A program may use at most 64 MiB of HBM per device.

```python
import jax
import jax.numpy as jnp
from jax import lax

BLOCK = 128
NR = 16384
N_REPLICA = 2


def level_of(key, dims, pieces, least, largest):
    def one(position, blocks):
        draws = jax.random.uniform(jax.random.fold_in(jax.random.fold_in(key, 6), position), (blocks,), jnp.float32, least / len(pieces), largest / len(pieces))
        return jnp.repeat(jnp.exp(draws), dims[position] // blocks).reshape((-1,) + (1,) * (len(dims) - position - 1))

    level = one(*pieces[0])
    for cut in pieces[1:]:
        level = level * one(*cut)
    return level


def centred(stream_key, dims, deviation, limit, split=(), kind=jnp.bfloat16):
    array = deviation * jax.random.normal(stream_key, dims, jnp.float32)
    if split:
        array = array * level_of(stream_key, dims, split, -0.22, 0.18)
    return jnp.clip(array, -limit, limit).astype(kind)


def setup_inputs(seed: int = 0) -> dict:
    seeds = jax.random.split(jax.random.key(seed), 5)
    partials = centred(seeds[0], (N_REPLICA, NR, BLOCK), 1.0, 6.0, ((0, 2), (1, 16)), jnp.float32)
    diag_stat = jnp.clip(0.8 + 2.2 * jax.random.uniform(seeds[1], (NR, BLOCK), jnp.float32) ** level_of(seeds[1], (NR, BLOCK), ((0, 16),), -0.2, 0.2), 0.8, 3.0)
    first_stat = jnp.clip(jax.random.uniform(seeds[2], (NR, BLOCK), jnp.float32, -0.35, 0.35) * level_of(seeds[2], (NR, BLOCK), ((0, 16),), -0.4, 0.0), -0.35, 0.35)
    second_stat = jnp.clip(jax.random.uniform(seeds[3], (NR, BLOCK), jnp.float32, -0.35, 0.35) * level_of(seeds[3], (NR, BLOCK), ((0, 16),), -0.4, 0.0), -0.35, 0.35)
    return dict(partials=partials, diag_stat=diag_stat, first_stat=first_stat, second_stat=second_stat)


decay_rate = 0.95
damping = 0.01


def reference(partials, diag_stat, first_stat, second_stat):
    gradient = jnp.sum(partials, axis=0) / N_REPLICA
    total_rows = gradient.shape[0]
    width = gradient.shape[1]
    row_index = lax.broadcasted_iota(jnp.int32, (total_rows + 2, width), 0)
    local_index = row_index[:total_rows]
    zeros_two = jnp.zeros((2, width), jnp.float32)
    grad_ext = jnp.concatenate([gradient, zeros_two], axis=0)
    diag_next = decay_rate * diag_stat + gradient * gradient
    first_next = jnp.where(local_index < total_rows - 1, decay_rate * first_stat + gradient * grad_ext[1:total_rows + 1], 0.0)
    second_next = jnp.where(local_index < total_rows - 2, decay_rate * second_stat + gradient * grad_ext[2:total_rows + 2], 0.0)
    damped = jnp.where(row_index < total_rows, jnp.concatenate([diag_next, zeros_two], axis=0) + damping, 1.0)
    first_ext = jnp.concatenate([first_next, zeros_two], axis=0)
    upper_diag = damped[1:total_rows + 1]
    lower_diag = damped[2:total_rows + 2]
    coupling = first_ext[1:total_rows + 1]
    determinant = upper_diag * lower_diag - coupling * coupling
    first_coef = (lower_diag * first_next - coupling * second_next) / determinant
    second_coef = (upper_diag * second_next - coupling * first_next) / determinant
    schur = damped[:total_rows] - first_next * first_coef - second_next * second_coef
    value = (gradient - first_coef * grad_ext[1:total_rows + 1] - second_coef * grad_ext[2:total_rows + 2]) / schur
    value_ext = jnp.concatenate([zeros_two, value], axis=0)
    first_prev = jnp.concatenate([zeros_two, first_coef], axis=0)
    second_prev = jnp.concatenate([zeros_two, second_coef], axis=0)
    update = value - first_prev[1:total_rows + 1] * value_ext[1:total_rows + 1] - second_prev[0:total_rows] * value_ext[0:total_rows]
    return update, diag_next, first_next, second_next
```

```python
import functools

import jax
import jax.numpy as jnp
from jax import lax
from jax.experimental import pallas as pl
from jax.experimental.pallas import tpu as pltpu
from jax.sharding import PartitionSpec as P

decay_rate = 0.95
damping = 0.01
PAD = 8


def kernel(
    parts, scale, rows, step,
    *refs,
):
    own = refs[:parts]
    diag_ref, first_ref, second_ref = refs[parts : parts + 3]
    before = refs[parts + 3 : 2 * parts + 3]
    after = refs[2 * parts + 3 : 3 * parts + 3]
    outs = refs[3 * parts + 3 : 3 * parts + 7]
    grad, diag, first, second, value, part1, part2, update, sems = refs[3 * parts + 7 :]
    width = diag_ref.shape[1]
    chunks = rows // step
    end = PAD + rows

    def total(pieces):
        out = pieces[0]
        for piece in pieces[1:]:
            out = out + piece
        return out * scale

    g_lo = total([r[0:2, :] for r in before])
    g_hi = total([r[0:2, :] for r in after])
    present = after[0][6:8, :]
    grad[PAD - 2 : PAD, :] = g_lo
    grad[end : end + 2, :] = g_hi
    diag[PAD - 2 : PAD, :] = decay_rate * before[0][2:4, :] + g_lo * g_lo
    diag[end : end + 2, :] = (
        decay_rate * after[0][2:4, :] + g_hi * g_hi + (1.0 - present) * (1.0 - damping)
    )

    def gradients(c, carry):
        at = pl.multiple_of(c * step, step)
        here = pl.ds(at, step)
        there = pl.ds(at + PAD, step)
        g = total([r[here, :] for r in own])
        grad[there, :] = g
        diag[there, :] = decay_rate * diag_ref[here, :] + g * g
        return carry

    lax.fori_loop(0, chunks, gradients, 0, unroll=True)

    def bands(c, carry):
        at = pl.multiple_of(c * step, step)
        here = pl.ds(at, step)
        g = grad[pl.ds(at + PAD, step), :]
        first[pl.ds(at + PAD, step), :] = (
            decay_rate * first_ref[here, :] + g * grad[pl.ds(at + PAD + 1, step), :]
        )
        second[pl.ds(at + PAD, step), :] = (
            decay_rate * second_ref[here, :] + g * grad[pl.ds(at + PAD + 2, step), :]
        )
        return carry

    lax.fori_loop(0, chunks, bands, 0, unroll=True)
    first[PAD - 2 : PAD, :] = (
        decay_rate * before[0][4:6, :] + g_lo * grad[PAD - 1 : PAD + 1, :]
    )
    second[PAD - 2 : PAD, :] = (
        decay_rate * before[0][6:8, :] + g_lo * grad[PAD : PAD + 2, :]
    )
    first[end - 1 : end, :] = first[end - 1 : end, :] * present[0:1, :]
    second[end - 2 : end, :] = second[end - 2 : end, :] * present
    first[end : end + 1, :] = (
        decay_rate * after[0][4:5, :] + g_hi[0:1, :] * g_hi[1:2, :]
    )

    copies = []

    def send(scratch, k):
        copy = pltpu.make_async_copy(scratch.at[PAD:end, :], outs[k], sems.at[k])
        copy.start()
        copies.append(copy)

    send(diag, 1)
    send(first, 2)
    send(second, 3)

    def solve(at, size):
        g = grad[pl.ds(at, size), :]
        g1 = grad[pl.ds(at + 1, size), :]
        g2 = grad[pl.ds(at + 2, size), :]
        d = diag[pl.ds(at, size), :] + damping
        upper = diag[pl.ds(at + 1, size), :] + damping
        lower = diag[pl.ds(at + 2, size), :] + damping
        f = first[pl.ds(at, size), :]
        c = first[pl.ds(at + 1, size), :]
        s = second[pl.ds(at, size), :]
        det = upper * lower - c * c
        n1 = lower * f - c * s
        n2 = upper * s - c * f
        schur = d * det - f * n1 - s * n2
        top = g * det - n1 * g1 - n2 * g2
        w = top / (schur * det)
        return w * det, w * n1, w * n2

    _, p1, p2 = solve(PAD - 2, 2)
    part1[PAD - 2 : PAD, :] = p1
    part2[PAD - 2 : PAD, :] = p2

    def values(c, carry):
        at = pl.multiple_of(c * step, step)
        v, p1, p2 = solve(at + PAD, step)
        there = pl.ds(at + PAD, step)
        part1[there, :] = p1
        part2[there, :] = p2
        update[pl.ds(at, step), :] = (
            v - part1[pl.ds(at + PAD - 1, step), :] - part2[pl.ds(at + PAD - 2, step), :]
        )
        return carry

    lax.fori_loop(0, chunks, values, 0, unroll=True)
    copy = pltpu.make_async_copy(update, outs[0], sems.at[0])
    copy.start()
    copies.append(copy)
    for copy in copies:
        copy.wait()


def body(partials, diag_stat, first_stat, second_stat):
    own = partials[0]
    rows, width = own.shape
    replicas = lax.axis_size("replica")
    shards = lax.axis_size("fsdp")
    scale = 1.0 / replicas
    axes = ("fsdp", "replica")

    def route(distance, turn):
        return [
            (i * replicas + r, (i + distance) * replicas + (r + turn) % replicas)
            for i in range(shards)
            for r in range(replicas)
            if 0 <= i + distance < shards
        ]

    if replicas > 2:
        own = lax.psum(own, "replica")
        turns = [0]
    else:
        turns = list(range(replicas))

    last = jnp.concatenate([own[-2:], diag_stat[-2:], first_stat[-2:], second_stat[-2:]])
    head = jnp.concatenate(
        [own[:2], diag_stat[:2], first_stat[:2], jnp.ones((2, width), jnp.float32)]
    )
    before = [
        lax.ppermute(last if t == 0 else own[-2:], axes, route(1, t)) for t in turns
    ]
    after = [
        lax.ppermute(head if t == 0 else own[:2], axes, route(-1, t)) for t in turns
    ]
    pieces = [own if t == 0 else lax.ppermute(own, axes, route(0, t)) for t in turns]
    parts = len(pieces)

    shape = jax.ShapeDtypeStruct((rows, width), jnp.float32)
    vmem = pl.BlockSpec(memory_space=pltpu.VMEM)
    hbm = pl.BlockSpec(memory_space=pl.ANY)
    padded = pltpu.VMEM((rows + 2 * PAD, width), jnp.float32)
    step = 64 if rows % 64 == 0 else 8
    return pl.pallas_call(
        functools.partial(kernel, parts, scale, rows, step),
        out_shape=(shape,) * 4,
        in_specs=[vmem] * (3 * parts + 3),
        out_specs=(hbm,) * 4,
        scratch_shapes=[padded] * 7
        + [pltpu.VMEM((rows, width), jnp.float32), pltpu.SemaphoreType.DMA((4,))],
        compiler_params=pltpu.CompilerParams(vmem_limit_bytes=24 * 2**20),
        name="precondition",
    )(*pieces, diag_stat, first_stat, second_stat, *before, *after)


def solution(mesh):
    return jax.shard_map(
        body,
        mesh=mesh,
        in_specs=(P("replica", "fsdp", None), P("fsdp", None), P("fsdp", None), P("fsdp", None)),
        out_specs=(P("fsdp", None), P("fsdp", None), P("fsdp", None), P("fsdp", None)),
        check_vma=False,
    )
```

```python
import functools

import jax
import jax.numpy as jnp
from jax import lax
from jax.experimental import pallas as pl
from jax.experimental.pallas import tpu as pltpu
from jax.sharding import PartitionSpec as P

decay_rate = 0.95
damping = 0.01
PAD = 8
TILE = 8


def solved(g, g1, g2, d, upper, lower, f, c, s):
    det = upper * lower - c * c
    n1 = lower * f - c * s
    n2 = upper * s - c * f
    schur = d * det - f * n1 - s * n2
    top = g * det - n1 * g1 - n2 * g2
    w = top / (schur * det)
    return w * det, w * n1, w * n2


def stage(count, *refs):
    sems = refs[2 * count]
    copies = [
        pltpu.make_async_copy(refs[k], refs[count + k], sems.at[k]) for k in range(count)
    ]
    for copy in copies:
        copy.start()
    for copy in copies:
        copy.wait()


def interior(parts, scale, rows, step, *refs):
    own = refs[:parts]
    diag_ref, first_ref, second_ref = refs[parts : parts + 3]
    outs = refs[parts + 3 : parts + 7]
    edges = refs[parts + 7]
    grad, diag, first, second, part1, part2, update, sems = refs[parts + 8 :]
    width = diag_ref.shape[1]
    chunks = rows // step
    end = PAD + rows

    zeros = jnp.zeros((PAD, width), jnp.float32)
    grad[end:, :] = zeros
    diag[end:, :] = zeros + 1.0
    first[end:, :] = zeros
    part1[:PAD, :] = zeros
    part2[:PAD, :] = zeros

    def gradients(c, carry):
        at = pl.multiple_of(c * step, step)
        here = pl.ds(at, step)
        there = pl.ds(at + PAD, step)
        g = own[0][here, :]
        for piece in own[1:]:
            g = g + piece[here, :]
        g = g * scale
        grad[there, :] = g
        diag[there, :] = decay_rate * diag_ref[here, :] + g * g
        return carry

    lax.fori_loop(0, chunks, gradients, 0, unroll=True)

    def bands(c, carry):
        at = pl.multiple_of(c * step, step)
        here = pl.ds(at, step)
        there = pl.ds(at + PAD, step)
        g = grad[there, :]
        g1 = grad[pl.ds(at + PAD + 1, step), :]
        g2 = grad[pl.ds(at + PAD + 2, step), :]
        first[there, :] = decay_rate * first_ref[here, :] + g * g1
        second[there, :] = decay_rate * second_ref[here, :] + g * g2
        return carry

    lax.fori_loop(0, chunks, bands, 0, unroll=True)

    copies = []

    def send(source, k):
        copy = pltpu.make_async_copy(source, outs[k], sems.at[k])
        copy.start()
        copies.append(copy)

    send(diag.at[PAD:end, :], 1)
    send(first.at[PAD:end, :], 2)
    send(second.at[PAD:end, :], 3)

    def values(c, carry):
        at = pl.multiple_of(c * step, step)
        there = pl.ds(at + PAD, step)
        after = pl.ds(at + PAD + 1, step)
        later = pl.ds(at + PAD + 2, step)
        v, p1, p2 = solved(
            grad[there, :],
            grad[after, :],
            grad[later, :],
            diag[there, :] + damping,
            diag[after, :] + damping,
            diag[later, :] + damping,
            first[there, :],
            first[after, :],
            second[there, :],
        )
        part1[there, :] = p1
        part2[there, :] = p2
        update[pl.ds(at, step), :] = (
            v - part1[pl.ds(at + PAD - 1, step), :] - part2[pl.ds(at + PAD - 2, step), :]
        )
        return carry

    lax.fori_loop(0, chunks, values, 0, unroll=True)
    send(update, 0)
    tops = [grad[PAD : PAD + TILE, :], diag[PAD : PAD + TILE, :], first[PAD : PAD + TILE, :]]
    tops.append(update[:TILE, :])
    tails = [r[end - TILE : end, :] for r in (grad, diag, first, second)]
    tails.append(update[rows - TILE :, :])
    tails += [r[end - TILE : end, :] for r in (part1, part2)]
    for k, tile in enumerate(tops + tails):
        edges[k * TILE : (k + 1) * TILE, :] = tile
    for copy in copies:
        copy.wait()


def border(rows, shards, paired, *refs):
    edges, got, other = refs[:3]
    outs = refs[6:9]
    work, tiles, sems = refs[9:]

    def edge(k, at, size):
        return edges[k * TILE + at : k * TILE + at + size, :]

    shard = lax.axis_index("fsdp")
    if paired:
        low = lax.axis_index("replica") == 0
        before = jnp.where(low, got[...], other[...])
        after = jnp.where(low, other[...], got[...])
    else:
        before, after = got[...], other[...]
    work[0:8, :] = jnp.where(shard == 0, 0.0, before)
    work[8:16, :] = jnp.where(shard == shards - 1, 0.0, after)

    g = work[0:2, :]
    g_next = edge(0, 0, 2)
    d = decay_rate * work[2:4, :] + g * g + damping
    d_next = edge(1, 0, 2) + damping
    g1 = jnp.concatenate([g[1:2], g_next[0:1]])
    d1 = jnp.concatenate([d[1:2], d_next[0:1]])
    f = decay_rate * work[4:6, :] + g * g1
    s = decay_rate * work[6:8, :] + g * g_next
    c = jnp.concatenate([f[1:2], edge(2, 0, 1)])
    _, p1, p2 = solved(g, g1, g_next, d, d1, d_next, f, c, s)
    tiles[0:8, :] = edges[3 * TILE : 4 * TILE, :]
    tiles[0:1, :] = tiles[0:1, :] - p1[1:2] - p2[0:1]
    tiles[1:2, :] = tiles[1:2, :] - p2[1:2]

    g = edge(4, 6, 2)
    g_next = work[8:10, :]
    present = work[14:16, :]
    d = edge(5, 6, 2) + damping
    d_next = (
        decay_rate * work[10:12, :] + g_next * g_next + present * damping + (1.0 - present)
    )
    g1 = jnp.concatenate([g[1:2], g_next[0:1]])
    d1 = jnp.concatenate([d[1:2], d_next[0:1]])
    f_last = (edge(6, 7, 1) + g[1:2] * g_next[0:1]) * present[0:1]
    f = jnp.concatenate([edge(6, 6, 1), f_last])
    s = (edge(7, 6, 2) + g * g_next) * present
    f_next = decay_rate * work[12:13, :] + g_next[0:1] * g_next[1:2]
    c = jnp.concatenate([f_last, f_next])
    v, p1, _ = solved(g, g1, g_next, d, d1, d_next, f, c, s)
    tiles[8:16, :] = edges[8 * TILE : 9 * TILE, :]
    tiles[14:15, :] = v[0:1] - edge(9, 5, 1) - edge(10, 4, 1)
    tiles[15:16, :] = v[1:2] - p1[0:1] - edge(10, 5, 1)
    tiles[16:24, :] = edges[6 * TILE : 7 * TILE, :]
    tiles[23:24, :] = f_last
    tiles[24:32, :] = edges[7 * TILE : 8 * TILE, :]
    tiles[30:32, :] = s

    copies = [
        pltpu.make_async_copy(tiles.at[0:8, :], outs[0].at[0:TILE, :], sems.at[0]),
        pltpu.make_async_copy(tiles.at[8:16, :], outs[0].at[rows - TILE : rows, :], sems.at[1]),
        pltpu.make_async_copy(tiles.at[16:24, :], outs[1].at[rows - TILE : rows, :], sems.at[2]),
        pltpu.make_async_copy(tiles.at[24:32, :], outs[2].at[rows - TILE : rows, :], sems.at[3]),
    ]
    for copy in copies:
        copy.start()
    for copy in copies:
        copy.wait()


def body(partials, diag_stat, first_stat, second_stat):
    own = partials[0]
    rows, width = own.shape
    replicas = lax.axis_size("replica")
    shards = lax.axis_size("fsdp")
    scale = 1.0 / replicas
    core = lax.axis_index("replica")
    paired = replicas == 2

    shape = jax.ShapeDtypeStruct((rows, width), jnp.float32)
    vmem = pl.BlockSpec(memory_space=pltpu.VMEM)
    hbm = pl.BlockSpec(memory_space=pltpu.HBM)
    params = pltpu.CompilerParams(vmem_limit_bytes=16 * 2**20)

    def swap(block):
        return lax.ppermute(block, "replica", [(0, 1), (1, 0)])

    if paired:
        pieces = [own, swap(own)]
    else:
        pieces = [lax.psum(own, "replica")]
    parts = len(pieces)

    moved = [own] * (parts - 1) + [diag_stat, first_stat, second_stat]
    count = len(moved)
    staged = pl.pallas_call(
        functools.partial(stage, count),
        out_shape=(shape,) * count,
        in_specs=[hbm] * count,
        out_specs=(vmem,) * count,
        scratch_shapes=[pltpu.SemaphoreType.DMA((count,))],
        compiler_params=pltpu.CompilerParams(vmem_limit_bytes=51 * 2**20),
        cost_estimate=pl.CostEstimate(
            flops=0, bytes_accessed=4 * count * rows * width, transcendentals=0
        ),
        name="stage",
    )(*moved)
    if paired:
        pieces[0] = staged[0]
    diag_in, first_in, second_in = staged[-3:]

    def edge(at):
        return sum(p[at : at + 2] for p in pieces) * scale

    ones = jnp.ones((2, width), jnp.float32)
    tail = rows - 2
    last = jnp.concatenate([edge(tail), diag_in[tail:], first_in[tail:], second_in[tail:]])
    head = jnp.concatenate([edge(0), diag_in[:2], first_in[:2], ones])
    if paired:
        up = [(2 * i, 2 * i + 2) for i in range(shards - 1)]
        down = [(2 * i + 1, 2 * i - 1) for i in range(1, shards)]
        turns = [(2 * shards - 2, 2 * shards - 1), (1, 0)]
        got = lax.ppermute(
            jnp.where(core == 0, last, head), ("fsdp", "replica"), up + down + turns
        )
        other = swap(got)
    else:
        got = lax.ppermute(last, "fsdp", [(i, i + 1) for i in range(shards - 1)])
        other = lax.ppermute(head, "fsdp", [(i + 1, i) for i in range(shards - 1)])

    padded = pltpu.VMEM((rows + 2 * PAD, width), jnp.float32)
    step = 64 if rows % 64 == 0 else 8
    update, diag_next, first_next, second_next, edges = pl.pallas_call(
        functools.partial(interior, parts, scale, rows, step),
        out_shape=(shape,) * 4 + (jax.ShapeDtypeStruct((11 * TILE, width), jnp.float32),),
        in_specs=[vmem] * (parts + 3),
        out_specs=(hbm,) * 4 + (vmem,),
        scratch_shapes=[padded] * 6
        + [pltpu.VMEM((rows, width), jnp.float32), pltpu.SemaphoreType.DMA((4,))],
        compiler_params=params,
        cost_estimate=pl.CostEstimate(
            flops=45 * rows * width, bytes_accessed=16 * rows * width, transcendentals=0
        ),
        name="interior",
    )(*pieces, diag_in, first_in, second_in)

    update, first_next, second_next = pl.pallas_call(
        functools.partial(border, rows, shards, paired),
        out_shape=(shape,) * 3,
        in_specs=[vmem] * 3 + [hbm] * 3,
        out_specs=(hbm,) * 3,
        input_output_aliases={3: 0, 4: 1, 5: 2},
        scratch_shapes=[
            pltpu.VMEM((16, width), jnp.float32),
            pltpu.VMEM((32, width), jnp.float32),
            pltpu.SemaphoreType.DMA((4,)),
        ],
        compiler_params=params,
        name="border",
    )(edges, got, other, update, first_next, second_next)
    return update, diag_next, first_next, second_next


def solution(mesh):
    return jax.shard_map(
        body,
        mesh=mesh,
        in_specs=(P("replica", "fsdp", None), P("fsdp", None), P("fsdp", None), P("fsdp", None)),
        out_specs=(P("fsdp", None), P("fsdp", None), P("fsdp", None), P("fsdp", None)),
        check_vma=False,
    )
```

```python
import functools

import jax
import jax.numpy as jnp
from jax import lax
from jax.experimental import pallas as pl
from jax.experimental.pallas import tpu as pltpu
from jax.sharding import PartitionSpec as P

decay_rate = 0.95
damping = 0.01
PAD = 8
TILE = 8


def solved(g, g1, g2, d, upper, lower, f, c, s):
    det = upper * lower - c * c
    n1 = lower * f - c * s
    n2 = upper * s - c * f
    schur = d * det - f * n1 - s * n2
    top = g * det - n1 * g1 - n2 * g2
    w = top / (schur * det)
    return w * det, w * n1, w * n2


def collect(count, rows, *refs):
    tiles, sems = refs[count], refs[count + 1]
    copies = []
    for k in range(count):
        for half, at in enumerate((0, rows - TILE)):
            row = (2 * k + half) * TILE
            copies.append(
                pltpu.make_async_copy(
                    refs[k].at[at : at + TILE, :],
                    tiles.at[row : row + TILE, :],
                    sems.at[2 * k + half],
                )
            )
    for copy in copies:
        copy.start()
    for copy in copies:
        copy.wait()


def message(scale, rows, tiles, other, out):
    core = lax.axis_index("replica")

    @pl.when(core == 0)
    def _():
        out[0:2, :] = (tiles[14:16, :] + other[rows - 2 : rows, :]) * scale
        for k in range(1, 4):
            at = (2 * k + 2) * TILE
            out[2 * k : 2 * k + 2, :] = tiles[at - 2 : at, :]

    @pl.when(core != 0)
    def _():
        out[0:2, :] = (tiles[0:2, :] + other[0:2, :]) * scale
        for k in range(1, 3):
            out[2 * k : 2 * k + 2, :] = tiles[2 * k * TILE : 2 * k * TILE + 2, :]
        out[6:8, :] = jnp.ones((2, out.shape[1]), jnp.float32)


def interior(parts, scale, rows, chunk, step, *refs):
    count = parts + 3
    sources = refs[:count]
    outs = refs[count : count + 4]
    edges = refs[count + 4]
    staged = refs[count + 5 : 2 * count + 5]
    pieces = staged[:parts]
    diag_in, first_in, second_in = staged[parts:]
    grad, diag, first, second, part1, part2, update, in_sems, out_sems = refs[2 * count + 5 :]
    width = edges.shape[1]
    end = PAD + rows
    chunks = rows // chunk

    loads = []
    for c in range(chunks):
        at = slice(c * chunk, (c + 1) * chunk)
        row = []
        for k, (source, target) in enumerate(zip(sources, staged)):
            copy = pltpu.make_async_copy(source.at[at, :], target.at[at, :], in_sems.at[k, c])
            copy.start()
            row.append(copy)
        loads.append(row)

    zeros = jnp.zeros((PAD, width), jnp.float32)
    grad[end:, :] = zeros
    diag[end:, :] = zeros + 1.0
    first[end:, :] = zeros
    part1[:PAD, :] = zeros
    part2[:PAD, :] = zeros

    def gradients(at, size):
        here, there = pl.ds(at, size), pl.ds(at + PAD, size)
        g = pieces[0][here, :]
        for piece in pieces[1:]:
            g = g + piece[here, :]
        g = g * scale
        grad[there, :] = g
        diag[there, :] = decay_rate * diag_in[here, :] + g * g

    def bands(at, size):
        here, there = pl.ds(at, size), pl.ds(at + PAD, size)
        g = grad[there, :]
        g1 = grad[pl.ds(at + PAD + 1, size), :]
        g2 = grad[pl.ds(at + PAD + 2, size), :]
        first[there, :] = decay_rate * first_in[here, :] + g * g1
        second[there, :] = decay_rate * second_in[here, :] + g * g2

    def values(at, size):
        there = pl.ds(at + PAD, size)
        after = pl.ds(at + PAD + 1, size)
        later = pl.ds(at + PAD + 2, size)
        v, p1, p2 = solved(
            grad[there, :],
            grad[after, :],
            grad[later, :],
            diag[there, :] + damping,
            diag[after, :] + damping,
            diag[later, :] + damping,
            first[there, :],
            first[after, :],
            second[there, :],
        )
        part1[there, :] = p1
        part2[there, :] = p2
        update[pl.ds(at, size), :] = (
            v - part1[pl.ds(at + PAD - 1, size), :] - part2[pl.ds(at + PAD - 2, size), :]
        )

    def over(work, low, high):
        for at in range(low, high, step):
            work(at, min(step, high - at))

    stores = []

    def send(source, pad, k, c, low, high):
        copy = pltpu.make_async_copy(
            source.at[low + pad : high + pad, :], outs[k].at[low:high, :], out_sems.at[k, c]
        )
        copy.start()
        stores.append(copy)

    for c in range(chunks):
        for copy in loads[c]:
            copy.wait()
        last = c == chunks - 1
        low, high = c * chunk, (c + 1) * chunk
        over(gradients, low, high)
        send(diag, PAD, 1, c, low, high)
        low, high = max(low - TILE, 0), high if last else high - TILE
        over(bands, low, high)
        send(first, PAD, 2, c, low, high)
        send(second, PAD, 3, c, low, high)
        low, high = max(c * chunk - 2 * TILE, 0), high if last else high - TILE
        over(values, low, high)
        send(update, 0, 0, c, low, high)

    tops = [grad[PAD : PAD + TILE, :], diag[PAD : PAD + TILE, :], first[PAD : PAD + TILE, :]]
    tops.append(update[:TILE, :])
    tails = [r[end - TILE : end, :] for r in (grad, diag, first, second)]
    tails.append(update[rows - TILE :, :])
    tails += [r[end - TILE : end, :] for r in (part1, part2)]
    for k, tile in enumerate(tops + tails):
        edges[k * TILE : (k + 1) * TILE, :] = tile
    for copy in stores:
        copy.wait()


def border(rows, shards, paired, *refs):
    edges, got, other = refs[:3]
    outs = refs[6:9]
    work, tiles, sems = refs[9:]

    def edge(k, at, size):
        return edges[k * TILE + at : k * TILE + at + size, :]

    shard = lax.axis_index("fsdp")
    if paired:
        low = lax.axis_index("replica") == 0
        before = jnp.where(low, got[...], other[...])
        after = jnp.where(low, other[...], got[...])
    else:
        before, after = got[...], other[...]
    work[0:8, :] = jnp.where(shard == 0, 0.0, before)
    work[8:16, :] = jnp.where(shard == shards - 1, 0.0, after)

    g = work[0:2, :]
    g_next = edge(0, 0, 2)
    d = decay_rate * work[2:4, :] + g * g + damping
    d_next = edge(1, 0, 2) + damping
    g1 = jnp.concatenate([g[1:2], g_next[0:1]])
    d1 = jnp.concatenate([d[1:2], d_next[0:1]])
    f = decay_rate * work[4:6, :] + g * g1
    s = decay_rate * work[6:8, :] + g * g_next
    c = jnp.concatenate([f[1:2], edge(2, 0, 1)])
    _, p1, p2 = solved(g, g1, g_next, d, d1, d_next, f, c, s)
    tiles[0:8, :] = edges[3 * TILE : 4 * TILE, :]
    tiles[0:1, :] = tiles[0:1, :] - p1[1:2] - p2[0:1]
    tiles[1:2, :] = tiles[1:2, :] - p2[1:2]

    g = edge(4, 6, 2)
    g_next = work[8:10, :]
    present = work[14:16, :]
    d = edge(5, 6, 2) + damping
    d_next = (
        decay_rate * work[10:12, :] + g_next * g_next + present * damping + (1.0 - present)
    )
    g1 = jnp.concatenate([g[1:2], g_next[0:1]])
    d1 = jnp.concatenate([d[1:2], d_next[0:1]])
    f_last = (edge(6, 7, 1) + g[1:2] * g_next[0:1]) * present[0:1]
    f = jnp.concatenate([edge(6, 6, 1), f_last])
    s = (edge(7, 6, 2) + g * g_next) * present
    f_next = decay_rate * work[12:13, :] + g_next[0:1] * g_next[1:2]
    c = jnp.concatenate([f_last, f_next])
    v, p1, _ = solved(g, g1, g_next, d, d1, d_next, f, c, s)
    tiles[8:16, :] = edges[8 * TILE : 9 * TILE, :]
    tiles[14:15, :] = v[0:1] - edge(9, 5, 1) - edge(10, 4, 1)
    tiles[15:16, :] = v[1:2] - p1[0:1] - edge(10, 5, 1)
    tiles[16:24, :] = edges[6 * TILE : 7 * TILE, :]
    tiles[23:24, :] = f_last
    tiles[24:32, :] = edges[7 * TILE : 8 * TILE, :]
    tiles[30:32, :] = s

    copies = [
        pltpu.make_async_copy(tiles.at[0:8, :], outs[0].at[0:TILE, :], sems.at[0]),
        pltpu.make_async_copy(tiles.at[8:16, :], outs[0].at[rows - TILE : rows, :], sems.at[1]),
        pltpu.make_async_copy(tiles.at[16:24, :], outs[1].at[rows - TILE : rows, :], sems.at[2]),
        pltpu.make_async_copy(tiles.at[24:32, :], outs[2].at[rows - TILE : rows, :], sems.at[3]),
    ]
    for copy in copies:
        copy.start()
    for copy in copies:
        copy.wait()


def body(partials, diag_stat, first_stat, second_stat):
    own = partials[0]
    rows, width = own.shape
    replicas = lax.axis_size("replica")
    shards = lax.axis_size("fsdp")
    scale = 1.0 / replicas
    paired = replicas == 2

    shape = jax.ShapeDtypeStruct((rows, width), jnp.float32)
    vmem = pl.BlockSpec(memory_space=pltpu.VMEM)
    hbm = pl.BlockSpec(memory_space=pltpu.HBM)
    params = pltpu.CompilerParams(vmem_limit_bytes=24 * 2**20)

    def swap(block):
        return lax.ppermute(block, "replica", [(0, 1), (1, 0)])

    roomy = pltpu.CompilerParams(vmem_limit_bytes=int(53.5 * 2**20))
    stats = (diag_stat, first_stat, second_stat)
    if paired:
        other = swap(own)
        pieces = [own, other]
        tiles = pl.pallas_call(
            functools.partial(collect, 4, rows),
            out_shape=jax.ShapeDtypeStruct((8 * TILE, width), jnp.float32),
            in_specs=[hbm] * 4,
            out_specs=vmem,
            scratch_shapes=[pltpu.SemaphoreType.DMA((8,))],
            compiler_params=roomy,
            name="collect",
        )(own, *stats)
        sent = pl.pallas_call(
            functools.partial(message, scale, rows),
            out_shape=jax.ShapeDtypeStruct((TILE, width), jnp.float32),
            in_specs=[vmem] * 2,
            out_specs=vmem,
            compiler_params=params,
            name="message",
        )(tiles, other)
        up = [(2 * i, 2 * i + 2) for i in range(shards - 1)]
        down = [(2 * i + 1, 2 * i - 1) for i in range(1, shards)]
        turns = [(2 * shards - 2, 2 * shards - 1), (1, 0)]
        got = lax.ppermute(sent, ("fsdp", "replica"), up + down + turns)
    else:
        pieces = [lax.psum(own, "replica") * scale]
        scale = 1.0
        tail = rows - 2
        ones = jnp.ones((2, width), jnp.float32)
        last = jnp.concatenate([x[tail:] for x in (*pieces, *stats)])
        head = jnp.concatenate([x[:2] for x in (*pieces, *stats[:2])] + [ones])
        got = lax.ppermute(last, "fsdp", [(i, i + 1) for i in range(shards - 1)])
        across = lax.ppermute(head, "fsdp", [(i + 1, i) for i in range(shards - 1)])

    parts = len(pieces)
    whole = pltpu.VMEM((rows, width), jnp.float32)
    padded = pltpu.VMEM((rows + 2 * PAD, width), jnp.float32)
    chunk = 256 if rows % 256 == 0 else rows
    update, diag_next, first_next, second_next, edges = pl.pallas_call(
        functools.partial(interior, parts, scale, rows, chunk, 64),
        out_shape=(shape,) * 4 + (jax.ShapeDtypeStruct((11 * TILE, width), jnp.float32),),
        in_specs=[hbm] * (parts + 3),
        out_specs=(hbm,) * 4 + (vmem,),
        scratch_shapes=[whole] * (parts + 3)
        + [padded] * 6
        + [whole]
        + [pltpu.SemaphoreType.DMA((n, rows // chunk)) for n in (parts + 3, 4)],
        compiler_params=roomy,
        cost_estimate=pl.CostEstimate(
            flops=45 * rows * width, bytes_accessed=36 * rows * width, transcendentals=0
        ),
        name="interior",
    )(*pieces, *stats)

    if paired:
        got, edges = lax.optimization_barrier((got, edges))
        across = swap(got)

    update, first_next, second_next = pl.pallas_call(
        functools.partial(border, rows, shards, paired),
        out_shape=(shape,) * 3,
        in_specs=[vmem] * 3 + [hbm] * 3,
        out_specs=(hbm,) * 3,
        input_output_aliases={3: 0, 4: 1, 5: 2},
        scratch_shapes=[
            pltpu.VMEM((16, width), jnp.float32),
            pltpu.VMEM((32, width), jnp.float32),
            pltpu.SemaphoreType.DMA((4,)),
        ],
        compiler_params=params,
        name="border",
    )(edges, got, across, update, first_next, second_next)
    return update, diag_next, first_next, second_next


def solution(mesh):
    return jax.shard_map(
        body,
        mesh=mesh,
        in_specs=(P("replica", "fsdp", None), P("fsdp", None), P("fsdp", None), P("fsdp", None)),
        out_specs=(P("fsdp", None), P("fsdp", None), P("fsdp", None), P("fsdp", None)),
        check_vma=False,
    )
```

```python
import functools

import jax
import jax.numpy as jnp
from jax import lax
from jax.experimental import pallas as pl
from jax.experimental.pallas import tpu as pltpu
from jax.sharding import PartitionSpec as P

decay_rate = 0.95
damping = 0.01
PAD = 8
TILE = 8


def solved(g, g1, g2, d, upper, lower, f, c, s):
    det = upper * lower - c * c
    n1 = lower * f - c * s
    n2 = upper * s - c * f
    schur = d * det - f * n1 - s * n2
    top = g * det - n1 * g1 - n2 * g2
    w = top / (schur * det)
    return w * det, w * n1, w * n2


def collect(rows, own, diag, first, second, far, near, tiles, sems):
    width = tiles.shape[1]
    copies = []
    for k, source in enumerate((own, diag, first, second)):
        for half, at in enumerate((0, rows - TILE)):
            row = (2 * k + half) * TILE
            copies.append(
                pltpu.make_async_copy(
                    source.at[at : at + TILE, :],
                    tiles.at[row : row + TILE, :],
                    sems.at[2 * k + half],
                )
            )
    for copy in copies:
        copy.start()
    for copy in copies:
        copy.wait()
    head = [tiles[2 * k * TILE : 2 * k * TILE + 2, :] for k in range(3)]
    head.append(jnp.ones((2, width), jnp.float32))
    last = [tiles[(2 * k + 2) * TILE - 2 : (2 * k + 2) * TILE, :] for k in range(4)]
    even = lax.rem(lax.axis_index("fsdp"), 2) == 0

    def fill(out, blocks):
        for k, block in enumerate(blocks):
            out[2 * k : 2 * k + 2, :] = block

    @pl.when(even)
    def _():
        fill(near, last)
        fill(far, head)

    @pl.when(jnp.logical_not(even))
    def _():
        fill(near, head)
        fill(far, last)


def join(far, near, out):
    out[0:2, :] = near[0:2, :]
    out[2:4, :] = far[0:2, :]
    out[4:8, :] = jnp.zeros((4, out.shape[1]), jnp.float32)


def interior(parts, scale, rows, chunk, step, *refs):
    sources = refs[0], *refs[parts : parts + 3]
    outs = refs[parts + 3 : parts + 7]
    edges = refs[parts + 7]
    staged = refs[parts + 8 : parts + 12]
    own, diag_in, first_in, second_in = staged
    pieces = [own, *refs[1:parts]]
    grad, diag, first, second, part1, part2, update, in_sems, out_sems = refs[parts + 12 :]
    width = edges.shape[1]
    end = PAD + rows
    chunks = rows // chunk

    loads = []
    for c in range(chunks):
        at = slice(c * chunk, (c + 1) * chunk)
        row = []
        for k, (source, target) in enumerate(zip(sources, staged)):
            copy = pltpu.make_async_copy(source.at[at, :], target.at[at, :], in_sems.at[k, c])
            copy.start()
            row.append(copy)
        loads.append(row)

    zeros = jnp.zeros((PAD, width), jnp.float32)
    grad[end:, :] = zeros
    diag[end:, :] = zeros + 1.0
    first[end:, :] = zeros
    part1[:PAD, :] = zeros
    part2[:PAD, :] = zeros

    def gradients(at, size):
        here, there = pl.ds(at, size), pl.ds(at + PAD, size)
        g = pieces[0][here, :]
        for piece in pieces[1:]:
            g = g + piece[here, :]
        g = g * scale
        grad[there, :] = g
        diag[there, :] = decay_rate * diag_in[here, :] + g * g

    def bands(at, size):
        here, there = pl.ds(at, size), pl.ds(at + PAD, size)
        g = grad[there, :]
        g1 = grad[pl.ds(at + PAD + 1, size), :]
        g2 = grad[pl.ds(at + PAD + 2, size), :]
        first[there, :] = decay_rate * first_in[here, :] + g * g1
        second[there, :] = decay_rate * second_in[here, :] + g * g2

    def values(at, size):
        there = pl.ds(at + PAD, size)
        after = pl.ds(at + PAD + 1, size)
        later = pl.ds(at + PAD + 2, size)
        v, p1, p2 = solved(
            grad[there, :],
            grad[after, :],
            grad[later, :],
            diag[there, :] + damping,
            diag[after, :] + damping,
            diag[later, :] + damping,
            first[there, :],
            first[after, :],
            second[there, :],
        )
        part1[there, :] = p1
        part2[there, :] = p2
        update[pl.ds(at, size), :] = (
            v - part1[pl.ds(at + PAD - 1, size), :] - part2[pl.ds(at + PAD - 2, size), :]
        )

    def over(work, low, high):
        for at in range(low, high, step):
            work(at, min(step, high - at))

    stores = []

    def send(source, pad, k, c, low, high):
        copy = pltpu.make_async_copy(
            source.at[low + pad : high + pad, :], outs[k].at[low:high, :], out_sems.at[k, c]
        )
        copy.start()
        stores.append(copy)

    for c in range(chunks):
        for copy in loads[c]:
            copy.wait()
        last = c == chunks - 1
        low, high = c * chunk, (c + 1) * chunk
        over(gradients, low, high)
        send(diag, PAD, 1, c, low, high)
        low, high = max(low - TILE, 0), high if last else high - TILE
        over(bands, low, high)
        send(first, PAD, 2, c, low, high)
        send(second, PAD, 3, c, low, high)
        low, high = max(c * chunk - 2 * TILE, 0), high if last else high - TILE
        over(values, low, high)
        send(update, 0, 0, c, low, high)

    tops = [grad[PAD : PAD + TILE, :], diag[PAD : PAD + TILE, :], first[PAD : PAD + TILE, :]]
    tops.append(update[:TILE, :])
    tails = [r[end - TILE : end, :] for r in (grad, diag, first, second)]
    tails.append(update[rows - TILE :, :])
    tails += [r[end - TILE : end, :] for r in (part1, part2)]
    for k, tile in enumerate(tops + tails):
        edges[k * TILE : (k + 1) * TILE, :] = tile
    for copy in stores:
        copy.wait()


def border(rows, shards, parts, *refs):
    edges, far, near, across = refs[:4]
    outs = refs[7:10]
    work, tiles, sems = refs[10:]

    def edge(k, at, size):
        return edges[k * TILE + at : k * TILE + at + size, :]

    shard = lax.axis_index("fsdp")
    even = lax.rem(shard, 2) == 0
    near_rows, far_rows = near[...], far[...]
    if parts > 1:
        half = 1.0 / parts
        near_rows = jnp.concatenate([(near_rows[0:2] + across[0:2, :]) * half, near_rows[2:8]])
        far_rows = jnp.concatenate([(far_rows[0:2] + across[2:4, :]) * half, far_rows[2:8]])
    before = jnp.where(even, far_rows, near_rows)
    after = jnp.where(even, near_rows, far_rows)
    work[0:8, :] = jnp.where(shard == 0, 0.0, before)
    work[8:16, :] = jnp.where(shard == shards - 1, 0.0, after)

    g = work[0:2, :]
    g_next = edge(0, 0, 2)
    d = decay_rate * work[2:4, :] + g * g + damping
    d_next = edge(1, 0, 2) + damping
    g1 = jnp.concatenate([g[1:2], g_next[0:1]])
    d1 = jnp.concatenate([d[1:2], d_next[0:1]])
    f = decay_rate * work[4:6, :] + g * g1
    s = decay_rate * work[6:8, :] + g * g_next
    c = jnp.concatenate([f[1:2], edge(2, 0, 1)])
    _, p1, p2 = solved(g, g1, g_next, d, d1, d_next, f, c, s)
    tiles[0:8, :] = edges[3 * TILE : 4 * TILE, :]
    tiles[0:1, :] = tiles[0:1, :] - p1[1:2] - p2[0:1]
    tiles[1:2, :] = tiles[1:2, :] - p2[1:2]

    g = edge(4, 6, 2)
    g_next = work[8:10, :]
    present = work[14:16, :]
    d = edge(5, 6, 2) + damping
    d_next = (
        decay_rate * work[10:12, :] + g_next * g_next + present * damping + (1.0 - present)
    )
    g1 = jnp.concatenate([g[1:2], g_next[0:1]])
    d1 = jnp.concatenate([d[1:2], d_next[0:1]])
    f_last = (edge(6, 7, 1) + g[1:2] * g_next[0:1]) * present[0:1]
    f = jnp.concatenate([edge(6, 6, 1), f_last])
    s = (edge(7, 6, 2) + g * g_next) * present
    f_next = decay_rate * work[12:13, :] + g_next[0:1] * g_next[1:2]
    c = jnp.concatenate([f_last, f_next])
    v, p1, _ = solved(g, g1, g_next, d, d1, d_next, f, c, s)
    tiles[8:16, :] = edges[8 * TILE : 9 * TILE, :]
    tiles[14:15, :] = v[0:1] - edge(9, 5, 1) - edge(10, 4, 1)
    tiles[15:16, :] = v[1:2] - p1[0:1] - edge(10, 5, 1)
    tiles[16:24, :] = edges[6 * TILE : 7 * TILE, :]
    tiles[23:24, :] = f_last
    tiles[24:32, :] = edges[7 * TILE : 8 * TILE, :]
    tiles[30:32, :] = s

    copies = [
        pltpu.make_async_copy(tiles.at[0:8, :], outs[0].at[0:TILE, :], sems.at[0]),
        pltpu.make_async_copy(tiles.at[8:16, :], outs[0].at[rows - TILE : rows, :], sems.at[1]),
        pltpu.make_async_copy(tiles.at[16:24, :], outs[1].at[rows - TILE : rows, :], sems.at[2]),
        pltpu.make_async_copy(tiles.at[24:32, :], outs[2].at[rows - TILE : rows, :], sems.at[3]),
    ]
    for copy in copies:
        copy.start()
    for copy in copies:
        copy.wait()


def matching(shards, low):
    turn = []
    partner = {}
    for i in range(low, shards - 1, 2):
        partner[i], partner[i + 1] = i + 1, i
    for i in range(shards):
        for core in range(2):
            target = (partner[i], core) if i in partner else (i, 1 - core)
            turn.append((2 * i + core, 2 * target[0] + target[1]))
    return turn


def body(partials, diag_stat, first_stat, second_stat):
    own = partials[0]
    rows, width = own.shape
    replicas = lax.axis_size("replica")
    shards = lax.axis_size("fsdp")
    scale = 1.0 / replicas
    shard = lax.axis_index("fsdp")
    axes = ("fsdp", "replica")
    paired = replicas == 2

    shape = jax.ShapeDtypeStruct((rows, width), jnp.float32)
    vmem = pl.BlockSpec(memory_space=pltpu.VMEM)
    hbm = pl.BlockSpec(memory_space=pl.ANY)
    params = pltpu.CompilerParams(vmem_limit_bytes=24 * 2**20)

    def swap(block):
        return lax.ppermute(block, "replica", [(0, 1), (1, 0)])

    def stay(block):
        return pltpu.with_memory_space_constraint(block, pltpu.HBM)

    stats = (diag_stat, first_stat, second_stat)
    held = [stay(x) for x in (own, *stats)]
    small = pltpu.VMEM((TILE, width), jnp.float32)
    if paired:
        far, near = pl.pallas_call(
            functools.partial(collect, rows),
            out_shape=(small,) * 2,
            in_specs=[hbm] * 4,
            out_specs=(vmem,) * 2,
            scratch_shapes=[
                pltpu.VMEM((8 * TILE, width), jnp.float32),
                pltpu.SemaphoreType.DMA((8,)),
            ],
            compiler_params=params,
            name="collect",
        )(*held)
        pieces = [own, swap(own)]
        far = lax.ppermute(far, axes, matching(shards, 1))
        near = lax.ppermute(near, axes, matching(shards, 0))
    else:
        pieces = [lax.psum(own, "replica") * scale]
        scale = 1.0
        tail = rows - 2
        ones = jnp.ones((2, width), jnp.float32)
        last = jnp.concatenate([x[tail:] for x in (*pieces, *stats)])
        head = jnp.concatenate([x[:2] for x in (*pieces, *stats[:2])] + [ones])
        even = shard % 2 == 0
        before = lax.ppermute(last, "fsdp", [(i, i + 1) for i in range(shards - 1)])
        after = lax.ppermute(head, "fsdp", [(i + 1, i) for i in range(shards - 1)])
        near, far = jnp.where(even, after, before), jnp.where(even, before, after)

    parts = len(pieces)
    pieces_in = [held[0], *pieces[1:]] if paired else [stay(pieces[0])]
    whole = pltpu.VMEM((rows, width), jnp.float32)
    padded = pltpu.VMEM((rows + 2 * PAD, width), jnp.float32)
    chunk = 256 if rows % 256 == 0 else rows
    update, diag_next, first_next, second_next, edges = pl.pallas_call(
        functools.partial(interior, parts, scale, rows, chunk, 64),
        out_shape=(shape,) * 4 + (pltpu.VMEM((11 * TILE, width), jnp.float32),),
        in_specs=[hbm] + [vmem] * (parts - 1) + [hbm] * 3,
        out_specs=(hbm,) * 4 + (vmem,),
        scratch_shapes=[whole] * 4
        + [padded] * 6
        + [whole]
        + [pltpu.SemaphoreType.DMA((4, rows // chunk))] * 2,
        compiler_params=params,
        cost_estimate=pl.CostEstimate(
            flops=45 * rows * width, bytes_accessed=36 * rows * width, transcendentals=0
        ),
        name="interior",
    )(*pieces_in, *held[1:])

    far, near, edges = lax.optimization_barrier((far, near, edges))
    across = near
    if paired:
        across = swap(
            pl.pallas_call(
                join,
                out_shape=small,
                in_specs=[vmem] * 2,
                out_specs=vmem,
                compiler_params=params,
                name="join",
            )(far, near)
        )

    update, first_next, second_next = pl.pallas_call(
        functools.partial(border, rows, shards, parts),
        out_shape=(shape,) * 3,
        in_specs=[vmem] * 4 + [hbm] * 3,
        out_specs=(hbm,) * 3,
        input_output_aliases={4: 0, 5: 1, 6: 2},
        scratch_shapes=[
            pltpu.VMEM((16, width), jnp.float32),
            pltpu.VMEM((32, width), jnp.float32),
            pltpu.SemaphoreType.DMA((4,)),
        ],
        compiler_params=params,
        name="border",
    )(edges, far, near, across, update, first_next, second_next)
    return update, diag_next, first_next, second_next


def solution(mesh):
    return jax.shard_map(
        body,
        mesh=mesh,
        in_specs=(P("replica", "fsdp", None), P("fsdp", None), P("fsdp", None), P("fsdp", None)),
        out_specs=(P("fsdp", None), P("fsdp", None), P("fsdp", None), P("fsdp", None)),
        check_vma=False,
    )
```

```python
import functools

import jax
import jax.numpy as jnp
from jax import lax
from jax.experimental import pallas as pl
from jax.experimental.pallas import tpu as pltpu
from jax.sharding import PartitionSpec as P

decay_rate = 0.95
damping = 0.01
PAD = 8
TILE = 8


def solved(g, g1, g2, d, upper, lower, f, c, s):
    det = upper * lower - c * c
    n1 = lower * f - c * s
    n2 = upper * s - c * f
    schur = d * det - f * n1 - s * n2
    top = g * det - n1 * g1 - n2 * g2
    w = top / (schur * det)
    return w * det, w * n1, w * n2


def collect(rows, own, diag, first, second, far, near, tiles, sems):
    width = tiles.shape[1]
    copies = []
    for k, source in enumerate((own, diag, first, second)):
        for half, at in enumerate((0, rows - TILE)):
            row = (2 * k + half) * TILE
            copies.append(
                pltpu.make_async_copy(
                    source.at[at : at + TILE, :],
                    tiles.at[row : row + TILE, :],
                    sems.at[2 * k + half],
                )
            )
    for copy in copies:
        copy.start()
    for copy in copies:
        copy.wait()
    head = [tiles[2 * k * TILE : 2 * k * TILE + 2, :] for k in range(3)]
    head.append(jnp.ones((2, width), jnp.float32))
    last = [tiles[(2 * k + 2) * TILE - 2 : (2 * k + 2) * TILE, :] for k in range(4)]
    even = lax.rem(lax.axis_index("fsdp"), 2) == 0

    def fill(out, blocks):
        for k, block in enumerate(blocks):
            out[2 * k : 2 * k + 2, :] = block

    @pl.when(even)
    def _():
        fill(near, last)
        fill(far, head)

    @pl.when(jnp.logical_not(even))
    def _():
        fill(near, head)
        fill(far, last)


def join(far, near, out):
    out[0:2, :] = near[0:2, :]
    out[2:4, :] = far[0:2, :]
    out[4:8, :] = jnp.zeros((4, out.shape[1]), jnp.float32)


def interior(parts, scale, rows, chunk, step, *refs):
    pieces = refs[:parts]
    diag_in, first_in, second_in = refs[parts : parts + 3]
    outs = refs[parts + 3 : parts + 7]
    edges = refs[parts + 7]
    grad, diag, first, second, part1, part2, update, sems = refs[parts + 8 :]
    width = edges.shape[1]
    end = PAD + rows
    chunks = rows // chunk

    zeros = jnp.zeros((PAD, width), jnp.float32)
    grad[end:, :] = zeros
    diag[end:, :] = zeros + 1.0
    first[end:, :] = zeros
    part1[:PAD, :] = zeros
    part2[:PAD, :] = zeros

    def gradients(at, size):
        here, there = pl.ds(at, size), pl.ds(at + PAD, size)
        g = pieces[0][here, :]
        for piece in pieces[1:]:
            g = g + piece[here, :]
        g = g * scale
        grad[there, :] = g
        diag[there, :] = decay_rate * diag_in[here, :] + g * g

    def bands(at, size):
        here, there = pl.ds(at, size), pl.ds(at + PAD, size)
        g = grad[there, :]
        g1 = grad[pl.ds(at + PAD + 1, size), :]
        g2 = grad[pl.ds(at + PAD + 2, size), :]
        first[there, :] = decay_rate * first_in[here, :] + g * g1
        second[there, :] = decay_rate * second_in[here, :] + g * g2

    def values(at, size):
        there = pl.ds(at + PAD, size)
        after = pl.ds(at + PAD + 1, size)
        later = pl.ds(at + PAD + 2, size)
        v, p1, p2 = solved(
            grad[there, :],
            grad[after, :],
            grad[later, :],
            diag[there, :] + damping,
            diag[after, :] + damping,
            diag[later, :] + damping,
            first[there, :],
            first[after, :],
            second[there, :],
        )
        part1[there, :] = p1
        part2[there, :] = p2
        update[pl.ds(at, size), :] = (
            v - part1[pl.ds(at + PAD - 1, size), :] - part2[pl.ds(at + PAD - 2, size), :]
        )

    def over(work, low, high):
        for at in range(low, high, step):
            work(at, min(step, high - at))

    stores = []

    def send(source, pad, k, c, low, high):
        copy = pltpu.make_async_copy(
            source.at[low + pad : high + pad, :], outs[k].at[low:high, :], sems.at[k, c]
        )
        copy.start()
        stores.append(copy)

    for c in range(chunks):
        last = c == chunks - 1
        low, high = c * chunk, (c + 1) * chunk
        over(gradients, low, high)
        send(diag, PAD, 1, c, low, high)
        low, high = max(low - TILE, 0), high if last else high - TILE
        over(bands, low, high)
        send(first, PAD, 2, c, low, high)
        send(second, PAD, 3, c, low, high)
        low, high = max(c * chunk - 2 * TILE, 0), high if last else high - TILE
        over(values, low, high)
        send(update, 0, 0, c, low, high)

    tops = [grad[PAD : PAD + TILE, :], diag[PAD : PAD + TILE, :], first[PAD : PAD + TILE, :]]
    tops.append(update[:TILE, :])
    tails = [r[end - TILE : end, :] for r in (grad, diag, first, second)]
    tails.append(update[rows - TILE :, :])
    tails += [r[end - TILE : end, :] for r in (part1, part2)]
    for k, tile in enumerate(tops + tails):
        edges[k * TILE : (k + 1) * TILE, :] = tile
    for copy in stores:
        copy.wait()


def border(rows, shards, parts, *refs):
    edges, far, near, across = refs[:4]
    outs = refs[7:10]
    work, tiles, sems = refs[10:]

    def edge(k, at, size):
        return edges[k * TILE + at : k * TILE + at + size, :]

    shard = lax.axis_index("fsdp")
    even = lax.rem(shard, 2) == 0
    near_rows, far_rows = near[...], far[...]
    if parts > 1:
        half = 1.0 / parts
        near_rows = jnp.concatenate([(near_rows[0:2] + across[0:2, :]) * half, near_rows[2:8]])
        far_rows = jnp.concatenate([(far_rows[0:2] + across[2:4, :]) * half, far_rows[2:8]])
    before = jnp.where(even, far_rows, near_rows)
    after = jnp.where(even, near_rows, far_rows)
    work[0:8, :] = jnp.where(shard == 0, 0.0, before)
    work[8:16, :] = jnp.where(shard == shards - 1, 0.0, after)

    g = work[0:2, :]
    g_next = edge(0, 0, 2)
    d = decay_rate * work[2:4, :] + g * g + damping
    d_next = edge(1, 0, 2) + damping
    g1 = jnp.concatenate([g[1:2], g_next[0:1]])
    d1 = jnp.concatenate([d[1:2], d_next[0:1]])
    f = decay_rate * work[4:6, :] + g * g1
    s = decay_rate * work[6:8, :] + g * g_next
    c = jnp.concatenate([f[1:2], edge(2, 0, 1)])
    _, p1, p2 = solved(g, g1, g_next, d, d1, d_next, f, c, s)
    tiles[0:8, :] = edges[3 * TILE : 4 * TILE, :]
    tiles[0:1, :] = tiles[0:1, :] - p1[1:2] - p2[0:1]
    tiles[1:2, :] = tiles[1:2, :] - p2[1:2]

    g = edge(4, 6, 2)
    g_next = work[8:10, :]
    present = work[14:16, :]
    d = edge(5, 6, 2) + damping
    d_next = (
        decay_rate * work[10:12, :] + g_next * g_next + present * damping + (1.0 - present)
    )
    g1 = jnp.concatenate([g[1:2], g_next[0:1]])
    d1 = jnp.concatenate([d[1:2], d_next[0:1]])
    f_last = (edge(6, 7, 1) + g[1:2] * g_next[0:1]) * present[0:1]
    f = jnp.concatenate([edge(6, 6, 1), f_last])
    s = (edge(7, 6, 2) + g * g_next) * present
    f_next = decay_rate * work[12:13, :] + g_next[0:1] * g_next[1:2]
    c = jnp.concatenate([f_last, f_next])
    v, p1, _ = solved(g, g1, g_next, d, d1, d_next, f, c, s)
    tiles[8:16, :] = edges[8 * TILE : 9 * TILE, :]
    tiles[14:15, :] = v[0:1] - edge(9, 5, 1) - edge(10, 4, 1)
    tiles[15:16, :] = v[1:2] - p1[0:1] - edge(10, 5, 1)
    tiles[16:24, :] = edges[6 * TILE : 7 * TILE, :]
    tiles[23:24, :] = f_last
    tiles[24:32, :] = edges[7 * TILE : 8 * TILE, :]
    tiles[30:32, :] = s

    copies = [
        pltpu.make_async_copy(tiles.at[0:8, :], outs[0].at[0:TILE, :], sems.at[0]),
        pltpu.make_async_copy(tiles.at[8:16, :], outs[0].at[rows - TILE : rows, :], sems.at[1]),
        pltpu.make_async_copy(tiles.at[16:24, :], outs[1].at[rows - TILE : rows, :], sems.at[2]),
        pltpu.make_async_copy(tiles.at[24:32, :], outs[2].at[rows - TILE : rows, :], sems.at[3]),
    ]
    for copy in copies:
        copy.start()
    for copy in copies:
        copy.wait()


def matching(shards, low):
    turn = []
    partner = {}
    for i in range(low, shards - 1, 2):
        partner[i], partner[i + 1] = i + 1, i
    for i in range(shards):
        for core in range(2):
            target = (partner[i], core) if i in partner else (i, 1 - core)
            turn.append((2 * i + core, 2 * target[0] + target[1]))
    return turn


def body(partials, diag_stat, first_stat, second_stat):
    own = partials[0]
    rows, width = own.shape
    replicas = lax.axis_size("replica")
    shards = lax.axis_size("fsdp")
    scale = 1.0 / replicas
    shard = lax.axis_index("fsdp")
    axes = ("fsdp", "replica")
    paired = replicas == 2

    shape = jax.ShapeDtypeStruct((rows, width), jnp.float32)
    vmem = pl.BlockSpec(memory_space=pltpu.VMEM)
    hbm = pl.BlockSpec(memory_space=pl.ANY)
    params = pltpu.CompilerParams(vmem_limit_bytes=24 * 2**20)

    def swap(block):
        return lax.ppermute(block, "replica", [(0, 1), (1, 0)])

    def stay(block):
        return pltpu.with_memory_space_constraint(block, pltpu.HBM)

    stats = (diag_stat, first_stat, second_stat)
    held = [stay(x) for x in (own, *stats)]
    small = pltpu.VMEM((TILE, width), jnp.float32)
    if paired:
        far, near = pl.pallas_call(
            functools.partial(collect, rows),
            out_shape=(small,) * 2,
            in_specs=[hbm] * 4,
            out_specs=(vmem,) * 2,
            scratch_shapes=[
                pltpu.VMEM((8 * TILE, width), jnp.float32),
                pltpu.SemaphoreType.DMA((8,)),
            ],
            compiler_params=params,
            name="collect",
        )(*held)
        pieces = [own, swap(own)]
        far = lax.ppermute(far, axes, matching(shards, 1))
        near = lax.ppermute(near, axes, matching(shards, 0))
    else:
        pieces = [lax.psum(own, "replica") * scale]
        scale = 1.0
        tail = rows - 2
        ones = jnp.ones((2, width), jnp.float32)
        last = jnp.concatenate([x[tail:] for x in (*pieces, *stats)])
        head = jnp.concatenate([x[:2] for x in (*pieces, *stats[:2])] + [ones])
        even = shard % 2 == 0
        before = lax.ppermute(last, "fsdp", [(i, i + 1) for i in range(shards - 1)])
        after = lax.ppermute(head, "fsdp", [(i + 1, i) for i in range(shards - 1)])
        near, far = jnp.where(even, after, before), jnp.where(even, before, after)

    parts = len(pieces)
    whole = pltpu.VMEM((rows, width), jnp.float32)
    padded = pltpu.VMEM((rows + 2 * PAD, width), jnp.float32)
    chunk = 256 if rows % 256 == 0 else rows
    update, diag_next, first_next, second_next, edges = pl.pallas_call(
        functools.partial(interior, parts, scale, rows, chunk, 64),
        out_shape=(shape,) * 4 + (pltpu.VMEM((11 * TILE, width), jnp.float32),),
        in_specs=[vmem] * (parts + 3),
        out_specs=(hbm,) * 4 + (vmem,),
        scratch_shapes=[padded] * 6 + [whole, pltpu.SemaphoreType.DMA((4, rows // chunk))],
        compiler_params=params,
        cost_estimate=pl.CostEstimate(
            flops=45 * rows * width, bytes_accessed=36 * rows * width, transcendentals=0
        ),
        name="interior",
    )(*[pltpu.with_memory_space_constraint(x, pltpu.VMEM) for x in (*pieces, *stats)])

    far, near, edges = lax.optimization_barrier((far, near, edges))
    across = near
    if paired:
        across = swap(
            pl.pallas_call(
                join,
                out_shape=small,
                in_specs=[vmem] * 2,
                out_specs=vmem,
                compiler_params=params,
                name="join",
            )(far, near)
        )

    update, first_next, second_next = pl.pallas_call(
        functools.partial(border, rows, shards, parts),
        out_shape=(shape,) * 3,
        in_specs=[vmem] * 4 + [hbm] * 3,
        out_specs=(hbm,) * 3,
        input_output_aliases={4: 0, 5: 1, 6: 2},
        scratch_shapes=[
            pltpu.VMEM((16, width), jnp.float32),
            pltpu.VMEM((32, width), jnp.float32),
            pltpu.SemaphoreType.DMA((4,)),
        ],
        compiler_params=params,
        name="border",
    )(edges, far, near, across, update, first_next, second_next)
    return update, diag_next, first_next, second_next


def solution(mesh):
    return jax.shard_map(
        body,
        mesh=mesh,
        in_specs=(P("replica", "fsdp", None), P("fsdp", None), P("fsdp", None), P("fsdp", None)),
        out_specs=(P("fsdp", None), P("fsdp", None), P("fsdp", None), P("fsdp", None)),
        check_vma=False,
    )
```

```python
import functools

import jax
import jax.numpy as jnp
from jax import lax
from jax.experimental import pallas as pl
from jax.experimental.pallas import tpu as pltpu
from jax.sharding import PartitionSpec as P

decay_rate = 0.95
damping = 0.01
PAD = 8
TILE = 8


def solved(g, g1, g2, d, upper, lower, f, c, s):
    det = upper * lower - c * c
    n1 = lower * f - c * s
    n2 = upper * s - c * f
    schur = d * det - f * n1 - s * n2
    top = g * det - n1 * g1 - n2 * g2
    w = top / (schur * det)
    return w * det, w * n1, w * n2


def over(work, low, high, step):
    for at in range(low, high, step):
        work(at, min(step, high - at))


def collect(rows, own, diag, first, second, far, near, tiles, sems):
    width = tiles.shape[1]
    copies = []
    for k, source in enumerate((own, diag, first, second)):
        for half, at in enumerate((0, rows - TILE)):
            row = (2 * k + half) * TILE
            copies.append(
                pltpu.make_async_copy(
                    source.at[at : at + TILE, :],
                    tiles.at[row : row + TILE, :],
                    sems.at[2 * k + half],
                )
            )
    for copy in copies:
        copy.start()
    for copy in copies:
        copy.wait()
    head = [tiles[2 * k * TILE : 2 * k * TILE + 2, :] for k in range(3)]
    head.append(jnp.ones((2, width), jnp.float32))
    last = [tiles[(2 * k + 2) * TILE - 2 : (2 * k + 2) * TILE, :] for k in range(4)]
    even = lax.rem(lax.axis_index("fsdp"), 2) == 0

    def fill(out, blocks):
        for k, block in enumerate(blocks):
            out[2 * k : 2 * k + 2, :] = block

    @pl.when(even)
    def _():
        fill(near, last)
        fill(far, head)

    @pl.when(jnp.logical_not(even))
    def _():
        fill(near, head)
        fill(far, last)


def ready(scale, rows, near, other, out):
    even = lax.rem(lax.axis_index("fsdp"), 2) == 0
    out[2:8, :] = near[2:8, :]

    @pl.when(even)
    def _():
        out[0:2, :] = (near[0:2, :] + other[rows - 2 : rows, :]) * scale

    @pl.when(jnp.logical_not(even))
    def _():
        out[0:2, :] = (near[0:2, :] + other[0:2, :]) * scale


def bands(parts, scale, rows, chunk, step, *refs):
    pieces = refs[:parts]
    diag_in, first_in, second_in = refs[parts : parts + 3]
    outs = refs[parts + 3 : parts + 6]
    grad, diag, first, second, sems = refs[parts + 6 :]
    width = diag_in.shape[1]
    end = PAD + rows
    chunks = rows // chunk

    zeros = jnp.zeros((PAD, width), jnp.float32)
    for padded, edge in ((grad, zeros), (diag, zeros + 1.0), (first, zeros), (second, zeros)):
        padded[:PAD, :] = edge
        padded[end:, :] = edge

    def gradients(at, size):
        here, there = pl.ds(at, size), pl.ds(at + PAD, size)
        g = pieces[0][here, :]
        for piece in pieces[1:]:
            g = g + piece[here, :]
        g = g * scale
        grad[there, :] = g
        diag[there, :] = decay_rate * diag_in[here, :] + g * g

    def products(at, size):
        here, there = pl.ds(at, size), pl.ds(at + PAD, size)
        g = grad[there, :]
        g1 = grad[pl.ds(at + PAD + 1, size), :]
        g2 = grad[pl.ds(at + PAD + 2, size), :]
        first[there, :] = decay_rate * first_in[here, :] + g * g1
        second[there, :] = decay_rate * second_in[here, :] + g * g2

    stores = []

    def send(source, k, c, low, high):
        copy = pltpu.make_async_copy(
            source.at[low + PAD : high + PAD, :], outs[k].at[low:high, :], sems.at[k, c]
        )
        copy.start()
        stores.append(copy)

    for c in range(chunks):
        low, high = c * chunk, (c + 1) * chunk
        over(gradients, low, high, step)
        send(diag, 0, c, low, high)
        low, high = max(low - TILE, 0), high if c == chunks - 1 else high - TILE
        over(products, low, high, step)
        send(first, 1, c, low, high)
        send(second, 2, c, low, high)
    for copy in stores:
        copy.wait()


def updates(rows, chunk, step, *refs):
    grad, diag, first, second, out, edges, part1, part2, update, sems = refs
    width = grad.shape[1]
    end = PAD + rows
    zeros = jnp.zeros((PAD, width), jnp.float32)
    part1[:PAD, :] = zeros
    part2[:PAD, :] = zeros

    def values(at, size):
        there = pl.ds(at + PAD, size)
        after = pl.ds(at + PAD + 1, size)
        later = pl.ds(at + PAD + 2, size)
        v, p1, p2 = solved(
            grad[there, :],
            grad[after, :],
            grad[later, :],
            diag[there, :] + damping,
            diag[after, :] + damping,
            diag[later, :] + damping,
            first[there, :],
            first[after, :],
            second[there, :],
        )
        part1[there, :] = p1
        part2[there, :] = p2
        update[pl.ds(at, size), :] = (
            v - part1[pl.ds(at + PAD - 1, size), :] - part2[pl.ds(at + PAD - 2, size), :]
        )

    stores = []
    for c in range(rows // chunk):
        low, high = c * chunk, (c + 1) * chunk
        over(values, low, high, step)
        copy = pltpu.make_async_copy(update.at[low:high, :], out.at[low:high, :], sems.at[c])
        copy.start()
        stores.append(copy)

    tops = [grad[PAD : PAD + TILE, :], diag[PAD : PAD + TILE, :], first[PAD : PAD + TILE, :]]
    tops.append(update[:TILE, :])
    tails = [r[end - TILE : end, :] for r in (grad, diag, first, second)]
    tails.append(update[rows - TILE :, :])
    tails += [r[end - TILE : end, :] for r in (part1, part2)]
    for k, tile in enumerate(tops + tails):
        edges[k * TILE : (k + 1) * TILE, :] = tile
    for copy in stores:
        copy.wait()


def border(rows, shards, parts, *refs):
    edges, far, near, across = refs[:4]
    outs = refs[7:10]
    work, tiles, sems = refs[10:]

    def edge(k, at, size):
        return edges[k * TILE + at : k * TILE + at + size, :]

    shard = lax.axis_index("fsdp")
    even = lax.rem(shard, 2) == 0
    near_rows, far_rows = near[...], far[...]
    if parts > 1:
        far_sum = (far_rows[0:2] + across[0:2, :]) * (1.0 / parts)
        far_rows = jnp.concatenate([far_sum, far_rows[2:8]])
    before = jnp.where(even, far_rows, near_rows)
    after = jnp.where(even, near_rows, far_rows)
    work[0:8, :] = jnp.where(shard == 0, 0.0, before)
    work[8:16, :] = jnp.where(shard == shards - 1, 0.0, after)

    g = work[0:2, :]
    g_next = edge(0, 0, 2)
    d = decay_rate * work[2:4, :] + g * g + damping
    d_next = edge(1, 0, 2) + damping
    g1 = jnp.concatenate([g[1:2], g_next[0:1]])
    d1 = jnp.concatenate([d[1:2], d_next[0:1]])
    f = decay_rate * work[4:6, :] + g * g1
    s = decay_rate * work[6:8, :] + g * g_next
    c = jnp.concatenate([f[1:2], edge(2, 0, 1)])
    _, p1, p2 = solved(g, g1, g_next, d, d1, d_next, f, c, s)
    tiles[0:8, :] = edges[3 * TILE : 4 * TILE, :]
    tiles[0:1, :] = tiles[0:1, :] - p1[1:2] - p2[0:1]
    tiles[1:2, :] = tiles[1:2, :] - p2[1:2]

    g = edge(4, 6, 2)
    g_next = work[8:10, :]
    present = work[14:16, :]
    d = edge(5, 6, 2) + damping
    d_next = (
        decay_rate * work[10:12, :] + g_next * g_next + present * damping + (1.0 - present)
    )
    g1 = jnp.concatenate([g[1:2], g_next[0:1]])
    d1 = jnp.concatenate([d[1:2], d_next[0:1]])
    f_last = (edge(6, 7, 1) + g[1:2] * g_next[0:1]) * present[0:1]
    f = jnp.concatenate([edge(6, 6, 1), f_last])
    s = (edge(7, 6, 2) + g * g_next) * present
    f_next = decay_rate * work[12:13, :] + g_next[0:1] * g_next[1:2]
    c = jnp.concatenate([f_last, f_next])
    v, p1, _ = solved(g, g1, g_next, d, d1, d_next, f, c, s)
    tiles[8:16, :] = edges[8 * TILE : 9 * TILE, :]
    tiles[14:15, :] = v[0:1] - edge(9, 5, 1) - edge(10, 4, 1)
    tiles[15:16, :] = v[1:2] - p1[0:1] - edge(10, 5, 1)
    tiles[16:24, :] = edges[6 * TILE : 7 * TILE, :]
    tiles[23:24, :] = f_last
    tiles[24:32, :] = edges[7 * TILE : 8 * TILE, :]
    tiles[30:32, :] = s

    copies = [
        pltpu.make_async_copy(tiles.at[0:8, :], outs[0].at[0:TILE, :], sems.at[0]),
        pltpu.make_async_copy(tiles.at[8:16, :], outs[0].at[rows - TILE : rows, :], sems.at[1]),
        pltpu.make_async_copy(tiles.at[16:24, :], outs[1].at[rows - TILE : rows, :], sems.at[2]),
        pltpu.make_async_copy(tiles.at[24:32, :], outs[2].at[rows - TILE : rows, :], sems.at[3]),
    ]
    for copy in copies:
        copy.start()
    for copy in copies:
        copy.wait()


def matching(shards, low):
    turn = []
    partner = {}
    for i in range(low, shards - 1, 2):
        partner[i], partner[i + 1] = i + 1, i
    for i in range(shards):
        for core in range(2):
            target = (partner[i], core) if i in partner else (i, 1 - core)
            turn.append((2 * i + core, 2 * target[0] + target[1]))
    return turn


def body(partials, diag_stat, first_stat, second_stat):
    own = partials[0]
    rows, width = own.shape
    replicas = lax.axis_size("replica")
    shards = lax.axis_size("fsdp")
    scale = 1.0 / replicas
    shard = lax.axis_index("fsdp")
    axes = ("fsdp", "replica")
    paired = replicas == 2

    shape = jax.ShapeDtypeStruct((rows, width), jnp.float32)
    vmem = pl.BlockSpec(memory_space=pltpu.VMEM)
    hbm = pl.BlockSpec(memory_space=pl.ANY)
    params = pltpu.CompilerParams(vmem_limit_bytes=24 * 2**20)

    def swap(block):
        return lax.ppermute(block, "replica", [(0, 1), (1, 0)])

    def stay(block):
        return pltpu.with_memory_space_constraint(block, pltpu.HBM)

    stats = (diag_stat, first_stat, second_stat)
    held = [stay(x) for x in (own, *stats)]
    small = pltpu.VMEM((TILE, width), jnp.float32)
    if paired:
        far, near = pl.pallas_call(
            functools.partial(collect, rows),
            out_shape=(small,) * 2,
            in_specs=[hbm] * 4,
            out_specs=(vmem,) * 2,
            scratch_shapes=[
                pltpu.VMEM((8 * TILE, width), jnp.float32),
                pltpu.SemaphoreType.DMA((8,)),
            ],
            compiler_params=params,
            name="collect",
        )(*held)
        pieces = [own, swap(own)]
        far = lax.ppermute(far, axes, matching(shards, 1))
        near = pl.pallas_call(
            functools.partial(ready, scale, rows),
            out_shape=small,
            in_specs=[vmem] * 2,
            out_specs=vmem,
            compiler_params=params,
            name="ready",
        )(near, pieces[1])
        near = lax.ppermute(near, axes, matching(shards, 0))
    else:
        pieces = [lax.psum(own, "replica") * scale]
        scale = 1.0
        tail = rows - 2
        ones = jnp.ones((2, width), jnp.float32)
        last = jnp.concatenate([x[tail:] for x in (*pieces, *stats)])
        head = jnp.concatenate([x[:2] for x in (*pieces, *stats[:2])] + [ones])
        even = shard % 2 == 0
        before = lax.ppermute(last, "fsdp", [(i, i + 1) for i in range(shards - 1)])
        after = lax.ppermute(head, "fsdp", [(i + 1, i) for i in range(shards - 1)])
        near, far = jnp.where(even, after, before), jnp.where(even, before, after)

    parts = len(pieces)
    whole = pltpu.VMEM((rows, width), jnp.float32)
    padded = pltpu.VMEM((rows + 2 * PAD, width), jnp.float32)
    chunk = 256 if rows % 256 == 0 else rows
    cost = 20 * rows * width
    diag_next, first_next, second_next, *work = pl.pallas_call(
        functools.partial(bands, parts, scale, rows, chunk, 64),
        out_shape=(shape,) * 3 + (padded,) * 4,
        in_specs=[vmem] * (parts + 3),
        out_specs=(hbm,) * 3 + (vmem,) * 4,
        scratch_shapes=[pltpu.SemaphoreType.DMA((3, rows // chunk))],
        compiler_params=params,
        cost_estimate=pl.CostEstimate(flops=cost, bytes_accessed=cost, transcendentals=0),
        name="bands",
    )(*[pltpu.with_memory_space_constraint(x, pltpu.VMEM) for x in (*pieces, *stats)])
    far, work[0] = lax.optimization_barrier((far, work[0]))
    across = swap(far) if paired else far
    update, edges = pl.pallas_call(
        functools.partial(updates, rows, chunk, 64),
        out_shape=(shape, pltpu.VMEM((11 * TILE, width), jnp.float32)),
        in_specs=[vmem] * 4,
        out_specs=(hbm, vmem),
        scratch_shapes=[padded] * 2 + [whole, pltpu.SemaphoreType.DMA((rows // chunk,))],
        compiler_params=params,
        cost_estimate=pl.CostEstimate(flops=cost, bytes_accessed=cost, transcendentals=0),
        name="updates",
    )(*[pltpu.with_memory_space_constraint(x, pltpu.VMEM) for x in work])

    update, first_next, second_next = pl.pallas_call(
        functools.partial(border, rows, shards, parts),
        out_shape=(shape,) * 3,
        in_specs=[vmem] * 4 + [hbm] * 3,
        out_specs=(hbm,) * 3,
        input_output_aliases={4: 0, 5: 1, 6: 2},
        scratch_shapes=[
            pltpu.VMEM((16, width), jnp.float32),
            pltpu.VMEM((32, width), jnp.float32),
            pltpu.SemaphoreType.DMA((4,)),
        ],
        compiler_params=params,
        name="border",
    )(edges, far, near, across, update, first_next, second_next)
    return update, diag_next, first_next, second_next


def solution(mesh):
    return jax.shard_map(
        body,
        mesh=mesh,
        in_specs=(P("replica", "fsdp", None), P("fsdp", None), P("fsdp", None), P("fsdp", None)),
        out_specs=(P("fsdp", None), P("fsdp", None), P("fsdp", None), P("fsdp", None)),
        check_vma=False,
    )
```

```python
import functools

import jax
import jax.numpy as jnp
from jax import lax
from jax.experimental import pallas as pl
from jax.experimental.pallas import tpu as pltpu
from jax.sharding import PartitionSpec as P

decay_rate = 0.95
damping = 0.01
PAD = 8
TILE = 8


def solved(g, g1, g2, d, upper, lower, f, c, s):
    det = upper * lower - c * c
    n1 = lower * f - c * s
    n2 = upper * s - c * f
    schur = d * det - f * n1 - s * n2
    top = g * det - n1 * g1 - n2 * g2
    w = top / (schur * det)
    return w * det, w * n1, w * n2


def collect(rows, own, diag, first, second, far, near, tiles, sems):
    width = tiles.shape[1]
    copies = []
    for k, source in enumerate((own, diag, first, second)):
        for half, at in enumerate((0, rows - TILE)):
            row = (2 * k + half) * TILE
            copies.append(
                pltpu.make_async_copy(
                    source.at[at : at + TILE, :],
                    tiles.at[row : row + TILE, :],
                    sems.at[2 * k + half],
                )
            )
    for copy in copies:
        copy.start()
    for copy in copies:
        copy.wait()
    head = [tiles[2 * k * TILE : 2 * k * TILE + 2, :] for k in range(3)]
    head.append(jnp.ones((2, width), jnp.float32))
    last = [tiles[(2 * k + 2) * TILE - 2 : (2 * k + 2) * TILE, :] for k in range(4)]
    even = lax.rem(lax.axis_index("fsdp"), 2) == 0

    def fill(out, blocks):
        for k, block in enumerate(blocks):
            out[2 * k : 2 * k + 2, :] = block

    @pl.when(even)
    def _():
        fill(near, last)
        fill(far, head)

    @pl.when(jnp.logical_not(even))
    def _():
        fill(near, head)
        fill(far, last)


def ready(scale, rows, far, near, other, far_out, near_out):
    even = lax.rem(lax.axis_index("fsdp"), 2) == 0
    for out, block in ((far_out, far), (near_out, near)):
        out[2:8, :] = block[2:8, :]

    def fill(out, block, at):
        out[0:2, :] = (block[0:2, :] + other[at : at + 2, :]) * scale

    @pl.when(even)
    def _():
        fill(far_out, far, 0)
        fill(near_out, near, rows - 2)

    @pl.when(jnp.logical_not(even))
    def _():
        fill(far_out, far, rows - 2)
        fill(near_out, near, 0)


def interior(parts, early, scale, rows, chunk, step, *refs):
    chosen = lax.axis_index("fsdp") == 0

    @pl.when(chosen if early else jnp.logical_not(chosen))
    def _():
        everything(parts, scale, rows, chunk, step, refs[: parts + 3], refs[-13:])


def everything(parts, scale, rows, chunk, step, ins, rest):
    pieces = ins[:parts]
    diag_in, first_in, second_in = ins[parts:]
    outs, edges = rest[:4], rest[4]
    grad, diag, first, second, part1, part2, update, sems = rest[5:]
    width = edges.shape[1]
    end = PAD + rows
    chunks = rows // chunk

    zeros = jnp.zeros((PAD, width), jnp.float32)
    grad[end:, :] = zeros
    diag[end:, :] = zeros + 1.0
    first[end:, :] = zeros
    part1[:PAD, :] = zeros
    part2[:PAD, :] = zeros

    def gradients(at, size):
        here, there = pl.ds(at, size), pl.ds(at + PAD, size)
        g = pieces[0][here, :]
        for piece in pieces[1:]:
            g = g + piece[here, :]
        g = g * scale
        grad[there, :] = g
        diag[there, :] = decay_rate * diag_in[here, :] + g * g

    def bands(at, size):
        here, there = pl.ds(at, size), pl.ds(at + PAD, size)
        g = grad[there, :]
        g1 = grad[pl.ds(at + PAD + 1, size), :]
        g2 = grad[pl.ds(at + PAD + 2, size), :]
        first[there, :] = decay_rate * first_in[here, :] + g * g1
        second[there, :] = decay_rate * second_in[here, :] + g * g2

    def values(at, size):
        there = pl.ds(at + PAD, size)
        after = pl.ds(at + PAD + 1, size)
        later = pl.ds(at + PAD + 2, size)
        v, p1, p2 = solved(
            grad[there, :],
            grad[after, :],
            grad[later, :],
            diag[there, :] + damping,
            diag[after, :] + damping,
            diag[later, :] + damping,
            first[there, :],
            first[after, :],
            second[there, :],
        )
        part1[there, :] = p1
        part2[there, :] = p2
        update[pl.ds(at, size), :] = (
            v - part1[pl.ds(at + PAD - 1, size), :] - part2[pl.ds(at + PAD - 2, size), :]
        )

    def over(work, low, high):
        for at in range(low, high, step):
            work(at, min(step, high - at))

    stores = []

    def send(source, pad, k, c, low, high):
        copy = pltpu.make_async_copy(
            source.at[low + pad : high + pad, :], outs[k].at[low:high, :], sems.at[k, c]
        )
        copy.start()
        stores.append(copy)

    for c in range(chunks):
        last = c == chunks - 1
        low, high = c * chunk, (c + 1) * chunk
        over(gradients, low, high)
        send(diag, PAD, 1, c, low, high)
        low, high = max(low - TILE, 0), high if last else high - TILE
        over(bands, low, high)
        send(first, PAD, 2, c, low, high)
        send(second, PAD, 3, c, low, high)
        low, high = max(c * chunk - 2 * TILE, 0), high if last else high - TILE
        over(values, low, high)
        send(update, 0, 0, c, low, high)

    tops = [grad[PAD : PAD + TILE, :], diag[PAD : PAD + TILE, :], first[PAD : PAD + TILE, :]]
    tops.append(update[:TILE, :])
    tails = [r[end - TILE : end, :] for r in (grad, diag, first, second)]
    tails.append(update[rows - TILE :, :])
    tails += [r[end - TILE : end, :] for r in (part1, part2)]
    for k, tile in enumerate(tops + tails):
        edges[k * TILE : (k + 1) * TILE, :] = tile
    for copy in stores:
        copy.wait()


def border(rows, shards, *refs):
    edges, far, near = refs[:3]
    outs = refs[6:9]
    work, tiles, sems = refs[9:]

    def edge(k, at, size):
        return edges[k * TILE + at : k * TILE + at + size, :]

    shard = lax.axis_index("fsdp")
    even = lax.rem(shard, 2) == 0
    far_rows, near_rows = far[...], near[...]
    before = jnp.where(even, far_rows, near_rows)
    after = jnp.where(even, near_rows, far_rows)
    work[0:8, :] = jnp.where(shard == 0, 0.0, before)
    work[8:16, :] = jnp.where(shard == shards - 1, 0.0, after)

    g = work[0:2, :]
    g_next = edge(0, 0, 2)
    d = decay_rate * work[2:4, :] + g * g + damping
    d_next = edge(1, 0, 2) + damping
    g1 = jnp.concatenate([g[1:2], g_next[0:1]])
    d1 = jnp.concatenate([d[1:2], d_next[0:1]])
    f = decay_rate * work[4:6, :] + g * g1
    s = decay_rate * work[6:8, :] + g * g_next
    c = jnp.concatenate([f[1:2], edge(2, 0, 1)])
    _, p1, p2 = solved(g, g1, g_next, d, d1, d_next, f, c, s)
    tiles[0:8, :] = edges[3 * TILE : 4 * TILE, :]
    tiles[0:1, :] = tiles[0:1, :] - p1[1:2] - p2[0:1]
    tiles[1:2, :] = tiles[1:2, :] - p2[1:2]

    g = edge(4, 6, 2)
    g_next = work[8:10, :]
    present = work[14:16, :]
    d = edge(5, 6, 2) + damping
    d_next = (
        decay_rate * work[10:12, :] + g_next * g_next + present * damping + (1.0 - present)
    )
    g1 = jnp.concatenate([g[1:2], g_next[0:1]])
    d1 = jnp.concatenate([d[1:2], d_next[0:1]])
    f_last = (edge(6, 7, 1) + g[1:2] * g_next[0:1]) * present[0:1]
    f = jnp.concatenate([edge(6, 6, 1), f_last])
    s = (edge(7, 6, 2) + g * g_next) * present
    f_next = decay_rate * work[12:13, :] + g_next[0:1] * g_next[1:2]
    c = jnp.concatenate([f_last, f_next])
    v, p1, _ = solved(g, g1, g_next, d, d1, d_next, f, c, s)
    tiles[8:16, :] = edges[8 * TILE : 9 * TILE, :]
    tiles[14:15, :] = v[0:1] - edge(9, 5, 1) - edge(10, 4, 1)
    tiles[15:16, :] = v[1:2] - p1[0:1] - edge(10, 5, 1)
    tiles[16:24, :] = edges[6 * TILE : 7 * TILE, :]
    tiles[23:24, :] = f_last
    tiles[24:32, :] = edges[7 * TILE : 8 * TILE, :]
    tiles[30:32, :] = s

    copies = [
        pltpu.make_async_copy(tiles.at[0:8, :], outs[0].at[0:TILE, :], sems.at[0]),
        pltpu.make_async_copy(tiles.at[8:16, :], outs[0].at[rows - TILE : rows, :], sems.at[1]),
        pltpu.make_async_copy(tiles.at[16:24, :], outs[1].at[rows - TILE : rows, :], sems.at[2]),
        pltpu.make_async_copy(tiles.at[24:32, :], outs[2].at[rows - TILE : rows, :], sems.at[3]),
    ]
    for copy in copies:
        copy.start()
    for copy in copies:
        copy.wait()


def matching(shards, replicas, low):
    partner = {}
    for i in range(low, shards - 1, 2):
        partner[i], partner[i + 1] = i + 1, i
    turn = []
    for i in range(shards):
        for r in range(replicas):
            target = (partner[i], r) if i in partner else (i, r ^ 1)
            turn.append((replicas * i + r, replicas * target[0] + target[1]))
    return turn


def body(partials, diag_stat, first_stat, second_stat):
    own = partials[0]
    rows, width = own.shape
    replicas = lax.axis_size("replica")
    shards = lax.axis_size("fsdp")
    scale = 1.0 / replicas
    shard = lax.axis_index("fsdp")
    axes = ("fsdp", "replica")
    paired = replicas == 2

    shape = jax.ShapeDtypeStruct((rows, width), jnp.float32)
    vmem = pl.BlockSpec(memory_space=pltpu.VMEM)
    hbm = pl.BlockSpec(memory_space=pl.ANY)
    params = pltpu.CompilerParams(vmem_limit_bytes=24 * 2**20)

    def swap(block):
        return lax.ppermute(block, "replica", [(0, 1), (1, 0)])

    def stay(block):
        return pltpu.with_memory_space_constraint(block, pltpu.HBM)

    stats = (diag_stat, first_stat, second_stat)
    held = [stay(x) for x in (own, *stats)]
    small = pltpu.VMEM((TILE, width), jnp.float32)
    if paired:
        far, near = pl.pallas_call(
            functools.partial(collect, rows),
            out_shape=(small,) * 2,
            in_specs=[hbm] * 4,
            out_specs=(vmem,) * 2,
            scratch_shapes=[
                pltpu.VMEM((8 * TILE, width), jnp.float32),
                pltpu.SemaphoreType.DMA((8,)),
            ],
            compiler_params=params,
            name="collect",
        )(*held)
        pieces = [own, swap(own)]
        far, near = pl.pallas_call(
            functools.partial(ready, scale, rows),
            out_shape=(small,) * 2,
            in_specs=[vmem] * 3,
            out_specs=(vmem,) * 2,
            compiler_params=params,
            name="ready",
        )(far, near, pieces[1])
    else:
        pieces = [lax.psum(own, "replica") * scale]
        scale = 1.0
        tail = rows - 2
        ones = jnp.ones((2, width), jnp.float32)
        last = jnp.concatenate([x[tail:] for x in (*pieces, *stats)])
        head = jnp.concatenate([x[:2] for x in (*pieces, *stats[:2])] + [ones])
        even = shard % 2 == 0
        far, near = jnp.where(even, head, last), jnp.where(even, last, head)

    parts = len(pieces)
    whole = pltpu.VMEM((rows, width), jnp.float32)
    padded = pltpu.VMEM((rows + 2 * PAD, width), jnp.float32)
    chunk = 256 if rows % 256 == 0 else rows
    inner = [pltpu.with_memory_space_constraint(x, pltpu.VMEM) for x in (*pieces, *stats)]
    edge_shape = pltpu.VMEM((11 * TILE, width), jnp.float32)

    def inside(early, *done):
        return pl.pallas_call(
            functools.partial(interior, parts, early, scale, rows, chunk, 64),
            out_shape=(shape,) * 4 + (edge_shape,),
            in_specs=[vmem] * (parts + 3) + ([hbm] * 4 + [vmem] if done else []),
            out_specs=(hbm,) * 4 + (vmem,),
            input_output_aliases={parts + 3 + k: k for k in range(len(done))},
            scratch_shapes=[padded] * 6 + [whole, pltpu.SemaphoreType.DMA((4, rows // chunk))],
            compiler_params=params,
            cost_estimate=pl.CostEstimate(
                flops=45 * rows * width, bytes_accessed=36 * rows * width, transcendentals=0
            ),
            name="early" if early else "late",
        )(*inner, *done)

    far = lax.ppermute(far, axes, matching(shards, replicas, 1))
    done = inside(True)
    near, *done = lax.optimization_barrier((near, *done))
    near = lax.ppermute(near, axes, matching(shards, replicas, 0))
    update, diag_next, first_next, second_next, edges = inside(False, *done)

    update, first_next, second_next = pl.pallas_call(
        functools.partial(border, rows, shards),
        out_shape=(shape,) * 3,
        in_specs=[vmem] * 3 + [hbm] * 3,
        out_specs=(hbm,) * 3,
        input_output_aliases={3: 0, 4: 1, 5: 2},
        scratch_shapes=[
            pltpu.VMEM((16, width), jnp.float32),
            pltpu.VMEM((32, width), jnp.float32),
            pltpu.SemaphoreType.DMA((4,)),
        ],
        compiler_params=params,
        name="border",
    )(edges, far, near, update, first_next, second_next)
    return update, diag_next, first_next, second_next


def solution(mesh):
    return jax.shard_map(
        body,
        mesh=mesh,
        in_specs=(P("replica", "fsdp", None), P("fsdp", None), P("fsdp", None), P("fsdp", None)),
        out_specs=(P("fsdp", None), P("fsdp", None), P("fsdp", None), P("fsdp", None)),
        check_vma=False,
    )
```

```python
import functools

import jax
import jax.numpy as jnp
from jax import lax
from jax.experimental import pallas as pl
from jax.experimental.pallas import tpu as pltpu
from jax.sharding import PartitionSpec as P

decay_rate = 0.95
damping = 0.01
PAD = 8
TILE = 8


def solved(g, g1, g2, d, upper, lower, f, c, s):
    det = upper * lower - c * c
    n1 = lower * f - c * s
    n2 = upper * s - c * f
    schur = d * det - f * n1 - s * n2
    top = g * det - n1 * g1 - n2 * g2
    w = top / (schur * det)
    return w * det, w * n1, w * n2


def peek(rows, own, tiles, sems):
    copies = [
        pltpu.make_async_copy(
            own.at[at : at + TILE, :], tiles.at[k * TILE : (k + 1) * TILE, :], sems.at[k]
        )
        for k, at in enumerate((0, rows - TILE))
    ]
    for copy in copies:
        copy.start()
    for copy in copies:
        copy.wait()


def gives_last():
    even = lax.rem(lax.axis_index("fsdp"), 2) == 0
    return even == (lax.axis_index("replica") == 0)


def collect(rows, diag, first, second, out, tiles, sems):
    width = tiles.shape[1]
    copies = []
    for k, source in enumerate((diag, first, second)):
        for half, at in enumerate((0, rows - TILE)):
            row = (2 * k + half) * TILE
            copies.append(
                pltpu.make_async_copy(
                    source.at[at : at + TILE, :],
                    tiles.at[row : row + TILE, :],
                    sems.at[2 * k + half],
                )
            )
    for copy in copies:
        copy.start()
    for copy in copies:
        copy.wait()
    out[0:2, :] = jnp.zeros((2, width), jnp.float32)
    last = gives_last()

    @pl.when(last)
    def _():
        for k in range(3):
            at = (2 * k + 2) * TILE
            out[2 * k + 2 : 2 * k + 4, :] = tiles[at - 2 : at, :]

    @pl.when(jnp.logical_not(last))
    def _():
        for k in range(2):
            at = 2 * k * TILE
            out[2 * k + 2 : 2 * k + 4, :] = tiles[at : at + 2, :]
        out[6:8, :] = jnp.ones((2, width), jnp.float32)


def ready(scale, stats, own, other, out):
    last = gives_last()
    out[2:8, :] = stats[2:8, :]

    @pl.when(last)
    def _():
        at = 2 * TILE - 2
        out[0:2, :] = (own[at : at + 2, :] + other[at : at + 2, :]) * scale

    @pl.when(jnp.logical_not(last))
    def _():
        out[0:2, :] = (own[0:2, :] + other[0:2, :]) * scale


def interior(parts, scale, rows, chunk, step, *refs):
    pieces = refs[:parts]
    diag_in, first_in, second_in = refs[parts : parts + 3]
    outs = refs[parts + 3 : parts + 7]
    edges = refs[parts + 7]
    grad, diag, first, second, part1, part2, update, sems = refs[parts + 8 :]
    width = edges.shape[1]
    end = PAD + rows
    chunks = rows // chunk

    zeros = jnp.zeros((PAD, width), jnp.float32)
    grad[end:, :] = zeros
    diag[end:, :] = zeros + 1.0
    first[end:, :] = zeros
    part1[:PAD, :] = zeros
    part2[:PAD, :] = zeros

    def gradients(at, size):
        here, there = pl.ds(at, size), pl.ds(at + PAD, size)
        g = pieces[0][here, :]
        for piece in pieces[1:]:
            g = g + piece[here, :]
        g = g * scale
        grad[there, :] = g
        diag[there, :] = decay_rate * diag_in[here, :] + g * g

    def bands(at, size):
        here, there = pl.ds(at, size), pl.ds(at + PAD, size)
        g = grad[there, :]
        g1 = grad[pl.ds(at + PAD + 1, size), :]
        g2 = grad[pl.ds(at + PAD + 2, size), :]
        first[there, :] = decay_rate * first_in[here, :] + g * g1
        second[there, :] = decay_rate * second_in[here, :] + g * g2

    def values(at, size):
        there = pl.ds(at + PAD, size)
        after = pl.ds(at + PAD + 1, size)
        later = pl.ds(at + PAD + 2, size)
        v, p1, p2 = solved(
            grad[there, :],
            grad[after, :],
            grad[later, :],
            diag[there, :] + damping,
            diag[after, :] + damping,
            diag[later, :] + damping,
            first[there, :],
            first[after, :],
            second[there, :],
        )
        part1[there, :] = p1
        part2[there, :] = p2
        update[pl.ds(at, size), :] = (
            v - part1[pl.ds(at + PAD - 1, size), :] - part2[pl.ds(at + PAD - 2, size), :]
        )

    def over(work, low, high):
        for at in range(low, high, step):
            work(at, min(step, high - at))

    stores = []

    def send(source, pad, k, c, low, high):
        copy = pltpu.make_async_copy(
            source.at[low + pad : high + pad, :], outs[k].at[low:high, :], sems.at[k, c]
        )
        copy.start()
        stores.append(copy)

    for c in range(chunks):
        last = c == chunks - 1
        low, high = c * chunk, (c + 1) * chunk
        over(gradients, low, high)
        send(diag, PAD, 1, c, low, high)
        low, high = max(low - TILE, 0), high if last else high - TILE
        over(bands, low, high)
        send(first, PAD, 2, c, low, high)
        send(second, PAD, 3, c, low, high)
        low, high = max(c * chunk - 2 * TILE, 0), high if last else high - TILE
        over(values, low, high)
        send(update, 0, 0, c, low, high)

    tops = [grad[PAD : PAD + TILE, :], diag[PAD : PAD + TILE, :], first[PAD : PAD + TILE, :]]
    tops.append(update[:TILE, :])
    tails = [r[end - TILE : end, :] for r in (grad, diag, first, second)]
    tails.append(update[rows - TILE :, :])
    tails += [r[end - TILE : end, :] for r in (part1, part2)]
    for k, tile in enumerate(tops + tails):
        edges[k * TILE : (k + 1) * TILE, :] = tile
    for copy in stores:
        copy.wait()


def border(rows, shards, paired, *refs):
    edges, near, far = refs[:3]
    outs = refs[6:9]
    work, tiles, sems = refs[9:]

    def edge(k, at, size):
        return edges[k * TILE + at : k * TILE + at + size, :]

    shard = lax.axis_index("fsdp")
    even = lax.rem(shard, 2) == 0
    near_rows, far_rows = near[...], far[...]
    if paired:
        low = lax.axis_index("replica") == 0
        near_rows, far_rows = (
            jnp.where(low, near_rows, far_rows),
            jnp.where(low, far_rows, near_rows),
        )
    before = jnp.where(even, far_rows, near_rows)
    after = jnp.where(even, near_rows, far_rows)
    work[0:8, :] = jnp.where(shard == 0, 0.0, before)
    work[8:16, :] = jnp.where(shard == shards - 1, 0.0, after)

    g = work[0:2, :]
    g_next = edge(0, 0, 2)
    d = decay_rate * work[2:4, :] + g * g + damping
    d_next = edge(1, 0, 2) + damping
    g1 = jnp.concatenate([g[1:2], g_next[0:1]])
    d1 = jnp.concatenate([d[1:2], d_next[0:1]])
    f = decay_rate * work[4:6, :] + g * g1
    s = decay_rate * work[6:8, :] + g * g_next
    c = jnp.concatenate([f[1:2], edge(2, 0, 1)])
    _, p1, p2 = solved(g, g1, g_next, d, d1, d_next, f, c, s)
    tiles[0:8, :] = edges[3 * TILE : 4 * TILE, :]
    tiles[0:1, :] = tiles[0:1, :] - p1[1:2] - p2[0:1]
    tiles[1:2, :] = tiles[1:2, :] - p2[1:2]

    g = edge(4, 6, 2)
    g_next = work[8:10, :]
    present = work[14:16, :]
    d = edge(5, 6, 2) + damping
    d_next = (
        decay_rate * work[10:12, :] + g_next * g_next + present * damping + (1.0 - present)
    )
    g1 = jnp.concatenate([g[1:2], g_next[0:1]])
    d1 = jnp.concatenate([d[1:2], d_next[0:1]])
    f_last = (edge(6, 7, 1) + g[1:2] * g_next[0:1]) * present[0:1]
    f = jnp.concatenate([edge(6, 6, 1), f_last])
    s = (edge(7, 6, 2) + g * g_next) * present
    f_next = decay_rate * work[12:13, :] + g_next[0:1] * g_next[1:2]
    c = jnp.concatenate([f_last, f_next])
    v, p1, _ = solved(g, g1, g_next, d, d1, d_next, f, c, s)
    tiles[8:16, :] = edges[8 * TILE : 9 * TILE, :]
    tiles[14:15, :] = v[0:1] - edge(9, 5, 1) - edge(10, 4, 1)
    tiles[15:16, :] = v[1:2] - p1[0:1] - edge(10, 5, 1)
    tiles[16:24, :] = edges[6 * TILE : 7 * TILE, :]
    tiles[23:24, :] = f_last
    tiles[24:32, :] = edges[7 * TILE : 8 * TILE, :]
    tiles[30:32, :] = s

    copies = [
        pltpu.make_async_copy(tiles.at[0:8, :], outs[0].at[0:TILE, :], sems.at[0]),
        pltpu.make_async_copy(tiles.at[8:16, :], outs[0].at[rows - TILE : rows, :], sems.at[1]),
        pltpu.make_async_copy(tiles.at[16:24, :], outs[1].at[rows - TILE : rows, :], sems.at[2]),
        pltpu.make_async_copy(tiles.at[24:32, :], outs[2].at[rows - TILE : rows, :], sems.at[3]),
    ]
    for copy in copies:
        copy.start()
    for copy in copies:
        copy.wait()


def trades(shards, replicas):
    turn = []
    for core in range(replicas):
        partner = {}
        for i in range(core, shards - 1, 2):
            partner[i], partner[i + 1] = i + 1, i
        for i in range(shards):
            turn.append((replicas * i + core, replicas * partner.get(i, i) + core))
    return sorted(turn)


def body(partials, diag_stat, first_stat, second_stat):
    own = partials[0]
    rows, width = own.shape
    replicas = lax.axis_size("replica")
    shards = lax.axis_size("fsdp")
    scale = 1.0 / replicas
    paired = replicas == 2

    shape = jax.ShapeDtypeStruct((rows, width), jnp.float32)
    vmem = pl.BlockSpec(memory_space=pltpu.VMEM)
    hbm = pl.BlockSpec(memory_space=pl.ANY)
    params = pltpu.CompilerParams(vmem_limit_bytes=24 * 2**20)

    def swap(block):
        return lax.ppermute(block, "replica", [(0, 1), (1, 0)])

    def stay(block):
        return pltpu.with_memory_space_constraint(block, pltpu.HBM)

    stats = (diag_stat, first_stat, second_stat)
    tile = pltpu.VMEM((TILE, width), jnp.float32)
    if paired:
        own_edges = pl.pallas_call(
            functools.partial(peek, rows),
            out_shape=pltpu.VMEM((2 * TILE, width), jnp.float32),
            in_specs=[hbm],
            out_specs=vmem,
            scratch_shapes=[pltpu.SemaphoreType.DMA((2,))],
            compiler_params=params,
            name="peek",
        )(stay(own))
        other_edges = swap(own_edges)
        message = pl.pallas_call(
            functools.partial(collect, rows),
            out_shape=tile,
            in_specs=[hbm] * 3,
            out_specs=vmem,
            scratch_shapes=[
                pltpu.VMEM((6 * TILE, width), jnp.float32),
                pltpu.SemaphoreType.DMA((6,)),
            ],
            compiler_params=params,
            name="collect",
        )(*[stay(x) for x in stats])
        pieces = [own, swap(own)]
        message = pl.pallas_call(
            functools.partial(ready, scale),
            out_shape=tile,
            in_specs=[vmem] * 3,
            out_specs=vmem,
            compiler_params=params,
            name="ready",
        )(message, own_edges, other_edges)
        near = lax.ppermute(message, ("fsdp", "replica"), trades(shards, replicas))
    else:
        pieces = [lax.psum(own, "replica") * scale]
        scale = 1.0
        tail = rows - 2
        ones = jnp.ones((2, width), jnp.float32)
        last = jnp.concatenate([x[tail:] for x in (*pieces, *stats)])
        head = jnp.concatenate([x[:2] for x in (*pieces, *stats[:2])] + [ones])
        before = lax.ppermute(last, "fsdp", [(i, i + 1) for i in range(shards - 1)])
        after = lax.ppermute(head, "fsdp", [(i + 1, i) for i in range(shards - 1)])
        even = lax.axis_index("fsdp") % 2 == 0
        near, far = jnp.where(even, after, before), jnp.where(even, before, after)

    parts = len(pieces)
    whole = pltpu.VMEM((rows, width), jnp.float32)
    padded = pltpu.VMEM((rows + 2 * PAD, width), jnp.float32)
    chunk = 256 if rows % 256 == 0 else rows
    update, diag_next, first_next, second_next, edges = pl.pallas_call(
        functools.partial(interior, parts, scale, rows, chunk, 64),
        out_shape=(shape,) * 4 + (pltpu.VMEM((11 * TILE, width), jnp.float32),),
        in_specs=[vmem] * (parts + 3),
        out_specs=(hbm,) * 4 + (vmem,),
        scratch_shapes=[padded] * 6 + [whole, pltpu.SemaphoreType.DMA((4, rows // chunk))],
        compiler_params=params,
        cost_estimate=pl.CostEstimate(
            flops=45 * rows * width, bytes_accessed=36 * rows * width, transcendentals=0
        ),
        name="interior",
    )(*[pltpu.with_memory_space_constraint(x, pltpu.VMEM) for x in (*pieces, *stats)])
    if paired:
        near, edges = lax.optimization_barrier((near, edges))
        far = swap(near)

    update, first_next, second_next = pl.pallas_call(
        functools.partial(border, rows, shards, paired),
        out_shape=(shape,) * 3,
        in_specs=[vmem] * 3 + [hbm] * 3,
        out_specs=(hbm,) * 3,
        input_output_aliases={3: 0, 4: 1, 5: 2},
        scratch_shapes=[
            pltpu.VMEM((16, width), jnp.float32),
            pltpu.VMEM((32, width), jnp.float32),
            pltpu.SemaphoreType.DMA((4,)),
        ],
        compiler_params=params,
        name="border",
    )(edges, near, far, update, first_next, second_next)
    return update, diag_next, first_next, second_next


def solution(mesh):
    return jax.shard_map(
        body,
        mesh=mesh,
        in_specs=(P("replica", "fsdp", None), P("fsdp", None), P("fsdp", None), P("fsdp", None)),
        out_specs=(P("fsdp", None), P("fsdp", None), P("fsdp", None), P("fsdp", None)),
        check_vma=False,
    )
```

```python
import functools

import jax
import jax.numpy as jnp
from jax import lax
from jax.experimental import pallas as pl
from jax.experimental.pallas import tpu as pltpu
from jax.sharding import PartitionSpec as P

decay_rate = 0.95
damping = 0.01
PAD = 8
TILE = 8


def solved(g, g1, g2, d, upper, lower, f, c, s):
    det = upper * lower - c * c
    n1 = lower * f - c * s
    n2 = upper * s - c * f
    schur = d * det - f * n1 - s * n2
    top = g * det - n1 * g1 - n2 * g2
    w = top / (schur * det)
    return w * det, w * n1, w * n2


def collect(rows, shards, own, diag, first, second, out, tiles, sems):
    width = tiles.shape[1]
    copies = []
    for k, source in enumerate((own, diag, first, second)):
        for half, at in enumerate((0, rows - TILE)):
            row = (2 * k + half) * TILE
            copies.append(
                pltpu.make_async_copy(
                    source.at[at : at + TILE, :],
                    tiles.at[row : row + TILE, :],
                    sems.at[2 * k + half],
                )
            )
    for copy in copies:
        copy.start()
    for copy in copies:
        copy.wait()
    last = gives_last(shards)

    @pl.when(last)
    def _():
        for k in range(4):
            at = (2 * k + 2) * TILE
            out[2 * k : 2 * k + 2, :] = tiles[at - 2 : at, :]

    @pl.when(jnp.logical_not(last))
    def _():
        for k in range(3):
            at = 2 * k * TILE
            out[2 * k : 2 * k + 2, :] = tiles[at : at + 2, :]
        out[6:8, :] = jnp.ones((2, width), jnp.float32)


def gives_last(shards):
    shard = lax.axis_index("fsdp")
    even = lax.rem(shard, 2) == 0
    up = even == (lax.axis_index("replica") == 0)
    return jnp.logical_and(jnp.logical_or(up, shard == 0), shard != shards - 1)


def ready(scale, rows, shards, block, other, out):
    last = gives_last(shards)
    out[2:8, :] = block[2:8, :]

    @pl.when(last)
    def _():
        out[0:2, :] = (block[0:2, :] + other[rows - 2 : rows, :]) * scale

    @pl.when(jnp.logical_not(last))
    def _():
        out[0:2, :] = (block[0:2, :] + other[0:2, :]) * scale


def interior(parts, scale, rows, chunk, step, *refs):
    pieces = refs[:parts]
    diag_in, first_in, second_in = refs[parts : parts + 3]
    outs = refs[parts + 3 : parts + 7]
    edges = refs[parts + 7]
    grad, diag, first, second, part1, part2, update, sems = refs[parts + 8 :]
    width = edges.shape[1]
    end = PAD + rows
    chunks = rows // chunk

    zeros = jnp.zeros((PAD, width), jnp.float32)
    grad[end:, :] = zeros
    diag[end:, :] = zeros + 1.0
    first[end:, :] = zeros
    part1[:PAD, :] = zeros
    part2[:PAD, :] = zeros

    def gradients(at, size):
        here, there = pl.ds(at, size), pl.ds(at + PAD, size)
        g = pieces[0][here, :]
        for piece in pieces[1:]:
            g = g + piece[here, :]
        g = g * scale
        grad[there, :] = g
        diag[there, :] = decay_rate * diag_in[here, :] + g * g

    def bands(at, size):
        here, there = pl.ds(at, size), pl.ds(at + PAD, size)
        g = grad[there, :]
        g1 = grad[pl.ds(at + PAD + 1, size), :]
        g2 = grad[pl.ds(at + PAD + 2, size), :]
        first[there, :] = decay_rate * first_in[here, :] + g * g1
        second[there, :] = decay_rate * second_in[here, :] + g * g2

    def values(at, size):
        there = pl.ds(at + PAD, size)
        after = pl.ds(at + PAD + 1, size)
        later = pl.ds(at + PAD + 2, size)
        v, p1, p2 = solved(
            grad[there, :],
            grad[after, :],
            grad[later, :],
            diag[there, :] + damping,
            diag[after, :] + damping,
            diag[later, :] + damping,
            first[there, :],
            first[after, :],
            second[there, :],
        )
        part1[there, :] = p1
        part2[there, :] = p2
        update[pl.ds(at, size), :] = (
            v - part1[pl.ds(at + PAD - 1, size), :] - part2[pl.ds(at + PAD - 2, size), :]
        )

    def over(work, low, high):
        for at in range(low, high, step):
            work(at, min(step, high - at))

    stores = []

    def send(source, pad, k, c, low, high):
        copy = pltpu.make_async_copy(
            source.at[low + pad : high + pad, :], outs[k].at[low:high, :], sems.at[k, c]
        )
        copy.start()
        stores.append(copy)

    for c in range(chunks):
        last = c == chunks - 1
        low, high = c * chunk, (c + 1) * chunk
        over(gradients, low, high)
        send(diag, PAD, 1, c, low, high)
        low, high = max(low - TILE, 0), high if last else high - TILE
        over(bands, low, high)
        send(first, PAD, 2, c, low, high)
        send(second, PAD, 3, c, low, high)
        low, high = max(c * chunk - 2 * TILE, 0), high if last else high - TILE
        over(values, low, high)
        send(update, 0, 0, c, low, high)

    tops = [grad[PAD : PAD + TILE, :], diag[PAD : PAD + TILE, :], first[PAD : PAD + TILE, :]]
    tops.append(update[:TILE, :])
    tails = [r[end - TILE : end, :] for r in (grad, diag, first, second)]
    tails.append(update[rows - TILE :, :])
    tails += [r[end - TILE : end, :] for r in (part1, part2)]
    for k, tile in enumerate(tops + tails):
        edges[k * TILE : (k + 1) * TILE, :] = tile
    for copy in stores:
        copy.wait()


def border(rows, shards, paired, *refs):
    edges, near, far = refs[:3]
    outs = refs[6:9]
    work, tiles, sems = refs[9:]

    def edge(k, at, size):
        return edges[k * TILE + at : k * TILE + at + size, :]

    shard = lax.axis_index("fsdp")
    even = lax.rem(shard, 2) == 0
    near_rows, far_rows = near[...], far[...]
    if paired:
        low = (lax.axis_index("replica") == 0) != (shard == 0)
        near_rows, far_rows = (
            jnp.where(low, near_rows, far_rows),
            jnp.where(low, far_rows, near_rows),
        )
    before = jnp.where(even, far_rows, near_rows)
    after = jnp.where(even, near_rows, far_rows)
    work[0:8, :] = jnp.where(shard == 0, 0.0, before)
    work[8:16, :] = jnp.where(shard == shards - 1, 0.0, after)

    g = work[0:2, :]
    g_next = edge(0, 0, 2)
    d = decay_rate * work[2:4, :] + g * g + damping
    d_next = edge(1, 0, 2) + damping
    g1 = jnp.concatenate([g[1:2], g_next[0:1]])
    d1 = jnp.concatenate([d[1:2], d_next[0:1]])
    f = decay_rate * work[4:6, :] + g * g1
    s = decay_rate * work[6:8, :] + g * g_next
    c = jnp.concatenate([f[1:2], edge(2, 0, 1)])
    _, p1, p2 = solved(g, g1, g_next, d, d1, d_next, f, c, s)
    tiles[0:8, :] = edges[3 * TILE : 4 * TILE, :]
    tiles[0:1, :] = tiles[0:1, :] - p1[1:2] - p2[0:1]
    tiles[1:2, :] = tiles[1:2, :] - p2[1:2]

    g = edge(4, 6, 2)
    g_next = work[8:10, :]
    present = work[14:16, :]
    d = edge(5, 6, 2) + damping
    d_next = (
        decay_rate * work[10:12, :] + g_next * g_next + present * damping + (1.0 - present)
    )
    g1 = jnp.concatenate([g[1:2], g_next[0:1]])
    d1 = jnp.concatenate([d[1:2], d_next[0:1]])
    f_last = (edge(6, 7, 1) + g[1:2] * g_next[0:1]) * present[0:1]
    f = jnp.concatenate([edge(6, 6, 1), f_last])
    s = (edge(7, 6, 2) + g * g_next) * present
    f_next = decay_rate * work[12:13, :] + g_next[0:1] * g_next[1:2]
    c = jnp.concatenate([f_last, f_next])
    v, p1, _ = solved(g, g1, g_next, d, d1, d_next, f, c, s)
    tiles[8:16, :] = edges[8 * TILE : 9 * TILE, :]
    tiles[14:15, :] = v[0:1] - edge(9, 5, 1) - edge(10, 4, 1)
    tiles[15:16, :] = v[1:2] - p1[0:1] - edge(10, 5, 1)
    tiles[16:24, :] = edges[6 * TILE : 7 * TILE, :]
    tiles[23:24, :] = f_last
    tiles[24:32, :] = edges[7 * TILE : 8 * TILE, :]
    tiles[30:32, :] = s

    copies = [
        pltpu.make_async_copy(tiles.at[0:8, :], outs[0].at[0:TILE, :], sems.at[0]),
        pltpu.make_async_copy(tiles.at[8:16, :], outs[0].at[rows - TILE : rows, :], sems.at[1]),
        pltpu.make_async_copy(tiles.at[16:24, :], outs[1].at[rows - TILE : rows, :], sems.at[2]),
        pltpu.make_async_copy(tiles.at[24:32, :], outs[2].at[rows - TILE : rows, :], sems.at[3]),
    ]
    for copy in copies:
        copy.start()
    for copy in copies:
        copy.wait()


def trades(shards):
    target = {}
    for core in range(2):
        for i in range(core, shards - 1, 2):
            target[i, core], target[i + 1, core] = (i + 1, core), (i, core)
    target[1, 0], target[0, 1] = (0, 1), (0, 0)
    core, end = shards % 2, shards - 1
    target[end, core], target[end, 1 - core] = (end, 1 - core), (end - 1, core)
    return sorted((2 * i + a, 2 * j + b) for (i, a), (j, b) in target.items())


def body(partials, diag_stat, first_stat, second_stat):
    own = partials[0]
    rows, width = own.shape
    replicas = lax.axis_size("replica")
    shards = lax.axis_size("fsdp")
    scale = 1.0 / replicas
    paired = replicas == 2 and shards > 3

    shape = jax.ShapeDtypeStruct((rows, width), jnp.float32)
    vmem = pl.BlockSpec(memory_space=pltpu.VMEM)
    hbm = pl.BlockSpec(memory_space=pl.ANY)
    params = pltpu.CompilerParams(vmem_limit_bytes=24 * 2**20)

    def swap(block):
        return lax.ppermute(block, "replica", [(0, 1), (1, 0)])

    def stay(block):
        return pltpu.with_memory_space_constraint(block, pltpu.HBM)

    stats = (diag_stat, first_stat, second_stat)
    tile = pltpu.VMEM((TILE, width), jnp.float32)
    if paired:
        pieces = [own, swap(own)]
        message = pl.pallas_call(
            functools.partial(collect, rows, shards),
            out_shape=tile,
            in_specs=[hbm] * 4,
            out_specs=vmem,
            scratch_shapes=[
                pltpu.VMEM((8 * TILE, width), jnp.float32),
                pltpu.SemaphoreType.DMA((8,)),
            ],
            compiler_params=params,
            name="collect",
        )(*[stay(x) for x in (own, *stats)])
        message = pl.pallas_call(
            functools.partial(ready, scale, rows, shards),
            out_shape=tile,
            in_specs=[vmem] * 2,
            out_specs=vmem,
            compiler_params=params,
            name="ready",
        )(message, pieces[1])
        near = lax.ppermute(message, ("fsdp", "replica"), trades(shards))
    else:
        pieces = [lax.psum(own, "replica") * scale]
        scale = 1.0
        tail = rows - 2
        ones = jnp.ones((2, width), jnp.float32)
        last = jnp.concatenate([x[tail:] for x in (*pieces, *stats)])
        head = jnp.concatenate([x[:2] for x in (*pieces, *stats[:2])] + [ones])
        before = lax.ppermute(last, "fsdp", [(i, i + 1) for i in range(shards - 1)])
        after = lax.ppermute(head, "fsdp", [(i + 1, i) for i in range(shards - 1)])
        even = lax.axis_index("fsdp") % 2 == 0
        near, far = jnp.where(even, after, before), jnp.where(even, before, after)

    parts = len(pieces)
    whole = pltpu.VMEM((rows, width), jnp.float32)
    padded = pltpu.VMEM((rows + 2 * PAD, width), jnp.float32)
    chunk = 256 if rows % 256 == 0 else rows
    update, diag_next, first_next, second_next, edges = pl.pallas_call(
        functools.partial(interior, parts, scale, rows, chunk, 64),
        out_shape=(shape,) * 4 + (pltpu.VMEM((11 * TILE, width), jnp.float32),),
        in_specs=[vmem] * (parts + 3),
        out_specs=(hbm,) * 4 + (vmem,),
        scratch_shapes=[padded] * 6 + [whole, pltpu.SemaphoreType.DMA((4, rows // chunk))],
        compiler_params=params,
        cost_estimate=pl.CostEstimate(
            flops=45 * rows * width, bytes_accessed=36 * rows * width, transcendentals=0
        ),
        name="interior",
    )(*[pltpu.with_memory_space_constraint(x, pltpu.VMEM) for x in (*pieces, *stats)])
    if paired:
        near, edges = lax.optimization_barrier((near, edges))
        far = swap(near)

    update, first_next, second_next = pl.pallas_call(
        functools.partial(border, rows, shards, paired),
        out_shape=(shape,) * 3,
        in_specs=[vmem] * 3 + [hbm] * 3,
        out_specs=(hbm,) * 3,
        input_output_aliases={3: 0, 4: 1, 5: 2},
        scratch_shapes=[
            pltpu.VMEM((16, width), jnp.float32),
            pltpu.VMEM((32, width), jnp.float32),
            pltpu.SemaphoreType.DMA((4,)),
        ],
        compiler_params=params,
        name="border",
    )(edges, near, far, update, first_next, second_next)
    return update, diag_next, first_next, second_next


def solution(mesh):
    return jax.shard_map(
        body,
        mesh=mesh,
        in_specs=(P("replica", "fsdp", None), P("fsdp", None), P("fsdp", None), P("fsdp", None)),
        out_specs=(P("fsdp", None), P("fsdp", None), P("fsdp", None), P("fsdp", None)),
        check_vma=False,
    )
```

```python
import functools

import jax
import jax.numpy as jnp
from jax import lax
from jax.experimental import pallas as pl
from jax.experimental.pallas import tpu as pltpu
from jax.sharding import PartitionSpec as P

decay_rate = 0.95
damping = 0.01
PAD = 8
TILE = 8


def solved(g, g1, g2, d, upper, lower, f, c, s):
    det = upper * lower - c * c
    n1 = lower * f - c * s
    n2 = upper * s - c * f
    schur = d * det - f * n1 - s * n2
    top = g * det - n1 * g1 - n2 * g2
    w = top / (schur * det)
    return w * det, w * n1, w * n2


def collect(rows, shards, own, diag, first, second, out, tiles, sems):
    width = tiles.shape[1]
    copies = []
    for k, source in enumerate((own, diag, first, second)):
        for half, at in enumerate((0, rows - TILE)):
            row = (2 * k + half) * TILE
            copies.append(
                pltpu.make_async_copy(
                    source.at[at : at + TILE, :],
                    tiles.at[row : row + TILE, :],
                    sems.at[2 * k + half],
                )
            )
    for copy in copies:
        copy.start()
    for copy in copies:
        copy.wait()
    last = gives_last(shards)

    @pl.when(last)
    def _():
        for k in range(4):
            at = (2 * k + 2) * TILE
            out[2 * k : 2 * k + 2, :] = tiles[at - 2 : at, :]

    @pl.when(jnp.logical_not(last))
    def _():
        for k in range(3):
            at = 2 * k * TILE
            out[2 * k : 2 * k + 2, :] = tiles[at : at + 2, :]
        out[6:8, :] = jnp.ones((2, width), jnp.float32)


def gives_last(shards):
    shard = lax.axis_index("fsdp")
    even = lax.rem(shard, 2) == 0
    up = even == (lax.axis_index("replica") == 0)
    return jnp.logical_and(jnp.logical_or(up, shard == 0), shard != shards - 1)


def ready(scale, rows, shards, block, other, out):
    last = gives_last(shards)
    out[2:8, :] = block[2:8, :]

    @pl.when(last)
    def _():
        out[0:2, :] = (block[0:2, :] + other[rows - 2 : rows, :]) * scale

    @pl.when(jnp.logical_not(last))
    def _():
        out[0:2, :] = (block[0:2, :] + other[0:2, :]) * scale


def interior(parts, scale, rows, chunk, step, *refs):
    pieces = refs[:parts]
    diag_in, first_in, second_in = refs[parts : parts + 3]
    outs = refs[parts + 3 : parts + 6]
    update, edges = refs[parts + 6 : parts + 8]
    grad, diag, first, second, part1, part2, sems = refs[parts + 8 :]
    width = edges.shape[1]
    end = PAD + rows
    chunks = rows // chunk

    zeros = jnp.zeros((PAD, width), jnp.float32)
    grad[end:, :] = zeros
    diag[end:, :] = zeros + 1.0
    first[end:, :] = zeros
    part1[:PAD, :] = zeros
    part2[:PAD, :] = zeros

    def gradients(at, size):
        here, there = pl.ds(at, size), pl.ds(at + PAD, size)
        g = pieces[0][here, :]
        for piece in pieces[1:]:
            g = g + piece[here, :]
        g = g * scale
        grad[there, :] = g
        diag[there, :] = decay_rate * diag_in[here, :] + g * g

    def bands(at, size):
        here, there = pl.ds(at, size), pl.ds(at + PAD, size)
        g = grad[there, :]
        g1 = grad[pl.ds(at + PAD + 1, size), :]
        g2 = grad[pl.ds(at + PAD + 2, size), :]
        first[there, :] = decay_rate * first_in[here, :] + g * g1
        second[there, :] = decay_rate * second_in[here, :] + g * g2

    def values(at, size):
        there = pl.ds(at + PAD, size)
        after = pl.ds(at + PAD + 1, size)
        later = pl.ds(at + PAD + 2, size)
        v, p1, p2 = solved(
            grad[there, :],
            grad[after, :],
            grad[later, :],
            diag[there, :] + damping,
            diag[after, :] + damping,
            diag[later, :] + damping,
            first[there, :],
            first[after, :],
            second[there, :],
        )
        part1[there, :] = p1
        part2[there, :] = p2
        update[pl.ds(at, size), :] = (
            v - part1[pl.ds(at + PAD - 1, size), :] - part2[pl.ds(at + PAD - 2, size), :]
        )

    def over(work, low, high):
        for at in range(low, high, step):
            work(at, min(step, high - at))

    stores = []

    def send(source, k, c, low, high):
        copy = pltpu.make_async_copy(
            source.at[low + PAD : high + PAD, :], outs[k].at[low:high, :], sems.at[k, c]
        )
        copy.start()
        stores.append(copy)

    for c in range(chunks):
        low, high = c * chunk, (c + 1) * chunk
        over(gradients, low, high)
        send(diag, 0, c, low, high)
        low, high = max(low - TILE, 0), high if c == chunks - 1 else high - TILE
        over(bands, low, high)
        send(first, 1, c, low, high)
        send(second, 2, c, low, high)
    over(values, 0, rows)

    tops = [grad[PAD : PAD + TILE, :], diag[PAD : PAD + TILE, :], first[PAD : PAD + TILE, :]]
    tops.append(update[:TILE, :])
    tails = [r[end - TILE : end, :] for r in (grad, diag, first, second)]
    tails.append(update[rows - TILE :, :])
    tails += [r[end - TILE : end, :] for r in (part1, part2)]
    for k, tile in enumerate(tops + tails):
        edges[k * TILE : (k + 1) * TILE, :] = tile
    for copy in stores:
        copy.wait()


def store(rows, chunk, update, out, sems):
    copies = []
    for c in range(rows // chunk):
        low, high = max(c * chunk, TILE), min((c + 1) * chunk, rows - TILE)
        copies.append(
            pltpu.make_async_copy(update.at[low:high, :], out.at[low:high, :], sems.at[c])
        )
    for copy in copies:
        copy.start()
    for copy in copies:
        copy.wait()


def border(rows, shards, paired, *refs):
    edges, near, far = refs[:3]
    outs = refs[6:9]
    work, tiles, sems = refs[9:]

    def edge(k, at, size):
        return edges[k * TILE + at : k * TILE + at + size, :]

    shard = lax.axis_index("fsdp")
    even = lax.rem(shard, 2) == 0
    near_rows, far_rows = near[...], far[...]
    if paired:
        low = (lax.axis_index("replica") == 0) != (shard == 0)
        near_rows, far_rows = (
            jnp.where(low, near_rows, far_rows),
            jnp.where(low, far_rows, near_rows),
        )
    before = jnp.where(even, far_rows, near_rows)
    after = jnp.where(even, near_rows, far_rows)
    work[0:8, :] = jnp.where(shard == 0, 0.0, before)
    work[8:16, :] = jnp.where(shard == shards - 1, 0.0, after)

    g = work[0:2, :]
    g_next = edge(0, 0, 2)
    d = decay_rate * work[2:4, :] + g * g + damping
    d_next = edge(1, 0, 2) + damping
    g1 = jnp.concatenate([g[1:2], g_next[0:1]])
    d1 = jnp.concatenate([d[1:2], d_next[0:1]])
    f = decay_rate * work[4:6, :] + g * g1
    s = decay_rate * work[6:8, :] + g * g_next
    c = jnp.concatenate([f[1:2], edge(2, 0, 1)])
    _, p1, p2 = solved(g, g1, g_next, d, d1, d_next, f, c, s)
    tiles[0:8, :] = edges[3 * TILE : 4 * TILE, :]
    tiles[0:1, :] = tiles[0:1, :] - p1[1:2] - p2[0:1]
    tiles[1:2, :] = tiles[1:2, :] - p2[1:2]

    g = edge(4, 6, 2)
    g_next = work[8:10, :]
    present = work[14:16, :]
    d = edge(5, 6, 2) + damping
    d_next = (
        decay_rate * work[10:12, :] + g_next * g_next + present * damping + (1.0 - present)
    )
    g1 = jnp.concatenate([g[1:2], g_next[0:1]])
    d1 = jnp.concatenate([d[1:2], d_next[0:1]])
    f_last = (edge(6, 7, 1) + g[1:2] * g_next[0:1]) * present[0:1]
    f = jnp.concatenate([edge(6, 6, 1), f_last])
    s = (edge(7, 6, 2) + g * g_next) * present
    f_next = decay_rate * work[12:13, :] + g_next[0:1] * g_next[1:2]
    c = jnp.concatenate([f_last, f_next])
    v, p1, _ = solved(g, g1, g_next, d, d1, d_next, f, c, s)
    tiles[8:16, :] = edges[8 * TILE : 9 * TILE, :]
    tiles[14:15, :] = v[0:1] - edge(9, 5, 1) - edge(10, 4, 1)
    tiles[15:16, :] = v[1:2] - p1[0:1] - edge(10, 5, 1)
    tiles[16:24, :] = edges[6 * TILE : 7 * TILE, :]
    tiles[23:24, :] = f_last
    tiles[24:32, :] = edges[7 * TILE : 8 * TILE, :]
    tiles[30:32, :] = s

    copies = [
        pltpu.make_async_copy(tiles.at[0:8, :], outs[0].at[0:TILE, :], sems.at[0]),
        pltpu.make_async_copy(tiles.at[8:16, :], outs[0].at[rows - TILE : rows, :], sems.at[1]),
        pltpu.make_async_copy(tiles.at[16:24, :], outs[1].at[rows - TILE : rows, :], sems.at[2]),
        pltpu.make_async_copy(tiles.at[24:32, :], outs[2].at[rows - TILE : rows, :], sems.at[3]),
    ]
    for copy in copies:
        copy.start()
    for copy in copies:
        copy.wait()


def trades(shards):
    target = {}
    for core in range(2):
        for i in range(core, shards - 1, 2):
            target[i, core], target[i + 1, core] = (i + 1, core), (i, core)
    target[1, 0], target[0, 1] = (0, 1), (0, 0)
    core, end = shards % 2, shards - 1
    target[end, core], target[end, 1 - core] = (end, 1 - core), (end - 1, core)
    return sorted((2 * i + a, 2 * j + b) for (i, a), (j, b) in target.items())


def body(partials, diag_stat, first_stat, second_stat):
    own = partials[0]
    rows, width = own.shape
    replicas = lax.axis_size("replica")
    shards = lax.axis_size("fsdp")
    scale = 1.0 / replicas
    paired = replicas == 2 and shards > 3

    shape = jax.ShapeDtypeStruct((rows, width), jnp.float32)
    vmem = pl.BlockSpec(memory_space=pltpu.VMEM)
    hbm = pl.BlockSpec(memory_space=pl.ANY)
    params = pltpu.CompilerParams(vmem_limit_bytes=24 * 2**20)

    def swap(block):
        return lax.ppermute(block, "replica", [(0, 1), (1, 0)])

    def stay(block):
        return pltpu.with_memory_space_constraint(block, pltpu.HBM)

    stats = (diag_stat, first_stat, second_stat)
    tile = pltpu.VMEM((TILE, width), jnp.float32)
    if paired:
        pieces = [own, swap(own)]
        message = pl.pallas_call(
            functools.partial(collect, rows, shards),
            out_shape=tile,
            in_specs=[hbm] * 4,
            out_specs=vmem,
            scratch_shapes=[
                pltpu.VMEM((8 * TILE, width), jnp.float32),
                pltpu.SemaphoreType.DMA((8,)),
            ],
            compiler_params=params,
            name="collect",
        )(*[stay(x) for x in (own, *stats)])
        message = pl.pallas_call(
            functools.partial(ready, scale, rows, shards),
            out_shape=tile,
            in_specs=[vmem] * 2,
            out_specs=vmem,
            compiler_params=params,
            name="ready",
        )(message, pieces[1])
        near = lax.ppermute(message, ("fsdp", "replica"), trades(shards))
    else:
        pieces = [lax.psum(own, "replica") * scale]
        scale = 1.0
        tail = rows - 2
        ones = jnp.ones((2, width), jnp.float32)
        last = jnp.concatenate([x[tail:] for x in (*pieces, *stats)])
        head = jnp.concatenate([x[:2] for x in (*pieces, *stats[:2])] + [ones])
        before = lax.ppermute(last, "fsdp", [(i, i + 1) for i in range(shards - 1)])
        after = lax.ppermute(head, "fsdp", [(i + 1, i) for i in range(shards - 1)])
        even = lax.axis_index("fsdp") % 2 == 0
        near, far = jnp.where(even, after, before), jnp.where(even, before, after)

    parts = len(pieces)
    whole = pltpu.VMEM((rows, width), jnp.float32)
    padded = pltpu.VMEM((rows + 2 * PAD, width), jnp.float32)
    chunk = 256 if rows % 256 == 0 else rows
    diag_next, first_next, second_next, update, edges = pl.pallas_call(
        functools.partial(interior, parts, scale, rows, chunk, 64),
        out_shape=(shape,) * 3 + (whole, pltpu.VMEM((11 * TILE, width), jnp.float32)),
        in_specs=[vmem] * (parts + 3),
        out_specs=(hbm,) * 3 + (vmem,) * 2,
        scratch_shapes=[padded] * 6 + [pltpu.SemaphoreType.DMA((3, rows // chunk))],
        compiler_params=params,
        cost_estimate=pl.CostEstimate(
            flops=45 * rows * width, bytes_accessed=36 * rows * width, transcendentals=0
        ),
        name="interior",
    )(*[pltpu.with_memory_space_constraint(x, pltpu.VMEM) for x in (*pieces, *stats)])
    if paired:
        near, edges = lax.optimization_barrier((near, edges))
        far = swap(near)
    update = pl.pallas_call(
        functools.partial(store, rows, chunk),
        out_shape=shape,
        in_specs=[vmem],
        out_specs=hbm,
        scratch_shapes=[pltpu.SemaphoreType.DMA((rows // chunk,))],
        compiler_params=params,
        cost_estimate=pl.CostEstimate(
            flops=0, bytes_accessed=8 * rows * width, transcendentals=0
        ),
        name="store",
    )(pltpu.with_memory_space_constraint(update, pltpu.VMEM))

    update, first_next, second_next = pl.pallas_call(
        functools.partial(border, rows, shards, paired),
        out_shape=(shape,) * 3,
        in_specs=[vmem] * 3 + [hbm] * 3,
        out_specs=(hbm,) * 3,
        input_output_aliases={3: 0, 4: 1, 5: 2},
        scratch_shapes=[
            pltpu.VMEM((16, width), jnp.float32),
            pltpu.VMEM((32, width), jnp.float32),
            pltpu.SemaphoreType.DMA((4,)),
        ],
        compiler_params=params,
        name="border",
    )(edges, near, far, update, first_next, second_next)
    return update, diag_next, first_next, second_next


def solution(mesh):
    return jax.shard_map(
        body,
        mesh=mesh,
        in_specs=(P("replica", "fsdp", None), P("fsdp", None), P("fsdp", None), P("fsdp", None)),
        out_specs=(P("fsdp", None), P("fsdp", None), P("fsdp", None), P("fsdp", None)),
        check_vma=False,
    )
```

```python
import functools

import jax
import jax.numpy as jnp
from jax import lax
from jax.experimental import pallas as pl
from jax.experimental.pallas import tpu as pltpu
from jax.sharding import PartitionSpec as P

decay_rate = 0.95
damping = 0.01
PAD = 8
TILE = 8


def solved(g, g1, g2, d, upper, lower, f, c, s):
    det = upper * lower - c * c
    n1 = lower * f - c * s
    n2 = upper * s - c * f
    schur = d * det - f * n1 - s * n2
    top = g * det - n1 * g1 - n2 * g2
    w = top / (schur * det)
    return w * det, w * n1, w * n2


def collect(rows, own, diag, first, second, far, near, tiles, sems):
    width = tiles.shape[1]
    copies = []
    for k, source in enumerate((own, diag, first, second)):
        for half, at in enumerate((0, rows - TILE)):
            row = (2 * k + half) * TILE
            copies.append(
                pltpu.make_async_copy(
                    source.at[at : at + TILE, :],
                    tiles.at[row : row + TILE, :],
                    sems.at[2 * k + half],
                )
            )
    for copy in copies:
        copy.start()
    for copy in copies:
        copy.wait()
    head = [tiles[2 * k * TILE : 2 * k * TILE + 2, :] for k in range(3)]
    head.append(jnp.ones((2, width), jnp.float32))
    last = [tiles[(2 * k + 2) * TILE - 2 : (2 * k + 2) * TILE, :] for k in range(4)]
    even = lax.rem(lax.axis_index("fsdp"), 2) == 0

    def fill(out, blocks):
        for k, block in enumerate(blocks):
            out[2 * k : 2 * k + 2, :] = block

    @pl.when(even)
    def _():
        fill(near, last)
        fill(far, head)

    @pl.when(jnp.logical_not(even))
    def _():
        fill(near, head)
        fill(far, last)


def ready(scale, rows, block, other, out):
    even = lax.rem(lax.axis_index("fsdp"), 2) == 0
    out[2:8, :] = block[2:8, :]

    @pl.when(even)
    def _():
        out[0:2, :] = (block[0:2, :] + other[0:2, :]) * scale

    @pl.when(jnp.logical_not(even))
    def _():
        out[0:2, :] = (block[0:2, :] + other[rows - 2 : rows, :]) * scale


def interior(parts, scale, rows, chunk, step, *refs):
    pieces = refs[:parts]
    diag_in, first_in, second_in = refs[parts : parts + 3]
    outs = refs[parts + 3 : parts + 6]
    update, edges = refs[parts + 6 : parts + 8]
    grad, diag, first, second, part1, part2, sems = refs[parts + 8 :]
    width = edges.shape[1]
    end = PAD + rows
    chunks = rows // chunk

    zeros = jnp.zeros((PAD, width), jnp.float32)
    grad[end:, :] = zeros
    diag[end:, :] = zeros + 1.0
    first[end:, :] = zeros
    part1[:PAD, :] = zeros
    part2[:PAD, :] = zeros

    def gradients(at, size):
        here, there = pl.ds(at, size), pl.ds(at + PAD, size)
        g = pieces[0][here, :]
        for piece in pieces[1:]:
            g = g + piece[here, :]
        g = g * scale
        grad[there, :] = g
        diag[there, :] = decay_rate * diag_in[here, :] + g * g

    def bands(at, size):
        here, there = pl.ds(at, size), pl.ds(at + PAD, size)
        g = grad[there, :]
        g1 = grad[pl.ds(at + PAD + 1, size), :]
        g2 = grad[pl.ds(at + PAD + 2, size), :]
        first[there, :] = decay_rate * first_in[here, :] + g * g1
        second[there, :] = decay_rate * second_in[here, :] + g * g2

    def values(at, size):
        there = pl.ds(at + PAD, size)
        after = pl.ds(at + PAD + 1, size)
        later = pl.ds(at + PAD + 2, size)
        v, p1, p2 = solved(
            grad[there, :],
            grad[after, :],
            grad[later, :],
            diag[there, :] + damping,
            diag[after, :] + damping,
            diag[later, :] + damping,
            first[there, :],
            first[after, :],
            second[there, :],
        )
        part1[there, :] = p1
        part2[there, :] = p2
        update[pl.ds(at, size), :] = (
            v - part1[pl.ds(at + PAD - 1, size), :] - part2[pl.ds(at + PAD - 2, size), :]
        )

    def over(work, low, high):
        for at in range(low, high, step):
            work(at, min(step, high - at))

    stores = []

    def send(source, k, c, low, high):
        copy = pltpu.make_async_copy(
            source.at[low + PAD : high + PAD, :], outs[k].at[low:high, :], sems.at[k, c]
        )
        copy.start()
        stores.append(copy)

    for c in range(chunks):
        low, high = c * chunk, (c + 1) * chunk
        over(gradients, low, high)
        send(diag, 0, c, low, high)
        low, high = max(low - TILE, 0), high if c == chunks - 1 else high - TILE
        over(bands, low, high)
        send(first, 1, c, low, high)
        send(second, 2, c, low, high)
    over(values, 0, rows)

    tops = [grad[PAD : PAD + TILE, :], diag[PAD : PAD + TILE, :], first[PAD : PAD + TILE, :]]
    tops.append(update[:TILE, :])
    tails = [r[end - TILE : end, :] for r in (grad, diag, first, second)]
    tails.append(update[rows - TILE :, :])
    tails += [r[end - TILE : end, :] for r in (part1, part2)]
    for k, tile in enumerate(tops + tails):
        edges[k * TILE : (k + 1) * TILE, :] = tile
    for copy in stores:
        copy.wait()


def store(rows, chunk, update, out, sems):
    copies = []
    for c in range(rows // chunk):
        low, high = max(c * chunk, TILE), min((c + 1) * chunk, rows - TILE)
        copies.append(
            pltpu.make_async_copy(update.at[low:high, :], out.at[low:high, :], sems.at[c])
        )
    for copy in copies:
        copy.start()
    for copy in copies:
        copy.wait()


def border(rows, shards, scale, turn, *refs):
    chosen = jnp.logical_or(lax.axis_index("replica") == 1, lax.axis_index("fsdp") == 0)
    if turn == 0:
        patch(rows, shards, scale, *refs)
    else:
        pl.when(chosen if turn == 1 else jnp.logical_not(chosen))(
            functools.partial(patch, rows, shards, scale, *refs)
        )


def patch(rows, shards, scale, *refs):
    edges, near, other, far = refs[:4]
    outs = refs[7:10]
    work, tiles, sems = refs[10:]

    def edge(k, at, size):
        return edges[k * TILE + at : k * TILE + at + size, :]

    shard = lax.axis_index("fsdp")
    even = lax.rem(shard, 2) == 0
    near_rows, far_rows = near[...], far[...]
    if scale != 1.0:
        near_sum = (near_rows[0:2] + other[0:2, :]) * scale
        near_rows = jnp.concatenate([near_sum, near_rows[2:8]])
    before = jnp.where(even, far_rows, near_rows)
    after = jnp.where(even, near_rows, far_rows)
    work[0:8, :] = jnp.where(shard == 0, 0.0, before)
    work[8:16, :] = jnp.where(shard == shards - 1, 0.0, after)

    g = work[0:2, :]
    g_next = edge(0, 0, 2)
    d = decay_rate * work[2:4, :] + g * g + damping
    d_next = edge(1, 0, 2) + damping
    g1 = jnp.concatenate([g[1:2], g_next[0:1]])
    d1 = jnp.concatenate([d[1:2], d_next[0:1]])
    f = decay_rate * work[4:6, :] + g * g1
    s = decay_rate * work[6:8, :] + g * g_next
    c = jnp.concatenate([f[1:2], edge(2, 0, 1)])
    _, p1, p2 = solved(g, g1, g_next, d, d1, d_next, f, c, s)
    tiles[0:8, :] = edges[3 * TILE : 4 * TILE, :]
    tiles[0:1, :] = tiles[0:1, :] - p1[1:2] - p2[0:1]
    tiles[1:2, :] = tiles[1:2, :] - p2[1:2]

    g = edge(4, 6, 2)
    g_next = work[8:10, :]
    present = work[14:16, :]
    d = edge(5, 6, 2) + damping
    d_next = (
        decay_rate * work[10:12, :] + g_next * g_next + present * damping + (1.0 - present)
    )
    g1 = jnp.concatenate([g[1:2], g_next[0:1]])
    d1 = jnp.concatenate([d[1:2], d_next[0:1]])
    f_last = (edge(6, 7, 1) + g[1:2] * g_next[0:1]) * present[0:1]
    f = jnp.concatenate([edge(6, 6, 1), f_last])
    s = (edge(7, 6, 2) + g * g_next) * present
    f_next = decay_rate * work[12:13, :] + g_next[0:1] * g_next[1:2]
    c = jnp.concatenate([f_last, f_next])
    v, p1, _ = solved(g, g1, g_next, d, d1, d_next, f, c, s)
    tiles[8:16, :] = edges[8 * TILE : 9 * TILE, :]
    tiles[14:15, :] = v[0:1] - edge(9, 5, 1) - edge(10, 4, 1)
    tiles[15:16, :] = v[1:2] - p1[0:1] - edge(10, 5, 1)
    tiles[16:24, :] = edges[6 * TILE : 7 * TILE, :]
    tiles[23:24, :] = f_last
    tiles[24:32, :] = edges[7 * TILE : 8 * TILE, :]
    tiles[30:32, :] = s

    copies = [
        pltpu.make_async_copy(tiles.at[0:8, :], outs[0].at[0:TILE, :], sems.at[0]),
        pltpu.make_async_copy(tiles.at[8:16, :], outs[0].at[rows - TILE : rows, :], sems.at[1]),
        pltpu.make_async_copy(tiles.at[16:24, :], outs[1].at[rows - TILE : rows, :], sems.at[2]),
        pltpu.make_async_copy(tiles.at[24:32, :], outs[2].at[rows - TILE : rows, :], sems.at[3]),
    ]
    for copy in copies:
        copy.start()
    for copy in copies:
        copy.wait()


def near_trades(shards):
    target = {}
    for i in range(shards):
        j = i ^ 1
        for core in range(2):
            target[i, core] = (j, core) if j < shards else (i, 1 - core)
    return flat(target)


def far_trades(shards):
    target = {}
    paired = list(range(1, shards - 1 + shards % 2))
    for i in set(range(shards)) - set(paired):
        target[i, 0], target[i, 1] = (i, 1), (i, 0)
    for i, j in zip(paired[0::2], paired[1::2]):
        target[i, 1], target[j, 1] = (j, 1), (i, 1)
    middle = paired[3:-3]
    circles = [paired[:3], paired[-3:], *zip(middle[0::2], middle[1::2])]
    for circle in circles:
        for i, j in zip(circle, (*circle[1:], circle[0])):
            target[i, 0] = (j, 0)
    return flat(target)


def flat(target):
    return sorted((2 * i + a, 2 * j + b) for (i, a), (j, b) in target.items())


def body(partials, diag_stat, first_stat, second_stat):
    own = partials[0]
    rows, width = own.shape
    replicas = lax.axis_size("replica")
    shards = lax.axis_size("fsdp")
    scale = 1.0 / replicas
    axes = ("fsdp", "replica")
    paired = replicas == 2 and shards > 7

    shape = jax.ShapeDtypeStruct((rows, width), jnp.float32)
    vmem = pl.BlockSpec(memory_space=pltpu.VMEM)
    hbm = pl.BlockSpec(memory_space=pl.ANY)
    params = pltpu.CompilerParams(vmem_limit_bytes=24 * 2**20)

    def swap(block):
        return lax.ppermute(block, "replica", [(0, 1), (1, 0)])

    def stay(block):
        return pltpu.with_memory_space_constraint(block, pltpu.HBM)

    stats = (diag_stat, first_stat, second_stat)
    tile = pltpu.VMEM((TILE, width), jnp.float32)
    if paired:
        pieces = [own, swap(own)]
        far, near = pl.pallas_call(
            functools.partial(collect, rows),
            out_shape=(tile,) * 2,
            in_specs=[hbm] * 4,
            out_specs=(vmem,) * 2,
            scratch_shapes=[
                pltpu.VMEM((8 * TILE, width), jnp.float32),
                pltpu.SemaphoreType.DMA((8,)),
            ],
            compiler_params=params,
            name="collect",
        )(*[stay(x) for x in (own, *stats)])
        near = lax.ppermute(near, axes, near_trades(shards))
        far = pl.pallas_call(
            functools.partial(ready, scale, rows),
            out_shape=tile,
            in_specs=[vmem] * 2,
            out_specs=vmem,
            compiler_params=params,
            name="ready",
        )(far, pieces[1])
        far = lax.ppermute(far, axes, far_trades(shards))
    else:
        pieces = [lax.psum(own, "replica") * scale]
        scale = 1.0
        tail = rows - 2
        ones = jnp.ones((2, width), jnp.float32)
        last = jnp.concatenate([x[tail:] for x in (*pieces, *stats)])
        head = jnp.concatenate([x[:2] for x in (*pieces, *stats[:2])] + [ones])
        before = lax.ppermute(last, "fsdp", [(i, i + 1) for i in range(shards - 1)])
        after = lax.ppermute(head, "fsdp", [(i + 1, i) for i in range(shards - 1)])
        even = lax.axis_index("fsdp") % 2 == 0
        near, far = jnp.where(even, after, before), jnp.where(even, before, after)

    parts = len(pieces)
    whole = pltpu.VMEM((rows, width), jnp.float32)
    padded = pltpu.VMEM((rows + 2 * PAD, width), jnp.float32)
    chunk = 256 if rows % 256 == 0 else rows
    diag_next, first_next, second_next, update, edges = pl.pallas_call(
        functools.partial(interior, parts, scale, rows, chunk, 64),
        out_shape=(shape,) * 3 + (whole, pltpu.VMEM((11 * TILE, width), jnp.float32)),
        in_specs=[vmem] * (parts + 3),
        out_specs=(hbm,) * 3 + (vmem,) * 2,
        scratch_shapes=[padded] * 6 + [pltpu.SemaphoreType.DMA((3, rows // chunk))],
        compiler_params=params,
        cost_estimate=pl.CostEstimate(
            flops=45 * rows * width, bytes_accessed=36 * rows * width, transcendentals=0
        ),
        name="interior",
    )(*[pltpu.with_memory_space_constraint(x, pltpu.VMEM) for x in (*pieces, *stats)])
    other = near
    if paired:
        near, edges = lax.optimization_barrier((near, edges))
        other = swap(near)
    update = pl.pallas_call(
        functools.partial(store, rows, chunk),
        out_shape=shape,
        in_specs=[vmem],
        out_specs=hbm,
        scratch_shapes=[pltpu.SemaphoreType.DMA((rows // chunk,))],
        compiler_params=params,
        cost_estimate=pl.CostEstimate(
            flops=0, bytes_accessed=8 * rows * width, transcendentals=0
        ),
        name="store",
    )(pltpu.with_memory_space_constraint(update, pltpu.VMEM))

    def patched(turn, far, *done):
        return pl.pallas_call(
            functools.partial(border, rows, shards, scale, turn),
            out_shape=(shape,) * 3,
            in_specs=[vmem] * 4 + [hbm] * 3,
            out_specs=(hbm,) * 3,
            input_output_aliases={4: 0, 5: 1, 6: 2},
            scratch_shapes=[
                pltpu.VMEM((16, width), jnp.float32),
                pltpu.VMEM((32, width), jnp.float32),
                pltpu.SemaphoreType.DMA((4,)),
            ],
            compiler_params=params,
            name="border",
        )(edges, near, other, far, *done)

    if paired:
        far, update = lax.optimization_barrier((far, update))
        done = patched(1, far, update, first_next, second_next)
        update, first_next, second_next = patched(2, swap(far), *done)
    else:
        update, first_next, second_next = patched(0, far, update, first_next, second_next)
    return update, diag_next, first_next, second_next


def solution(mesh):
    return jax.shard_map(
        body,
        mesh=mesh,
        in_specs=(P("replica", "fsdp", None), P("fsdp", None), P("fsdp", None), P("fsdp", None)),
        out_specs=(P("fsdp", None), P("fsdp", None), P("fsdp", None), P("fsdp", None)),
        check_vma=False,
    )
```

```python
import functools

import jax
import jax.numpy as jnp
from jax import lax
from jax.experimental import pallas as pl
from jax.experimental.pallas import tpu as pltpu
from jax.sharding import PartitionSpec as P

decay_rate = 0.95
damping = 0.01
PAD = 8
TILE = 8
GROUP = 4


def solved(g, g1, g2, d, upper, lower, f, c, s):
    det = upper * lower - c * c
    n1 = lower * f - c * s
    n2 = upper * s - c * f
    schur = d * det - f * n1 - s * n2
    top = g * det - n1 * g1 - n2 * g2
    w = top / (schur * det)
    return w * det, w * n1, w * n2


def collect(rows, own, diag, first, second, block_out, cross_out, tiles, messages, sems):
    width = tiles.shape[1]
    copies = []
    for k, source in enumerate((own, diag, first, second)):
        for half, at in enumerate((0, rows - TILE)):
            row = (2 * k + half) * TILE
            copies.append(
                pltpu.make_async_copy(
                    source.at[at : at + TILE, :],
                    tiles.at[row : row + TILE, :],
                    sems.at[2 * k + half],
                )
            )
    for copy in copies:
        copy.start()
    for copy in copies:
        copy.wait()
    for k in range(4):
        at = (2 * k + 2) * TILE
        messages[2 * k : 2 * k + 2, :] = tiles[at - 2 : at, :]
    for k in range(3):
        at = 2 * k * TILE
        messages[TILE + 2 * k : TILE + 2 * k + 2, :] = tiles[at : at + 2, :]
    messages[TILE + 6 : TILE + 8, :] = jnp.ones((2, width), jnp.float32)
    last, head = messages[0:TILE, :], messages[TILE : 2 * TILE, :]
    place = lax.rem(lax.axis_index("fsdp"), GROUP)
    for q in range(GROUP):
        message = jnp.where(place < q, last, head)
        for core in range(2):
            block_out[2 * q + core] = message
    message = jnp.where(place == 0, head, last)
    for k in range(4):
        cross_out[k] = message


def interior(parts, scale, rows, chunk, step, *refs):
    pieces = refs[:parts]
    diag_in, first_in, second_in = refs[parts : parts + 3]
    outs = refs[parts + 3 : parts + 6]
    update, edges = refs[parts + 6 : parts + 8]
    grad, diag, first, second, part1, part2, sems = refs[parts + 8 :]
    width = edges.shape[1]
    end = PAD + rows
    chunks = rows // chunk

    zeros = jnp.zeros((PAD, width), jnp.float32)
    grad[end:, :] = zeros
    diag[end:, :] = zeros + 1.0
    first[end:, :] = zeros
    part1[:PAD, :] = zeros
    part2[:PAD, :] = zeros

    def gradients(at, size):
        here, there = pl.ds(at, size), pl.ds(at + PAD, size)
        g = pieces[0][here, :]
        for piece in pieces[1:]:
            g = g + piece[here, :]
        g = g * scale
        grad[there, :] = g
        diag[there, :] = decay_rate * diag_in[here, :] + g * g

    def bands(at, size):
        here, there = pl.ds(at, size), pl.ds(at + PAD, size)
        g = grad[there, :]
        g1 = grad[pl.ds(at + PAD + 1, size), :]
        g2 = grad[pl.ds(at + PAD + 2, size), :]
        first[there, :] = decay_rate * first_in[here, :] + g * g1
        second[there, :] = decay_rate * second_in[here, :] + g * g2

    def values(at, size):
        there = pl.ds(at + PAD, size)
        after = pl.ds(at + PAD + 1, size)
        later = pl.ds(at + PAD + 2, size)
        v, p1, p2 = solved(
            grad[there, :],
            grad[after, :],
            grad[later, :],
            diag[there, :] + damping,
            diag[after, :] + damping,
            diag[later, :] + damping,
            first[there, :],
            first[after, :],
            second[there, :],
        )
        part1[there, :] = p1
        part2[there, :] = p2
        update[pl.ds(at, size), :] = (
            v - part1[pl.ds(at + PAD - 1, size), :] - part2[pl.ds(at + PAD - 2, size), :]
        )

    def over(work, low, high):
        for at in range(low, high, step):
            work(at, min(step, high - at))

    stores = []

    def send(source, k, c, low, high):
        copy = pltpu.make_async_copy(
            source.at[low + PAD : high + PAD, :], outs[k].at[low:high, :], sems.at[k, c]
        )
        copy.start()
        stores.append(copy)

    for c in range(chunks):
        low, high = c * chunk, (c + 1) * chunk
        over(gradients, low, high)
        send(diag, 0, c, low, high)
        low, high = max(low - TILE, 0), high if c == chunks - 1 else high - TILE
        over(bands, low, high)
        send(first, 1, c, low, high)
        send(second, 2, c, low, high)
    over(values, 0, rows)

    tops = [grad[PAD : PAD + TILE, :], diag[PAD : PAD + TILE, :], first[PAD : PAD + TILE, :]]
    tops.append(update[:TILE, :])
    tails = [r[end - TILE : end, :] for r in (grad, diag, first, second)]
    tails.append(update[rows - TILE :, :])
    tails += [r[end - TILE : end, :] for r in (part1, part2)]
    for k, tile in enumerate(tops + tails):
        edges[k * TILE : (k + 1) * TILE, :] = tile
    for copy in stores:
        copy.wait()


def store(rows, chunk, update, out, sems):
    copies = []
    for c in range(rows // chunk):
        low, high = max(c * chunk, TILE), min((c + 1) * chunk, rows - TILE)
        copies.append(
            pltpu.make_async_copy(update.at[low:high, :], out.at[low:high, :], sems.at[c])
        )
    for copy in copies:
        copy.start()
    for copy in copies:
        copy.wait()


def border(rows, shards, scale, *refs):
    edges, block, cross = refs[:3]
    outs = refs[6:9]
    work, tiles, sems = refs[9:]

    def edge(k, at, size):
        return edges[k * TILE + at : k * TILE + at + size, :]

    shard = lax.axis_index("fsdp")
    if scale == 1.0:
        before, after = block[...], cross[...]
    else:
        place = lax.rem(shard, GROUP)
        below = 2 * jnp.maximum(place - 1, 0)
        above = 2 * jnp.minimum(place + 1, GROUP - 1)
        pairs = [
            (place == 0, cross[0], cross[1], block[below], block[below + 1]),
            (place == GROUP - 1, cross[2], cross[3], block[above], block[above + 1]),
        ]
        rows_of = []
        for outer, far0, far1, near0, near1 in pairs:
            one = jnp.where(outer, far0, near0)
            two = jnp.where(outer, far1, near1)
            rows_of.append(jnp.concatenate([(one[0:2] + two[0:2]) * scale, one[2:8]]))
        before, after = rows_of
    work[0:8, :] = jnp.where(shard == 0, 0.0, before)
    work[8:16, :] = jnp.where(shard == shards - 1, 0.0, after)

    g = work[0:2, :]
    g_next = edge(0, 0, 2)
    d = decay_rate * work[2:4, :] + g * g + damping
    d_next = edge(1, 0, 2) + damping
    g1 = jnp.concatenate([g[1:2], g_next[0:1]])
    d1 = jnp.concatenate([d[1:2], d_next[0:1]])
    f = decay_rate * work[4:6, :] + g * g1
    s = decay_rate * work[6:8, :] + g * g_next
    c = jnp.concatenate([f[1:2], edge(2, 0, 1)])
    _, p1, p2 = solved(g, g1, g_next, d, d1, d_next, f, c, s)
    tiles[0:8, :] = edges[3 * TILE : 4 * TILE, :]
    tiles[0:1, :] = tiles[0:1, :] - p1[1:2] - p2[0:1]
    tiles[1:2, :] = tiles[1:2, :] - p2[1:2]

    g = edge(4, 6, 2)
    g_next = work[8:10, :]
    present = work[14:16, :]
    d = edge(5, 6, 2) + damping
    d_next = (
        decay_rate * work[10:12, :] + g_next * g_next + present * damping + (1.0 - present)
    )
    g1 = jnp.concatenate([g[1:2], g_next[0:1]])
    d1 = jnp.concatenate([d[1:2], d_next[0:1]])
    f_last = (edge(6, 7, 1) + g[1:2] * g_next[0:1]) * present[0:1]
    f = jnp.concatenate([edge(6, 6, 1), f_last])
    s = (edge(7, 6, 2) + g * g_next) * present
    f_next = decay_rate * work[12:13, :] + g_next[0:1] * g_next[1:2]
    c = jnp.concatenate([f_last, f_next])
    v, p1, _ = solved(g, g1, g_next, d, d1, d_next, f, c, s)
    tiles[8:16, :] = edges[8 * TILE : 9 * TILE, :]
    tiles[14:15, :] = v[0:1] - edge(9, 5, 1) - edge(10, 4, 1)
    tiles[15:16, :] = v[1:2] - p1[0:1] - edge(10, 5, 1)
    tiles[16:24, :] = edges[6 * TILE : 7 * TILE, :]
    tiles[23:24, :] = f_last
    tiles[24:32, :] = edges[7 * TILE : 8 * TILE, :]
    tiles[30:32, :] = s

    copies = [
        pltpu.make_async_copy(tiles.at[0:8, :], outs[0].at[0:TILE, :], sems.at[0]),
        pltpu.make_async_copy(tiles.at[8:16, :], outs[0].at[rows - TILE : rows, :], sems.at[1]),
        pltpu.make_async_copy(tiles.at[16:24, :], outs[1].at[rows - TILE : rows, :], sems.at[2]),
        pltpu.make_async_copy(tiles.at[24:32, :], outs[2].at[rows - TILE : rows, :], sems.at[3]),
    ]
    for copy in copies:
        copy.start()
    for copy in copies:
        copy.wait()


def block_groups(shards):
    size = 2 * GROUP
    return [list(range(i, i + size)) for i in range(0, 2 * shards, size)]


def cross_groups(shards):
    ends = [(i - 1, i) for i in range(GROUP, shards, GROUP)]
    taken = {i for pair in ends for i in pair}
    rest = [i for i in range(shards) if i not in taken]
    pairs = ends + list(zip(rest[0::2], rest[1::2]))
    return [[2 * i, 2 * i + 1, 2 * j, 2 * j + 1] for i, j in pairs]


def body(partials, diag_stat, first_stat, second_stat):
    own = partials[0]
    rows, width = own.shape
    replicas = lax.axis_size("replica")
    shards = lax.axis_size("fsdp")
    scale = 1.0 / replicas
    paired = replicas == 2 and shards % GROUP == 0

    shape = jax.ShapeDtypeStruct((rows, width), jnp.float32)
    vmem = pl.BlockSpec(memory_space=pltpu.VMEM)
    hbm = pl.BlockSpec(memory_space=pl.ANY)
    params = pltpu.CompilerParams(vmem_limit_bytes=24 * 2**20)

    def swap(block):
        return lax.ppermute(block, "replica", [(0, 1), (1, 0)])

    def stay(block):
        return pltpu.with_memory_space_constraint(block, pltpu.HBM)

    stats = (diag_stat, first_stat, second_stat)
    tile = pltpu.VMEM((TILE, width), jnp.float32)
    if paired:
        pieces = [own, swap(own)]
        block, cross = pl.pallas_call(
            functools.partial(collect, rows),
            out_shape=(
                pltpu.VMEM((2 * GROUP, TILE, width), jnp.float32),
                pltpu.VMEM((4, TILE, width), jnp.float32),
            ),
            in_specs=[hbm] * 4,
            out_specs=(vmem,) * 2,
            scratch_shapes=[
                pltpu.VMEM((8 * TILE, width), jnp.float32),
                pltpu.VMEM((2 * TILE, width), jnp.float32),
                pltpu.SemaphoreType.DMA((8,)),
            ],
            compiler_params=params,
            name="collect",
        )(*[stay(x) for x in (own, *stats)])

        def exchange(blocks, groups):
            return lax.all_to_all(
                blocks, ("fsdp", "replica"), 0, 0, axis_index_groups=groups, tiled=True
            )

        cross = exchange(cross, cross_groups(shards))
        block = exchange(block, block_groups(shards))
    else:
        pieces = [lax.psum(own, "replica") * scale]
        scale = 1.0
        tail = rows - 2
        ones = jnp.ones((2, width), jnp.float32)
        last = jnp.concatenate([x[tail:] for x in (*pieces, *stats)])
        head = jnp.concatenate([x[:2] for x in (*pieces, *stats[:2])] + [ones])
        before = lax.ppermute(last, "fsdp", [(i, i + 1) for i in range(shards - 1)])
        after = lax.ppermute(head, "fsdp", [(i + 1, i) for i in range(shards - 1)])
        block, cross = before, after

    parts = len(pieces)
    whole = pltpu.VMEM((rows, width), jnp.float32)
    padded = pltpu.VMEM((rows + 2 * PAD, width), jnp.float32)
    chunk = 256 if rows % 256 == 0 else rows
    diag_next, first_next, second_next, update, edges = pl.pallas_call(
        functools.partial(interior, parts, scale, rows, chunk, 64),
        out_shape=(shape,) * 3 + (whole, pltpu.VMEM((11 * TILE, width), jnp.float32)),
        in_specs=[vmem] * (parts + 3),
        out_specs=(hbm,) * 3 + (vmem,) * 2,
        scratch_shapes=[padded] * 6 + [pltpu.SemaphoreType.DMA((3, rows // chunk))],
        compiler_params=params,
        cost_estimate=pl.CostEstimate(
            flops=45 * rows * width, bytes_accessed=36 * rows * width, transcendentals=0
        ),
        name="interior",
    )(*[pltpu.with_memory_space_constraint(x, pltpu.VMEM) for x in (*pieces, *stats)])
    update = pl.pallas_call(
        functools.partial(store, rows, chunk),
        out_shape=shape,
        in_specs=[vmem],
        out_specs=hbm,
        scratch_shapes=[pltpu.SemaphoreType.DMA((rows // chunk,))],
        compiler_params=params,
        cost_estimate=pl.CostEstimate(
            flops=0, bytes_accessed=8 * rows * width, transcendentals=0
        ),
        name="store",
    )(pltpu.with_memory_space_constraint(update, pltpu.VMEM))

    update, first_next, second_next = pl.pallas_call(
        functools.partial(border, rows, shards, scale),
        out_shape=(shape,) * 3,
        in_specs=[vmem] * 3 + [hbm] * 3,
        out_specs=(hbm,) * 3,
        input_output_aliases={3: 0, 4: 1, 5: 2},
        scratch_shapes=[
            pltpu.VMEM((16, width), jnp.float32),
            pltpu.VMEM((32, width), jnp.float32),
            pltpu.SemaphoreType.DMA((4,)),
        ],
        compiler_params=params,
        name="border",
    )(edges, block, cross, update, first_next, second_next)
    return update, diag_next, first_next, second_next


def solution(mesh):
    return jax.shard_map(
        body,
        mesh=mesh,
        in_specs=(P("replica", "fsdp", None), P("fsdp", None), P("fsdp", None), P("fsdp", None)),
        out_specs=(P("fsdp", None), P("fsdp", None), P("fsdp", None), P("fsdp", None)),
        check_vma=False,
    )
```

```python
import functools

import jax
import jax.numpy as jnp
from jax import lax
from jax.experimental import pallas as pl
from jax.experimental.pallas import tpu as pltpu
from jax.sharding import PartitionSpec as P

decay_rate = 0.95
damping = 0.01
PAD = 8
TILE = 8


def solved(g, g1, g2, d, upper, lower, f, c, s):
    det = upper * lower - c * c
    n1 = lower * f - c * s
    n2 = upper * s - c * f
    schur = d * det - f * n1 - s * n2
    top = g * det - n1 * g1 - n2 * g2
    w = top / (schur * det)
    return w * det, w * n1, w * n2


def collect(rows, own, diag, first, second, far, near, tiles, sems):
    width = tiles.shape[1]
    copies = []
    for k, source in enumerate((own, diag, first, second)):
        for half, at in enumerate((0, rows - TILE)):
            row = (2 * k + half) * TILE
            copies.append(
                pltpu.make_async_copy(
                    source.at[at : at + TILE, :],
                    tiles.at[row : row + TILE, :],
                    sems.at[2 * k + half],
                )
            )
    for copy in copies:
        copy.start()
    for copy in copies:
        copy.wait()
    head = [tiles[2 * k * TILE : 2 * k * TILE + 2, :] for k in range(3)]
    head.append(jnp.ones((2, width), jnp.float32))
    last = [tiles[(2 * k + 2) * TILE - 2 : (2 * k + 2) * TILE, :] for k in range(4)]
    even = lax.rem(lax.axis_index("fsdp"), 2) == 0

    def fill(out, blocks):
        for k, block in enumerate(blocks):
            out[2 * k : 2 * k + 2, :] = block

    @pl.when(even)
    def _():
        fill(near, last)
        fill(far, head)

    @pl.when(jnp.logical_not(even))
    def _():
        fill(near, head)
        fill(far, last)


def ready(scale, rows, block, other, out):
    even = lax.rem(lax.axis_index("fsdp"), 2) == 0
    out[2:8, :] = block[2:8, :]

    @pl.when(even)
    def _():
        out[0:2, :] = (block[0:2, :] + other[rows - 2 : rows, :]) * scale

    @pl.when(jnp.logical_not(even))
    def _():
        out[0:2, :] = (block[0:2, :] + other[0:2, :]) * scale


def interior(parts, scale, rows, chunk, step, *refs):
    pieces = refs[:parts]
    diag_in, first_in, second_in = refs[parts : parts + 3]
    outs = refs[parts + 3 : parts + 6]
    update, edges = refs[parts + 6 : parts + 8]
    grad, diag, first, second, part1, part2, sems = refs[parts + 8 :]
    width = edges.shape[1]
    end = PAD + rows
    chunks = rows // chunk

    zeros = jnp.zeros((PAD, width), jnp.float32)
    grad[end:, :] = zeros
    diag[end:, :] = zeros + 1.0
    first[end:, :] = zeros
    part1[:PAD, :] = zeros
    part2[:PAD, :] = zeros

    def gradients(at, size):
        here, there = pl.ds(at, size), pl.ds(at + PAD, size)
        g = pieces[0][here, :]
        for piece in pieces[1:]:
            g = g + piece[here, :]
        g = g * scale
        grad[there, :] = g
        diag[there, :] = decay_rate * diag_in[here, :] + g * g

    def bands(at, size):
        here, there = pl.ds(at, size), pl.ds(at + PAD, size)
        g = grad[there, :]
        g1 = grad[pl.ds(at + PAD + 1, size), :]
        g2 = grad[pl.ds(at + PAD + 2, size), :]
        first[there, :] = decay_rate * first_in[here, :] + g * g1
        second[there, :] = decay_rate * second_in[here, :] + g * g2

    def values(at, size):
        there = pl.ds(at + PAD, size)
        after = pl.ds(at + PAD + 1, size)
        later = pl.ds(at + PAD + 2, size)
        v, p1, p2 = solved(
            grad[there, :],
            grad[after, :],
            grad[later, :],
            diag[there, :] + damping,
            diag[after, :] + damping,
            diag[later, :] + damping,
            first[there, :],
            first[after, :],
            second[there, :],
        )
        part1[there, :] = p1
        part2[there, :] = p2
        update[pl.ds(at, size), :] = (
            v - part1[pl.ds(at + PAD - 1, size), :] - part2[pl.ds(at + PAD - 2, size), :]
        )

    def over(work, low, high):
        for at in range(low, high, step):
            work(at, min(step, high - at))

    stores = []

    def send(source, k, c, low, high):
        copy = pltpu.make_async_copy(
            source.at[low + PAD : high + PAD, :], outs[k].at[low:high, :], sems.at[k, c]
        )
        copy.start()
        stores.append(copy)

    for c in range(chunks):
        low, high = c * chunk, (c + 1) * chunk
        over(gradients, low, high)
        send(diag, 0, c, low, high)
        low, high = max(low - TILE, 0), high if c == chunks - 1 else high - TILE
        over(bands, low, high)
        send(first, 1, c, low, high)
        send(second, 2, c, low, high)
    over(values, 0, rows)

    tops = [grad[PAD : PAD + TILE, :], diag[PAD : PAD + TILE, :], first[PAD : PAD + TILE, :]]
    tops.append(update[:TILE, :])
    tails = [r[end - TILE : end, :] for r in (grad, diag, first, second)]
    tails.append(update[rows - TILE :, :])
    tails += [r[end - TILE : end, :] for r in (part1, part2)]
    for k, tile in enumerate(tops + tails):
        edges[k * TILE : (k + 1) * TILE, :] = tile
    for copy in stores:
        copy.wait()


def store(rows, chunk, update, out, sems):
    copies = []
    for c in range(rows // chunk):
        low, high = max(c * chunk, TILE), min((c + 1) * chunk, rows - TILE)
        copies.append(
            pltpu.make_async_copy(update.at[low:high, :], out.at[low:high, :], sems.at[c])
        )
    for copy in copies:
        copy.start()
    for copy in copies:
        copy.wait()


def border(rows, shards, scale, turn, *refs):
    chosen = lax.axis_index("fsdp") == 0
    if turn == 0:
        patch(rows, shards, scale, *refs)
    else:
        pl.when(chosen if turn == 1 else jnp.logical_not(chosen))(
            functools.partial(patch, rows, shards, scale, *refs)
        )


def patch(rows, shards, scale, *refs):
    edges, near, far, other = refs[:4]
    outs = refs[7:10]
    work, tiles, sems = refs[10:]

    def edge(k, at, size):
        return edges[k * TILE + at : k * TILE + at + size, :]

    shard = lax.axis_index("fsdp")
    even = lax.rem(shard, 2) == 0
    near_rows, far_rows = near[...], far[...]
    if scale != 1.0:
        far_sum = (far_rows[0:2] + other[0:2, :]) * scale
        far_rows = jnp.concatenate([far_sum, far_rows[2:8]])
    before = jnp.where(even, far_rows, near_rows)
    after = jnp.where(even, near_rows, far_rows)
    work[0:8, :] = jnp.where(shard == 0, 0.0, before)
    work[8:16, :] = jnp.where(shard == shards - 1, 0.0, after)

    g = work[0:2, :]
    g_next = edge(0, 0, 2)
    d = decay_rate * work[2:4, :] + g * g + damping
    d_next = edge(1, 0, 2) + damping
    g1 = jnp.concatenate([g[1:2], g_next[0:1]])
    d1 = jnp.concatenate([d[1:2], d_next[0:1]])
    f = decay_rate * work[4:6, :] + g * g1
    s = decay_rate * work[6:8, :] + g * g_next
    c = jnp.concatenate([f[1:2], edge(2, 0, 1)])
    _, p1, p2 = solved(g, g1, g_next, d, d1, d_next, f, c, s)
    tiles[0:8, :] = edges[3 * TILE : 4 * TILE, :]
    tiles[0:1, :] = tiles[0:1, :] - p1[1:2] - p2[0:1]
    tiles[1:2, :] = tiles[1:2, :] - p2[1:2]

    g = edge(4, 6, 2)
    g_next = work[8:10, :]
    present = work[14:16, :]
    d = edge(5, 6, 2) + damping
    d_next = (
        decay_rate * work[10:12, :] + g_next * g_next + present * damping + (1.0 - present)
    )
    g1 = jnp.concatenate([g[1:2], g_next[0:1]])
    d1 = jnp.concatenate([d[1:2], d_next[0:1]])
    f_last = (edge(6, 7, 1) + g[1:2] * g_next[0:1]) * present[0:1]
    f = jnp.concatenate([edge(6, 6, 1), f_last])
    s = (edge(7, 6, 2) + g * g_next) * present
    f_next = decay_rate * work[12:13, :] + g_next[0:1] * g_next[1:2]
    c = jnp.concatenate([f_last, f_next])
    v, p1, _ = solved(g, g1, g_next, d, d1, d_next, f, c, s)
    tiles[8:16, :] = edges[8 * TILE : 9 * TILE, :]
    tiles[14:15, :] = v[0:1] - edge(9, 5, 1) - edge(10, 4, 1)
    tiles[15:16, :] = v[1:2] - p1[0:1] - edge(10, 5, 1)
    tiles[16:24, :] = edges[6 * TILE : 7 * TILE, :]
    tiles[23:24, :] = f_last
    tiles[24:32, :] = edges[7 * TILE : 8 * TILE, :]
    tiles[30:32, :] = s

    copies = [
        pltpu.make_async_copy(tiles.at[0:8, :], outs[0].at[0:TILE, :], sems.at[0]),
        pltpu.make_async_copy(tiles.at[8:16, :], outs[0].at[rows - TILE : rows, :], sems.at[1]),
        pltpu.make_async_copy(tiles.at[16:24, :], outs[1].at[rows - TILE : rows, :], sems.at[2]),
        pltpu.make_async_copy(tiles.at[24:32, :], outs[2].at[rows - TILE : rows, :], sems.at[3]),
    ]
    for copy in copies:
        copy.start()
    for copy in copies:
        copy.wait()


def trades(shards, low):
    partner = {}
    for i in range(low, shards - 1, 2):
        partner[i], partner[i + 1] = i + 1, i
    return [
        (2 * i + core, 2 * partner.get(i, i) + 1 - core) for i in range(shards) for core in range(2)
    ]


def body(partials, diag_stat, first_stat, second_stat):
    own = partials[0]
    rows, width = own.shape
    replicas = lax.axis_size("replica")
    shards = lax.axis_size("fsdp")
    scale = 1.0 / replicas
    axes = ("fsdp", "replica")
    paired = replicas == 2 and shards > 1

    shape = jax.ShapeDtypeStruct((rows, width), jnp.float32)
    vmem = pl.BlockSpec(memory_space=pltpu.VMEM)
    hbm = pl.BlockSpec(memory_space=pl.ANY)
    params = pltpu.CompilerParams(vmem_limit_bytes=24 * 2**20)

    def swap(block):
        return lax.ppermute(block, "replica", [(0, 1), (1, 0)])

    def stay(block):
        return pltpu.with_memory_space_constraint(block, pltpu.HBM)

    stats = (diag_stat, first_stat, second_stat)
    tile = pltpu.VMEM((TILE, width), jnp.float32)
    if paired:
        pieces = [own, swap(own)]
        far, near = pl.pallas_call(
            functools.partial(collect, rows),
            out_shape=(tile,) * 2,
            in_specs=[hbm] * 4,
            out_specs=(vmem,) * 2,
            scratch_shapes=[
                pltpu.VMEM((8 * TILE, width), jnp.float32),
                pltpu.SemaphoreType.DMA((8,)),
            ],
            compiler_params=params,
            name="collect",
        )(*[stay(x) for x in (own, *stats)])
        far = lax.ppermute(far, axes, trades(shards, 1))
        near = pl.pallas_call(
            functools.partial(ready, scale, rows),
            out_shape=tile,
            in_specs=[vmem] * 2,
            out_specs=vmem,
            compiler_params=params,
            name="ready",
        )(near, pieces[1])
        near = lax.ppermute(near, axes, trades(shards, 0))
    else:
        pieces = [lax.psum(own, "replica") * scale]
        scale = 1.0
        tail = rows - 2
        ones = jnp.ones((2, width), jnp.float32)
        last = jnp.concatenate([x[tail:] for x in (*pieces, *stats)])
        head = jnp.concatenate([x[:2] for x in (*pieces, *stats[:2])] + [ones])
        before = lax.ppermute(last, "fsdp", [(i, i + 1) for i in range(shards - 1)])
        after = lax.ppermute(head, "fsdp", [(i + 1, i) for i in range(shards - 1)])
        even = lax.axis_index("fsdp") % 2 == 0
        near, far = jnp.where(even, after, before), jnp.where(even, before, after)

    parts = len(pieces)
    whole = pltpu.VMEM((rows, width), jnp.float32)
    padded = pltpu.VMEM((rows + 2 * PAD, width), jnp.float32)
    chunk = 256 if rows % 256 == 0 else rows
    diag_next, first_next, second_next, update, edges = pl.pallas_call(
        functools.partial(interior, parts, scale, rows, chunk, 64),
        out_shape=(shape,) * 3 + (whole, pltpu.VMEM((11 * TILE, width), jnp.float32)),
        in_specs=[vmem] * (parts + 3),
        out_specs=(hbm,) * 3 + (vmem,) * 2,
        scratch_shapes=[padded] * 6 + [pltpu.SemaphoreType.DMA((3, rows // chunk))],
        compiler_params=params,
        cost_estimate=pl.CostEstimate(
            flops=45 * rows * width, bytes_accessed=36 * rows * width, transcendentals=0
        ),
        name="interior",
    )(*[pltpu.with_memory_space_constraint(x, pltpu.VMEM) for x in (*pieces, *stats)])
    other = far
    if paired:
        far, edges = lax.optimization_barrier((far, edges))
        other = swap(far)
    update = pl.pallas_call(
        functools.partial(store, rows, chunk),
        out_shape=shape,
        in_specs=[vmem],
        out_specs=hbm,
        scratch_shapes=[pltpu.SemaphoreType.DMA((rows // chunk,))],
        compiler_params=params,
        cost_estimate=pl.CostEstimate(
            flops=0, bytes_accessed=8 * rows * width, transcendentals=0
        ),
        name="store",
    )(pltpu.with_memory_space_constraint(update, pltpu.VMEM))

    def patched(turn, other, *done):
        return pl.pallas_call(
            functools.partial(border, rows, shards, scale, turn),
            out_shape=(shape,) * 3,
            in_specs=[vmem] * 4 + [hbm] * 3,
            out_specs=(hbm,) * 3,
            input_output_aliases={4: 0, 5: 1, 6: 2},
            scratch_shapes=[
                pltpu.VMEM((16, width), jnp.float32),
                pltpu.VMEM((32, width), jnp.float32),
                pltpu.SemaphoreType.DMA((4,)),
            ],
            compiler_params=params,
            name="border",
        )(edges, near, far, other, *done)

    if paired:
        done = patched(1, far, update, first_next, second_next)
        update, first_next, second_next = patched(2, other, *done)
    else:
        update, first_next, second_next = patched(0, far, update, first_next, second_next)
    return update, diag_next, first_next, second_next


def solution(mesh):
    return jax.shard_map(
        body,
        mesh=mesh,
        in_specs=(P("replica", "fsdp", None), P("fsdp", None), P("fsdp", None), P("fsdp", None)),
        out_specs=(P("fsdp", None), P("fsdp", None), P("fsdp", None), P("fsdp", None)),
        check_vma=False,
    )
```

```python
import functools

import jax
import jax.numpy as jnp
from jax import lax
from jax.experimental import pallas as pl
from jax.experimental.pallas import tpu as pltpu
from jax.sharding import PartitionSpec as P

decay_rate = 0.95
damping = 0.01
PAD = 8
TILE = 8


def solved(g, g1, g2, d, upper, lower, f, c, s):
    det = upper * lower - c * c
    n1 = lower * f - c * s
    n2 = upper * s - c * f
    schur = d * det - f * n1 - s * n2
    top = g * det - n1 * g1 - n2 * g2
    w = top / (schur * det)
    return w * det, w * n1, w * n2


def collect(rows, own, diag, first, second, far, near, tiles, sems):
    width = tiles.shape[1]
    copies = []
    for k, source in enumerate((own, diag, first, second)):
        for half, at in enumerate((0, rows - TILE)):
            row = (2 * k + half) * TILE
            copies.append(
                pltpu.make_async_copy(
                    source.at[at : at + TILE, :],
                    tiles.at[row : row + TILE, :],
                    sems.at[2 * k + half],
                )
            )
    for copy in copies:
        copy.start()
    for copy in copies:
        copy.wait()
    head = [tiles[2 * k * TILE : 2 * k * TILE + 2, :] for k in range(3)]
    head.append(jnp.ones((2, width), jnp.float32))
    last = [tiles[(2 * k + 2) * TILE - 2 : (2 * k + 2) * TILE, :] for k in range(4)]
    even = lax.rem(lax.axis_index("fsdp"), 2) == 0

    def fill(out, blocks):
        for k, block in enumerate(blocks):
            out[2 * k : 2 * k + 2, :] = block

    @pl.when(even)
    def _():
        fill(near, last)
        fill(far, head)

    @pl.when(jnp.logical_not(even))
    def _():
        fill(near, head)
        fill(far, last)


def ready(scale, rows, block, other, out):
    even = lax.rem(lax.axis_index("fsdp"), 2) == 0
    out[2:8, :] = block[2:8, :]

    @pl.when(even)
    def _():
        out[0:2, :] = (block[0:2, :] + other[rows - 2 : rows, :]) * scale

    @pl.when(jnp.logical_not(even))
    def _():
        out[0:2, :] = (block[0:2, :] + other[0:2, :]) * scale


def interior(parts, early, scale, rows, chunk, step, *refs):
    chosen = lax.axis_index("fsdp") == 0
    pl.when(chosen if early else jnp.logical_not(chosen))(
        functools.partial(
            everything, parts, scale, rows, chunk, step, *refs[: parts + 3], *refs[-12:]
        )
    )


def everything(parts, scale, rows, chunk, step, *refs):
    pieces = refs[:parts]
    diag_in, first_in, second_in = refs[parts : parts + 3]
    outs = refs[parts + 3 : parts + 6]
    update, edges = refs[parts + 6 : parts + 8]
    grad, diag, first, second, part1, part2, sems = refs[parts + 8 :]
    width = edges.shape[1]
    end = PAD + rows
    chunks = rows // chunk

    zeros = jnp.zeros((PAD, width), jnp.float32)
    grad[end:, :] = zeros
    diag[end:, :] = zeros + 1.0
    first[end:, :] = zeros
    part1[:PAD, :] = zeros
    part2[:PAD, :] = zeros

    def gradients(at, size):
        here, there = pl.ds(at, size), pl.ds(at + PAD, size)
        g = pieces[0][here, :]
        for piece in pieces[1:]:
            g = g + piece[here, :]
        g = g * scale
        grad[there, :] = g
        diag[there, :] = decay_rate * diag_in[here, :] + g * g

    def bands(at, size):
        here, there = pl.ds(at, size), pl.ds(at + PAD, size)
        g = grad[there, :]
        g1 = grad[pl.ds(at + PAD + 1, size), :]
        g2 = grad[pl.ds(at + PAD + 2, size), :]
        first[there, :] = decay_rate * first_in[here, :] + g * g1
        second[there, :] = decay_rate * second_in[here, :] + g * g2

    def values(at, size):
        there = pl.ds(at + PAD, size)
        after = pl.ds(at + PAD + 1, size)
        later = pl.ds(at + PAD + 2, size)
        v, p1, p2 = solved(
            grad[there, :],
            grad[after, :],
            grad[later, :],
            diag[there, :] + damping,
            diag[after, :] + damping,
            diag[later, :] + damping,
            first[there, :],
            first[after, :],
            second[there, :],
        )
        part1[there, :] = p1
        part2[there, :] = p2
        update[pl.ds(at, size), :] = (
            v - part1[pl.ds(at + PAD - 1, size), :] - part2[pl.ds(at + PAD - 2, size), :]
        )

    def over(work, low, high):
        for at in range(low, high, step):
            work(at, min(step, high - at))

    stores = []

    def send(source, k, c, low, high):
        copy = pltpu.make_async_copy(
            source.at[low + PAD : high + PAD, :], outs[k].at[low:high, :], sems.at[k, c]
        )
        copy.start()
        stores.append(copy)

    for c in range(chunks):
        low, high = c * chunk, (c + 1) * chunk
        over(gradients, low, high)
        send(diag, 0, c, low, high)
        low, high = max(low - TILE, 0), high if c == chunks - 1 else high - TILE
        over(bands, low, high)
        send(first, 1, c, low, high)
        send(second, 2, c, low, high)
    over(values, 0, rows)

    tops = [grad[PAD : PAD + TILE, :], diag[PAD : PAD + TILE, :], first[PAD : PAD + TILE, :]]
    tops.append(update[:TILE, :])
    tails = [r[end - TILE : end, :] for r in (grad, diag, first, second)]
    tails.append(update[rows - TILE :, :])
    tails += [r[end - TILE : end, :] for r in (part1, part2)]
    for k, tile in enumerate(tops + tails):
        edges[k * TILE : (k + 1) * TILE, :] = tile
    for copy in stores:
        copy.wait()


def store(rows, chunk, update, out, sems):
    copies = []
    for c in range(rows // chunk):
        low, high = max(c * chunk, TILE), min((c + 1) * chunk, rows - TILE)
        copies.append(
            pltpu.make_async_copy(update.at[low:high, :], out.at[low:high, :], sems.at[c])
        )
    for copy in copies:
        copy.start()
    for copy in copies:
        copy.wait()


def border(rows, shards, scale, turn, *refs):
    chosen = lax.axis_index("fsdp") == 0
    if turn == 0:
        patch(rows, shards, scale, *refs)
    else:
        pl.when(chosen if turn == 1 else jnp.logical_not(chosen))(
            functools.partial(patch, rows, shards, scale, *refs)
        )


def patch(rows, shards, scale, *refs):
    edges, near, far, other = refs[:4]
    outs = refs[7:10]
    work, tiles, sems = refs[10:]

    def edge(k, at, size):
        return edges[k * TILE + at : k * TILE + at + size, :]

    shard = lax.axis_index("fsdp")
    even = lax.rem(shard, 2) == 0
    near_rows, far_rows = near[...], far[...]
    if scale != 1.0:
        far_sum = (far_rows[0:2] + other[0:2, :]) * scale
        far_rows = jnp.concatenate([far_sum, far_rows[2:8]])
    before = jnp.where(even, far_rows, near_rows)
    after = jnp.where(even, near_rows, far_rows)
    work[0:8, :] = jnp.where(shard == 0, 0.0, before)
    work[8:16, :] = jnp.where(shard == shards - 1, 0.0, after)

    g = work[0:2, :]
    g_next = edge(0, 0, 2)
    d = decay_rate * work[2:4, :] + g * g + damping
    d_next = edge(1, 0, 2) + damping
    g1 = jnp.concatenate([g[1:2], g_next[0:1]])
    d1 = jnp.concatenate([d[1:2], d_next[0:1]])
    f = decay_rate * work[4:6, :] + g * g1
    s = decay_rate * work[6:8, :] + g * g_next
    c = jnp.concatenate([f[1:2], edge(2, 0, 1)])
    _, p1, p2 = solved(g, g1, g_next, d, d1, d_next, f, c, s)
    tiles[0:8, :] = edges[3 * TILE : 4 * TILE, :]
    tiles[0:1, :] = tiles[0:1, :] - p1[1:2] - p2[0:1]
    tiles[1:2, :] = tiles[1:2, :] - p2[1:2]

    g = edge(4, 6, 2)
    g_next = work[8:10, :]
    present = work[14:16, :]
    d = edge(5, 6, 2) + damping
    d_next = (
        decay_rate * work[10:12, :] + g_next * g_next + present * damping + (1.0 - present)
    )
    g1 = jnp.concatenate([g[1:2], g_next[0:1]])
    d1 = jnp.concatenate([d[1:2], d_next[0:1]])
    f_last = (edge(6, 7, 1) + g[1:2] * g_next[0:1]) * present[0:1]
    f = jnp.concatenate([edge(6, 6, 1), f_last])
    s = (edge(7, 6, 2) + g * g_next) * present
    f_next = decay_rate * work[12:13, :] + g_next[0:1] * g_next[1:2]
    c = jnp.concatenate([f_last, f_next])
    v, p1, _ = solved(g, g1, g_next, d, d1, d_next, f, c, s)
    tiles[8:16, :] = edges[8 * TILE : 9 * TILE, :]
    tiles[14:15, :] = v[0:1] - edge(9, 5, 1) - edge(10, 4, 1)
    tiles[15:16, :] = v[1:2] - p1[0:1] - edge(10, 5, 1)
    tiles[16:24, :] = edges[6 * TILE : 7 * TILE, :]
    tiles[23:24, :] = f_last
    tiles[24:32, :] = edges[7 * TILE : 8 * TILE, :]
    tiles[30:32, :] = s

    copies = [
        pltpu.make_async_copy(tiles.at[0:8, :], outs[0].at[0:TILE, :], sems.at[0]),
        pltpu.make_async_copy(tiles.at[8:16, :], outs[0].at[rows - TILE : rows, :], sems.at[1]),
        pltpu.make_async_copy(tiles.at[16:24, :], outs[1].at[rows - TILE : rows, :], sems.at[2]),
        pltpu.make_async_copy(tiles.at[24:32, :], outs[2].at[rows - TILE : rows, :], sems.at[3]),
    ]
    for copy in copies:
        copy.start()
    for copy in copies:
        copy.wait()


def trades(shards, low):
    partner = {}
    for i in range(low, shards - 1, 2):
        partner[i], partner[i + 1] = i + 1, i
    return [
        (2 * i + core, 2 * partner.get(i, i) + 1 - core) for i in range(shards) for core in range(2)
    ]


def body(partials, diag_stat, first_stat, second_stat):
    own = partials[0]
    rows, width = own.shape
    replicas = lax.axis_size("replica")
    shards = lax.axis_size("fsdp")
    scale = 1.0 / replicas
    axes = ("fsdp", "replica")
    paired = replicas == 2 and shards > 1

    shape = jax.ShapeDtypeStruct((rows, width), jnp.float32)
    vmem = pl.BlockSpec(memory_space=pltpu.VMEM)
    hbm = pl.BlockSpec(memory_space=pl.ANY)
    params = pltpu.CompilerParams(vmem_limit_bytes=24 * 2**20)

    def swap(block):
        return lax.ppermute(block, "replica", [(0, 1), (1, 0)])

    def stay(block):
        return pltpu.with_memory_space_constraint(block, pltpu.HBM)

    stats = (diag_stat, first_stat, second_stat)
    tile = pltpu.VMEM((TILE, width), jnp.float32)
    if paired:
        pieces = [own, swap(own)]
        far, near = pl.pallas_call(
            functools.partial(collect, rows),
            out_shape=(tile,) * 2,
            in_specs=[hbm] * 4,
            out_specs=(vmem,) * 2,
            scratch_shapes=[
                pltpu.VMEM((8 * TILE, width), jnp.float32),
                pltpu.SemaphoreType.DMA((8,)),
            ],
            compiler_params=params,
            name="collect",
        )(*[stay(x) for x in (own, *stats)])
        far = lax.ppermute(far, axes, trades(shards, 1))
        near = pl.pallas_call(
            functools.partial(ready, scale, rows),
            out_shape=tile,
            in_specs=[vmem] * 2,
            out_specs=vmem,
            compiler_params=params,
            name="ready",
        )(near, pieces[1])
    else:
        pieces = [lax.psum(own, "replica") * scale]
        scale = 1.0
        tail = rows - 2
        ones = jnp.ones((2, width), jnp.float32)
        last = jnp.concatenate([x[tail:] for x in (*pieces, *stats)])
        head = jnp.concatenate([x[:2] for x in (*pieces, *stats[:2])] + [ones])
        before = lax.ppermute(last, "fsdp", [(i, i + 1) for i in range(shards - 1)])
        after = lax.ppermute(head, "fsdp", [(i + 1, i) for i in range(shards - 1)])
        even = lax.axis_index("fsdp") % 2 == 0
        near, far = jnp.where(even, after, before), jnp.where(even, before, after)

    parts = len(pieces)
    whole = pltpu.VMEM((rows, width), jnp.float32)
    padded = pltpu.VMEM((rows + 2 * PAD, width), jnp.float32)
    chunk = 256 if rows % 256 == 0 else rows
    inner = [pltpu.with_memory_space_constraint(x, pltpu.VMEM) for x in (*pieces, *stats)]

    def inside(early, *done):
        return pl.pallas_call(
            functools.partial(interior, parts, early, scale, rows, chunk, 64),
            out_shape=(shape,) * 3 + (whole, pltpu.VMEM((11 * TILE, width), jnp.float32)),
            in_specs=[vmem] * (parts + 3) + ([hbm] * 3 + [vmem] * 2 if done else []),
            out_specs=(hbm,) * 3 + (vmem,) * 2,
            input_output_aliases={parts + 3 + k: k for k in range(len(done))},
            scratch_shapes=[padded] * 6 + [pltpu.SemaphoreType.DMA((3, rows // chunk))],
            compiler_params=params,
            cost_estimate=pl.CostEstimate(
                flops=45 * rows * width, bytes_accessed=36 * rows * width, transcendentals=0
            ),
            name="early" if early else "late",
        )(*inner, *done)

    done = inside(True)
    if paired:
        near, *done = lax.optimization_barrier((near, *done))
        near = lax.ppermute(near, axes, trades(shards, 0))
    diag_next, first_next, second_next, update, edges = inside(False, *done)
    other = far
    if paired:
        far, edges = lax.optimization_barrier((far, edges))
        other = swap(far)
    update = pl.pallas_call(
        functools.partial(store, rows, chunk),
        out_shape=shape,
        in_specs=[vmem],
        out_specs=hbm,
        scratch_shapes=[pltpu.SemaphoreType.DMA((rows // chunk,))],
        compiler_params=params,
        cost_estimate=pl.CostEstimate(
            flops=0, bytes_accessed=8 * rows * width, transcendentals=0
        ),
        name="store",
    )(pltpu.with_memory_space_constraint(update, pltpu.VMEM))

    def patched(turn, other, *done):
        return pl.pallas_call(
            functools.partial(border, rows, shards, scale, turn),
            out_shape=(shape,) * 3,
            in_specs=[vmem] * 4 + [hbm] * 3,
            out_specs=(hbm,) * 3,
            input_output_aliases={4: 0, 5: 1, 6: 2},
            scratch_shapes=[
                pltpu.VMEM((16, width), jnp.float32),
                pltpu.VMEM((32, width), jnp.float32),
                pltpu.SemaphoreType.DMA((4,)),
            ],
            compiler_params=params,
            name="border",
        )(edges, near, far, other, *done)

    if paired:
        done = patched(1, far, update, first_next, second_next)
        update, first_next, second_next = patched(2, other, *done)
    else:
        update, first_next, second_next = patched(0, far, update, first_next, second_next)
    return update, diag_next, first_next, second_next


def solution(mesh):
    return jax.shard_map(
        body,
        mesh=mesh,
        in_specs=(P("replica", "fsdp", None), P("fsdp", None), P("fsdp", None), P("fsdp", None)),
        out_specs=(P("fsdp", None), P("fsdp", None), P("fsdp", None), P("fsdp", None)),
        check_vma=False,
    )
```

```python
import functools

import jax
import jax.numpy as jnp
from jax import lax
from jax.experimental import pallas as pl
from jax.experimental.pallas import tpu as pltpu
from jax.sharding import PartitionSpec as P

decay_rate = 0.95
damping = 0.01
PAD = 8
TILE = 8


def solved(g, g1, g2, d, upper, lower, f, c, s):
    det = upper * lower - c * c
    n1 = lower * f - c * s
    n2 = upper * s - c * f
    schur = d * det - f * n1 - s * n2
    top = g * det - n1 * g1 - n2 * g2
    w = top / (schur * det)
    return w * det, w * n1, w * n2


def collect(rows, own, diag, first, second, out, tiles, sems):
    even = lax.rem(lax.axis_index("fsdp"), 2) == 0
    at = pl.multiple_of(jnp.where(even, 0, rows - TILE), TILE)
    copies = [
        pltpu.make_async_copy(
            source.at[pl.ds(at, TILE), :], tiles.at[k * TILE : (k + 1) * TILE, :], sems.at[k]
        )
        for k, source in enumerate((own, diag, first, second))
    ]
    for copy in copies:
        copy.start()
    for copy in copies:
        copy.wait()

    @pl.when(even)
    def _():
        for k in range(3):
            out[2 * k : 2 * k + 2, :] = tiles[k * TILE : k * TILE + 2, :]
        out[6:8, :] = jnp.ones((2, out.shape[1]), jnp.float32)

    @pl.when(jnp.logical_not(even))
    def _():
        for k in range(4):
            out[2 * k : 2 * k + 2, :] = tiles[(k + 1) * TILE - 2 : (k + 1) * TILE, :]


def ready(scale, rows, own, other, diag, first, second, out):
    even = lax.rem(lax.axis_index("fsdp"), 2) == 0

    def fill(at, sources):
        out[0:2, :] = (own[at : at + 2, :] + other[at : at + 2, :]) * scale
        for k, source in enumerate(sources):
            out[2 * k + 2 : 2 * k + 4, :] = source[at : at + 2, :]

    @pl.when(even)
    def _():
        fill(rows - 2, (diag, first, second))

    @pl.when(jnp.logical_not(even))
    def _():
        fill(0, (diag, first))
        out[6:8, :] = jnp.ones((2, out.shape[1]), jnp.float32)


def interior(parts, early, scale, rows, chunk, step, *refs):
    chosen = lax.axis_index("fsdp") == 0
    pl.when(chosen if early else jnp.logical_not(chosen))(
        functools.partial(
            everything, parts, scale, rows, chunk, step, *refs[: parts + 3], *refs[-12:]
        )
    )


def everything(parts, scale, rows, chunk, step, *refs):
    pieces = refs[:parts]
    diag_in, first_in, second_in = refs[parts : parts + 3]
    outs = refs[parts + 3 : parts + 6]
    update, edges = refs[parts + 6 : parts + 8]
    grad, diag, first, second, part1, part2, sems = refs[parts + 8 :]
    width = edges.shape[1]
    end = PAD + rows
    chunks = rows // chunk

    zeros = jnp.zeros((PAD, width), jnp.float32)
    grad[end:, :] = zeros
    diag[end:, :] = zeros + 1.0
    first[end:, :] = zeros
    part1[:PAD, :] = zeros
    part2[:PAD, :] = zeros

    def gradients(at, size):
        here, there = pl.ds(at, size), pl.ds(at + PAD, size)
        g = pieces[0][here, :]
        for piece in pieces[1:]:
            g = g + piece[here, :]
        g = g * scale
        grad[there, :] = g
        diag[there, :] = decay_rate * diag_in[here, :] + g * g

    def bands(at, size):
        here, there = pl.ds(at, size), pl.ds(at + PAD, size)
        g = grad[there, :]
        g1 = grad[pl.ds(at + PAD + 1, size), :]
        g2 = grad[pl.ds(at + PAD + 2, size), :]
        first[there, :] = decay_rate * first_in[here, :] + g * g1
        second[there, :] = decay_rate * second_in[here, :] + g * g2

    def values(at, size):
        there = pl.ds(at + PAD, size)
        after = pl.ds(at + PAD + 1, size)
        later = pl.ds(at + PAD + 2, size)
        v, p1, p2 = solved(
            grad[there, :],
            grad[after, :],
            grad[later, :],
            diag[there, :] + damping,
            diag[after, :] + damping,
            diag[later, :] + damping,
            first[there, :],
            first[after, :],
            second[there, :],
        )
        part1[there, :] = p1
        part2[there, :] = p2
        update[pl.ds(at, size), :] = (
            v - part1[pl.ds(at + PAD - 1, size), :] - part2[pl.ds(at + PAD - 2, size), :]
        )

    def over(work, low, high):
        for at in range(low, high, step):
            work(at, min(step, high - at))

    stores = []

    def send(source, k, c, low, high):
        copy = pltpu.make_async_copy(
            source.at[low + PAD : high + PAD, :], outs[k].at[low:high, :], sems.at[k, c]
        )
        copy.start()
        stores.append(copy)

    for c in range(chunks):
        low, high = c * chunk, (c + 1) * chunk
        over(gradients, low, high)
        send(diag, 0, c, low, high)
        low, high = max(low - TILE, 0), high if c == chunks - 1 else high - TILE
        over(bands, low, high)
        send(first, 1, c, low, high)
        send(second, 2, c, low, high)
    over(values, 0, rows)

    tops = [grad[PAD : PAD + TILE, :], diag[PAD : PAD + TILE, :], first[PAD : PAD + TILE, :]]
    tops.append(update[:TILE, :])
    tails = [r[end - TILE : end, :] for r in (grad, diag, first, second)]
    tails.append(update[rows - TILE :, :])
    tails += [r[end - TILE : end, :] for r in (part1, part2)]
    for k, tile in enumerate(tops + tails):
        edges[k * TILE : (k + 1) * TILE, :] = tile
    for copy in stores:
        copy.wait()


def store(rows, chunk, update, out, sems):
    copies = []
    for c in range(rows // chunk):
        low, high = max(c * chunk, TILE), min((c + 1) * chunk, rows - TILE)
        copies.append(
            pltpu.make_async_copy(update.at[low:high, :], out.at[low:high, :], sems.at[c])
        )
    for copy in copies:
        copy.start()
    for copy in copies:
        copy.wait()


def border(rows, shards, scale, turn, *refs):
    chosen = lax.axis_index("fsdp") == 0
    if turn == 0:
        patch(rows, shards, scale, *refs)
    else:
        pl.when(chosen if turn == 1 else jnp.logical_not(chosen))(
            functools.partial(patch, rows, shards, scale, *refs)
        )


def patch(rows, shards, scale, *refs):
    edges, near, far, other = refs[:4]
    outs = refs[7:10]
    work, tiles, sems = refs[10:]

    def edge(k, at, size):
        return edges[k * TILE + at : k * TILE + at + size, :]

    shard = lax.axis_index("fsdp")
    even = lax.rem(shard, 2) == 0
    near_rows, far_rows = near[...], far[...]
    if scale != 1.0:
        far_sum = (far_rows[0:2] + other[0:2, :]) * scale
        far_rows = jnp.concatenate([far_sum, far_rows[2:8]])
    before = jnp.where(even, far_rows, near_rows)
    after = jnp.where(even, near_rows, far_rows)
    work[0:8, :] = jnp.where(shard == 0, 0.0, before)
    work[8:16, :] = jnp.where(shard == shards - 1, 0.0, after)

    g = work[0:2, :]
    g_next = edge(0, 0, 2)
    d = decay_rate * work[2:4, :] + g * g + damping
    d_next = edge(1, 0, 2) + damping
    g1 = jnp.concatenate([g[1:2], g_next[0:1]])
    d1 = jnp.concatenate([d[1:2], d_next[0:1]])
    f = decay_rate * work[4:6, :] + g * g1
    s = decay_rate * work[6:8, :] + g * g_next
    c = jnp.concatenate([f[1:2], edge(2, 0, 1)])
    _, p1, p2 = solved(g, g1, g_next, d, d1, d_next, f, c, s)
    tiles[0:8, :] = edges[3 * TILE : 4 * TILE, :]
    tiles[0:1, :] = tiles[0:1, :] - p1[1:2] - p2[0:1]
    tiles[1:2, :] = tiles[1:2, :] - p2[1:2]

    g = edge(4, 6, 2)
    g_next = work[8:10, :]
    present = work[14:16, :]
    d = edge(5, 6, 2) + damping
    d_next = (
        decay_rate * work[10:12, :] + g_next * g_next + present * damping + (1.0 - present)
    )
    g1 = jnp.concatenate([g[1:2], g_next[0:1]])
    d1 = jnp.concatenate([d[1:2], d_next[0:1]])
    f_last = (edge(6, 7, 1) + g[1:2] * g_next[0:1]) * present[0:1]
    f = jnp.concatenate([edge(6, 6, 1), f_last])
    s = (edge(7, 6, 2) + g * g_next) * present
    f_next = decay_rate * work[12:13, :] + g_next[0:1] * g_next[1:2]
    c = jnp.concatenate([f_last, f_next])
    v, p1, _ = solved(g, g1, g_next, d, d1, d_next, f, c, s)
    tiles[8:16, :] = edges[8 * TILE : 9 * TILE, :]
    tiles[14:15, :] = v[0:1] - edge(9, 5, 1) - edge(10, 4, 1)
    tiles[15:16, :] = v[1:2] - p1[0:1] - edge(10, 5, 1)
    tiles[16:24, :] = edges[6 * TILE : 7 * TILE, :]
    tiles[23:24, :] = f_last
    tiles[24:32, :] = edges[7 * TILE : 8 * TILE, :]
    tiles[30:32, :] = s

    copies = [
        pltpu.make_async_copy(tiles.at[0:8, :], outs[0].at[0:TILE, :], sems.at[0]),
        pltpu.make_async_copy(tiles.at[8:16, :], outs[0].at[rows - TILE : rows, :], sems.at[1]),
        pltpu.make_async_copy(tiles.at[16:24, :], outs[1].at[rows - TILE : rows, :], sems.at[2]),
        pltpu.make_async_copy(tiles.at[24:32, :], outs[2].at[rows - TILE : rows, :], sems.at[3]),
    ]
    for copy in copies:
        copy.start()
    for copy in copies:
        copy.wait()


def trades(shards, low):
    partner = {}
    for i in range(low, shards - 1, 2):
        partner[i], partner[i + 1] = i + 1, i
    return [
        (2 * i + core, 2 * partner.get(i, i) + 1 - core) for i in range(shards) for core in range(2)
    ]


def body(partials, diag_stat, first_stat, second_stat):
    own = partials[0]
    rows, width = own.shape
    replicas = lax.axis_size("replica")
    shards = lax.axis_size("fsdp")
    scale = 1.0 / replicas
    axes = ("fsdp", "replica")
    paired = replicas == 2 and shards > 1

    shape = jax.ShapeDtypeStruct((rows, width), jnp.float32)
    vmem = pl.BlockSpec(memory_space=pltpu.VMEM)
    hbm = pl.BlockSpec(memory_space=pl.ANY)
    params = pltpu.CompilerParams(vmem_limit_bytes=24 * 2**20)

    def swap(block):
        return lax.ppermute(block, "replica", [(0, 1), (1, 0)])

    def stay(block):
        return pltpu.with_memory_space_constraint(block, pltpu.HBM)

    stats = (diag_stat, first_stat, second_stat)
    tile = pltpu.VMEM((TILE, width), jnp.float32)
    if paired:
        pieces = [own, swap(own)]
        far = pl.pallas_call(
            functools.partial(collect, rows),
            out_shape=tile,
            in_specs=[hbm] * 4,
            out_specs=vmem,
            scratch_shapes=[
                pltpu.VMEM((4 * TILE, width), jnp.float32),
                pltpu.SemaphoreType.DMA((4,)),
            ],
            compiler_params=params,
            name="collect",
        )(*[stay(x) for x in (own, *stats)])
        far = lax.ppermute(far, axes, trades(shards, 1))
    else:
        pieces = [lax.psum(own, "replica") * scale]
        scale = 1.0
        tail = rows - 2
        ones = jnp.ones((2, width), jnp.float32)
        last = jnp.concatenate([x[tail:] for x in (*pieces, *stats)])
        head = jnp.concatenate([x[:2] for x in (*pieces, *stats[:2])] + [ones])
        before = lax.ppermute(last, "fsdp", [(i, i + 1) for i in range(shards - 1)])
        after = lax.ppermute(head, "fsdp", [(i + 1, i) for i in range(shards - 1)])
        even = lax.axis_index("fsdp") % 2 == 0
        near, far = jnp.where(even, after, before), jnp.where(even, before, after)

    parts = len(pieces)
    whole = pltpu.VMEM((rows, width), jnp.float32)
    padded = pltpu.VMEM((rows + 2 * PAD, width), jnp.float32)
    chunk = 256 if rows % 256 == 0 else rows
    inner = [pltpu.with_memory_space_constraint(x, pltpu.VMEM) for x in (*pieces, *stats)]

    def inside(early, *done):
        return pl.pallas_call(
            functools.partial(interior, parts, early, scale, rows, chunk, 64),
            out_shape=(shape,) * 3 + (whole, pltpu.VMEM((11 * TILE, width), jnp.float32)),
            in_specs=[vmem] * (parts + 3) + ([hbm] * 3 + [vmem] * 2 if done else []),
            out_specs=(hbm,) * 3 + (vmem,) * 2,
            input_output_aliases={parts + 3 + k: k for k in range(len(done))},
            scratch_shapes=[padded] * 6 + [pltpu.SemaphoreType.DMA((3, rows // chunk))],
            compiler_params=params,
            cost_estimate=pl.CostEstimate(
                flops=45 * rows * width, bytes_accessed=36 * rows * width, transcendentals=0
            ),
            name="early" if early else "late",
        )(*inner, *done)

    done = inside(True)
    if paired:
        near = pl.pallas_call(
            functools.partial(ready, scale, rows),
            out_shape=tile,
            in_specs=[vmem] * 5,
            out_specs=vmem,
            compiler_params=params,
            name="ready",
        )(*inner)
        near, *done = lax.optimization_barrier((near, *done))
        near = lax.ppermute(near, axes, trades(shards, 0))
    diag_next, first_next, second_next, update, edges = inside(False, *done)
    other = far
    if paired:
        far, edges = lax.optimization_barrier((far, edges))
        other = swap(far)
    update = pl.pallas_call(
        functools.partial(store, rows, chunk),
        out_shape=shape,
        in_specs=[vmem],
        out_specs=hbm,
        scratch_shapes=[pltpu.SemaphoreType.DMA((rows // chunk,))],
        compiler_params=params,
        cost_estimate=pl.CostEstimate(
            flops=0, bytes_accessed=8 * rows * width, transcendentals=0
        ),
        name="store",
    )(pltpu.with_memory_space_constraint(update, pltpu.VMEM))

    def patched(turn, other, *done):
        return pl.pallas_call(
            functools.partial(border, rows, shards, scale, turn),
            out_shape=(shape,) * 3,
            in_specs=[vmem] * 4 + [hbm] * 3,
            out_specs=(hbm,) * 3,
            input_output_aliases={4: 0, 5: 1, 6: 2},
            scratch_shapes=[
                pltpu.VMEM((16, width), jnp.float32),
                pltpu.VMEM((32, width), jnp.float32),
                pltpu.SemaphoreType.DMA((4,)),
            ],
            compiler_params=params,
            name="border",
        )(edges, near, far, other, *done)

    if paired:
        done = patched(1, far, update, first_next, second_next)
        update, first_next, second_next = patched(2, other, *done)
    else:
        update, first_next, second_next = patched(0, far, update, first_next, second_next)
    return update, diag_next, first_next, second_next


def solution(mesh):
    return jax.shard_map(
        body,
        mesh=mesh,
        in_specs=(P("replica", "fsdp", None), P("fsdp", None), P("fsdp", None), P("fsdp", None)),
        out_specs=(P("fsdp", None), P("fsdp", None), P("fsdp", None), P("fsdp", None)),
        check_vma=False,
    )
```

```python
import functools

import jax
import jax.numpy as jnp
from jax import lax
from jax.experimental import pallas as pl
from jax.experimental.pallas import tpu as pltpu
from jax.sharding import PartitionSpec as P

decay_rate = 0.95
damping = 0.01
PAD = 8
TILE = 8


def solved(g, g1, g2, d, upper, lower, f, c, s):
    det = upper * lower - c * c
    n1 = lower * f - c * s
    n2 = upper * s - c * f
    schur = d * det - f * n1 - s * n2
    top = g * det - n1 * g1 - n2 * g2
    w = top / (schur * det)
    return w * det, w * n1, w * n2


def collect(rows, own, diag, first, second, out, tiles, sems):
    even = lax.rem(lax.axis_index("fsdp"), 2) == 0
    at = pl.multiple_of(jnp.where(even, 0, rows - TILE), TILE)
    copies = [
        pltpu.make_async_copy(
            source.at[pl.ds(at, TILE), :], tiles.at[k * TILE : (k + 1) * TILE, :], sems.at[k]
        )
        for k, source in enumerate((own, diag, first, second))
    ]
    for copy in copies:
        copy.start()
    for copy in copies:
        copy.wait()

    @pl.when(even)
    def _():
        for k in range(3):
            out[2 * k : 2 * k + 2, :] = tiles[k * TILE : k * TILE + 2, :]
        out[6:8, :] = jnp.zeros((2, out.shape[1]), jnp.float32)

    @pl.when(jnp.logical_not(even))
    def _():
        for k in range(4):
            out[2 * k : 2 * k + 2, :] = tiles[(k + 1) * TILE - 2 : (k + 1) * TILE, :]


def ready(scale, rows, own, other, diag, first, second, out):
    even = lax.rem(lax.axis_index("fsdp"), 2) == 0

    def fill(at, sources):
        out[0:2, :] = (own[at : at + 2, :] + other[at : at + 2, :]) * scale
        for k, source in enumerate(sources):
            out[2 * k + 2 : 2 * k + 4, :] = source[at : at + 2, :]

    @pl.when(even)
    def _():
        fill(rows - 2, (diag, first, second))

    @pl.when(jnp.logical_not(even))
    def _():
        fill(0, (diag, first))
        out[6:8, :] = jnp.zeros((2, out.shape[1]), jnp.float32)


def interior(parts, early, scale, rows, chunk, step, *refs):
    chosen = lax.axis_index("fsdp") == 0
    pl.when(chosen if early else jnp.logical_not(chosen))(
        functools.partial(
            everything, parts, scale, rows, chunk, step, *refs[: parts + 3], *refs[-12:]
        )
    )


def everything(parts, scale, rows, chunk, step, *refs):
    pieces = refs[:parts]
    diag_in, first_in, second_in = refs[parts : parts + 3]
    outs = refs[parts + 3 : parts + 6]
    update, edges = refs[parts + 6 : parts + 8]
    grad, diag, first, second, part1, part2, sems = refs[parts + 8 :]
    width = edges.shape[1]
    end = PAD + rows
    chunks = rows // chunk

    zeros = jnp.zeros((PAD, width), jnp.float32)
    grad[end:, :] = zeros
    diag[end:, :] = zeros + 1.0
    first[end:, :] = zeros
    part1[:PAD, :] = zeros
    part2[:PAD, :] = zeros

    def gradients(at, size):
        here, there = pl.ds(at, size), pl.ds(at + PAD, size)
        g = pieces[0][here, :]
        for piece in pieces[1:]:
            g = g + piece[here, :]
        g = g * scale
        grad[there, :] = g
        diag[there, :] = decay_rate * diag_in[here, :] + g * g

    def bands(at, size):
        here, there = pl.ds(at, size), pl.ds(at + PAD, size)
        g = grad[there, :]
        g1 = grad[pl.ds(at + PAD + 1, size), :]
        g2 = grad[pl.ds(at + PAD + 2, size), :]
        first[there, :] = decay_rate * first_in[here, :] + g * g1
        second[there, :] = decay_rate * second_in[here, :] + g * g2

    def values(at, size):
        there = pl.ds(at + PAD, size)
        after = pl.ds(at + PAD + 1, size)
        later = pl.ds(at + PAD + 2, size)
        v, p1, p2 = solved(
            grad[there, :],
            grad[after, :],
            grad[later, :],
            diag[there, :] + damping,
            diag[after, :] + damping,
            diag[later, :] + damping,
            first[there, :],
            first[after, :],
            second[there, :],
        )
        part1[there, :] = p1
        part2[there, :] = p2
        update[pl.ds(at, size), :] = (
            v - part1[pl.ds(at + PAD - 1, size), :] - part2[pl.ds(at + PAD - 2, size), :]
        )

    def over(work, low, high):
        for at in range(low, high, step):
            work(at, min(step, high - at))

    stores = []

    def send(source, k, c, low, high):
        copy = pltpu.make_async_copy(
            source.at[low + PAD : high + PAD, :], outs[k].at[low:high, :], sems.at[k, c]
        )
        copy.start()
        stores.append(copy)

    for c in range(chunks):
        low, high = c * chunk, (c + 1) * chunk
        over(gradients, low, high)
        send(diag, 0, c, low, high)
        low, high = max(low - TILE, 0), high if c == chunks - 1 else high - TILE
        over(bands, low, high)
        send(first, 1, c, low, high)
        send(second, 2, c, low, high)
    over(values, 0, rows)

    tops = [grad[PAD : PAD + TILE, :], diag[PAD : PAD + TILE, :], first[PAD : PAD + TILE, :]]
    tops.append(update[:TILE, :])
    tails = [r[end - TILE : end, :] for r in (grad, diag, first, second)]
    tails.append(update[rows - TILE :, :])
    tails += [r[end - TILE : end, :] for r in (part1, part2)]
    for k, tile in enumerate(tops + tails):
        edges[k * TILE : (k + 1) * TILE, :] = tile
    for copy in stores:
        copy.wait()


def store(rows, chunk, update, out, sems):
    copies = []
    for c in range(rows // chunk):
        low, high = max(c * chunk, TILE), min((c + 1) * chunk, rows - TILE)
        copies.append(
            pltpu.make_async_copy(update.at[low:high, :], out.at[low:high, :], sems.at[c])
        )
    for copy in copies:
        copy.start()
    for copy in copies:
        copy.wait()


def border(rows, shards, scale, turn, *refs):
    chosen = lax.axis_index("fsdp") == 0
    if turn == 0:
        patch(rows, shards, scale, *refs)
    else:
        pl.when(chosen if turn == 1 else jnp.logical_not(chosen))(
            functools.partial(patch, rows, shards, scale, *refs)
        )


def patch(rows, shards, scale, *refs):
    edges, near, far, other = refs[:4]
    outs = refs[7:10]
    tiles, sems = refs[10:]
    tiles[0:8, :] = edges[3 * TILE : 4 * TILE, :]
    tiles[8:16, :] = edges[8 * TILE : 9 * TILE, :]
    tiles[16:24, :] = edges[6 * TILE : 7 * TILE, :]
    tiles[24:32, :] = edges[7 * TILE : 8 * TILE, :]
    rest = other if scale != 1.0 else None
    even = lax.rem(lax.axis_index("fsdp"), 2) == 0

    @pl.when(even)
    def _():
        lower(scale, edges, far, rest, tiles)
        upper(scale, shards, edges, near, None, tiles)

    @pl.when(jnp.logical_not(even))
    def _():
        lower(scale, edges, near, None, tiles)
        upper(scale, shards, edges, far, rest, tiles)

    copies = [
        pltpu.make_async_copy(tiles.at[0:8, :], outs[0].at[0:TILE, :], sems.at[0]),
        pltpu.make_async_copy(tiles.at[8:16, :], outs[0].at[rows - TILE : rows, :], sems.at[1]),
        pltpu.make_async_copy(tiles.at[16:24, :], outs[1].at[rows - TILE : rows, :], sems.at[2]),
        pltpu.make_async_copy(tiles.at[24:32, :], outs[2].at[rows - TILE : rows, :], sems.at[3]),
    ]
    for copy in copies:
        copy.start()
    for copy in copies:
        copy.wait()


def neighbour(scale, block, rest):
    g = [block[k : k + 1, :] for k in range(2)]
    if rest is not None:
        g = [(g[k] + rest[k : k + 1, :]) * scale for k in range(2)]
    d = [decay_rate * block[k + 2 : k + 3, :] + g[k] * g[k] + damping for k in range(2)]
    f = decay_rate * block[4:5, :] + g[0] * g[1]
    return g, d, f


def lower(scale, edges, block, rest, tiles):
    def edge(k, at):
        return edges[k * TILE + at : k * TILE + at + 1, :]

    (ga, gb), (da, db), fa = neighbour(scale, block, rest)
    g0, g1 = edge(0, 0), edge(0, 1)
    d0, d1 = edge(1, 0) + damping, edge(1, 1) + damping
    f0 = edge(2, 0)
    fb = decay_rate * block[5:6, :] + gb * g0
    sa = decay_rate * block[6:7, :] + ga * g0
    sb = decay_rate * block[7:8, :] + gb * g1
    _, _, far_a = solved(ga, gb, g0, da, db, d0, fa, fb, sa)
    _, near_b, far_b = solved(gb, g0, g1, db, d0, d1, fb, f0, sb)
    none = lax.axis_index("fsdp") == 0
    tiles[0:1, :] = edge(3, 0) - jnp.where(none, 0.0, near_b) - jnp.where(none, 0.0, far_a)
    tiles[1:2, :] = edge(3, 1) - jnp.where(none, 0.0, far_b)


def upper(scale, shards, edges, block, rest, tiles):
    def edge(k, at):
        return edges[k * TILE + at : k * TILE + at + 1, :]

    none = lax.axis_index("fsdp") == shards - 1
    (gp, gq), (dp, dq), fp = neighbour(scale, block, rest)
    gp, gq = jnp.where(none, 0.0, gp), jnp.where(none, 0.0, gq)
    dp, dq = jnp.where(none, 1.0, dp), jnp.where(none, 1.0, dq)
    fp = jnp.where(none, 0.0, fp)
    gx, gy = edge(4, 6), edge(4, 7)
    dx, dy = edge(5, 6) + damping, edge(5, 7) + damping
    fx = edge(6, 6)
    fy = jnp.where(none, 0.0, edge(6, 7) + gy * gp)
    sx = jnp.where(none, 0.0, edge(7, 6) + gx * gp)
    sy = jnp.where(none, 0.0, edge(7, 7) + gy * gq)
    vx, near_x, _ = solved(gx, gy, gp, dx, dy, dp, fx, fy, sx)
    vy, _, _ = solved(gy, gp, gq, dy, dp, dq, fy, fp, sy)
    tiles[14:15, :] = vx - edge(9, 5) - edge(10, 4)
    tiles[15:16, :] = vy - near_x - edge(10, 5)
    tiles[23:24, :] = fy
    tiles[30:31, :] = sx
    tiles[31:32, :] = sy


def trades(shards, low):
    partner = {}
    for i in range(low, shards - 1, 2):
        partner[i], partner[i + 1] = i + 1, i
    return [
        (2 * i + core, 2 * partner.get(i, i) + 1 - core) for i in range(shards) for core in range(2)
    ]


def body(partials, diag_stat, first_stat, second_stat):
    own = partials[0]
    rows, width = own.shape
    replicas = lax.axis_size("replica")
    shards = lax.axis_size("fsdp")
    scale = 1.0 / replicas
    axes = ("fsdp", "replica")
    paired = replicas == 2 and shards > 1

    shape = jax.ShapeDtypeStruct((rows, width), jnp.float32)
    vmem = pl.BlockSpec(memory_space=pltpu.VMEM)
    hbm = pl.BlockSpec(memory_space=pl.ANY)
    params = pltpu.CompilerParams(vmem_limit_bytes=24 * 2**20)

    def swap(block):
        return lax.ppermute(block, "replica", [(0, 1), (1, 0)])

    def stay(block):
        return pltpu.with_memory_space_constraint(block, pltpu.HBM)

    stats = (diag_stat, first_stat, second_stat)
    tile = pltpu.VMEM((TILE, width), jnp.float32)
    if paired:
        pieces = [own, swap(own)]
        far = pl.pallas_call(
            functools.partial(collect, rows),
            out_shape=tile,
            in_specs=[hbm] * 4,
            out_specs=vmem,
            scratch_shapes=[
                pltpu.VMEM((4 * TILE, width), jnp.float32),
                pltpu.SemaphoreType.DMA((4,)),
            ],
            compiler_params=params,
            name="collect",
        )(*[stay(x) for x in (own, *stats)])
        far = lax.ppermute(far, axes, trades(shards, 1))
    else:
        pieces = [lax.psum(own, "replica") * scale]
        scale = 1.0
        tail = rows - 2
        unused = jnp.zeros((2, width), jnp.float32)
        last = jnp.concatenate([x[tail:] for x in (*pieces, *stats)])
        head = jnp.concatenate([x[:2] for x in (*pieces, *stats[:2])] + [unused])
        before = lax.ppermute(last, "fsdp", [(i, i + 1) for i in range(shards - 1)])
        after = lax.ppermute(head, "fsdp", [(i + 1, i) for i in range(shards - 1)])
        even = lax.axis_index("fsdp") % 2 == 0
        near, far = jnp.where(even, after, before), jnp.where(even, before, after)

    parts = len(pieces)
    whole = pltpu.VMEM((rows, width), jnp.float32)
    padded = pltpu.VMEM((rows + 2 * PAD, width), jnp.float32)
    chunk = 256 if rows % 256 == 0 else rows
    inner = [pltpu.with_memory_space_constraint(x, pltpu.VMEM) for x in (*pieces, *stats)]

    def inside(early, *done):
        return pl.pallas_call(
            functools.partial(interior, parts, early, scale, rows, chunk, 64),
            out_shape=(shape,) * 3 + (whole, pltpu.VMEM((11 * TILE, width), jnp.float32)),
            in_specs=[vmem] * (parts + 3) + ([hbm] * 3 + [vmem] * 2 if done else []),
            out_specs=(hbm,) * 3 + (vmem,) * 2,
            input_output_aliases={parts + 3 + k: k for k in range(len(done))},
            scratch_shapes=[padded] * 6 + [pltpu.SemaphoreType.DMA((3, rows // chunk))],
            compiler_params=params,
            cost_estimate=pl.CostEstimate(
                flops=45 * rows * width, bytes_accessed=36 * rows * width, transcendentals=0
            ),
            name="early" if early else "late",
        )(*inner, *done)

    done = inside(True)
    if paired:
        near = pl.pallas_call(
            functools.partial(ready, scale, rows),
            out_shape=tile,
            in_specs=[vmem] * 5,
            out_specs=vmem,
            compiler_params=params,
            name="ready",
        )(*inner)
        near, *done = lax.optimization_barrier((near, *done))
        near = lax.ppermute(near, axes, trades(shards, 0))
    diag_next, first_next, second_next, update, edges = inside(False, *done)
    other = far
    if paired:
        far, edges = lax.optimization_barrier((far, edges))
        other = swap(far)
    update = pl.pallas_call(
        functools.partial(store, rows, chunk),
        out_shape=shape,
        in_specs=[vmem],
        out_specs=hbm,
        scratch_shapes=[pltpu.SemaphoreType.DMA((rows // chunk,))],
        compiler_params=params,
        cost_estimate=pl.CostEstimate(
            flops=0, bytes_accessed=8 * rows * width, transcendentals=0
        ),
        name="store",
    )(pltpu.with_memory_space_constraint(update, pltpu.VMEM))

    def patched(turn, other, *done):
        return pl.pallas_call(
            functools.partial(border, rows, shards, scale, turn),
            out_shape=(shape,) * 3,
            in_specs=[vmem] * 4 + [hbm] * 3,
            out_specs=(hbm,) * 3,
            input_output_aliases={4: 0, 5: 1, 6: 2},
            scratch_shapes=[
                pltpu.VMEM((4 * TILE, width), jnp.float32),
                pltpu.SemaphoreType.DMA((4,)),
            ],
            compiler_params=params,
            name="border",
        )(edges, near, far, other, *done)

    if paired:
        done = patched(1, far, update, first_next, second_next)
        update, first_next, second_next = patched(2, other, *done)
    else:
        update, first_next, second_next = patched(0, far, update, first_next, second_next)
    return update, diag_next, first_next, second_next


def solution(mesh):
    return jax.shard_map(
        body,
        mesh=mesh,
        in_specs=(P("replica", "fsdp", None), P("fsdp", None), P("fsdp", None), P("fsdp", None)),
        out_specs=(P("fsdp", None), P("fsdp", None), P("fsdp", None), P("fsdp", None)),
        check_vma=False,
    )
```

```python
import functools

import jax
import jax.numpy as jnp
from jax import lax
from jax.experimental import pallas as pl
from jax.experimental.pallas import tpu as pltpu
from jax.sharding import PartitionSpec as P

decay_rate = 0.95
damping = 0.01
PAD = 8
TILE = 8


def solved(g, g1, g2, d, upper, lower, f, c, s):
    det = upper * lower - c * c
    n1 = lower * f - c * s
    n2 = upper * s - c * f
    schur = d * det - f * n1 - s * n2
    top = g * det - n1 * g1 - n2 * g2
    w = top / (schur * det)
    return w * det, w * n1, w * n2


def collect(rows, own, diag, first, second, out, tiles, sems):
    even = lax.rem(lax.axis_index("fsdp"), 2) == 0
    low = lax.axis_index("replica") == 0

    @pl.when(low)
    def _():
        at = pl.multiple_of(jnp.where(even, 0, rows - TILE), TILE)
        copies = [
            pltpu.make_async_copy(
                source.at[pl.ds(at, TILE), :], tiles.at[k * TILE : (k + 1) * TILE, :], sems.at[k]
            )
            for k, source in enumerate((own, diag, first, second))
        ]
        for copy in copies:
            copy.start()
        for copy in copies:
            copy.wait()

    @pl.when(jnp.logical_and(low, even))
    def _():
        for k in range(3):
            out[2 * k : 2 * k + 2, :] = tiles[k * TILE : k * TILE + 2, :]
        out[6:8, :] = jnp.zeros((2, out.shape[1]), jnp.float32)

    @pl.when(jnp.logical_and(low, jnp.logical_not(even)))
    def _():
        for k in range(4):
            out[2 * k : 2 * k + 2, :] = tiles[(k + 1) * TILE - 2 : (k + 1) * TILE, :]


def choose(rows, block, own, out):
    even = lax.rem(lax.axis_index("fsdp"), 2) == 0
    low = lax.axis_index("replica") == 0

    @pl.when(low)
    def _():
        out[...] = block[...]

    @pl.when(jnp.logical_not(low))
    def _():
        out[2:8, :] = jnp.zeros((6, out.shape[1]), jnp.float32)
        out[0:2, :] = jnp.where(even, own[0:2, :], own[rows - 2 : rows, :])


def ready(scale, rows, own, other, diag, first, second, out):
    even = lax.rem(lax.axis_index("fsdp"), 2) == 0

    def fill(at, sources):
        out[0:2, :] = (own[at : at + 2, :] + other[at : at + 2, :]) * scale
        for k, source in enumerate(sources):
            out[2 * k + 2 : 2 * k + 4, :] = source[at : at + 2, :]

    @pl.when(even)
    def _():
        fill(rows - 2, (diag, first, second))

    @pl.when(jnp.logical_not(even))
    def _():
        fill(0, (diag, first))
        out[6:8, :] = jnp.zeros((2, out.shape[1]), jnp.float32)


def interior(parts, early, scale, rows, chunk, step, *refs):
    chosen = lax.axis_index("fsdp") == 0
    pl.when(chosen if early else jnp.logical_not(chosen))(
        functools.partial(
            everything, parts, scale, rows, chunk, step, *refs[: parts + 3], *refs[-12:]
        )
    )


def everything(parts, scale, rows, chunk, step, *refs):
    pieces = refs[:parts]
    diag_in, first_in, second_in = refs[parts : parts + 3]
    outs = refs[parts + 3 : parts + 6]
    update, edges = refs[parts + 6 : parts + 8]
    grad, diag, first, second, part1, part2, sems = refs[parts + 8 :]
    width = edges.shape[1]
    end = PAD + rows
    chunks = rows // chunk

    zeros = jnp.zeros((PAD, width), jnp.float32)
    grad[end:, :] = zeros
    diag[end:, :] = zeros + 1.0
    first[end:, :] = zeros
    part1[:PAD, :] = zeros
    part2[:PAD, :] = zeros

    def gradients(at, size):
        here, there = pl.ds(at, size), pl.ds(at + PAD, size)
        g = pieces[0][here, :]
        for piece in pieces[1:]:
            g = g + piece[here, :]
        g = g * scale
        grad[there, :] = g
        diag[there, :] = decay_rate * diag_in[here, :] + g * g

    def bands(at, size):
        here, there = pl.ds(at, size), pl.ds(at + PAD, size)
        g = grad[there, :]
        g1 = grad[pl.ds(at + PAD + 1, size), :]
        g2 = grad[pl.ds(at + PAD + 2, size), :]
        first[there, :] = decay_rate * first_in[here, :] + g * g1
        second[there, :] = decay_rate * second_in[here, :] + g * g2

    def values(at, size):
        there = pl.ds(at + PAD, size)
        after = pl.ds(at + PAD + 1, size)
        later = pl.ds(at + PAD + 2, size)
        v, p1, p2 = solved(
            grad[there, :],
            grad[after, :],
            grad[later, :],
            diag[there, :] + damping,
            diag[after, :] + damping,
            diag[later, :] + damping,
            first[there, :],
            first[after, :],
            second[there, :],
        )
        part1[there, :] = p1
        part2[there, :] = p2
        update[pl.ds(at, size), :] = (
            v - part1[pl.ds(at + PAD - 1, size), :] - part2[pl.ds(at + PAD - 2, size), :]
        )

    def over(work, low, high):
        for at in range(low, high, step):
            work(at, min(step, high - at))

    stores = []

    def send(source, k, c, low, high):
        copy = pltpu.make_async_copy(
            source.at[low + PAD : high + PAD, :], outs[k].at[low:high, :], sems.at[k, c]
        )
        copy.start()
        stores.append(copy)

    for c in range(chunks):
        low, high = c * chunk, (c + 1) * chunk
        over(gradients, low, high)
        send(diag, 0, c, low, high)
        low, high = max(low - TILE, 0), high if c == chunks - 1 else high - TILE
        over(bands, low, high)
        send(first, 1, c, low, high)
        send(second, 2, c, low, high)
    over(values, 0, rows)

    tops = [grad[PAD : PAD + TILE, :], diag[PAD : PAD + TILE, :], first[PAD : PAD + TILE, :]]
    tops.append(update[:TILE, :])
    tails = [r[end - TILE : end, :] for r in (grad, diag, first, second)]
    tails.append(update[rows - TILE :, :])
    tails += [r[end - TILE : end, :] for r in (part1, part2)]
    for k, tile in enumerate(tops + tails):
        edges[k * TILE : (k + 1) * TILE, :] = tile
    for copy in stores:
        copy.wait()


def store(rows, chunk, update, out, sems):
    copies = []
    for c in range(rows // chunk):
        low, high = max(c * chunk, TILE), min((c + 1) * chunk, rows - TILE)
        copies.append(
            pltpu.make_async_copy(update.at[low:high, :], out.at[low:high, :], sems.at[c])
        )
    for copy in copies:
        copy.start()
    for copy in copies:
        copy.wait()


def border(rows, shards, scale, turn, *refs):
    chosen = lax.axis_index("fsdp") == 0
    if turn == 0:
        patch(rows, shards, scale, *refs)
    else:
        pl.when(chosen if turn == 1 else jnp.logical_not(chosen))(
            functools.partial(patch, rows, shards, scale, *refs)
        )


def patch(rows, shards, scale, *refs):
    edges, near, far, other = refs[:4]
    outs = refs[7:10]
    tiles, mixed, sems = refs[10:]
    tiles[0:8, :] = edges[3 * TILE : 4 * TILE, :]
    tiles[8:16, :] = edges[8 * TILE : 9 * TILE, :]
    tiles[16:24, :] = edges[6 * TILE : 7 * TILE, :]
    tiles[24:32, :] = edges[7 * TILE : 8 * TILE, :]
    rest = None
    if scale != 1.0:
        low = lax.axis_index("replica") == 0
        mine, theirs = far[...], other[...]
        mixed[0:8, :] = jnp.where(low, theirs, mine)
        mixed[8:16, :] = jnp.where(low, mine, theirs)
        far, rest = mixed.at[0:8, :], mixed.at[8:16, :]
    even = lax.rem(lax.axis_index("fsdp"), 2) == 0

    @pl.when(even)
    def _():
        lower(scale, edges, far, rest, tiles)
        upper(scale, shards, edges, near, None, tiles)

    @pl.when(jnp.logical_not(even))
    def _():
        lower(scale, edges, near, None, tiles)
        upper(scale, shards, edges, far, rest, tiles)

    copies = [
        pltpu.make_async_copy(tiles.at[0:8, :], outs[0].at[0:TILE, :], sems.at[0]),
        pltpu.make_async_copy(tiles.at[8:16, :], outs[0].at[rows - TILE : rows, :], sems.at[1]),
        pltpu.make_async_copy(tiles.at[16:24, :], outs[1].at[rows - TILE : rows, :], sems.at[2]),
        pltpu.make_async_copy(tiles.at[24:32, :], outs[2].at[rows - TILE : rows, :], sems.at[3]),
    ]
    for copy in copies:
        copy.start()
    for copy in copies:
        copy.wait()


def neighbour(scale, block, rest):
    g = [block[k : k + 1, :] for k in range(2)]
    if rest is not None:
        g = [(g[k] + rest[k : k + 1, :]) * scale for k in range(2)]
    d = [decay_rate * block[k + 2 : k + 3, :] + g[k] * g[k] + damping for k in range(2)]
    f = decay_rate * block[4:5, :] + g[0] * g[1]
    return g, d, f


def lower(scale, edges, block, rest, tiles):
    def edge(k, at):
        return edges[k * TILE + at : k * TILE + at + 1, :]

    (ga, gb), (da, db), fa = neighbour(scale, block, rest)
    g0, g1 = edge(0, 0), edge(0, 1)
    d0, d1 = edge(1, 0) + damping, edge(1, 1) + damping
    f0 = edge(2, 0)
    fb = decay_rate * block[5:6, :] + gb * g0
    sa = decay_rate * block[6:7, :] + ga * g0
    sb = decay_rate * block[7:8, :] + gb * g1
    _, _, far_a = solved(ga, gb, g0, da, db, d0, fa, fb, sa)
    _, near_b, far_b = solved(gb, g0, g1, db, d0, d1, fb, f0, sb)
    none = lax.axis_index("fsdp") == 0
    tiles[0:1, :] = edge(3, 0) - jnp.where(none, 0.0, near_b) - jnp.where(none, 0.0, far_a)
    tiles[1:2, :] = edge(3, 1) - jnp.where(none, 0.0, far_b)


def upper(scale, shards, edges, block, rest, tiles):
    def edge(k, at):
        return edges[k * TILE + at : k * TILE + at + 1, :]

    none = lax.axis_index("fsdp") == shards - 1
    (gp, gq), (dp, dq), fp = neighbour(scale, block, rest)
    gp, gq = jnp.where(none, 0.0, gp), jnp.where(none, 0.0, gq)
    dp, dq = jnp.where(none, 1.0, dp), jnp.where(none, 1.0, dq)
    fp = jnp.where(none, 0.0, fp)
    gx, gy = edge(4, 6), edge(4, 7)
    dx, dy = edge(5, 6) + damping, edge(5, 7) + damping
    fx = edge(6, 6)
    fy = jnp.where(none, 0.0, edge(6, 7) + gy * gp)
    sx = jnp.where(none, 0.0, edge(7, 6) + gx * gp)
    sy = jnp.where(none, 0.0, edge(7, 7) + gy * gq)
    vx, near_x, _ = solved(gx, gy, gp, dx, dy, dp, fx, fy, sx)
    vy, _, _ = solved(gy, gp, gq, dy, dp, dq, fy, fp, sy)
    tiles[14:15, :] = vx - edge(9, 5) - edge(10, 4)
    tiles[15:16, :] = vy - near_x - edge(10, 5)
    tiles[23:24, :] = fy
    tiles[30:31, :] = sx
    tiles[31:32, :] = sy


def trades(shards, low):
    partner = {}
    for i in range(low, shards - 1, 2):
        partner[i], partner[i + 1] = i + 1, i
    return [
        (2 * i + core, 2 * partner.get(i, i) + 1 - core) for i in range(shards) for core in range(2)
    ]


def body(partials, diag_stat, first_stat, second_stat):
    own = partials[0]
    rows, width = own.shape
    replicas = lax.axis_size("replica")
    shards = lax.axis_size("fsdp")
    scale = 1.0 / replicas
    axes = ("fsdp", "replica")
    paired = replicas == 2 and shards > 1

    shape = jax.ShapeDtypeStruct((rows, width), jnp.float32)
    vmem = pl.BlockSpec(memory_space=pltpu.VMEM)
    hbm = pl.BlockSpec(memory_space=pl.ANY)
    params = pltpu.CompilerParams(vmem_limit_bytes=24 * 2**20)

    def swap(block):
        return lax.ppermute(block, "replica", [(0, 1), (1, 0)])

    def stay(block):
        return pltpu.with_memory_space_constraint(block, pltpu.HBM)

    stats = (diag_stat, first_stat, second_stat)
    tile = pltpu.VMEM((TILE, width), jnp.float32)
    if paired:
        pieces = [own, swap(own)]
        far = pl.pallas_call(
            functools.partial(collect, rows),
            out_shape=tile,
            in_specs=[hbm] * 4,
            out_specs=vmem,
            scratch_shapes=[
                pltpu.VMEM((4 * TILE, width), jnp.float32),
                pltpu.SemaphoreType.DMA((4,)),
            ],
            compiler_params=params,
            name="collect",
        )(*[stay(x) for x in (own, *stats)])
        far = pl.pallas_call(
            functools.partial(choose, rows),
            out_shape=tile,
            in_specs=[vmem] * 2,
            out_specs=vmem,
            compiler_params=params,
            name="choose",
        )(far, pltpu.with_memory_space_constraint(own, pltpu.VMEM))
        far = lax.ppermute(far, axes, trades(shards, 1))
    else:
        pieces = [lax.psum(own, "replica") * scale]
        scale = 1.0
        tail = rows - 2
        unused = jnp.zeros((2, width), jnp.float32)
        last = jnp.concatenate([x[tail:] for x in (*pieces, *stats)])
        head = jnp.concatenate([x[:2] for x in (*pieces, *stats[:2])] + [unused])
        before = lax.ppermute(last, "fsdp", [(i, i + 1) for i in range(shards - 1)])
        after = lax.ppermute(head, "fsdp", [(i + 1, i) for i in range(shards - 1)])
        even = lax.axis_index("fsdp") % 2 == 0
        near, far = jnp.where(even, after, before), jnp.where(even, before, after)

    parts = len(pieces)
    whole = pltpu.VMEM((rows, width), jnp.float32)
    padded = pltpu.VMEM((rows + 2 * PAD, width), jnp.float32)
    chunk = 256 if rows % 256 == 0 else rows
    inner = [pltpu.with_memory_space_constraint(x, pltpu.VMEM) for x in (*pieces, *stats)]

    def inside(early, *done):
        return pl.pallas_call(
            functools.partial(interior, parts, early, scale, rows, chunk, 64),
            out_shape=(shape,) * 3 + (whole, pltpu.VMEM((11 * TILE, width), jnp.float32)),
            in_specs=[vmem] * (parts + 3) + ([hbm] * 3 + [vmem] * 2 if done else []),
            out_specs=(hbm,) * 3 + (vmem,) * 2,
            input_output_aliases={parts + 3 + k: k for k in range(len(done))},
            scratch_shapes=[padded] * 6 + [pltpu.SemaphoreType.DMA((3, rows // chunk))],
            compiler_params=params,
            cost_estimate=pl.CostEstimate(
                flops=45 * rows * width, bytes_accessed=36 * rows * width, transcendentals=0
            ),
            name="early" if early else "late",
        )(*inner, *done)

    done = inside(True)
    if paired:
        near = pl.pallas_call(
            functools.partial(ready, scale, rows),
            out_shape=tile,
            in_specs=[vmem] * 5,
            out_specs=vmem,
            compiler_params=params,
            name="ready",
        )(*inner)
        near, *done = lax.optimization_barrier((near, *done))
        near = lax.ppermute(near, axes, trades(shards, 0))
    diag_next, first_next, second_next, update, edges = inside(False, *done)
    other = far
    if paired:
        far, edges = lax.optimization_barrier((far, edges))
        other = swap(far)
    update = pl.pallas_call(
        functools.partial(store, rows, chunk),
        out_shape=shape,
        in_specs=[vmem],
        out_specs=hbm,
        scratch_shapes=[pltpu.SemaphoreType.DMA((rows // chunk,))],
        compiler_params=params,
        cost_estimate=pl.CostEstimate(
            flops=0, bytes_accessed=8 * rows * width, transcendentals=0
        ),
        name="store",
    )(pltpu.with_memory_space_constraint(update, pltpu.VMEM))

    def patched(turn, other, *done):
        return pl.pallas_call(
            functools.partial(border, rows, shards, scale, turn),
            out_shape=(shape,) * 3,
            in_specs=[vmem] * 4 + [hbm] * 3,
            out_specs=(hbm,) * 3,
            input_output_aliases={4: 0, 5: 1, 6: 2},
            scratch_shapes=[
                pltpu.VMEM((4 * TILE, width), jnp.float32),
                pltpu.VMEM((2 * TILE, width), jnp.float32),
                pltpu.SemaphoreType.DMA((4,)),
            ],
            compiler_params=params,
            name="border",
        )(edges, near, far, other, *done)

    if paired:
        done = patched(1, far, update, first_next, second_next)
        update, first_next, second_next = patched(2, other, *done)
    else:
        update, first_next, second_next = patched(0, far, update, first_next, second_next)
    return update, diag_next, first_next, second_next


def solution(mesh):
    return jax.shard_map(
        body,
        mesh=mesh,
        in_specs=(P("replica", "fsdp", None), P("fsdp", None), P("fsdp", None), P("fsdp", None)),
        out_specs=(P("fsdp", None), P("fsdp", None), P("fsdp", None), P("fsdp", None)),
        check_vma=False,
    )
```

```python
import functools

import jax
import jax.numpy as jnp
from jax import lax
from jax.experimental import pallas as pl
from jax.experimental.pallas import tpu as pltpu
from jax.sharding import PartitionSpec as P

decay_rate = 0.95
damping = 0.01
PAD = 8
TILE = 8


def solved(g, g1, g2, d, upper, lower, f, c, s):
    det = upper * lower - c * c
    n1 = lower * f - c * s
    n2 = upper * s - c * f
    schur = d * det - f * n1 - s * n2
    top = g * det - n1 * g1 - n2 * g2
    w = top / (schur * det)
    return w * det, w * n1, w * n2


def collect(rows, own, diag, first, second, out, tiles, sems):
    even = lax.rem(lax.axis_index("fsdp"), 2) == 0
    low = lax.axis_index("replica") == 0

    @pl.when(low)
    def _():
        at = pl.multiple_of(jnp.where(even, 0, rows - TILE), TILE)
        copies = [
            pltpu.make_async_copy(
                source.at[pl.ds(at, TILE), :], tiles.at[k * TILE : (k + 1) * TILE, :], sems.at[k]
            )
            for k, source in enumerate((own, diag, first, second))
        ]
        for copy in copies:
            copy.start()
        for copy in copies:
            copy.wait()

    @pl.when(jnp.logical_and(low, even))
    def _():
        for k in range(3):
            out[2 * k : 2 * k + 2, :] = tiles[k * TILE : k * TILE + 2, :]
        out[6:8, :] = jnp.zeros((2, out.shape[1]), jnp.float32)

    @pl.when(jnp.logical_and(low, jnp.logical_not(even)))
    def _():
        for k in range(4):
            out[2 * k : 2 * k + 2, :] = tiles[(k + 1) * TILE - 2 : (k + 1) * TILE, :]


def choose(rows, block, own, out):
    even = lax.rem(lax.axis_index("fsdp"), 2) == 0
    low = lax.axis_index("replica") == 0

    @pl.when(low)
    def _():
        out[...] = block[...]

    @pl.when(jnp.logical_not(low))
    def _():
        out[2:8, :] = jnp.zeros((6, out.shape[1]), jnp.float32)
        out[0:2, :] = jnp.where(even, own[0:2, :], own[rows - 2 : rows, :])


def ready(scale, rows, own, other, diag, first, second, out):
    even = lax.rem(lax.axis_index("fsdp"), 2) == 0

    def fill(at, sources):
        out[0:2, :] = (own[at : at + 2, :] + other[at : at + 2, :]) * scale
        for k, source in enumerate(sources):
            out[2 * k + 2 : 2 * k + 4, :] = source[at : at + 2, :]

    @pl.when(even)
    def _():
        fill(rows - 2, (diag, first, second))

    @pl.when(jnp.logical_not(even))
    def _():
        fill(0, (diag, first))
        out[6:8, :] = jnp.zeros((2, out.shape[1]), jnp.float32)


def interior(parts, early, scale, rows, chunk, step, *refs):
    chosen = lax.axis_index("fsdp") == 0
    pl.when(chosen if early else jnp.logical_not(chosen))(
        functools.partial(
            everything, parts, scale, rows, chunk, step, *refs[: parts + 3], *refs[-13:]
        )
    )


def everything(parts, scale, rows, chunk, step, *refs):
    pieces = refs[:parts]
    diag_in, first_in, second_in = refs[parts : parts + 3]
    outs = refs[parts + 3 : parts + 7]
    edges = refs[parts + 7]
    grad, diag, first, second, part1, part2, update, sems = refs[parts + 8 :]
    width = edges.shape[1]
    end = PAD + rows
    chunks = rows // chunk

    zeros = jnp.zeros((PAD, width), jnp.float32)
    grad[end:, :] = zeros
    diag[end:, :] = zeros + 1.0
    first[end:, :] = zeros
    part1[:PAD, :] = zeros
    part2[:PAD, :] = zeros

    def gradients(at, size):
        here, there = pl.ds(at, size), pl.ds(at + PAD, size)
        g = pieces[0][here, :]
        for piece in pieces[1:]:
            g = g + piece[here, :]
        g = g * scale
        grad[there, :] = g
        diag[there, :] = decay_rate * diag_in[here, :] + g * g

    def bands(at, size):
        here, there = pl.ds(at, size), pl.ds(at + PAD, size)
        g = grad[there, :]
        g1 = grad[pl.ds(at + PAD + 1, size), :]
        g2 = grad[pl.ds(at + PAD + 2, size), :]
        first[there, :] = decay_rate * first_in[here, :] + g * g1
        second[there, :] = decay_rate * second_in[here, :] + g * g2

    def values(at, size):
        there = pl.ds(at + PAD, size)
        after = pl.ds(at + PAD + 1, size)
        later = pl.ds(at + PAD + 2, size)
        v, p1, p2 = solved(
            grad[there, :],
            grad[after, :],
            grad[later, :],
            diag[there, :] + damping,
            diag[after, :] + damping,
            diag[later, :] + damping,
            first[there, :],
            first[after, :],
            second[there, :],
        )
        part1[there, :] = p1
        part2[there, :] = p2
        update[pl.ds(at, size), :] = (
            v - part1[pl.ds(at + PAD - 1, size), :] - part2[pl.ds(at + PAD - 2, size), :]
        )

    def over(work, low, high):
        for at in range(low, high, step):
            work(at, min(step, high - at))

    stores = []

    def send(source, pad, k, c, low, high):
        copy = pltpu.make_async_copy(
            source.at[low + pad : high + pad, :], outs[k].at[low:high, :], sems.at[k, c]
        )
        copy.start()
        stores.append(copy)

    for c in range(chunks):
        last = c == chunks - 1
        low, high = c * chunk, (c + 1) * chunk
        over(gradients, low, high)
        send(diag, PAD, 1, c, low, high)
        low, high = max(low - TILE, 0), high if last else high - TILE
        over(bands, low, high)
        send(first, PAD, 2, c, low, high)
        send(second, PAD, 3, c, low, high)
        low, high = max(c * chunk - 2 * TILE, 0), high if last else high - TILE
        over(values, low, high)
        send(update, 0, 0, c, low, high)

    tops = [grad[PAD : PAD + TILE, :], diag[PAD : PAD + TILE, :], first[PAD : PAD + TILE, :]]
    tops.append(update[:TILE, :])
    tails = [r[end - TILE : end, :] for r in (grad, diag, first, second)]
    tails.append(update[rows - TILE :, :])
    tails += [r[end - TILE : end, :] for r in (part1, part2)]
    for k, tile in enumerate(tops + tails):
        edges[k * TILE : (k + 1) * TILE, :] = tile
    for copy in stores:
        copy.wait()


def border(rows, shards, scale, turn, *refs):
    chosen = lax.axis_index("fsdp") == 0
    if turn == 0:
        patch(rows, shards, scale, *refs)
    else:
        pl.when(chosen if turn == 1 else jnp.logical_not(chosen))(
            functools.partial(patch, rows, shards, scale, *refs)
        )


def patch(rows, shards, scale, *refs):
    edges, near, far, other = refs[:4]
    outs = refs[7:10]
    tiles, mixed, sems = refs[10:]
    tiles[0:8, :] = edges[3 * TILE : 4 * TILE, :]
    tiles[8:16, :] = edges[8 * TILE : 9 * TILE, :]
    tiles[16:24, :] = edges[6 * TILE : 7 * TILE, :]
    tiles[24:32, :] = edges[7 * TILE : 8 * TILE, :]
    rest = None
    if scale != 1.0:
        low = lax.axis_index("replica") == 0
        mine, theirs = far[...], other[...]
        mixed[0:8, :] = jnp.where(low, theirs, mine)
        mixed[8:16, :] = jnp.where(low, mine, theirs)
        far, rest = mixed.at[0:8, :], mixed.at[8:16, :]
    even = lax.rem(lax.axis_index("fsdp"), 2) == 0

    @pl.when(even)
    def _():
        lower(scale, edges, far, rest, tiles)
        upper(scale, shards, edges, near, None, tiles)

    @pl.when(jnp.logical_not(even))
    def _():
        lower(scale, edges, near, None, tiles)
        upper(scale, shards, edges, far, rest, tiles)

    copies = [
        pltpu.make_async_copy(tiles.at[0:8, :], outs[0].at[0:TILE, :], sems.at[0]),
        pltpu.make_async_copy(tiles.at[8:16, :], outs[0].at[rows - TILE : rows, :], sems.at[1]),
        pltpu.make_async_copy(tiles.at[16:24, :], outs[1].at[rows - TILE : rows, :], sems.at[2]),
        pltpu.make_async_copy(tiles.at[24:32, :], outs[2].at[rows - TILE : rows, :], sems.at[3]),
    ]
    for copy in copies:
        copy.start()
    for copy in copies:
        copy.wait()


def neighbour(scale, block, rest):
    g = [block[k : k + 1, :] for k in range(2)]
    if rest is not None:
        g = [(g[k] + rest[k : k + 1, :]) * scale for k in range(2)]
    d = [decay_rate * block[k + 2 : k + 3, :] + g[k] * g[k] + damping for k in range(2)]
    f = decay_rate * block[4:5, :] + g[0] * g[1]
    return g, d, f


def lower(scale, edges, block, rest, tiles):
    def edge(k, at):
        return edges[k * TILE + at : k * TILE + at + 1, :]

    (ga, gb), (da, db), fa = neighbour(scale, block, rest)
    g0, g1 = edge(0, 0), edge(0, 1)
    d0, d1 = edge(1, 0) + damping, edge(1, 1) + damping
    f0 = edge(2, 0)
    fb = decay_rate * block[5:6, :] + gb * g0
    sa = decay_rate * block[6:7, :] + ga * g0
    sb = decay_rate * block[7:8, :] + gb * g1
    _, _, far_a = solved(ga, gb, g0, da, db, d0, fa, fb, sa)
    _, near_b, far_b = solved(gb, g0, g1, db, d0, d1, fb, f0, sb)
    none = lax.axis_index("fsdp") == 0
    tiles[0:1, :] = edge(3, 0) - jnp.where(none, 0.0, near_b) - jnp.where(none, 0.0, far_a)
    tiles[1:2, :] = edge(3, 1) - jnp.where(none, 0.0, far_b)


def upper(scale, shards, edges, block, rest, tiles):
    def edge(k, at):
        return edges[k * TILE + at : k * TILE + at + 1, :]

    none = lax.axis_index("fsdp") == shards - 1
    (gp, gq), (dp, dq), fp = neighbour(scale, block, rest)
    gp, gq = jnp.where(none, 0.0, gp), jnp.where(none, 0.0, gq)
    dp, dq = jnp.where(none, 1.0, dp), jnp.where(none, 1.0, dq)
    fp = jnp.where(none, 0.0, fp)
    gx, gy = edge(4, 6), edge(4, 7)
    dx, dy = edge(5, 6) + damping, edge(5, 7) + damping
    fx = edge(6, 6)
    fy = jnp.where(none, 0.0, edge(6, 7) + gy * gp)
    sx = jnp.where(none, 0.0, edge(7, 6) + gx * gp)
    sy = jnp.where(none, 0.0, edge(7, 7) + gy * gq)
    vx, near_x, _ = solved(gx, gy, gp, dx, dy, dp, fx, fy, sx)
    vy, _, _ = solved(gy, gp, gq, dy, dp, dq, fy, fp, sy)
    tiles[14:15, :] = vx - edge(9, 5) - edge(10, 4)
    tiles[15:16, :] = vy - near_x - edge(10, 5)
    tiles[23:24, :] = fy
    tiles[30:31, :] = sx
    tiles[31:32, :] = sy


def trades(shards, low):
    partner = {}
    for i in range(low, shards - 1, 2):
        partner[i], partner[i + 1] = i + 1, i
    return [
        (2 * i + core, 2 * partner.get(i, i) + 1 - core) for i in range(shards) for core in range(2)
    ]


def body(partials, diag_stat, first_stat, second_stat):
    own = partials[0]
    rows, width = own.shape
    replicas = lax.axis_size("replica")
    shards = lax.axis_size("fsdp")
    scale = 1.0 / replicas
    axes = ("fsdp", "replica")
    paired = replicas == 2 and shards > 1

    shape = jax.ShapeDtypeStruct((rows, width), jnp.float32)
    vmem = pl.BlockSpec(memory_space=pltpu.VMEM)
    hbm = pl.BlockSpec(memory_space=pl.ANY)
    params = pltpu.CompilerParams(vmem_limit_bytes=24 * 2**20)

    def swap(block):
        return lax.ppermute(block, "replica", [(0, 1), (1, 0)])

    def stay(block):
        return pltpu.with_memory_space_constraint(block, pltpu.HBM)

    stats = (diag_stat, first_stat, second_stat)
    tile = pltpu.VMEM((TILE, width), jnp.float32)
    if paired:
        pieces = [own, swap(own)]
        far = pl.pallas_call(
            functools.partial(collect, rows),
            out_shape=tile,
            in_specs=[hbm] * 4,
            out_specs=vmem,
            scratch_shapes=[
                pltpu.VMEM((4 * TILE, width), jnp.float32),
                pltpu.SemaphoreType.DMA((4,)),
            ],
            compiler_params=params,
            name="collect",
        )(*[stay(x) for x in (own, *stats)])
        far = pl.pallas_call(
            functools.partial(choose, rows),
            out_shape=tile,
            in_specs=[vmem] * 2,
            out_specs=vmem,
            compiler_params=params,
            name="choose",
        )(far, pltpu.with_memory_space_constraint(own, pltpu.VMEM))
        far = lax.ppermute(far, axes, trades(shards, 1))
    else:
        pieces = [lax.psum(own, "replica") * scale]
        scale = 1.0
        tail = rows - 2
        unused = jnp.zeros((2, width), jnp.float32)
        last = jnp.concatenate([x[tail:] for x in (*pieces, *stats)])
        head = jnp.concatenate([x[:2] for x in (*pieces, *stats[:2])] + [unused])
        before = lax.ppermute(last, "fsdp", [(i, i + 1) for i in range(shards - 1)])
        after = lax.ppermute(head, "fsdp", [(i + 1, i) for i in range(shards - 1)])
        even = lax.axis_index("fsdp") % 2 == 0
        near, far = jnp.where(even, after, before), jnp.where(even, before, after)

    parts = len(pieces)
    whole = pltpu.VMEM((rows, width), jnp.float32)
    padded = pltpu.VMEM((rows + 2 * PAD, width), jnp.float32)
    chunk = 256 if rows % 256 == 0 else rows
    inner = [pltpu.with_memory_space_constraint(x, pltpu.VMEM) for x in (*pieces, *stats)]

    def inside(early, *done):
        return pl.pallas_call(
            functools.partial(interior, parts, early, scale, rows, chunk, 64),
            out_shape=(shape,) * 4 + (pltpu.VMEM((11 * TILE, width), jnp.float32),),
            in_specs=[vmem] * (parts + 3) + ([hbm] * 4 + [vmem] if done else []),
            out_specs=(hbm,) * 4 + (vmem,),
            input_output_aliases={parts + 3 + k: k for k in range(len(done))},
            scratch_shapes=[padded] * 6 + [whole, pltpu.SemaphoreType.DMA((4, rows // chunk))],
            compiler_params=params,
            cost_estimate=pl.CostEstimate(
                flops=45 * rows * width, bytes_accessed=36 * rows * width, transcendentals=0
            ),
            name="early" if early else "late",
        )(*inner, *done)

    done = inside(True)
    if paired:
        near = pl.pallas_call(
            functools.partial(ready, scale, rows),
            out_shape=tile,
            in_specs=[vmem] * 5,
            out_specs=vmem,
            compiler_params=params,
            name="ready",
        )(*inner)
        near, *done = lax.optimization_barrier((near, *done))
        near = lax.ppermute(near, axes, trades(shards, 0))
    update, diag_next, first_next, second_next, edges = inside(False, *done)
    other = far
    if paired:
        far, edges = lax.optimization_barrier((far, edges))
        other = swap(far)
    def patched(turn, other, *done):
        return pl.pallas_call(
            functools.partial(border, rows, shards, scale, turn),
            out_shape=(shape,) * 3,
            in_specs=[vmem] * 4 + [hbm] * 3,
            out_specs=(hbm,) * 3,
            input_output_aliases={4: 0, 5: 1, 6: 2},
            scratch_shapes=[
                pltpu.VMEM((4 * TILE, width), jnp.float32),
                pltpu.VMEM((2 * TILE, width), jnp.float32),
                pltpu.SemaphoreType.DMA((4,)),
            ],
            compiler_params=params,
            name="border",
        )(edges, near, far, other, *done)

    if paired:
        done = patched(1, far, update, first_next, second_next)
        update, first_next, second_next = patched(2, other, *done)
    else:
        update, first_next, second_next = patched(0, far, update, first_next, second_next)
    return update, diag_next, first_next, second_next


def solution(mesh):
    return jax.shard_map(
        body,
        mesh=mesh,
        in_specs=(P("replica", "fsdp", None), P("fsdp", None), P("fsdp", None), P("fsdp", None)),
        out_specs=(P("fsdp", None), P("fsdp", None), P("fsdp", None), P("fsdp", None)),
        check_vma=False,
    )
```

```python
import functools

import jax
import jax.numpy as jnp
from jax import lax
from jax.experimental import pallas as pl
from jax.experimental.pallas import tpu as pltpu
from jax.sharding import PartitionSpec as P

decay_rate = 0.95
damping = 0.01
PAD = 8
TILE = 8


def solved(g, g1, g2, d, upper, lower, f, c, s):
    det = upper * lower - c * c
    n1 = lower * f - c * s
    n2 = upper * s - c * f
    schur = d * det - f * n1 - s * n2
    top = g * det - n1 * g1 - n2 * g2
    w = top / (schur * det)
    return w * det, w * n1, w * n2


def collect(rows, own, diag, first, second, out, tiles, sems):
    even = lax.rem(lax.axis_index("fsdp"), 2) == 0
    low = lax.axis_index("replica") == 0

    @pl.when(low)
    def _():
        at = pl.multiple_of(jnp.where(even, 0, rows - TILE), TILE)
        copies = [
            pltpu.make_async_copy(
                source.at[pl.ds(at, TILE), :], tiles.at[k * TILE : (k + 1) * TILE, :], sems.at[k]
            )
            for k, source in enumerate((own, diag, first, second))
        ]
        for copy in copies:
            copy.start(priority=1)
        for copy in copies:
            copy.wait()

    @pl.when(jnp.logical_and(low, even))
    def _():
        for k in range(3):
            out[2 * k : 2 * k + 2, :] = tiles[k * TILE : k * TILE + 2, :]
        out[6:8, :] = jnp.zeros((2, out.shape[1]), jnp.float32)

    @pl.when(jnp.logical_and(low, jnp.logical_not(even)))
    def _():
        for k in range(4):
            out[2 * k : 2 * k + 2, :] = tiles[(k + 1) * TILE - 2 : (k + 1) * TILE, :]


def choose(rows, block, own, out):
    even = lax.rem(lax.axis_index("fsdp"), 2) == 0
    low = lax.axis_index("replica") == 0

    @pl.when(low)
    def _():
        out[...] = block[...]

    @pl.when(jnp.logical_not(low))
    def _():
        out[2:8, :] = jnp.zeros((6, out.shape[1]), jnp.float32)
        out[0:2, :] = jnp.where(even, own[0:2, :], own[rows - 2 : rows, :])


def ready(scale, rows, own, other, diag, first, second, out):
    even = lax.rem(lax.axis_index("fsdp"), 2) == 0

    def fill(at, sources):
        out[0:2, :] = (own[at : at + 2, :] + other[at : at + 2, :]) * scale
        for k, source in enumerate(sources):
            out[2 * k + 2 : 2 * k + 4, :] = source[at : at + 2, :]

    @pl.when(even)
    def _():
        fill(rows - 2, (diag, first, second))

    @pl.when(jnp.logical_not(even))
    def _():
        fill(0, (diag, first))
        out[6:8, :] = jnp.zeros((2, out.shape[1]), jnp.float32)


def interior(parts, early, scale, rows, chunk, step, *refs):
    chosen = lax.axis_index("fsdp") == 0
    pl.when(chosen if early else jnp.logical_not(chosen))(
        functools.partial(
            everything, parts, scale, rows, chunk, step, *refs[: parts + 3], *refs[-13:]
        )
    )


def everything(parts, scale, rows, chunk, step, *refs):
    pieces = refs[:parts]
    diag_in, first_in, second_in = refs[parts : parts + 3]
    outs = refs[parts + 3 : parts + 7]
    edges = refs[parts + 7]
    grad, diag, first, second, part1, part2, update, sems = refs[parts + 8 :]
    width = edges.shape[1]
    end = PAD + rows
    chunks = rows // chunk

    zeros = jnp.zeros((PAD, width), jnp.float32)
    grad[end:, :] = zeros
    diag[end:, :] = zeros + 1.0
    first[end:, :] = zeros
    part1[:PAD, :] = zeros
    part2[:PAD, :] = zeros

    def gradients(at, size):
        here, there = pl.ds(at, size), pl.ds(at + PAD, size)
        g = pieces[0][here, :]
        for piece in pieces[1:]:
            g = g + piece[here, :]
        g = g * scale
        grad[there, :] = g
        diag[there, :] = decay_rate * diag_in[here, :] + g * g

    def bands(at, size):
        here, there = pl.ds(at, size), pl.ds(at + PAD, size)
        g = grad[there, :]
        g1 = grad[pl.ds(at + PAD + 1, size), :]
        g2 = grad[pl.ds(at + PAD + 2, size), :]
        first[there, :] = decay_rate * first_in[here, :] + g * g1
        second[there, :] = decay_rate * second_in[here, :] + g * g2

    def values(at, size):
        there = pl.ds(at + PAD, size)
        after = pl.ds(at + PAD + 1, size)
        later = pl.ds(at + PAD + 2, size)
        v, p1, p2 = solved(
            grad[there, :],
            grad[after, :],
            grad[later, :],
            diag[there, :] + damping,
            diag[after, :] + damping,
            diag[later, :] + damping,
            first[there, :],
            first[after, :],
            second[there, :],
        )
        part1[there, :] = p1
        part2[there, :] = p2
        update[pl.ds(at, size), :] = (
            v - part1[pl.ds(at + PAD - 1, size), :] - part2[pl.ds(at + PAD - 2, size), :]
        )

    def over(work, low, high):
        for at in range(low, high, step):
            work(at, min(step, high - at))

    stores = []

    def send(source, pad, k, c, low, high):
        copy = pltpu.make_async_copy(
            source.at[low + pad : high + pad, :], outs[k].at[low:high, :], sems.at[k, c]
        )
        copy.start(priority=k % 2)
        stores.append(copy)

    for c in range(chunks):
        last = c == chunks - 1
        low, high = c * chunk, (c + 1) * chunk
        over(gradients, low, high)
        send(diag, PAD, 1, c, low, high)
        low, high = max(low - TILE, 0), high if last else high - TILE
        over(bands, low, high)
        send(first, PAD, 2, c, low, high)
        send(second, PAD, 3, c, low, high)
        low, high = max(c * chunk - 2 * TILE, 0), high if last else high - TILE
        over(values, low, high)
        send(update, 0, 0, c, low, high)

    tops = [grad[PAD : PAD + TILE, :], diag[PAD : PAD + TILE, :], first[PAD : PAD + TILE, :]]
    tops.append(update[:TILE, :])
    tails = [r[end - TILE : end, :] for r in (grad, diag, first, second)]
    tails.append(update[rows - TILE :, :])
    tails += [r[end - TILE : end, :] for r in (part1, part2)]
    for k, tile in enumerate(tops + tails):
        edges[k * TILE : (k + 1) * TILE, :] = tile
    for copy in stores:
        copy.wait()


def border(rows, shards, scale, turn, *refs):
    chosen = lax.axis_index("fsdp") == 0
    if turn == 0:
        patch(rows, shards, scale, *refs)
    else:
        pl.when(chosen if turn == 1 else jnp.logical_not(chosen))(
            functools.partial(patch, rows, shards, scale, *refs)
        )


def patch(rows, shards, scale, *refs):
    edges, near, far, other = refs[:4]
    outs = refs[7:10]
    tiles, mixed, sems = refs[10:]
    tiles[0:8, :] = edges[3 * TILE : 4 * TILE, :]
    tiles[8:16, :] = edges[8 * TILE : 9 * TILE, :]
    tiles[16:24, :] = edges[6 * TILE : 7 * TILE, :]
    tiles[24:32, :] = edges[7 * TILE : 8 * TILE, :]
    rest = None
    if scale != 1.0:
        low = lax.axis_index("replica") == 0
        mine, theirs = far[...], other[...]
        mixed[0:8, :] = jnp.where(low, theirs, mine)
        mixed[8:16, :] = jnp.where(low, mine, theirs)
        far, rest = mixed.at[0:8, :], mixed.at[8:16, :]
    even = lax.rem(lax.axis_index("fsdp"), 2) == 0

    @pl.when(even)
    def _():
        lower(scale, edges, far, rest, tiles)
        upper(scale, shards, edges, near, None, tiles)

    @pl.when(jnp.logical_not(even))
    def _():
        lower(scale, edges, near, None, tiles)
        upper(scale, shards, edges, far, rest, tiles)

    copies = [
        pltpu.make_async_copy(tiles.at[0:8, :], outs[0].at[0:TILE, :], sems.at[0]),
        pltpu.make_async_copy(tiles.at[8:16, :], outs[0].at[rows - TILE : rows, :], sems.at[1]),
        pltpu.make_async_copy(tiles.at[16:24, :], outs[1].at[rows - TILE : rows, :], sems.at[2]),
        pltpu.make_async_copy(tiles.at[24:32, :], outs[2].at[rows - TILE : rows, :], sems.at[3]),
    ]
    for copy in copies:
        copy.start()
    for copy in copies:
        copy.wait()


def neighbour(scale, block, rest):
    g = [block[k : k + 1, :] for k in range(2)]
    if rest is not None:
        g = [(g[k] + rest[k : k + 1, :]) * scale for k in range(2)]
    d = [decay_rate * block[k + 2 : k + 3, :] + g[k] * g[k] + damping for k in range(2)]
    f = decay_rate * block[4:5, :] + g[0] * g[1]
    return g, d, f


def lower(scale, edges, block, rest, tiles):
    def edge(k, at):
        return edges[k * TILE + at : k * TILE + at + 1, :]

    (ga, gb), (da, db), fa = neighbour(scale, block, rest)
    g0, g1 = edge(0, 0), edge(0, 1)
    d0, d1 = edge(1, 0) + damping, edge(1, 1) + damping
    f0 = edge(2, 0)
    fb = decay_rate * block[5:6, :] + gb * g0
    sa = decay_rate * block[6:7, :] + ga * g0
    sb = decay_rate * block[7:8, :] + gb * g1
    _, _, far_a = solved(ga, gb, g0, da, db, d0, fa, fb, sa)
    _, near_b, far_b = solved(gb, g0, g1, db, d0, d1, fb, f0, sb)
    none = lax.axis_index("fsdp") == 0
    tiles[0:1, :] = edge(3, 0) - jnp.where(none, 0.0, near_b) - jnp.where(none, 0.0, far_a)
    tiles[1:2, :] = edge(3, 1) - jnp.where(none, 0.0, far_b)


def upper(scale, shards, edges, block, rest, tiles):
    def edge(k, at):
        return edges[k * TILE + at : k * TILE + at + 1, :]

    none = lax.axis_index("fsdp") == shards - 1
    (gp, gq), (dp, dq), fp = neighbour(scale, block, rest)
    gp, gq = jnp.where(none, 0.0, gp), jnp.where(none, 0.0, gq)
    dp, dq = jnp.where(none, 1.0, dp), jnp.where(none, 1.0, dq)
    fp = jnp.where(none, 0.0, fp)
    gx, gy = edge(4, 6), edge(4, 7)
    dx, dy = edge(5, 6) + damping, edge(5, 7) + damping
    fx = edge(6, 6)
    fy = jnp.where(none, 0.0, edge(6, 7) + gy * gp)
    sx = jnp.where(none, 0.0, edge(7, 6) + gx * gp)
    sy = jnp.where(none, 0.0, edge(7, 7) + gy * gq)
    vx, near_x, _ = solved(gx, gy, gp, dx, dy, dp, fx, fy, sx)
    vy, _, _ = solved(gy, gp, gq, dy, dp, dq, fy, fp, sy)
    tiles[14:15, :] = vx - edge(9, 5) - edge(10, 4)
    tiles[15:16, :] = vy - near_x - edge(10, 5)
    tiles[23:24, :] = fy
    tiles[30:31, :] = sx
    tiles[31:32, :] = sy


def trades(shards, low):
    partner = {}
    for i in range(low, shards - 1, 2):
        partner[i], partner[i + 1] = i + 1, i
    return [
        (2 * i + core, 2 * partner.get(i, i) + 1 - core) for i in range(shards) for core in range(2)
    ]


def body(partials, diag_stat, first_stat, second_stat):
    own = partials[0]
    rows, width = own.shape
    replicas = lax.axis_size("replica")
    shards = lax.axis_size("fsdp")
    scale = 1.0 / replicas
    axes = ("fsdp", "replica")
    paired = replicas == 2 and shards > 1

    shape = jax.ShapeDtypeStruct((rows, width), jnp.float32)
    vmem = pl.BlockSpec(memory_space=pltpu.VMEM)
    hbm = pl.BlockSpec(memory_space=pl.ANY)
    params = pltpu.CompilerParams(vmem_limit_bytes=24 * 2**20)

    def swap(block):
        return lax.ppermute(block, "replica", [(0, 1), (1, 0)])

    def stay(block):
        return pltpu.with_memory_space_constraint(block, pltpu.HBM)

    stats = (diag_stat, first_stat, second_stat)
    tile = pltpu.VMEM((TILE, width), jnp.float32)
    if paired:
        pieces = [own, swap(own)]
        far = pl.pallas_call(
            functools.partial(collect, rows),
            out_shape=tile,
            in_specs=[hbm] * 4,
            out_specs=vmem,
            scratch_shapes=[
                pltpu.VMEM((4 * TILE, width), jnp.float32),
                pltpu.SemaphoreType.DMA((4,)),
            ],
            compiler_params=params,
            name="collect",
        )(*[stay(x) for x in (own, *stats)])
        far = pl.pallas_call(
            functools.partial(choose, rows),
            out_shape=tile,
            in_specs=[vmem] * 2,
            out_specs=vmem,
            compiler_params=params,
            name="choose",
        )(far, pltpu.with_memory_space_constraint(own, pltpu.VMEM))
        far = lax.ppermute(far, axes, trades(shards, 1))
    else:
        pieces = [lax.psum(own, "replica") * scale]
        scale = 1.0
        tail = rows - 2
        unused = jnp.zeros((2, width), jnp.float32)
        last = jnp.concatenate([x[tail:] for x in (*pieces, *stats)])
        head = jnp.concatenate([x[:2] for x in (*pieces, *stats[:2])] + [unused])
        before = lax.ppermute(last, "fsdp", [(i, i + 1) for i in range(shards - 1)])
        after = lax.ppermute(head, "fsdp", [(i + 1, i) for i in range(shards - 1)])
        even = lax.axis_index("fsdp") % 2 == 0
        near, far = jnp.where(even, after, before), jnp.where(even, before, after)

    parts = len(pieces)
    whole = pltpu.VMEM((rows, width), jnp.float32)
    padded = pltpu.VMEM((rows + 2 * PAD, width), jnp.float32)
    chunk = 256 if rows % 256 == 0 else rows
    inner = [pltpu.with_memory_space_constraint(x, pltpu.VMEM) for x in (*pieces, *stats)]

    def inside(early, *done):
        return pl.pallas_call(
            functools.partial(interior, parts, early, scale, rows, chunk, 64),
            out_shape=(shape,) * 4 + (pltpu.VMEM((11 * TILE, width), jnp.float32),),
            in_specs=[vmem] * (parts + 3) + ([hbm] * 4 + [vmem] if done else []),
            out_specs=(hbm,) * 4 + (vmem,),
            input_output_aliases={parts + 3 + k: k for k in range(len(done))},
            scratch_shapes=[padded] * 6 + [whole, pltpu.SemaphoreType.DMA((4, rows // chunk))],
            compiler_params=params,
            cost_estimate=pl.CostEstimate(
                flops=45 * rows * width, bytes_accessed=36 * rows * width, transcendentals=0
            ),
            name="early" if early else "late",
        )(*inner, *done)

    done = inside(True)
    if paired:
        near = pl.pallas_call(
            functools.partial(ready, scale, rows),
            out_shape=tile,
            in_specs=[vmem] * 5,
            out_specs=vmem,
            compiler_params=params,
            name="ready",
        )(*inner)
        near, *done = lax.optimization_barrier((near, *done))
        near = lax.ppermute(near, axes, trades(shards, 0))
    update, diag_next, first_next, second_next, edges = inside(False, *done)
    other = far
    if paired:
        far, edges = lax.optimization_barrier((far, edges))
        other = swap(far)
    def patched(turn, other, *done):
        return pl.pallas_call(
            functools.partial(border, rows, shards, scale, turn),
            out_shape=(shape,) * 3,
            in_specs=[vmem] * 4 + [hbm] * 3,
            out_specs=(hbm,) * 3,
            input_output_aliases={4: 0, 5: 1, 6: 2},
            scratch_shapes=[
                pltpu.VMEM((4 * TILE, width), jnp.float32),
                pltpu.VMEM((2 * TILE, width), jnp.float32),
                pltpu.SemaphoreType.DMA((4,)),
            ],
            compiler_params=params,
            name="border",
        )(edges, near, far, other, *done)

    if paired:
        done = patched(1, far, update, first_next, second_next)
        update, first_next, second_next = patched(2, other, *done)
    else:
        update, first_next, second_next = patched(0, far, update, first_next, second_next)
    return update, diag_next, first_next, second_next


def solution(mesh):
    return jax.shard_map(
        body,
        mesh=mesh,
        in_specs=(P("replica", "fsdp", None), P("fsdp", None), P("fsdp", None), P("fsdp", None)),
        out_specs=(P("fsdp", None), P("fsdp", None), P("fsdp", None), P("fsdp", None)),
        check_vma=False,
    )
```

```python
import functools

import jax
import jax.numpy as jnp
from jax import lax
from jax.experimental import pallas as pl
from jax.experimental.pallas import tpu as pltpu
from jax.sharding import PartitionSpec as P

decay_rate = 0.95
damping = 0.01
PAD = 8
TILE = 8


def solved(g, g1, g2, d, upper, lower, f, c, s):
    det = upper * lower - c * c
    n1 = lower * f - c * s
    n2 = upper * s - c * f
    schur = d * det - f * n1 - s * n2
    top = g * det - n1 * g1 - n2 * g2
    w = top / (schur * det)
    return w * det, w * n1, w * n2


def collect(rows, own, diag, first, second, out, tiles, sems):
    even = lax.rem(lax.axis_index("fsdp"), 2) == 0
    low = lax.axis_index("replica") == 0

    @pl.when(low)
    def _():
        at = pl.multiple_of(jnp.where(even, 0, rows - TILE), TILE)
        copies = [
            pltpu.make_async_copy(
                source.at[pl.ds(at, TILE), :], tiles.at[k * TILE : (k + 1) * TILE, :], sems.at[k]
            )
            for k, source in enumerate((own, diag, first, second))
        ]
        for copy in copies:
            copy.start()
        for copy in copies:
            copy.wait()

    @pl.when(jnp.logical_and(low, even))
    def _():
        for k in range(3):
            out[2 * k : 2 * k + 2, :] = tiles[k * TILE : k * TILE + 2, :]
        out[6:8, :] = jnp.zeros((2, out.shape[1]), jnp.float32)

    @pl.when(jnp.logical_and(low, jnp.logical_not(even)))
    def _():
        for k in range(4):
            out[2 * k : 2 * k + 2, :] = tiles[(k + 1) * TILE - 2 : (k + 1) * TILE, :]


def choose(rows, block, own, out):
    even = lax.rem(lax.axis_index("fsdp"), 2) == 0
    low = lax.axis_index("replica") == 0

    @pl.when(low)
    def _():
        out[...] = block[...]

    @pl.when(jnp.logical_not(low))
    def _():
        out[2:8, :] = jnp.zeros((6, out.shape[1]), jnp.float32)
        out[0:2, :] = jnp.where(even, own[0:2, :], own[rows - 2 : rows, :])


def ready(scale, rows, own, other, diag, first, second, out):
    even = lax.rem(lax.axis_index("fsdp"), 2) == 0

    def fill(at, sources):
        out[0:2, :] = (own[at : at + 2, :] + other[at : at + 2, :]) * scale
        for k, source in enumerate(sources):
            out[2 * k + 2 : 2 * k + 4, :] = source[at : at + 2, :]

    @pl.when(even)
    def _():
        fill(rows - 2, (diag, first, second))

    @pl.when(jnp.logical_not(even))
    def _():
        fill(0, (diag, first))
        out[6:8, :] = jnp.zeros((2, out.shape[1]), jnp.float32)


def interior(parts, early, scale, rows, chunk, step, *refs):
    chosen = lax.axis_index("fsdp") == 0
    work = functools.partial(
        everything, parts, scale, rows, chunk, step, *refs[: parts + 3], *refs[-13:]
    )
    if early:
        pl.when(chosen)(work)
    else:
        pl.when(jnp.logical_not(chosen))(work)

        @pl.when(chosen)
        def _():
            refs[-9][...] = refs[parts + 7][...]


def everything(parts, scale, rows, chunk, step, *refs):
    pieces = refs[:parts]
    diag_in, first_in, second_in = refs[parts : parts + 3]
    outs = refs[parts + 3 : parts + 7]
    edges = refs[parts + 7]
    grad, diag, first, second, part1, part2, update, sems = refs[parts + 8 :]
    width = edges.shape[1]
    end = PAD + rows
    chunks = rows // chunk

    zeros = jnp.zeros((PAD, width), jnp.float32)
    grad[end:, :] = zeros
    diag[end:, :] = zeros + 1.0
    first[end:, :] = zeros
    part1[:PAD, :] = zeros
    part2[:PAD, :] = zeros

    def gradients(at, size):
        here, there = pl.ds(at, size), pl.ds(at + PAD, size)
        g = pieces[0][here, :]
        for piece in pieces[1:]:
            g = g + piece[here, :]
        g = g * scale
        grad[there, :] = g
        diag[there, :] = decay_rate * diag_in[here, :] + g * g

    def bands(at, size):
        here, there = pl.ds(at, size), pl.ds(at + PAD, size)
        g = grad[there, :]
        g1 = grad[pl.ds(at + PAD + 1, size), :]
        g2 = grad[pl.ds(at + PAD + 2, size), :]
        first[there, :] = decay_rate * first_in[here, :] + g * g1
        second[there, :] = decay_rate * second_in[here, :] + g * g2

    def values(at, size):
        there = pl.ds(at + PAD, size)
        after = pl.ds(at + PAD + 1, size)
        later = pl.ds(at + PAD + 2, size)
        v, p1, p2 = solved(
            grad[there, :],
            grad[after, :],
            grad[later, :],
            diag[there, :] + damping,
            diag[after, :] + damping,
            diag[later, :] + damping,
            first[there, :],
            first[after, :],
            second[there, :],
        )
        part1[there, :] = p1
        part2[there, :] = p2
        update[pl.ds(at, size), :] = (
            v - part1[pl.ds(at + PAD - 1, size), :] - part2[pl.ds(at + PAD - 2, size), :]
        )

    def over(work, low, high):
        for at in range(low, high, step):
            work(at, min(step, high - at))

    stores = []

    def send(source, pad, k, c, low, high):
        copy = pltpu.make_async_copy(
            source.at[low + pad : high + pad, :], outs[k].at[low:high, :], sems.at[k, c]
        )
        copy.start()
        stores.append(copy)

    for c in range(chunks):
        last = c == chunks - 1
        low, high = c * chunk, (c + 1) * chunk
        over(gradients, low, high)
        send(diag, PAD, 1, c, low, high)
        low, high = max(low - TILE, 0), high if last else high - TILE
        over(bands, low, high)
        send(first, PAD, 2, c, low, high)
        send(second, PAD, 3, c, low, high)
        low, high = max(c * chunk - 2 * TILE, 0), high if last else high - TILE
        over(values, low, high)
        send(update, 0, 0, c, low, high)

    tops = [grad[PAD : PAD + TILE, :], diag[PAD : PAD + TILE, :], first[PAD : PAD + TILE, :]]
    tops.append(update[:TILE, :])
    tails = [r[end - TILE : end, :] for r in (grad, diag, first, second)]
    tails.append(update[rows - TILE :, :])
    tails += [r[end - TILE : end, :] for r in (part1, part2)]
    for k, tile in enumerate(tops + tails):
        edges[k * TILE : (k + 1) * TILE, :] = tile
    for copy in stores:
        copy.wait()


def border(rows, shards, scale, turn, *refs):
    chosen = lax.axis_index("fsdp") == 0
    if turn == 0:
        patch(rows, shards, scale, *refs)
    else:
        pl.when(chosen if turn == 1 else jnp.logical_not(chosen))(
            functools.partial(patch, rows, shards, scale, *refs)
        )


def patch(rows, shards, scale, *refs):
    edges, near, far, other = refs[:4]
    outs = refs[7:10]
    tiles, mixed, sems = refs[10:]
    tiles[0:8, :] = edges[3 * TILE : 4 * TILE, :]
    tiles[8:16, :] = edges[8 * TILE : 9 * TILE, :]
    tiles[16:24, :] = edges[6 * TILE : 7 * TILE, :]
    tiles[24:32, :] = edges[7 * TILE : 8 * TILE, :]
    rest = None
    if scale != 1.0:
        low = lax.axis_index("replica") == 0
        mine, theirs = far[...], other[...]
        mixed[0:8, :] = jnp.where(low, theirs, mine)
        mixed[8:16, :] = jnp.where(low, mine, theirs)
        far, rest = mixed.at[0:8, :], mixed.at[8:16, :]
    even = lax.rem(lax.axis_index("fsdp"), 2) == 0

    @pl.when(even)
    def _():
        lower(scale, edges, far, rest, tiles)
        upper(scale, shards, edges, near, None, tiles)

    @pl.when(jnp.logical_not(even))
    def _():
        lower(scale, edges, near, None, tiles)
        upper(scale, shards, edges, far, rest, tiles)

    copies = [
        pltpu.make_async_copy(tiles.at[0:8, :], outs[0].at[0:TILE, :], sems.at[0]),
        pltpu.make_async_copy(tiles.at[8:16, :], outs[0].at[rows - TILE : rows, :], sems.at[1]),
        pltpu.make_async_copy(tiles.at[16:24, :], outs[1].at[rows - TILE : rows, :], sems.at[2]),
        pltpu.make_async_copy(tiles.at[24:32, :], outs[2].at[rows - TILE : rows, :], sems.at[3]),
    ]
    for copy in copies:
        copy.start()
    for copy in copies:
        copy.wait()


def neighbour(scale, block, rest):
    g = [block[k : k + 1, :] for k in range(2)]
    if rest is not None:
        g = [(g[k] + rest[k : k + 1, :]) * scale for k in range(2)]
    d = [decay_rate * block[k + 2 : k + 3, :] + g[k] * g[k] + damping for k in range(2)]
    f = decay_rate * block[4:5, :] + g[0] * g[1]
    return g, d, f


def lower(scale, edges, block, rest, tiles):
    def edge(k, at):
        return edges[k * TILE + at : k * TILE + at + 1, :]

    (ga, gb), (da, db), fa = neighbour(scale, block, rest)
    g0, g1 = edge(0, 0), edge(0, 1)
    d0, d1 = edge(1, 0) + damping, edge(1, 1) + damping
    f0 = edge(2, 0)
    fb = decay_rate * block[5:6, :] + gb * g0
    sa = decay_rate * block[6:7, :] + ga * g0
    sb = decay_rate * block[7:8, :] + gb * g1
    _, _, far_a = solved(ga, gb, g0, da, db, d0, fa, fb, sa)
    _, near_b, far_b = solved(gb, g0, g1, db, d0, d1, fb, f0, sb)
    none = lax.axis_index("fsdp") == 0
    tiles[0:1, :] = edge(3, 0) - jnp.where(none, 0.0, near_b) - jnp.where(none, 0.0, far_a)
    tiles[1:2, :] = edge(3, 1) - jnp.where(none, 0.0, far_b)


def upper(scale, shards, edges, block, rest, tiles):
    def edge(k, at):
        return edges[k * TILE + at : k * TILE + at + 1, :]

    none = lax.axis_index("fsdp") == shards - 1
    (gp, gq), (dp, dq), fp = neighbour(scale, block, rest)
    gp, gq = jnp.where(none, 0.0, gp), jnp.where(none, 0.0, gq)
    dp, dq = jnp.where(none, 1.0, dp), jnp.where(none, 1.0, dq)
    fp = jnp.where(none, 0.0, fp)
    gx, gy = edge(4, 6), edge(4, 7)
    dx, dy = edge(5, 6) + damping, edge(5, 7) + damping
    fx = edge(6, 6)
    fy = jnp.where(none, 0.0, edge(6, 7) + gy * gp)
    sx = jnp.where(none, 0.0, edge(7, 6) + gx * gp)
    sy = jnp.where(none, 0.0, edge(7, 7) + gy * gq)
    vx, near_x, _ = solved(gx, gy, gp, dx, dy, dp, fx, fy, sx)
    vy, _, _ = solved(gy, gp, gq, dy, dp, dq, fy, fp, sy)
    tiles[14:15, :] = vx - edge(9, 5) - edge(10, 4)
    tiles[15:16, :] = vy - near_x - edge(10, 5)
    tiles[23:24, :] = fy
    tiles[30:31, :] = sx
    tiles[31:32, :] = sy


def trades(shards, low):
    partner = {}
    for i in range(low, shards - 1, 2):
        partner[i], partner[i + 1] = i + 1, i
    return [
        (2 * i + core, 2 * partner.get(i, i) + 1 - core) for i in range(shards) for core in range(2)
    ]


def body(partials, diag_stat, first_stat, second_stat):
    own = partials[0]
    rows, width = own.shape
    replicas = lax.axis_size("replica")
    shards = lax.axis_size("fsdp")
    scale = 1.0 / replicas
    axes = ("fsdp", "replica")
    paired = replicas == 2 and shards > 1

    shape = jax.ShapeDtypeStruct((rows, width), jnp.float32)
    vmem = pl.BlockSpec(memory_space=pltpu.VMEM)
    hbm = pl.BlockSpec(memory_space=pl.ANY)
    params = pltpu.CompilerParams(vmem_limit_bytes=24 * 2**20)

    def swap(block):
        return lax.ppermute(block, "replica", [(0, 1), (1, 0)])

    def stay(block):
        return pltpu.with_memory_space_constraint(block, pltpu.HBM)

    stats = (diag_stat, first_stat, second_stat)
    tile = pltpu.VMEM((TILE, width), jnp.float32)
    if paired:
        pieces = [own, swap(own)]
        far = pl.pallas_call(
            functools.partial(collect, rows),
            out_shape=tile,
            in_specs=[hbm] * 4,
            out_specs=vmem,
            scratch_shapes=[
                pltpu.VMEM((4 * TILE, width), jnp.float32),
                pltpu.SemaphoreType.DMA((4,)),
            ],
            compiler_params=params,
            name="collect",
        )(*[stay(x) for x in (own, *stats)])
        far = pl.pallas_call(
            functools.partial(choose, rows),
            out_shape=tile,
            in_specs=[vmem] * 2,
            out_specs=vmem,
            compiler_params=params,
            name="choose",
        )(far, pltpu.with_memory_space_constraint(own, pltpu.VMEM))
        far = lax.ppermute(far, axes, trades(shards, 1))
    else:
        pieces = [lax.psum(own, "replica") * scale]
        scale = 1.0
        tail = rows - 2
        unused = jnp.zeros((2, width), jnp.float32)
        last = jnp.concatenate([x[tail:] for x in (*pieces, *stats)])
        head = jnp.concatenate([x[:2] for x in (*pieces, *stats[:2])] + [unused])
        before = lax.ppermute(last, "fsdp", [(i, i + 1) for i in range(shards - 1)])
        after = lax.ppermute(head, "fsdp", [(i + 1, i) for i in range(shards - 1)])
        even = lax.axis_index("fsdp") % 2 == 0
        near, far = jnp.where(even, after, before), jnp.where(even, before, after)

    parts = len(pieces)
    whole = pltpu.VMEM((rows, width), jnp.float32)
    padded = pltpu.VMEM((rows + 2 * PAD, width), jnp.float32)
    chunk = 256 if rows % 256 == 0 else rows
    inner = [pltpu.with_memory_space_constraint(x, pltpu.VMEM) for x in (*pieces, *stats)]

    def inside(early, *done):
        return pl.pallas_call(
            functools.partial(interior, parts, early, scale, rows, chunk, 64),
            out_shape=(shape,) * 4 + (pltpu.VMEM((11 * TILE, width), jnp.float32),),
            in_specs=[vmem] * (parts + 3) + ([hbm] * 4 + [vmem] if done else []),
            out_specs=(hbm,) * 4 + (vmem,),
            input_output_aliases={parts + 3 + k: k for k in range(len(done[:4]))},
            scratch_shapes=[padded] * 6 + [whole, pltpu.SemaphoreType.DMA((4, rows // chunk))],
            compiler_params=params,
            cost_estimate=pl.CostEstimate(
                flops=45 * rows * width, bytes_accessed=36 * rows * width, transcendentals=0
            ),
            name="early" if early else "late",
        )(*inner, *done)

    done = inside(True)
    if paired:
        near = pl.pallas_call(
            functools.partial(ready, scale, rows),
            out_shape=tile,
            in_specs=[vmem] * 5,
            out_specs=vmem,
            compiler_params=params,
            name="ready",
        )(*inner)
        near, *done = lax.optimization_barrier((near, *done))
        near = lax.ppermute(near, axes, trades(shards, 0))
    update, diag_next, first_next, second_next, edges = inside(False, *done)
    other = far
    if paired:
        far, edges = lax.optimization_barrier((far, edges))
        other = swap(far)
    def patched(turn, other, *done):
        return pl.pallas_call(
            functools.partial(border, rows, shards, scale, turn),
            out_shape=(shape,) * 3,
            in_specs=[vmem] * 4 + [hbm] * 3,
            out_specs=(hbm,) * 3,
            input_output_aliases={4: 0, 5: 1, 6: 2},
            scratch_shapes=[
                pltpu.VMEM((4 * TILE, width), jnp.float32),
                pltpu.VMEM((2 * TILE, width), jnp.float32),
                pltpu.SemaphoreType.DMA((4,)),
            ],
            compiler_params=params,
            name="border",
        )(edges, near, far, other, *done)

    if paired:
        done = patched(1, far, update, first_next, second_next)
        update, first_next, second_next = patched(2, other, *done)
    else:
        update, first_next, second_next = patched(0, far, update, first_next, second_next)
    return update, diag_next, first_next, second_next


def solution(mesh):
    return jax.shard_map(
        body,
        mesh=mesh,
        in_specs=(P("replica", "fsdp", None), P("fsdp", None), P("fsdp", None), P("fsdp", None)),
        out_specs=(P("fsdp", None), P("fsdp", None), P("fsdp", None), P("fsdp", None)),
        check_vma=False,
    )
```

```python
import functools

import jax
import jax.numpy as jnp
from jax import lax
from jax.experimental import pallas as pl
from jax.experimental.pallas import tpu as pltpu
from jax.sharding import PartitionSpec as P

decay_rate = 0.95
damping = 0.01
PAD = 8
TILE = 8


def solved(g, g1, g2, d, upper, lower, f, c, s):
    det = upper * lower - c * c
    n1 = lower * f - c * s
    n2 = upper * s - c * f
    schur = d * det - f * n1 - s * n2
    top = g * det - n1 * g1 - n2 * g2
    w = top / (schur * det)
    return w * det, w * n1, w * n2


def collect(rows, own, diag, first, second, out, tiles, sems):
    even = lax.rem(lax.axis_index("fsdp"), 2) == 0
    low = lax.axis_index("replica") == 0

    @pl.when(low)
    def _():
        at = pl.multiple_of(jnp.where(even, 0, rows - TILE), TILE)
        copies = [
            pltpu.make_async_copy(
                source.at[pl.ds(at, TILE), :], tiles.at[k * TILE : (k + 1) * TILE, :], sems.at[k]
            )
            for k, source in enumerate((own, diag, first, second))
        ]
        for copy in copies[:3]:
            copy.start()

        @pl.when(jnp.logical_not(even))
        def _():
            copies[3].start()
            copies[3].wait()

        for copy in copies[:3]:
            copy.wait()

    @pl.when(jnp.logical_and(low, even))
    def _():
        for k in range(3):
            out[2 * k : 2 * k + 2, :] = tiles[k * TILE : k * TILE + 2, :]
        out[6:8, :] = jnp.zeros((2, out.shape[1]), jnp.float32)

    @pl.when(jnp.logical_and(low, jnp.logical_not(even)))
    def _():
        for k in range(4):
            out[2 * k : 2 * k + 2, :] = tiles[(k + 1) * TILE - 2 : (k + 1) * TILE, :]


def choose(rows, block, own, out):
    even = lax.rem(lax.axis_index("fsdp"), 2) == 0
    low = lax.axis_index("replica") == 0

    @pl.when(low)
    def _():
        out[...] = block[...]

    @pl.when(jnp.logical_not(low))
    def _():
        out[2:8, :] = jnp.zeros((6, out.shape[1]), jnp.float32)
        out[0:2, :] = jnp.where(even, own[0:2, :], own[rows - 2 : rows, :])


def ready(scale, rows, own, other, diag, first, second, out):
    even = lax.rem(lax.axis_index("fsdp"), 2) == 0

    def fill(at, sources):
        out[0:2, :] = (own[at : at + 2, :] + other[at : at + 2, :]) * scale
        for k, source in enumerate(sources):
            out[2 * k + 2 : 2 * k + 4, :] = source[at : at + 2, :]

    @pl.when(even)
    def _():
        fill(rows - 2, (diag, first, second))

    @pl.when(jnp.logical_not(even))
    def _():
        fill(0, (diag, first))
        out[6:8, :] = jnp.zeros((2, out.shape[1]), jnp.float32)


def interior(parts, early, scale, rows, chunk, step, *refs):
    chosen = lax.axis_index("fsdp") == 0
    work = functools.partial(
        everything, parts, scale, rows, chunk, step, *refs[: parts + 3], *refs[-13:]
    )
    if early:
        pl.when(chosen)(work)
    else:
        pl.when(jnp.logical_not(chosen))(work)

        @pl.when(chosen)
        def _():
            refs[-9][...] = refs[parts + 7][...]


def everything(parts, scale, rows, chunk, step, *refs):
    pieces = refs[:parts]
    diag_in, first_in, second_in = refs[parts : parts + 3]
    outs = refs[parts + 3 : parts + 7]
    edges = refs[parts + 7]
    grad, diag, first, second, part1, part2, update, sems = refs[parts + 8 :]
    width = edges.shape[1]
    end = PAD + rows
    chunks = rows // chunk

    zeros = jnp.zeros((PAD, width), jnp.float32)
    grad[end:, :] = zeros
    diag[end:, :] = zeros + 1.0
    first[end:, :] = zeros
    part1[:PAD, :] = zeros
    part2[:PAD, :] = zeros

    def gradients(at, size):
        here, there = pl.ds(at, size), pl.ds(at + PAD, size)
        g = pieces[0][here, :]
        for piece in pieces[1:]:
            g = g + piece[here, :]
        g = g * scale
        grad[there, :] = g
        diag[there, :] = decay_rate * diag_in[here, :] + g * g

    def bands(at, size):
        here, there = pl.ds(at, size), pl.ds(at + PAD, size)
        g = grad[there, :]
        g1 = grad[pl.ds(at + PAD + 1, size), :]
        g2 = grad[pl.ds(at + PAD + 2, size), :]
        first[there, :] = decay_rate * first_in[here, :] + g * g1
        second[there, :] = decay_rate * second_in[here, :] + g * g2

    def values(at, size):
        there = pl.ds(at + PAD, size)
        after = pl.ds(at + PAD + 1, size)
        later = pl.ds(at + PAD + 2, size)
        v, p1, p2 = solved(
            grad[there, :],
            grad[after, :],
            grad[later, :],
            diag[there, :] + damping,
            diag[after, :] + damping,
            diag[later, :] + damping,
            first[there, :],
            first[after, :],
            second[there, :],
        )
        part1[there, :] = p1
        part2[there, :] = p2
        update[pl.ds(at, size), :] = (
            v - part1[pl.ds(at + PAD - 1, size), :] - part2[pl.ds(at + PAD - 2, size), :]
        )

    def over(work, low, high):
        whole = (high - low) // step

        def body(i, carry):
            work(pl.multiple_of(low + i * step, TILE), step)
            return carry

        lax.fori_loop(0, whole, body, 0)
        if low + whole * step < high:
            work(low + whole * step, high - low - whole * step)

    stores = []

    def send(source, pad, k, c, low, high):
        copy = pltpu.make_async_copy(
            source.at[low + pad : high + pad, :], outs[k].at[low:high, :], sems.at[k, c]
        )
        copy.start()
        stores.append(copy)

    for c in range(chunks):
        last = c == chunks - 1
        low, high = c * chunk, (c + 1) * chunk
        over(gradients, low, high)
        send(diag, PAD, 1, c, low, high)
        low, high = max(low - TILE, 0), high if last else high - TILE
        over(bands, low, high)
        send(first, PAD, 2, c, low, high)
        send(second, PAD, 3, c, low, high)
        low, high = max(c * chunk - 2 * TILE, 0), high if last else high - TILE
        over(values, low, high)
        send(update, 0, 0, c, low, high)

    tops = [grad[PAD : PAD + TILE, :], diag[PAD : PAD + TILE, :], first[PAD : PAD + TILE, :]]
    tops.append(update[:TILE, :])
    tails = [r[end - TILE : end, :] for r in (grad, diag, first, second)]
    tails.append(update[rows - TILE :, :])
    tails += [r[end - TILE : end, :] for r in (part1, part2)]
    for k, tile in enumerate(tops + tails):
        edges[k * TILE : (k + 1) * TILE, :] = tile
    for copy in stores:
        copy.wait()


def border(rows, shards, scale, turn, *refs):
    chosen = lax.axis_index("fsdp") == 0
    if turn == 0:
        patch(rows, shards, scale, *refs)
    else:
        pl.when(chosen if turn == 1 else jnp.logical_not(chosen))(
            functools.partial(patch, rows, shards, scale, *refs)
        )


def patch(rows, shards, scale, *refs):
    edges, near, far, other = refs[:4]
    outs = refs[7:10]
    tiles, mixed, sems = refs[10:]
    tiles[0:8, :] = edges[3 * TILE : 4 * TILE, :]
    tiles[8:16, :] = edges[8 * TILE : 9 * TILE, :]
    tiles[16:24, :] = edges[6 * TILE : 7 * TILE, :]
    tiles[24:32, :] = edges[7 * TILE : 8 * TILE, :]
    rest = None
    if scale != 1.0:
        low = lax.axis_index("replica") == 0
        mine, theirs = far[...], other[...]
        mixed[0:8, :] = jnp.where(low, theirs, mine)
        mixed[8:16, :] = jnp.where(low, mine, theirs)
        far, rest = mixed.at[0:8, :], mixed.at[8:16, :]
    even = lax.rem(lax.axis_index("fsdp"), 2) == 0

    @pl.when(even)
    def _():
        lower(scale, edges, far, rest, tiles)
        upper(scale, shards, edges, near, None, tiles)

    @pl.when(jnp.logical_not(even))
    def _():
        lower(scale, edges, near, None, tiles)
        upper(scale, shards, edges, far, rest, tiles)

    copies = [
        pltpu.make_async_copy(tiles.at[0:8, :], outs[0].at[0:TILE, :], sems.at[0]),
        pltpu.make_async_copy(tiles.at[8:16, :], outs[0].at[rows - TILE : rows, :], sems.at[1]),
        pltpu.make_async_copy(tiles.at[16:24, :], outs[1].at[rows - TILE : rows, :], sems.at[2]),
        pltpu.make_async_copy(tiles.at[24:32, :], outs[2].at[rows - TILE : rows, :], sems.at[3]),
    ]
    for copy in copies:
        copy.start()
    for copy in copies:
        copy.wait()


def neighbour(scale, block, rest):
    g = [block[k : k + 1, :] for k in range(2)]
    if rest is not None:
        g = [(g[k] + rest[k : k + 1, :]) * scale for k in range(2)]
    d = [decay_rate * block[k + 2 : k + 3, :] + g[k] * g[k] + damping for k in range(2)]
    f = decay_rate * block[4:5, :] + g[0] * g[1]
    return g, d, f


def lower(scale, edges, block, rest, tiles):
    def edge(k, at):
        return edges[k * TILE + at : k * TILE + at + 1, :]

    (ga, gb), (da, db), fa = neighbour(scale, block, rest)
    g0, g1 = edge(0, 0), edge(0, 1)
    d0, d1 = edge(1, 0) + damping, edge(1, 1) + damping
    f0 = edge(2, 0)
    fb = decay_rate * block[5:6, :] + gb * g0
    sa = decay_rate * block[6:7, :] + ga * g0
    sb = decay_rate * block[7:8, :] + gb * g1
    _, _, far_a = solved(ga, gb, g0, da, db, d0, fa, fb, sa)
    _, near_b, far_b = solved(gb, g0, g1, db, d0, d1, fb, f0, sb)
    none = lax.axis_index("fsdp") == 0
    tiles[0:1, :] = edge(3, 0) - jnp.where(none, 0.0, near_b) - jnp.where(none, 0.0, far_a)
    tiles[1:2, :] = edge(3, 1) - jnp.where(none, 0.0, far_b)


def upper(scale, shards, edges, block, rest, tiles):
    def edge(k, at):
        return edges[k * TILE + at : k * TILE + at + 1, :]

    none = lax.axis_index("fsdp") == shards - 1
    (gp, gq), (dp, dq), fp = neighbour(scale, block, rest)
    gp, gq = jnp.where(none, 0.0, gp), jnp.where(none, 0.0, gq)
    dp, dq = jnp.where(none, 1.0, dp), jnp.where(none, 1.0, dq)
    fp = jnp.where(none, 0.0, fp)
    gx, gy = edge(4, 6), edge(4, 7)
    dx, dy = edge(5, 6) + damping, edge(5, 7) + damping
    fx = edge(6, 6)
    fy = jnp.where(none, 0.0, edge(6, 7) + gy * gp)
    sx = jnp.where(none, 0.0, edge(7, 6) + gx * gp)
    sy = jnp.where(none, 0.0, edge(7, 7) + gy * gq)
    vx, near_x, _ = solved(gx, gy, gp, dx, dy, dp, fx, fy, sx)
    vy, _, _ = solved(gy, gp, gq, dy, dp, dq, fy, fp, sy)
    tiles[14:15, :] = vx - edge(9, 5) - edge(10, 4)
    tiles[15:16, :] = vy - near_x - edge(10, 5)
    tiles[23:24, :] = fy
    tiles[30:31, :] = sx
    tiles[31:32, :] = sy


def trades(shards, low):
    partner = {}
    for i in range(low, shards - 1, 2):
        partner[i], partner[i + 1] = i + 1, i
    return [
        (2 * i + core, 2 * partner.get(i, i) + 1 - core) for i in range(shards) for core in range(2)
    ]


def body(partials, diag_stat, first_stat, second_stat):
    own = partials[0]
    rows, width = own.shape
    replicas = lax.axis_size("replica")
    shards = lax.axis_size("fsdp")
    scale = 1.0 / replicas
    axes = ("fsdp", "replica")
    paired = replicas == 2 and shards > 1

    shape = jax.ShapeDtypeStruct((rows, width), jnp.float32)
    vmem = pl.BlockSpec(memory_space=pltpu.VMEM)
    hbm = pl.BlockSpec(memory_space=pl.ANY)
    params = pltpu.CompilerParams(vmem_limit_bytes=24 * 2**20)

    def swap(block):
        return lax.ppermute(block, "replica", [(0, 1), (1, 0)])

    def stay(block):
        return pltpu.with_memory_space_constraint(block, pltpu.HBM)

    stats = (diag_stat, first_stat, second_stat)
    tile = pltpu.VMEM((TILE, width), jnp.float32)
    if paired:
        pieces = [own, swap(own)]
        far = pl.pallas_call(
            functools.partial(collect, rows),
            out_shape=tile,
            in_specs=[hbm] * 4,
            out_specs=vmem,
            scratch_shapes=[
                pltpu.VMEM((4 * TILE, width), jnp.float32),
                pltpu.SemaphoreType.DMA((4,)),
            ],
            compiler_params=params,
            name="collect",
        )(*[stay(x) for x in (own, *stats)])
        far = pl.pallas_call(
            functools.partial(choose, rows),
            out_shape=tile,
            in_specs=[vmem] * 2,
            out_specs=vmem,
            compiler_params=params,
            name="choose",
        )(far, pltpu.with_memory_space_constraint(own, pltpu.VMEM))
        far = lax.ppermute(far, axes, trades(shards, 1))
    else:
        pieces = [lax.psum(own, "replica") * scale]
        scale = 1.0
        tail = rows - 2
        unused = jnp.zeros((2, width), jnp.float32)
        last = jnp.concatenate([x[tail:] for x in (*pieces, *stats)])
        head = jnp.concatenate([x[:2] for x in (*pieces, *stats[:2])] + [unused])
        before = lax.ppermute(last, "fsdp", [(i, i + 1) for i in range(shards - 1)])
        after = lax.ppermute(head, "fsdp", [(i + 1, i) for i in range(shards - 1)])
        even = lax.axis_index("fsdp") % 2 == 0
        near, far = jnp.where(even, after, before), jnp.where(even, before, after)

    parts = len(pieces)
    whole = pltpu.VMEM((rows, width), jnp.float32)
    padded = pltpu.VMEM((rows + 2 * PAD, width), jnp.float32)
    chunk = 256 if rows % 256 == 0 else rows
    inner = [pltpu.with_memory_space_constraint(x, pltpu.VMEM) for x in (*pieces, *stats)]

    def inside(early, *done):
        return pl.pallas_call(
            functools.partial(interior, parts, early, scale, rows, chunk, 64),
            out_shape=(shape,) * 4 + (pltpu.VMEM((11 * TILE, width), jnp.float32),),
            in_specs=[vmem] * (parts + 3) + ([hbm] * 4 + [vmem] if done else []),
            out_specs=(hbm,) * 4 + (vmem,),
            input_output_aliases={parts + 3 + k: k for k in range(len(done[:4]))},
            scratch_shapes=[padded] * 6 + [whole, pltpu.SemaphoreType.DMA((4, rows // chunk))],
            compiler_params=params,
            cost_estimate=pl.CostEstimate(
                flops=45 * rows * width, bytes_accessed=36 * rows * width, transcendentals=0
            ),
            name="early" if early else "late",
        )(*inner, *done)

    done = inside(True)
    if paired:
        near = pl.pallas_call(
            functools.partial(ready, scale, rows),
            out_shape=tile,
            in_specs=[vmem] * 5,
            out_specs=vmem,
            compiler_params=params,
            name="ready",
        )(*inner)
        near, *done = lax.optimization_barrier((near, *done))
        near = lax.ppermute(near, axes, trades(shards, 0))
    update, diag_next, first_next, second_next, edges = inside(False, *done)
    other = far
    if paired:
        far, edges = lax.optimization_barrier((far, edges))
        other = swap(far)
    def patched(turn, other, *done):
        return pl.pallas_call(
            functools.partial(border, rows, shards, scale, turn),
            out_shape=(shape,) * 3,
            in_specs=[vmem] * 4 + [hbm] * 3,
            out_specs=(hbm,) * 3,
            input_output_aliases={4: 0, 5: 1, 6: 2},
            scratch_shapes=[
                pltpu.VMEM((4 * TILE, width), jnp.float32),
                pltpu.VMEM((2 * TILE, width), jnp.float32),
                pltpu.SemaphoreType.DMA((4,)),
            ],
            compiler_params=params,
            name="border",
        )(edges, near, far, other, *done)

    if paired:
        done = patched(1, far, update, first_next, second_next)
        update, first_next, second_next = patched(2, other, *done)
    else:
        update, first_next, second_next = patched(0, far, update, first_next, second_next)
    return update, diag_next, first_next, second_next


def solution(mesh):
    return jax.shard_map(
        body,
        mesh=mesh,
        in_specs=(P("replica", "fsdp", None), P("fsdp", None), P("fsdp", None), P("fsdp", None)),
        out_specs=(P("fsdp", None), P("fsdp", None), P("fsdp", None), P("fsdp", None)),
        check_vma=False,
    )
```

```python
import functools

import jax
import jax.numpy as jnp
from jax import lax
from jax.experimental import pallas as pl
from jax.experimental.pallas import tpu as pltpu
from jax.sharding import PartitionSpec as P

decay_rate = 0.95
damping = 0.01
PAD = 8
TILE = 8


def solved(g, g1, g2, d, upper, lower, f, c, s):
    det = upper * lower - c * c
    n1 = lower * f - c * s
    n2 = upper * s - c * f
    schur = d * det - f * n1 - s * n2
    top = g * det - n1 * g1 - n2 * g2
    w = top / (schur * det)
    return w * det, w * n1, w * n2


def collect(rows, own, diag, first, second, out, tiles, sems):
    even = lax.rem(lax.axis_index("fsdp"), 2) == 0
    low = lax.axis_index("replica") == 0

    @pl.when(low)
    def _():
        at = pl.multiple_of(jnp.where(even, 0, rows - TILE), TILE)
        copies = [
            pltpu.make_async_copy(
                source.at[pl.ds(at, TILE), :], tiles.at[k * TILE : (k + 1) * TILE, :], sems.at[k]
            )
            for k, source in enumerate((own, diag, first, second))
        ]
        for copy in copies:
            copy.start()
        for copy in copies:
            copy.wait()

    @pl.when(jnp.logical_and(low, even))
    def _():
        for k in range(3):
            out[2 * k : 2 * k + 2, :] = tiles[k * TILE : k * TILE + 2, :]
        out[6:8, :] = jnp.zeros((2, out.shape[1]), jnp.float32)

    @pl.when(jnp.logical_and(low, jnp.logical_not(even)))
    def _():
        for k in range(4):
            out[2 * k : 2 * k + 2, :] = tiles[(k + 1) * TILE - 2 : (k + 1) * TILE, :]


def choose(rows, block, own, out):
    even = lax.rem(lax.axis_index("fsdp"), 2) == 0
    low = lax.axis_index("replica") == 0

    @pl.when(low)
    def _():
        out[...] = block[...]

    @pl.when(jnp.logical_not(low))
    def _():
        out[2:8, :] = jnp.zeros((6, out.shape[1]), jnp.float32)
        out[0:2, :] = jnp.where(even, own[0:2, :], own[rows - 2 : rows, :])


def ready(scale, rows, own, other, diag, first, second, out):
    even = lax.rem(lax.axis_index("fsdp"), 2) == 0

    def fill(at, sources):
        out[0:2, :] = (own[at : at + 2, :] + other[at : at + 2, :]) * scale
        for k, source in enumerate(sources):
            out[2 * k + 2 : 2 * k + 4, :] = source[at : at + 2, :]

    @pl.when(even)
    def _():
        fill(rows - 2, (diag, first, second))

    @pl.when(jnp.logical_not(even))
    def _():
        fill(0, (diag, first))
        out[6:8, :] = jnp.zeros((2, out.shape[1]), jnp.float32)


def interior(parts, early, scale, rows, chunk, step, *refs):
    chosen = lax.axis_index("fsdp") == 0
    work = functools.partial(
        everything, parts, scale, rows, chunk, step, *refs[: parts + 3], *refs[-13:]
    )
    if early:
        pl.when(chosen)(work)
    else:
        pl.when(jnp.logical_not(chosen))(work)

        @pl.when(chosen)
        def _():
            refs[-9][...] = refs[parts + 7][...]


def everything(parts, scale, rows, chunk, step, *refs):
    pieces = refs[:parts]
    diag_in, first_in, second_in = refs[parts : parts + 3]
    outs = refs[parts + 3 : parts + 7]
    edges = refs[parts + 7]
    grad, diag, first, second, part1, part2, update, sems = refs[parts + 8 :]
    width = edges.shape[1]
    end = PAD + rows
    chunks = rows // chunk

    zeros = jnp.zeros((PAD, width), jnp.float32)
    grad[end:, :] = zeros
    diag[end:, :] = zeros + 1.0
    first[end:, :] = zeros
    part1[:PAD, :] = zeros
    part2[:PAD, :] = zeros

    def gradients(at, size):
        here, there = pl.ds(at, size), pl.ds(at + PAD, size)
        g = pieces[0][here, :]
        for piece in pieces[1:]:
            g = g + piece[here, :]
        g = g * scale
        grad[there, :] = g
        diag[there, :] = decay_rate * diag_in[here, :] + g * g

    def bands(at, size):
        here, there = pl.ds(at, size), pl.ds(at + PAD, size)
        g = grad[there, :]
        g1 = grad[pl.ds(at + PAD + 1, size), :]
        g2 = grad[pl.ds(at + PAD + 2, size), :]
        first[there, :] = decay_rate * first_in[here, :] + g * g1
        second[there, :] = decay_rate * second_in[here, :] + g * g2

    def values(at, size):
        there = pl.ds(at + PAD, size)
        after = pl.ds(at + PAD + 1, size)
        later = pl.ds(at + PAD + 2, size)
        v, p1, p2 = solved(
            grad[there, :],
            grad[after, :],
            grad[later, :],
            diag[there, :] + damping,
            diag[after, :] + damping,
            diag[later, :] + damping,
            first[there, :],
            first[after, :],
            second[there, :],
        )
        part1[there, :] = p1
        part2[there, :] = p2
        update[pl.ds(at, size), :] = (
            v - part1[pl.ds(at + PAD - 1, size), :] - part2[pl.ds(at + PAD - 2, size), :]
        )

    def over(work, low, high):
        for at in range(low, high, step):
            work(at, min(step, high - at))

    stores = []

    def send(source, pad, k, c, low, high):
        copy = pltpu.make_async_copy(
            source.at[low + pad : high + pad, :], outs[k].at[low:high, :], sems.at[k, c]
        )
        copy.start()
        stores.append(copy)

    for c in range(chunks):
        last = c == chunks - 1
        low, high = c * chunk, (c + 1) * chunk
        over(gradients, low, high)
        send(diag, PAD, 1, c, low, high)
        low, high = max(low - TILE, 0), high if last else high - TILE
        over(bands, low, high)
        send(first, PAD, 2, c, low, high)
        send(second, PAD, 3, c, low, high)
        low, high = max(c * chunk - 2 * TILE, 0), high if last else high - TILE
        over(values, low, high)
        send(update, 0, 0, c, low, high)

    tops = [grad[PAD : PAD + TILE, :], diag[PAD : PAD + TILE, :], first[PAD : PAD + TILE, :]]
    tops.append(update[:TILE, :])
    tails = [r[end - TILE : end, :] for r in (grad, diag, first, second)]
    tails.append(update[rows - TILE :, :])
    tails += [r[end - TILE : end, :] for r in (part1, part2)]
    for k, tile in enumerate(tops + tails):
        edges[k * TILE : (k + 1) * TILE, :] = tile
    for copy in stores:
        copy.wait()


def border(rows, shards, scale, turn, *refs):
    chosen = lax.axis_index("fsdp") == 0
    if turn == 0:
        patch(rows, shards, scale, *refs)
    else:
        pl.when(chosen if turn == 1 else jnp.logical_not(chosen))(
            functools.partial(patch, rows, shards, scale, *refs)
        )


def patch(rows, shards, scale, *refs):
    edges, near, far, other = refs[:4]
    outs = refs[7:10]
    tiles, mixed, sems = refs[10:]
    tiles[0:8, :] = edges[3 * TILE : 4 * TILE, :]
    tiles[8:16, :] = edges[8 * TILE : 9 * TILE, :]
    tiles[16:24, :] = edges[6 * TILE : 7 * TILE, :]
    tiles[24:32, :] = edges[7 * TILE : 8 * TILE, :]
    rest = None
    if scale != 1.0:
        low = lax.axis_index("replica") == 0
        mine, theirs = far[...], other[...]
        mixed[0:8, :] = jnp.where(low, theirs, mine)
        mixed[8:16, :] = jnp.where(low, mine, theirs)
        far, rest = mixed.at[0:8, :], mixed.at[8:16, :]
    even = lax.rem(lax.axis_index("fsdp"), 2) == 0

    @pl.when(even)
    def _():
        lower(scale, edges, far, rest, tiles)
        upper(scale, shards, edges, near, None, tiles)

    @pl.when(jnp.logical_not(even))
    def _():
        lower(scale, edges, near, None, tiles)
        upper(scale, shards, edges, far, rest, tiles)

    copies = [
        pltpu.make_async_copy(tiles.at[0:8, :], outs[0].at[0:TILE, :], sems.at[0]),
        pltpu.make_async_copy(tiles.at[8:16, :], outs[0].at[rows - TILE : rows, :], sems.at[1]),
        pltpu.make_async_copy(tiles.at[16:24, :], outs[1].at[rows - TILE : rows, :], sems.at[2]),
        pltpu.make_async_copy(tiles.at[24:32, :], outs[2].at[rows - TILE : rows, :], sems.at[3]),
    ]
    for copy in copies:
        copy.start()
    for copy in copies:
        copy.wait()


def neighbour(scale, block, rest):
    g = [block[k : k + 1, :] for k in range(2)]
    if rest is not None:
        g = [(g[k] + rest[k : k + 1, :]) * scale for k in range(2)]
    d = [decay_rate * block[k + 2 : k + 3, :] + g[k] * g[k] + damping for k in range(2)]
    f = decay_rate * block[4:5, :] + g[0] * g[1]
    return g, d, f


def lower(scale, edges, block, rest, tiles):
    def edge(k, at):
        return edges[k * TILE + at : k * TILE + at + 1, :]

    (ga, gb), (da, db), fa = neighbour(scale, block, rest)
    g0, g1 = edge(0, 0), edge(0, 1)
    d0, d1 = edge(1, 0) + damping, edge(1, 1) + damping
    f0 = edge(2, 0)
    fb = decay_rate * block[5:6, :] + gb * g0
    sa = decay_rate * block[6:7, :] + ga * g0
    sb = decay_rate * block[7:8, :] + gb * g1
    _, _, far_a = solved(ga, gb, g0, da, db, d0, fa, fb, sa)
    _, near_b, far_b = solved(gb, g0, g1, db, d0, d1, fb, f0, sb)
    none = lax.axis_index("fsdp") == 0
    tiles[0:1, :] = edge(3, 0) - jnp.where(none, 0.0, near_b) - jnp.where(none, 0.0, far_a)
    tiles[1:2, :] = edge(3, 1) - jnp.where(none, 0.0, far_b)


def upper(scale, shards, edges, block, rest, tiles):
    def edge(k, at):
        return edges[k * TILE + at : k * TILE + at + 1, :]

    none = lax.axis_index("fsdp") == shards - 1
    (gp, gq), (dp, dq), fp = neighbour(scale, block, rest)
    gp, gq = jnp.where(none, 0.0, gp), jnp.where(none, 0.0, gq)
    dp, dq = jnp.where(none, 1.0, dp), jnp.where(none, 1.0, dq)
    fp = jnp.where(none, 0.0, fp)
    gx, gy = edge(4, 6), edge(4, 7)
    dx, dy = edge(5, 6) + damping, edge(5, 7) + damping
    fx = edge(6, 6)
    fy = jnp.where(none, 0.0, edge(6, 7) + gy * gp)
    sx = jnp.where(none, 0.0, edge(7, 6) + gx * gp)
    sy = jnp.where(none, 0.0, edge(7, 7) + gy * gq)
    vx, near_x, _ = solved(gx, gy, gp, dx, dy, dp, fx, fy, sx)
    vy, _, _ = solved(gy, gp, gq, dy, dp, dq, fy, fp, sy)
    tiles[14:15, :] = vx - edge(9, 5) - edge(10, 4)
    tiles[15:16, :] = vy - near_x - edge(10, 5)
    tiles[23:24, :] = fy
    tiles[30:31, :] = sx
    tiles[31:32, :] = sy


def trades(shards, low):
    partner = {}
    for i in range(low, shards - 1, 2):
        partner[i], partner[i + 1] = i + 1, i
    return [
        (2 * i + core, 2 * partner.get(i, i) + 1 - core) for i in range(shards) for core in range(2)
    ]


def body(partials, diag_stat, first_stat, second_stat):
    own = partials[0]
    rows, width = own.shape
    replicas = lax.axis_size("replica")
    shards = lax.axis_size("fsdp")
    scale = 1.0 / replicas
    axes = ("fsdp", "replica")
    paired = replicas == 2 and shards > 1

    shape = jax.ShapeDtypeStruct((rows, width), jnp.float32)
    vmem = pl.BlockSpec(memory_space=pltpu.VMEM)
    hbm = pl.BlockSpec(memory_space=pl.ANY)
    params = pltpu.CompilerParams(vmem_limit_bytes=24 * 2**20)

    def swap(block):
        return lax.ppermute(block, "replica", [(0, 1), (1, 0)])

    def stay(block):
        return pltpu.with_memory_space_constraint(block, pltpu.HBM)

    stats = (diag_stat, first_stat, second_stat)
    tile = pltpu.VMEM((TILE, width), jnp.float32)
    if paired:
        pieces = [own, swap(own)]
        far = pl.pallas_call(
            functools.partial(collect, rows),
            out_shape=tile,
            in_specs=[hbm] * 4,
            out_specs=vmem,
            scratch_shapes=[
                pltpu.VMEM((4 * TILE, width), jnp.float32),
                pltpu.SemaphoreType.DMA((4,)),
            ],
            compiler_params=params,
            name="collect",
        )(*[stay(x) for x in (own, *stats)])
        far = pl.pallas_call(
            functools.partial(choose, rows),
            out_shape=tile,
            in_specs=[vmem] * 2,
            out_specs=vmem,
            compiler_params=params,
            name="choose",
        )(far, pltpu.with_memory_space_constraint(own, pltpu.VMEM))
        far = lax.ppermute(far, axes, trades(shards, 1))
    else:
        pieces = [lax.psum(own, "replica") * scale]
        scale = 1.0
        tail = rows - 2
        unused = jnp.zeros((2, width), jnp.float32)
        last = jnp.concatenate([x[tail:] for x in (*pieces, *stats)])
        head = jnp.concatenate([x[:2] for x in (*pieces, *stats[:2])] + [unused])
        before = lax.ppermute(last, "fsdp", [(i, i + 1) for i in range(shards - 1)])
        after = lax.ppermute(head, "fsdp", [(i + 1, i) for i in range(shards - 1)])
        even = lax.axis_index("fsdp") % 2 == 0
        near, far = jnp.where(even, after, before), jnp.where(even, before, after)

    parts = len(pieces)
    whole = pltpu.VMEM((rows, width), jnp.float32)
    padded = pltpu.VMEM((rows + 2 * PAD, width), jnp.float32)
    chunk = 256 if rows % 256 == 0 else rows
    inner = [pltpu.with_memory_space_constraint(x, pltpu.VMEM) for x in (*pieces, *stats)]

    def inside(early, *done):
        return pl.pallas_call(
            functools.partial(interior, parts, early, scale, rows, chunk, 32),
            out_shape=(shape,) * 4 + (pltpu.VMEM((11 * TILE, width), jnp.float32),),
            in_specs=[vmem] * (parts + 3) + ([hbm] * 4 + [vmem] if done else []),
            out_specs=(hbm,) * 4 + (vmem,),
            input_output_aliases={parts + 3 + k: k for k in range(len(done[:4]))},
            scratch_shapes=[padded] * 6 + [whole, pltpu.SemaphoreType.DMA((4, rows // chunk))],
            compiler_params=params,
            cost_estimate=pl.CostEstimate(
                flops=45 * rows * width, bytes_accessed=36 * rows * width, transcendentals=0
            ),
            name="early" if early else "late",
        )(*inner, *done)

    done = inside(True)
    if paired:
        near = pl.pallas_call(
            functools.partial(ready, scale, rows),
            out_shape=tile,
            in_specs=[vmem] * 5,
            out_specs=vmem,
            compiler_params=params,
            name="ready",
        )(*inner)
        near, *done = lax.optimization_barrier((near, *done))
        near = lax.ppermute(near, axes, trades(shards, 0))
    update, diag_next, first_next, second_next, edges = inside(False, *done)
    other = far
    if paired:
        far, edges = lax.optimization_barrier((far, edges))
        other = swap(far)
    def patched(turn, other, *done):
        return pl.pallas_call(
            functools.partial(border, rows, shards, scale, turn),
            out_shape=(shape,) * 3,
            in_specs=[vmem] * 4 + [hbm] * 3,
            out_specs=(hbm,) * 3,
            input_output_aliases={4: 0, 5: 1, 6: 2},
            scratch_shapes=[
                pltpu.VMEM((4 * TILE, width), jnp.float32),
                pltpu.VMEM((2 * TILE, width), jnp.float32),
                pltpu.SemaphoreType.DMA((4,)),
            ],
            compiler_params=params,
            name="border",
        )(edges, near, far, other, *done)

    if paired:
        done = patched(1, far, update, first_next, second_next)
        update, first_next, second_next = patched(2, other, *done)
    else:
        update, first_next, second_next = patched(0, far, update, first_next, second_next)
    return update, diag_next, first_next, second_next


def solution(mesh):
    return jax.shard_map(
        body,
        mesh=mesh,
        in_specs=(P("replica", "fsdp", None), P("fsdp", None), P("fsdp", None), P("fsdp", None)),
        out_specs=(P("fsdp", None), P("fsdp", None), P("fsdp", None), P("fsdp", None)),
        check_vma=False,
    )
```

```python
import functools

import jax
import jax.numpy as jnp
from jax import lax
from jax.experimental import pallas as pl
from jax.experimental.pallas import tpu as pltpu
from jax.sharding import PartitionSpec as P

decay_rate = 0.95
damping = 0.01
PAD = 8
TILE = 8


def solved(g, g1, g2, d, upper, lower, f, c, s):
    det = upper * lower - c * c
    n1 = lower * f - c * s
    n2 = upper * s - c * f
    schur = d * det - f * n1 - s * n2
    top = g * det - n1 * g1 - n2 * g2
    scale = schur * det
    inverse = pl.reciprocal(scale, approx=True)
    w = top * (inverse * (2.0 - scale * inverse))
    return w * det, w * n1, w * n2


def collect(rows, own, diag, first, second, out, tiles, sems):
    even = lax.rem(lax.axis_index("fsdp"), 2) == 0
    low = lax.axis_index("replica") == 0

    @pl.when(low)
    def _():
        at = pl.multiple_of(jnp.where(even, 0, rows - TILE), TILE)
        copies = [
            pltpu.make_async_copy(
                source.at[pl.ds(at, TILE), :], tiles.at[k * TILE : (k + 1) * TILE, :], sems.at[k]
            )
            for k, source in enumerate((own, diag, first, second))
        ]
        for copy in copies:
            copy.start()
        for copy in copies:
            copy.wait()

    @pl.when(jnp.logical_and(low, even))
    def _():
        for k in range(3):
            out[2 * k : 2 * k + 2, :] = tiles[k * TILE : k * TILE + 2, :]
        out[6:8, :] = jnp.zeros((2, out.shape[1]), jnp.float32)

    @pl.when(jnp.logical_and(low, jnp.logical_not(even)))
    def _():
        for k in range(4):
            out[2 * k : 2 * k + 2, :] = tiles[(k + 1) * TILE - 2 : (k + 1) * TILE, :]


def choose(rows, block, own, out):
    even = lax.rem(lax.axis_index("fsdp"), 2) == 0
    low = lax.axis_index("replica") == 0

    @pl.when(low)
    def _():
        out[...] = block[...]

    @pl.when(jnp.logical_not(low))
    def _():
        out[2:8, :] = jnp.zeros((6, out.shape[1]), jnp.float32)
        out[0:2, :] = jnp.where(even, own[0:2, :], own[rows - 2 : rows, :])


def ready(scale, rows, own, other, diag, first, second, out):
    even = lax.rem(lax.axis_index("fsdp"), 2) == 0

    def fill(at, sources):
        out[0:2, :] = (own[at : at + 2, :] + other[at : at + 2, :]) * scale
        for k, source in enumerate(sources):
            out[2 * k + 2 : 2 * k + 4, :] = source[at : at + 2, :]

    @pl.when(even)
    def _():
        fill(rows - 2, (diag, first, second))

    @pl.when(jnp.logical_not(even))
    def _():
        fill(0, (diag, first))
        out[6:8, :] = jnp.zeros((2, out.shape[1]), jnp.float32)


def interior(parts, early, scale, rows, chunk, step, *refs):
    chosen = lax.axis_index("fsdp") == 0
    work = functools.partial(
        everything, parts, scale, rows, chunk, step, *refs[: parts + 3], *refs[-13:]
    )
    if early:
        pl.when(chosen)(work)
    else:
        pl.when(jnp.logical_not(chosen))(work)

        @pl.when(chosen)
        def _():
            refs[-9][...] = refs[parts + 7][...]


def everything(parts, scale, rows, chunk, step, *refs):
    pieces = refs[:parts]
    diag_in, first_in, second_in = refs[parts : parts + 3]
    outs = refs[parts + 3 : parts + 7]
    edges = refs[parts + 7]
    grad, diag, first, second, part1, part2, update, sems = refs[parts + 8 :]
    width = edges.shape[1]
    end = PAD + rows
    chunks = rows // chunk

    zeros = jnp.zeros((PAD, width), jnp.float32)
    grad[end:, :] = zeros
    diag[end:, :] = zeros + 1.0
    first[end:, :] = zeros
    part1[:PAD, :] = zeros
    part2[:PAD, :] = zeros

    def gradients(at, size):
        here, there = pl.ds(at, size), pl.ds(at + PAD, size)
        g = pieces[0][here, :]
        for piece in pieces[1:]:
            g = g + piece[here, :]
        g = g * scale
        grad[there, :] = g
        diag[there, :] = decay_rate * diag_in[here, :] + g * g

    def bands(at, size):
        here, there = pl.ds(at, size), pl.ds(at + PAD, size)
        g = grad[there, :]
        g1 = grad[pl.ds(at + PAD + 1, size), :]
        g2 = grad[pl.ds(at + PAD + 2, size), :]
        first[there, :] = decay_rate * first_in[here, :] + g * g1
        second[there, :] = decay_rate * second_in[here, :] + g * g2

    def values(at, size):
        there = pl.ds(at + PAD, size)
        after = pl.ds(at + PAD + 1, size)
        later = pl.ds(at + PAD + 2, size)
        v, p1, p2 = solved(
            grad[there, :],
            grad[after, :],
            grad[later, :],
            diag[there, :] + damping,
            diag[after, :] + damping,
            diag[later, :] + damping,
            first[there, :],
            first[after, :],
            second[there, :],
        )
        part1[there, :] = p1
        part2[there, :] = p2
        update[pl.ds(at, size), :] = (
            v - part1[pl.ds(at + PAD - 1, size), :] - part2[pl.ds(at + PAD - 2, size), :]
        )

    def over(work, low, high):
        for at in range(low, high, step):
            work(at, min(step, high - at))

    stores = []

    def send(source, pad, k, c, low, high):
        copy = pltpu.make_async_copy(
            source.at[low + pad : high + pad, :], outs[k].at[low:high, :], sems.at[k, c]
        )
        copy.start()
        stores.append(copy)

    for c in range(chunks):
        last = c == chunks - 1
        low, high = c * chunk, (c + 1) * chunk
        over(gradients, low, high)
        send(diag, PAD, 1, c, low, high)
        low, high = max(low - TILE, 0), high if last else high - TILE
        over(bands, low, high)
        send(first, PAD, 2, c, low, high)
        send(second, PAD, 3, c, low, high)
        low, high = max(c * chunk - 2 * TILE, 0), high if last else high - TILE
        over(values, low, high)
        send(update, 0, 0, c, low, high)

    tops = [grad[PAD : PAD + TILE, :], diag[PAD : PAD + TILE, :], first[PAD : PAD + TILE, :]]
    tops.append(update[:TILE, :])
    tails = [r[end - TILE : end, :] for r in (grad, diag, first, second)]
    tails.append(update[rows - TILE :, :])
    tails += [r[end - TILE : end, :] for r in (part1, part2)]
    for k, tile in enumerate(tops + tails):
        edges[k * TILE : (k + 1) * TILE, :] = tile
    for copy in stores:
        copy.wait()


def border(rows, shards, scale, turn, *refs):
    chosen = lax.axis_index("fsdp") == 0
    if turn == 0:
        patch(rows, shards, scale, *refs)
    else:
        pl.when(chosen if turn == 1 else jnp.logical_not(chosen))(
            functools.partial(patch, rows, shards, scale, *refs)
        )


def patch(rows, shards, scale, *refs):
    edges, near, far, other = refs[:4]
    outs = refs[7:10]
    tiles, mixed, sems = refs[10:]
    tiles[0:8, :] = edges[3 * TILE : 4 * TILE, :]
    tiles[8:16, :] = edges[8 * TILE : 9 * TILE, :]
    tiles[16:24, :] = edges[6 * TILE : 7 * TILE, :]
    tiles[24:32, :] = edges[7 * TILE : 8 * TILE, :]
    rest = None
    if scale != 1.0:
        low = lax.axis_index("replica") == 0
        mine, theirs = far[...], other[...]
        mixed[0:8, :] = jnp.where(low, theirs, mine)
        mixed[8:16, :] = jnp.where(low, mine, theirs)
        far, rest = mixed.at[0:8, :], mixed.at[8:16, :]
    even = lax.rem(lax.axis_index("fsdp"), 2) == 0

    @pl.when(even)
    def _():
        lower(scale, edges, far, rest, tiles)
        upper(scale, shards, edges, near, None, tiles)

    @pl.when(jnp.logical_not(even))
    def _():
        lower(scale, edges, near, None, tiles)
        upper(scale, shards, edges, far, rest, tiles)

    copies = [
        pltpu.make_async_copy(tiles.at[0:8, :], outs[0].at[0:TILE, :], sems.at[0]),
        pltpu.make_async_copy(tiles.at[8:16, :], outs[0].at[rows - TILE : rows, :], sems.at[1]),
        pltpu.make_async_copy(tiles.at[16:24, :], outs[1].at[rows - TILE : rows, :], sems.at[2]),
        pltpu.make_async_copy(tiles.at[24:32, :], outs[2].at[rows - TILE : rows, :], sems.at[3]),
    ]
    for copy in copies:
        copy.start()
    for copy in copies:
        copy.wait()


def neighbour(scale, block, rest):
    g = [block[k : k + 1, :] for k in range(2)]
    if rest is not None:
        g = [(g[k] + rest[k : k + 1, :]) * scale for k in range(2)]
    d = [decay_rate * block[k + 2 : k + 3, :] + g[k] * g[k] + damping for k in range(2)]
    f = decay_rate * block[4:5, :] + g[0] * g[1]
    return g, d, f


def lower(scale, edges, block, rest, tiles):
    def edge(k, at):
        return edges[k * TILE + at : k * TILE + at + 1, :]

    (ga, gb), (da, db), fa = neighbour(scale, block, rest)
    g0, g1 = edge(0, 0), edge(0, 1)
    d0, d1 = edge(1, 0) + damping, edge(1, 1) + damping
    f0 = edge(2, 0)
    fb = decay_rate * block[5:6, :] + gb * g0
    sa = decay_rate * block[6:7, :] + ga * g0
    sb = decay_rate * block[7:8, :] + gb * g1
    _, _, far_a = solved(ga, gb, g0, da, db, d0, fa, fb, sa)
    _, near_b, far_b = solved(gb, g0, g1, db, d0, d1, fb, f0, sb)
    none = lax.axis_index("fsdp") == 0
    tiles[0:1, :] = edge(3, 0) - jnp.where(none, 0.0, near_b) - jnp.where(none, 0.0, far_a)
    tiles[1:2, :] = edge(3, 1) - jnp.where(none, 0.0, far_b)


def upper(scale, shards, edges, block, rest, tiles):
    def edge(k, at):
        return edges[k * TILE + at : k * TILE + at + 1, :]

    none = lax.axis_index("fsdp") == shards - 1
    (gp, gq), (dp, dq), fp = neighbour(scale, block, rest)
    gp, gq = jnp.where(none, 0.0, gp), jnp.where(none, 0.0, gq)
    dp, dq = jnp.where(none, 1.0, dp), jnp.where(none, 1.0, dq)
    fp = jnp.where(none, 0.0, fp)
    gx, gy = edge(4, 6), edge(4, 7)
    dx, dy = edge(5, 6) + damping, edge(5, 7) + damping
    fx = edge(6, 6)
    fy = jnp.where(none, 0.0, edge(6, 7) + gy * gp)
    sx = jnp.where(none, 0.0, edge(7, 6) + gx * gp)
    sy = jnp.where(none, 0.0, edge(7, 7) + gy * gq)
    vx, near_x, _ = solved(gx, gy, gp, dx, dy, dp, fx, fy, sx)
    vy, _, _ = solved(gy, gp, gq, dy, dp, dq, fy, fp, sy)
    tiles[14:15, :] = vx - edge(9, 5) - edge(10, 4)
    tiles[15:16, :] = vy - near_x - edge(10, 5)
    tiles[23:24, :] = fy
    tiles[30:31, :] = sx
    tiles[31:32, :] = sy


def trades(shards, low):
    partner = {}
    for i in range(low, shards - 1, 2):
        partner[i], partner[i + 1] = i + 1, i
    return [
        (2 * i + core, 2 * partner.get(i, i) + 1 - core) for i in range(shards) for core in range(2)
    ]


def body(partials, diag_stat, first_stat, second_stat):
    own = partials[0]
    rows, width = own.shape
    replicas = lax.axis_size("replica")
    shards = lax.axis_size("fsdp")
    scale = 1.0 / replicas
    axes = ("fsdp", "replica")
    paired = replicas == 2 and shards > 1

    shape = jax.ShapeDtypeStruct((rows, width), jnp.float32)
    vmem = pl.BlockSpec(memory_space=pltpu.VMEM)
    hbm = pl.BlockSpec(memory_space=pl.ANY)
    params = pltpu.CompilerParams(vmem_limit_bytes=24 * 2**20)

    def swap(block):
        return lax.ppermute(block, "replica", [(0, 1), (1, 0)])

    def stay(block):
        return pltpu.with_memory_space_constraint(block, pltpu.HBM)

    stats = (diag_stat, first_stat, second_stat)
    tile = pltpu.VMEM((TILE, width), jnp.float32)
    if paired:
        pieces = [own, swap(own)]
        far = pl.pallas_call(
            functools.partial(collect, rows),
            out_shape=tile,
            in_specs=[hbm] * 4,
            out_specs=vmem,
            scratch_shapes=[
                pltpu.VMEM((4 * TILE, width), jnp.float32),
                pltpu.SemaphoreType.DMA((4,)),
            ],
            compiler_params=params,
            name="collect",
        )(*[stay(x) for x in (own, *stats)])
        far = pl.pallas_call(
            functools.partial(choose, rows),
            out_shape=tile,
            in_specs=[vmem] * 2,
            out_specs=vmem,
            compiler_params=params,
            name="choose",
        )(far, pltpu.with_memory_space_constraint(own, pltpu.VMEM))
        far = lax.ppermute(far, axes, trades(shards, 1))
    else:
        pieces = [lax.psum(own, "replica") * scale]
        scale = 1.0
        tail = rows - 2
        unused = jnp.zeros((2, width), jnp.float32)
        last = jnp.concatenate([x[tail:] for x in (*pieces, *stats)])
        head = jnp.concatenate([x[:2] for x in (*pieces, *stats[:2])] + [unused])
        before = lax.ppermute(last, "fsdp", [(i, i + 1) for i in range(shards - 1)])
        after = lax.ppermute(head, "fsdp", [(i + 1, i) for i in range(shards - 1)])
        even = lax.axis_index("fsdp") % 2 == 0
        near, far = jnp.where(even, after, before), jnp.where(even, before, after)

    parts = len(pieces)
    whole = pltpu.VMEM((rows, width), jnp.float32)
    padded = pltpu.VMEM((rows + 2 * PAD, width), jnp.float32)
    chunk = 128 if rows % 128 == 0 else rows
    inner = [pltpu.with_memory_space_constraint(x, pltpu.VMEM) for x in (*pieces, *stats)]

    def inside(early, *done):
        return pl.pallas_call(
            functools.partial(interior, parts, early, scale, rows, chunk, 32),
            out_shape=(shape,) * 4 + (pltpu.VMEM((11 * TILE, width), jnp.float32),),
            in_specs=[vmem] * (parts + 3) + ([hbm] * 4 + [vmem] if done else []),
            out_specs=(hbm,) * 4 + (vmem,),
            input_output_aliases={parts + 3 + k: k for k in range(len(done[:4]))},
            scratch_shapes=[padded] * 6 + [whole, pltpu.SemaphoreType.DMA((4, rows // chunk))],
            compiler_params=params,
            cost_estimate=pl.CostEstimate(
                flops=45 * rows * width, bytes_accessed=36 * rows * width, transcendentals=0
            ),
            name="early" if early else "late",
        )(*inner, *done)

    done = inside(True)
    if paired:
        near = pl.pallas_call(
            functools.partial(ready, scale, rows),
            out_shape=tile,
            in_specs=[vmem] * 5,
            out_specs=vmem,
            compiler_params=params,
            name="ready",
        )(*inner)
        near, *done = lax.optimization_barrier((near, *done))
        near = lax.ppermute(near, axes, trades(shards, 0))
    update, diag_next, first_next, second_next, edges = inside(False, *done)
    other = far
    if paired:
        far, edges = lax.optimization_barrier((far, edges))
        other = swap(far)
    def patched(turn, other, *done):
        return pl.pallas_call(
            functools.partial(border, rows, shards, scale, turn),
            out_shape=(shape,) * 3,
            in_specs=[vmem] * 4 + [hbm] * 3,
            out_specs=(hbm,) * 3,
            input_output_aliases={4: 0, 5: 1, 6: 2},
            scratch_shapes=[
                pltpu.VMEM((4 * TILE, width), jnp.float32),
                pltpu.VMEM((2 * TILE, width), jnp.float32),
                pltpu.SemaphoreType.DMA((4,)),
            ],
            compiler_params=params,
            name="border",
        )(edges, near, far, other, *done)

    if paired:
        done = patched(1, far, update, first_next, second_next)
        update, first_next, second_next = patched(2, other, *done)
    else:
        update, first_next, second_next = patched(0, far, update, first_next, second_next)
    return update, diag_next, first_next, second_next


def solution(mesh):
    return jax.shard_map(
        body,
        mesh=mesh,
        in_specs=(P("replica", "fsdp", None), P("fsdp", None), P("fsdp", None), P("fsdp", None)),
        out_specs=(P("fsdp", None), P("fsdp", None), P("fsdp", None), P("fsdp", None)),
        check_vma=False,
    )
```

```python
import functools

import jax
import jax.numpy as jnp
from jax import lax
from jax.experimental import pallas as pl
from jax.experimental.pallas import tpu as pltpu
from jax.sharding import PartitionSpec as P

decay_rate = 0.95
damping = 0.01
PAD = 8
TILE = 8


def solved(g, g1, g2, d, upper, lower, f, c, s):
    det = upper * lower - c * c
    n1 = lower * f - c * s
    n2 = upper * s - c * f
    schur = d * det - f * n1 - s * n2
    top = g * det - n1 * g1 - n2 * g2
    w = top / (schur * det)
    return w * det, w * n1, w * n2


def collect(rows, own, diag, first, second, out, tiles, sem):
    even = lax.rem(lax.axis_index("fsdp"), 2) == 0
    low = lax.axis_index("replica") == 0

    @pl.when(low)
    def _():
        at = pl.multiple_of(jnp.where(even, 0, rows - TILE), TILE)
        for k, source in enumerate((own, diag, first, second)):
            pltpu.make_async_copy(
                source.at[pl.ds(at, TILE), :], tiles.at[k * TILE : (k + 1) * TILE, :], sem
            ).start()
        pltpu.make_async_copy(own.at[0 : 4 * TILE, :], tiles, sem).wait()

    @pl.when(jnp.logical_and(low, even))
    def _():
        for k in range(3):
            out[2 * k : 2 * k + 2, :] = tiles[k * TILE : k * TILE + 2, :]
        out[6:8, :] = jnp.zeros((2, out.shape[1]), jnp.float32)

    @pl.when(jnp.logical_and(low, jnp.logical_not(even)))
    def _():
        for k in range(4):
            out[2 * k : 2 * k + 2, :] = tiles[(k + 1) * TILE - 2 : (k + 1) * TILE, :]


def choose(rows, block, own, out):
    even = lax.rem(lax.axis_index("fsdp"), 2) == 0
    low = lax.axis_index("replica") == 0

    @pl.when(low)
    def _():
        out[...] = block[...]

    @pl.when(jnp.logical_not(low))
    def _():
        out[2:8, :] = jnp.zeros((6, out.shape[1]), jnp.float32)
        out[0:2, :] = jnp.where(even, own[0:2, :], own[rows - 2 : rows, :])


def ready(scale, rows, own, other, diag, first, second, out):
    even = lax.rem(lax.axis_index("fsdp"), 2) == 0

    def fill(at, sources):
        out[0:2, :] = (own[at : at + 2, :] + other[at : at + 2, :]) * scale
        for k, source in enumerate(sources):
            out[2 * k + 2 : 2 * k + 4, :] = source[at : at + 2, :]

    @pl.when(even)
    def _():
        fill(rows - 2, (diag, first, second))

    @pl.when(jnp.logical_not(even))
    def _():
        fill(0, (diag, first))
        out[6:8, :] = jnp.zeros((2, out.shape[1]), jnp.float32)


def interior(parts, early, scale, rows, chunk, step, *refs):
    chosen = lax.axis_index("fsdp") == 0
    work = functools.partial(
        everything, parts, scale, rows, chunk, step, *refs[: parts + 3], *refs[-13:]
    )
    if early:
        pl.when(chosen)(work)
    else:
        pl.when(jnp.logical_not(chosen))(work)

        @pl.when(chosen)
        def _():
            refs[-9][...] = refs[parts + 7][...]


def everything(parts, scale, rows, chunk, step, *refs):
    pieces = refs[:parts]
    diag_in, first_in, second_in = refs[parts : parts + 3]
    outs = refs[parts + 3 : parts + 7]
    edges = refs[parts + 7]
    grad, diag, first, second, part1, part2, update, sems = refs[parts + 8 :]
    width = edges.shape[1]
    end = PAD + rows
    chunks = rows // chunk

    zeros = jnp.zeros((PAD, width), jnp.float32)
    grad[end:, :] = zeros
    diag[end:, :] = zeros + 1.0
    first[end:, :] = zeros
    part1[:PAD, :] = zeros
    part2[:PAD, :] = zeros

    def gradients(at, size):
        here, there = pl.ds(at, size), pl.ds(at + PAD, size)
        g = pieces[0][here, :]
        for piece in pieces[1:]:
            g = g + piece[here, :]
        g = g * scale
        grad[there, :] = g
        diag[there, :] = decay_rate * diag_in[here, :] + g * g

    def bands(at, size):
        here, there = pl.ds(at, size), pl.ds(at + PAD, size)
        g = grad[there, :]
        g1 = grad[pl.ds(at + PAD + 1, size), :]
        g2 = grad[pl.ds(at + PAD + 2, size), :]
        first[there, :] = decay_rate * first_in[here, :] + g * g1
        second[there, :] = decay_rate * second_in[here, :] + g * g2

    def values(at, size):
        there = pl.ds(at + PAD, size)
        after = pl.ds(at + PAD + 1, size)
        later = pl.ds(at + PAD + 2, size)
        v, p1, p2 = solved(
            grad[there, :],
            grad[after, :],
            grad[later, :],
            diag[there, :] + damping,
            diag[after, :] + damping,
            diag[later, :] + damping,
            first[there, :],
            first[after, :],
            second[there, :],
        )
        part1[there, :] = p1
        part2[there, :] = p2
        update[pl.ds(at, size), :] = (
            v - part1[pl.ds(at + PAD - 1, size), :] - part2[pl.ds(at + PAD - 2, size), :]
        )

    def over(work, low, high):
        for at in range(low, high, step):
            work(at, min(step, high - at))

    def send(source, pad, k, low, high):
        copy = pltpu.make_async_copy(
            source.at[low + pad : high + pad, :], outs[k].at[low:high, :], sems.at[k]
        )
        copy.start()

    for c in range(chunks):
        last = c == chunks - 1
        low, high = c * chunk, (c + 1) * chunk
        over(gradients, low, high)
        send(diag, PAD, 1, low, high)
        low, high = max(low - TILE, 0), high if last else high - TILE
        over(bands, low, high)
        send(first, PAD, 2, low, high)
        send(second, PAD, 3, low, high)
        low, high = max(c * chunk - 2 * TILE, 0), high if last else high - TILE
        over(values, low, high)
        send(update, 0, 0, low, high)

    tops = [grad[PAD : PAD + TILE, :], diag[PAD : PAD + TILE, :], first[PAD : PAD + TILE, :]]
    tops.append(update[:TILE, :])
    tails = [r[end - TILE : end, :] for r in (grad, diag, first, second)]
    tails.append(update[rows - TILE :, :])
    tails += [r[end - TILE : end, :] for r in (part1, part2)]
    for k, tile in enumerate(tops + tails):
        edges[k * TILE : (k + 1) * TILE, :] = tile
    for k, (source, pad) in enumerate(((update, 0), (diag, PAD), (first, PAD), (second, PAD))):
        pltpu.make_async_copy(source.at[pad : pad + rows, :], outs[k], sems.at[k]).wait()


def border(rows, shards, scale, turn, *refs):
    chosen = lax.axis_index("fsdp") == 0
    if turn == 0:
        patch(rows, shards, scale, *refs)
    else:
        pl.when(chosen if turn == 1 else jnp.logical_not(chosen))(
            functools.partial(patch, rows, shards, scale, *refs)
        )


def patch(rows, shards, scale, *refs):
    edges, near, far, other = refs[:4]
    outs = refs[7:10]
    tiles, mixed, sem = refs[10:]
    tiles[0:8, :] = edges[3 * TILE : 4 * TILE, :]
    tiles[8:16, :] = edges[8 * TILE : 9 * TILE, :]
    tiles[16:24, :] = edges[6 * TILE : 7 * TILE, :]
    tiles[24:32, :] = edges[7 * TILE : 8 * TILE, :]
    rest = None
    if scale != 1.0:
        low = lax.axis_index("replica") == 0
        mine, theirs = far[...], other[...]
        mixed[0:8, :] = jnp.where(low, theirs, mine)
        mixed[8:16, :] = jnp.where(low, mine, theirs)
        far, rest = mixed.at[0:8, :], mixed.at[8:16, :]
    even = lax.rem(lax.axis_index("fsdp"), 2) == 0

    @pl.when(even)
    def _():
        lower(scale, edges, far, rest, tiles)
        upper(scale, shards, edges, near, None, tiles)

    @pl.when(jnp.logical_not(even))
    def _():
        lower(scale, edges, near, None, tiles)
        upper(scale, shards, edges, far, rest, tiles)

    targets = [outs[0].at[0:TILE, :]] + [out.at[rows - TILE : rows, :] for out in outs]
    for k, target in enumerate(targets):
        pltpu.make_async_copy(tiles.at[k * TILE : (k + 1) * TILE, :], target, sem).start()
    pltpu.make_async_copy(tiles, outs[0].at[0 : 4 * TILE, :], sem).wait()


def neighbour(scale, block, rest):
    g = [block[k : k + 1, :] for k in range(2)]
    if rest is not None:
        g = [(g[k] + rest[k : k + 1, :]) * scale for k in range(2)]
    d = [decay_rate * block[k + 2 : k + 3, :] + g[k] * g[k] + damping for k in range(2)]
    f = decay_rate * block[4:5, :] + g[0] * g[1]
    return g, d, f


def lower(scale, edges, block, rest, tiles):
    def edge(k, at):
        return edges[k * TILE + at : k * TILE + at + 1, :]

    (ga, gb), (da, db), fa = neighbour(scale, block, rest)
    g0, g1 = edge(0, 0), edge(0, 1)
    d0, d1 = edge(1, 0) + damping, edge(1, 1) + damping
    f0 = edge(2, 0)
    fb = decay_rate * block[5:6, :] + gb * g0
    sa = decay_rate * block[6:7, :] + ga * g0
    sb = decay_rate * block[7:8, :] + gb * g1
    _, _, far_a = solved(ga, gb, g0, da, db, d0, fa, fb, sa)
    _, near_b, far_b = solved(gb, g0, g1, db, d0, d1, fb, f0, sb)
    none = lax.axis_index("fsdp") == 0
    tiles[0:1, :] = edge(3, 0) - jnp.where(none, 0.0, near_b) - jnp.where(none, 0.0, far_a)
    tiles[1:2, :] = edge(3, 1) - jnp.where(none, 0.0, far_b)


def upper(scale, shards, edges, block, rest, tiles):
    def edge(k, at):
        return edges[k * TILE + at : k * TILE + at + 1, :]

    none = lax.axis_index("fsdp") == shards - 1
    (gp, gq), (dp, dq), fp = neighbour(scale, block, rest)
    gp, gq = jnp.where(none, 0.0, gp), jnp.where(none, 0.0, gq)
    dp, dq = jnp.where(none, 1.0, dp), jnp.where(none, 1.0, dq)
    fp = jnp.where(none, 0.0, fp)
    gx, gy = edge(4, 6), edge(4, 7)
    dx, dy = edge(5, 6) + damping, edge(5, 7) + damping
    fx = edge(6, 6)
    fy = jnp.where(none, 0.0, edge(6, 7) + gy * gp)
    sx = jnp.where(none, 0.0, edge(7, 6) + gx * gp)
    sy = jnp.where(none, 0.0, edge(7, 7) + gy * gq)
    vx, near_x, _ = solved(gx, gy, gp, dx, dy, dp, fx, fy, sx)
    vy, _, _ = solved(gy, gp, gq, dy, dp, dq, fy, fp, sy)
    tiles[14:15, :] = vx - edge(9, 5) - edge(10, 4)
    tiles[15:16, :] = vy - near_x - edge(10, 5)
    tiles[23:24, :] = fy
    tiles[30:31, :] = sx
    tiles[31:32, :] = sy


def trades(shards, low):
    partner = {}
    for i in range(low, shards - 1, 2):
        partner[i], partner[i + 1] = i + 1, i
    return [
        (2 * i + core, 2 * partner.get(i, i) + 1 - core) for i in range(shards) for core in range(2)
    ]


def body(partials, diag_stat, first_stat, second_stat):
    own = partials[0]
    rows, width = own.shape
    replicas = lax.axis_size("replica")
    shards = lax.axis_size("fsdp")
    scale = 1.0 / replicas
    axes = ("fsdp", "replica")
    paired = replicas == 2 and shards > 1

    shape = jax.ShapeDtypeStruct((rows, width), jnp.float32)
    vmem = pl.BlockSpec(memory_space=pltpu.VMEM)
    hbm = pl.BlockSpec(memory_space=pl.ANY)
    params = pltpu.CompilerParams(vmem_limit_bytes=24 * 2**20)

    def swap(block):
        return lax.ppermute(block, "replica", [(0, 1), (1, 0)])

    def stay(block):
        return pltpu.with_memory_space_constraint(block, pltpu.HBM)

    stats = (diag_stat, first_stat, second_stat)
    tile = pltpu.VMEM((TILE, width), jnp.float32)
    if paired:
        pieces = [own, swap(own)]
        far = pl.pallas_call(
            functools.partial(collect, rows),
            out_shape=tile,
            in_specs=[hbm] * 4,
            out_specs=vmem,
            scratch_shapes=[
                pltpu.VMEM((4 * TILE, width), jnp.float32),
                pltpu.SemaphoreType.DMA,
            ],
            compiler_params=params,
            name="collect",
        )(*[stay(x) for x in (own, *stats)])
        far = pl.pallas_call(
            functools.partial(choose, rows),
            out_shape=tile,
            in_specs=[vmem] * 2,
            out_specs=vmem,
            compiler_params=params,
            name="choose",
        )(far, pltpu.with_memory_space_constraint(own, pltpu.VMEM))
        far = lax.ppermute(far, axes, trades(shards, 1))
    else:
        pieces = [lax.psum(own, "replica") * scale]
        scale = 1.0
        tail = rows - 2
        unused = jnp.zeros((2, width), jnp.float32)
        last = jnp.concatenate([x[tail:] for x in (*pieces, *stats)])
        head = jnp.concatenate([x[:2] for x in (*pieces, *stats[:2])] + [unused])
        before = lax.ppermute(last, "fsdp", [(i, i + 1) for i in range(shards - 1)])
        after = lax.ppermute(head, "fsdp", [(i + 1, i) for i in range(shards - 1)])
        even = lax.axis_index("fsdp") % 2 == 0
        near, far = jnp.where(even, after, before), jnp.where(even, before, after)

    parts = len(pieces)
    whole = pltpu.VMEM((rows, width), jnp.float32)
    padded = pltpu.VMEM((rows + 2 * PAD, width), jnp.float32)
    chunk = 256 if rows % 256 == 0 else rows
    inner = [pltpu.with_memory_space_constraint(x, pltpu.VMEM) for x in (*pieces, *stats)]

    def inside(early, *done):
        return pl.pallas_call(
            functools.partial(interior, parts, early, scale, rows, chunk, 32),
            out_shape=(shape,) * 4 + (pltpu.VMEM((11 * TILE, width), jnp.float32),),
            in_specs=[vmem] * (parts + 3) + ([hbm] * 4 + [vmem] if done else []),
            out_specs=(hbm,) * 4 + (vmem,),
            input_output_aliases={parts + 3 + k: k for k in range(len(done[:4]))},
            scratch_shapes=[padded] * 6 + [whole, pltpu.SemaphoreType.DMA((4,))],
            compiler_params=params,
            cost_estimate=pl.CostEstimate(
                flops=45 * rows * width, bytes_accessed=36 * rows * width, transcendentals=0
            ),
            name="early" if early else "late",
        )(*inner, *done)

    done = inside(True)
    if paired:
        near = pl.pallas_call(
            functools.partial(ready, scale, rows),
            out_shape=tile,
            in_specs=[vmem] * 5,
            out_specs=vmem,
            compiler_params=params,
            name="ready",
        )(*inner)
        near, *done = lax.optimization_barrier((near, *done))
        near = lax.ppermute(near, axes, trades(shards, 0))
    update, diag_next, first_next, second_next, edges = inside(False, *done)
    other = far
    if paired:
        far, edges = lax.optimization_barrier((far, edges))
        other = swap(far)
    def patched(turn, other, *done):
        return pl.pallas_call(
            functools.partial(border, rows, shards, scale, turn),
            out_shape=(shape,) * 3,
            in_specs=[vmem] * 4 + [hbm] * 3,
            out_specs=(hbm,) * 3,
            input_output_aliases={4: 0, 5: 1, 6: 2},
            scratch_shapes=[
                pltpu.VMEM((4 * TILE, width), jnp.float32),
                pltpu.VMEM((2 * TILE, width), jnp.float32),
                pltpu.SemaphoreType.DMA,
            ],
            compiler_params=params,
            name="border",
        )(edges, near, far, other, *done)

    if paired:
        done = patched(1, far, update, first_next, second_next)
        update, first_next, second_next = patched(2, other, *done)
    else:
        update, first_next, second_next = patched(0, far, update, first_next, second_next)
    return update, diag_next, first_next, second_next


def solution(mesh):
    return jax.shard_map(
        body,
        mesh=mesh,
        in_specs=(P("replica", "fsdp", None), P("fsdp", None), P("fsdp", None), P("fsdp", None)),
        out_specs=(P("fsdp", None), P("fsdp", None), P("fsdp", None), P("fsdp", None)),
        check_vma=False,
    )
```

```python
import functools

import jax
import jax.numpy as jnp
from jax import lax
from jax.experimental import pallas as pl
from jax.experimental.pallas import tpu as pltpu
from jax.sharding import PartitionSpec as P

decay_rate = 0.95
damping = 0.01
PAD = 8
TILE = 8


def solved(g, g1, g2, d, upper, lower, f, c, s):
    det = upper * lower - c * c
    n1 = lower * f - c * s
    n2 = upper * s - c * f
    schur = d * det - f * n1 - s * n2
    top = g * det - n1 * g1 - n2 * g2
    w = top / (schur * det)
    return w * det, w * n1, w * n2


def collect(rows, own, diag, first, second, out, tiles, sem):
    even = lax.rem(lax.axis_index("fsdp"), 2) == 0
    low = lax.axis_index("replica") == 0

    @pl.when(low)
    def _():
        at = pl.multiple_of(jnp.where(even, 0, rows - TILE), TILE)
        for k, source in enumerate((own, diag, first, second)):
            pltpu.make_async_copy(
                source.at[pl.ds(at, TILE), :], tiles.at[k * TILE : (k + 1) * TILE, :], sem
            ).start()
        pltpu.make_async_copy(own.at[0 : 4 * TILE, :], tiles, sem).wait()

    @pl.when(jnp.logical_and(low, even))
    def _():
        for k in range(3):
            out[2 * k : 2 * k + 2, :] = tiles[k * TILE : k * TILE + 2, :]
        out[6:8, :] = jnp.zeros((2, out.shape[1]), jnp.float32)

    @pl.when(jnp.logical_and(low, jnp.logical_not(even)))
    def _():
        for k in range(4):
            out[2 * k : 2 * k + 2, :] = tiles[(k + 1) * TILE - 2 : (k + 1) * TILE, :]


def choose(rows, block, own, out):
    even = lax.rem(lax.axis_index("fsdp"), 2) == 0
    low = lax.axis_index("replica") == 0

    @pl.when(low)
    def _():
        out[...] = block[...]

    @pl.when(jnp.logical_not(low))
    def _():
        out[2:8, :] = jnp.zeros((6, out.shape[1]), jnp.float32)
        out[0:2, :] = jnp.where(even, own[0:2, :], own[rows - 2 : rows, :])


def ready(scale, rows, own, other, diag, first, second, out):
    even = lax.rem(lax.axis_index("fsdp"), 2) == 0

    def fill(at, sources):
        out[0:2, :] = (own[at : at + 2, :] + other[at : at + 2, :]) * scale
        for k, source in enumerate(sources):
            out[2 * k + 2 : 2 * k + 4, :] = source[at : at + 2, :]

    @pl.when(even)
    def _():
        fill(rows - 2, (diag, first, second))

    @pl.when(jnp.logical_not(even))
    def _():
        fill(0, (diag, first))
        out[6:8, :] = jnp.zeros((2, out.shape[1]), jnp.float32)


def interior(parts, early, scale, rows, chunk, step, *refs):
    chosen = lax.axis_index("fsdp") == 0
    work = functools.partial(
        everything, parts, scale, rows, chunk, step, *refs[: parts + 3], *refs[-13:]
    )
    if early:
        pl.when(chosen)(work)
    else:
        pl.when(jnp.logical_not(chosen))(work)

        @pl.when(chosen)
        def _():
            refs[-9][...] = refs[parts + 7][...]


def everything(parts, scale, rows, chunk, step, *refs):
    pieces = refs[:parts]
    diag_in, first_in, second_in = refs[parts : parts + 3]
    outs = refs[parts + 3 : parts + 7]
    edges = refs[parts + 7]
    grad, diag, first, second, part1, part2, update, sems = refs[parts + 8 :]
    width = edges.shape[1]
    end = PAD + rows
    chunks = rows // chunk

    zeros = jnp.zeros((PAD, width), jnp.float32)
    grad[end:, :] = zeros
    diag[end:, :] = zeros + 1.0
    first[end:, :] = zeros
    part1[:PAD, :] = zeros
    part2[:PAD, :] = zeros

    def gradients(at, size):
        here, there = pl.ds(at, size), pl.ds(at + PAD, size)
        g = pieces[0][here, :]
        for piece in pieces[1:]:
            g = g + piece[here, :]
        g = g * scale
        grad[there, :] = g
        diag[there, :] = decay_rate * diag_in[here, :] + g * g

    def bands(at, size):
        here, there = pl.ds(at, size), pl.ds(at + PAD, size)
        g = grad[there, :]
        g1 = grad[pl.ds(at + PAD + 1, size), :]
        g2 = grad[pl.ds(at + PAD + 2, size), :]
        first[there, :] = decay_rate * first_in[here, :] + g * g1
        second[there, :] = decay_rate * second_in[here, :] + g * g2

    def values(at, size):
        there = pl.ds(at + PAD, size)
        after = pl.ds(at + PAD + 1, size)
        later = pl.ds(at + PAD + 2, size)
        v, p1, p2 = solved(
            grad[there, :],
            grad[after, :],
            grad[later, :],
            diag[there, :] + damping,
            diag[after, :] + damping,
            diag[later, :] + damping,
            first[there, :],
            first[after, :],
            second[there, :],
        )
        part1[there, :] = p1
        part2[there, :] = p2
        update[pl.ds(at, size), :] = (
            v - part1[pl.ds(at + PAD - 1, size), :] - part2[pl.ds(at + PAD - 2, size), :]
        )

    def over(work, low, high):
        for at in range(low, high, step):
            work(at, min(step, high - at))

    def send(source, pad, k, low, high):
        copy = pltpu.make_async_copy(
            source.at[low + pad : high + pad, :], outs[k].at[low:high, :], sems.at[k]
        )
        copy.start()

    for c in range(chunks):
        last = c == chunks - 1
        low, high = c * chunk, (c + 1) * chunk
        over(gradients, low, high)
        send(diag, PAD, 1, low, high)
        low, high = max(low - TILE, 0), high if last else high - TILE
        over(bands, low, high)
        send(first, PAD, 2, low, high)
        send(second, PAD, 3, low, high)
        low, high = max(c * chunk - 2 * TILE, 0), high if last else high - TILE
        over(values, low, high)
        send(update, 0, 0, low, high)

    tops = [grad[PAD : PAD + TILE, :], diag[PAD : PAD + TILE, :], first[PAD : PAD + TILE, :]]
    tops.append(update[:TILE, :])
    tails = [r[end - TILE : end, :] for r in (grad, diag, first, second)]
    tails.append(update[rows - TILE :, :])
    tails += [r[end - TILE : end, :] for r in (part1, part2)]
    for k, tile in enumerate(tops + tails):
        edges[k * TILE : (k + 1) * TILE, :] = tile
    for k, (source, pad) in enumerate(((update, 0), (diag, PAD), (first, PAD), (second, PAD))):
        pltpu.make_async_copy(source.at[pad : pad + rows, :], outs[k], sems.at[k]).wait()


def border(rows, shards, scale, turn, *refs):
    chosen = lax.axis_index("fsdp") == 0
    if turn == 0:
        patch(rows, shards, scale, *refs)
    else:
        pl.when(chosen if turn == 1 else jnp.logical_not(chosen))(
            functools.partial(patch, rows, shards, scale, *refs)
        )


def patch(rows, shards, scale, *refs):
    edges, near, far, other = refs[:4]
    outs = refs[7:10]
    tiles, mixed, sem = refs[10:]
    tiles[0:8, :] = edges[3 * TILE : 4 * TILE, :]
    tiles[8:16, :] = edges[8 * TILE : 9 * TILE, :]
    tiles[16:24, :] = edges[6 * TILE : 7 * TILE, :]
    tiles[24:32, :] = edges[7 * TILE : 8 * TILE, :]
    rest = None
    if scale != 1.0:
        low = lax.axis_index("replica") == 0
        mine, theirs = far[...], other[...]
        mixed[0:8, :] = jnp.where(low, theirs, mine)
        mixed[8:16, :] = jnp.where(low, mine, theirs)
        far, rest = mixed.at[0:8, :], mixed.at[8:16, :]
    even = lax.rem(lax.axis_index("fsdp"), 2) == 0

    @pl.when(even)
    def _():
        lower(scale, edges, far, rest, tiles)
        upper(scale, shards, edges, near, None, tiles)

    @pl.when(jnp.logical_not(even))
    def _():
        lower(scale, edges, near, None, tiles)
        upper(scale, shards, edges, far, rest, tiles)

    targets = [outs[0].at[0:TILE, :]] + [out.at[rows - TILE : rows, :] for out in outs]
    for k, target in enumerate(targets):
        pltpu.make_async_copy(tiles.at[k * TILE : (k + 1) * TILE, :], target, sem).start()
    pltpu.make_async_copy(tiles, outs[0].at[0 : 4 * TILE, :], sem).wait()


def neighbour(scale, block, rest):
    g = [block[k : k + 1, :] for k in range(2)]
    if rest is not None:
        g = [(g[k] + rest[k : k + 1, :]) * scale for k in range(2)]
    d = [decay_rate * block[k + 2 : k + 3, :] + g[k] * g[k] + damping for k in range(2)]
    f = decay_rate * block[4:5, :] + g[0] * g[1]
    return g, d, f


def lower(scale, edges, block, rest, tiles):
    def edge(k, at):
        return edges[k * TILE + at : k * TILE + at + 1, :]

    (ga, gb), (da, db), fa = neighbour(scale, block, rest)
    g0, g1 = edge(0, 0), edge(0, 1)
    d0, d1 = edge(1, 0) + damping, edge(1, 1) + damping
    f0 = edge(2, 0)
    fb = decay_rate * block[5:6, :] + gb * g0
    sa = decay_rate * block[6:7, :] + ga * g0
    sb = decay_rate * block[7:8, :] + gb * g1
    _, _, far_a = solved(ga, gb, g0, da, db, d0, fa, fb, sa)
    _, near_b, far_b = solved(gb, g0, g1, db, d0, d1, fb, f0, sb)
    none = lax.axis_index("fsdp") == 0
    tiles[0:1, :] = edge(3, 0) - jnp.where(none, 0.0, near_b) - jnp.where(none, 0.0, far_a)
    tiles[1:2, :] = edge(3, 1) - jnp.where(none, 0.0, far_b)


def upper(scale, shards, edges, block, rest, tiles):
    def edge(k, at):
        return edges[k * TILE + at : k * TILE + at + 1, :]

    none = lax.axis_index("fsdp") == shards - 1
    (gp, gq), (dp, dq), fp = neighbour(scale, block, rest)
    gp, gq = jnp.where(none, 0.0, gp), jnp.where(none, 0.0, gq)
    dp, dq = jnp.where(none, 1.0, dp), jnp.where(none, 1.0, dq)
    fp = jnp.where(none, 0.0, fp)
    gx, gy = edge(4, 6), edge(4, 7)
    dx, dy = edge(5, 6) + damping, edge(5, 7) + damping
    fx = edge(6, 6)
    fy = jnp.where(none, 0.0, edge(6, 7) + gy * gp)
    sx = jnp.where(none, 0.0, edge(7, 6) + gx * gp)
    sy = jnp.where(none, 0.0, edge(7, 7) + gy * gq)
    vx, near_x, _ = solved(gx, gy, gp, dx, dy, dp, fx, fy, sx)
    vy, _, _ = solved(gy, gp, gq, dy, dp, dq, fy, fp, sy)
    tiles[14:15, :] = vx - edge(9, 5) - edge(10, 4)
    tiles[15:16, :] = vy - near_x - edge(10, 5)
    tiles[23:24, :] = fy
    tiles[30:31, :] = sx
    tiles[31:32, :] = sy


def trades(shards, low):
    partner = {}
    for i in range(low, shards - 1, 2):
        partner[i], partner[i + 1] = i + 1, i
    return [
        (2 * i + core, 2 * partner.get(i, i) + 1 - core) for i in range(shards) for core in range(2)
    ]


def body(partials, diag_stat, first_stat, second_stat):
    own = partials[0]
    rows, width = own.shape
    replicas = lax.axis_size("replica")
    shards = lax.axis_size("fsdp")
    scale = 1.0 / replicas
    axes = ("fsdp", "replica")
    paired = replicas == 2 and shards > 1

    shape = jax.ShapeDtypeStruct((rows, width), jnp.float32)
    vmem = pl.BlockSpec(memory_space=pltpu.VMEM)
    hbm = pl.BlockSpec(memory_space=pl.ANY)
    params = pltpu.CompilerParams(vmem_limit_bytes=24 * 2**20)

    def swap(block):
        return lax.ppermute(block, "replica", [(0, 1), (1, 0)])

    def stay(block):
        return pltpu.with_memory_space_constraint(block, pltpu.HBM)

    stats = (diag_stat, first_stat, second_stat)
    tile = pltpu.VMEM((TILE, width), jnp.float32)
    if paired:
        pieces = [own, swap(own)]
        far = pl.pallas_call(
            functools.partial(collect, rows),
            out_shape=tile,
            in_specs=[hbm] * 4,
            out_specs=vmem,
            scratch_shapes=[
                pltpu.VMEM((4 * TILE, width), jnp.float32),
                pltpu.SemaphoreType.DMA,
            ],
            compiler_params=params,
            name="collect",
        )(*[stay(x) for x in (own, *stats)])
        far = pl.pallas_call(
            functools.partial(choose, rows),
            out_shape=tile,
            in_specs=[vmem] * 2,
            out_specs=vmem,
            compiler_params=params,
            name="choose",
        )(far, pltpu.with_memory_space_constraint(own, pltpu.VMEM))
        far = lax.ppermute(far, axes, trades(shards, 1))
    else:
        pieces = [lax.psum(own, "replica") * scale]
        scale = 1.0
        tail = rows - 2
        unused = jnp.zeros((2, width), jnp.float32)
        last = jnp.concatenate([x[tail:] for x in (*pieces, *stats)])
        head = jnp.concatenate([x[:2] for x in (*pieces, *stats[:2])] + [unused])
        before = lax.ppermute(last, "fsdp", [(i, i + 1) for i in range(shards - 1)])
        after = lax.ppermute(head, "fsdp", [(i + 1, i) for i in range(shards - 1)])
        even = lax.axis_index("fsdp") % 2 == 0
        near, far = jnp.where(even, after, before), jnp.where(even, before, after)

    parts = len(pieces)
    whole = pltpu.VMEM((rows, width), jnp.float32)
    padded = pltpu.VMEM((rows + 2 * PAD, width), jnp.float32)
    chunk = 128 if rows % 128 == 0 else rows
    inner = [pltpu.with_memory_space_constraint(x, pltpu.VMEM) for x in (*pieces, *stats)]

    def inside(early, *done):
        return pl.pallas_call(
            functools.partial(interior, parts, early, scale, rows, chunk, 32),
            out_shape=(shape,) * 4 + (pltpu.VMEM((11 * TILE, width), jnp.float32),),
            in_specs=[vmem] * (parts + 3) + ([hbm] * 4 + [vmem] if done else []),
            out_specs=(hbm,) * 4 + (vmem,),
            input_output_aliases={parts + 3 + k: k for k in range(len(done[:4]))},
            scratch_shapes=[padded] * 6 + [whole, pltpu.SemaphoreType.DMA((4,))],
            compiler_params=params,
            cost_estimate=pl.CostEstimate(
                flops=45 * rows * width, bytes_accessed=36 * rows * width, transcendentals=0
            ),
            name="early" if early else "late",
        )(*inner, *done)

    done = inside(True)
    if paired:
        near = pl.pallas_call(
            functools.partial(ready, scale, rows),
            out_shape=tile,
            in_specs=[vmem] * 5,
            out_specs=vmem,
            compiler_params=params,
            name="ready",
        )(*inner)
        near, *done = lax.optimization_barrier((near, *done))
        near = lax.ppermute(near, axes, trades(shards, 0))
    update, diag_next, first_next, second_next, edges = inside(False, *done)
    other = far
    if paired:
        far, edges = lax.optimization_barrier((far, edges))
        other = swap(far)
    def patched(turn, other, *done):
        return pl.pallas_call(
            functools.partial(border, rows, shards, scale, turn),
            out_shape=(shape,) * 3,
            in_specs=[vmem] * 4 + [hbm] * 3,
            out_specs=(hbm,) * 3,
            input_output_aliases={4: 0, 5: 1, 6: 2},
            scratch_shapes=[
                pltpu.VMEM((4 * TILE, width), jnp.float32),
                pltpu.VMEM((2 * TILE, width), jnp.float32),
                pltpu.SemaphoreType.DMA,
            ],
            compiler_params=params,
            name="border",
        )(edges, near, far, other, *done)

    if paired:
        done = patched(1, far, update, first_next, second_next)
        update, first_next, second_next = patched(2, other, *done)
    else:
        update, first_next, second_next = patched(0, far, update, first_next, second_next)
    return update, diag_next, first_next, second_next


def solution(mesh):
    return jax.shard_map(
        body,
        mesh=mesh,
        in_specs=(P("replica", "fsdp", None), P("fsdp", None), P("fsdp", None), P("fsdp", None)),
        out_specs=(P("fsdp", None), P("fsdp", None), P("fsdp", None), P("fsdp", None)),
        check_vma=False,
    )
```

```python
import functools

import jax
import jax.numpy as jnp
from jax import lax
from jax.experimental import pallas as pl
from jax.experimental.pallas import tpu as pltpu
from jax.sharding import PartitionSpec as P

decay_rate = 0.95
damping = 0.01
PAD = 8
TILE = 8


def solved(g, g1, g2, d, upper, lower, f, c, s):
    det = upper * lower - c * c
    n1 = lower * f - c * s
    n2 = upper * s - c * f
    schur = d * det - f * n1 - s * n2
    top = g * det - n1 * g1 - n2 * g2
    w = top / (schur * det)
    return w * det, w * n1, w * n2


def collect(rows, own, diag, first, second, out, tiles, sems):
    even = lax.rem(lax.axis_index("fsdp"), 2) == 0
    low = lax.axis_index("replica") == 0

    @pl.when(low)
    def _():
        at = pl.multiple_of(jnp.where(even, 0, rows - TILE), TILE)
        copies = [
            pltpu.make_async_copy(
                source.at[pl.ds(at, TILE), :], tiles.at[k * TILE : (k + 1) * TILE, :], sems.at[k]
            )
            for k, source in enumerate((own, diag, first, second))
        ]
        for copy in copies:
            copy.start()
        for copy in copies:
            copy.wait()

    @pl.when(jnp.logical_and(low, even))
    def _():
        for k in range(3):
            out[2 * k : 2 * k + 2, :] = tiles[k * TILE : k * TILE + 2, :]
        out[6:8, :] = jnp.zeros((2, out.shape[1]), jnp.float32)

    @pl.when(jnp.logical_and(low, jnp.logical_not(even)))
    def _():
        for k in range(4):
            out[2 * k : 2 * k + 2, :] = tiles[(k + 1) * TILE - 2 : (k + 1) * TILE, :]


def choose(rows, block, own, out):
    even = lax.rem(lax.axis_index("fsdp"), 2) == 0
    low = lax.axis_index("replica") == 0

    @pl.when(low)
    def _():
        out[...] = block[...]

    @pl.when(jnp.logical_not(low))
    def _():
        out[2:8, :] = jnp.zeros((6, out.shape[1]), jnp.float32)
        out[0:2, :] = jnp.where(even, own[0:2, :], own[rows - 2 : rows, :])


def ready(scale, rows, own, other, diag, first, second, out):
    even = lax.rem(lax.axis_index("fsdp"), 2) == 0

    def fill(at, sources):
        out[0:2, :] = (own[at : at + 2, :] + other[at : at + 2, :]) * scale
        for k, source in enumerate(sources):
            out[2 * k + 2 : 2 * k + 4, :] = source[at : at + 2, :]

    @pl.when(even)
    def _():
        fill(rows - 2, (diag, first, second))

    @pl.when(jnp.logical_not(even))
    def _():
        fill(0, (diag, first))
        out[6:8, :] = jnp.zeros((2, out.shape[1]), jnp.float32)


def interior(parts, early, scale, rows, chunk, step, *refs):
    chosen = lax.axis_index("fsdp") == 0
    work = functools.partial(
        everything, parts, scale, rows, chunk, step, *refs[: parts + 3], *refs[-13:]
    )
    if early:
        pl.when(chosen)(work)
    else:
        pl.when(jnp.logical_not(chosen))(work)

        @pl.when(chosen)
        def _():
            refs[-9][...] = refs[parts + 7][...]


def everything(parts, scale, rows, chunk, step, *refs):
    pieces = refs[:parts]
    diag_in, first_in, second_in = refs[parts : parts + 3]
    outs = refs[parts + 3 : parts + 7]
    edges = refs[parts + 7]
    grad, diag, first, second, part1, part2, update, sems = refs[parts + 8 :]
    width = edges.shape[1]
    end = PAD + rows
    chunks = rows // chunk

    zeros = jnp.zeros((PAD, width), jnp.float32)
    grad[end:, :] = zeros
    diag[end:, :] = zeros + 1.0
    first[end:, :] = zeros
    part1[:PAD, :] = zeros
    part2[:PAD, :] = zeros

    def gradients(at, size):
        here, there = pl.ds(at, size), pl.ds(at + PAD, size)
        g = pieces[0][here, :]
        for piece in pieces[1:]:
            g = g + piece[here, :]
        g = g * scale
        grad[there, :] = g
        diag[there, :] = decay_rate * diag_in[here, :] + g * g

    def bands(at, size):
        here, there = pl.ds(at, size), pl.ds(at + PAD, size)
        g = grad[there, :]
        g1 = grad[pl.ds(at + PAD + 1, size), :]
        g2 = grad[pl.ds(at + PAD + 2, size), :]
        first[there, :] = decay_rate * first_in[here, :] + g * g1
        second[there, :] = decay_rate * second_in[here, :] + g * g2

    def values(at, size):
        there = pl.ds(at + PAD, size)
        after = pl.ds(at + PAD + 1, size)
        later = pl.ds(at + PAD + 2, size)
        v, p1, p2 = solved(
            grad[there, :],
            grad[after, :],
            grad[later, :],
            diag[there, :] + damping,
            diag[after, :] + damping,
            diag[later, :] + damping,
            first[there, :],
            first[after, :],
            second[there, :],
        )
        part1[there, :] = p1
        part2[there, :] = p2
        update[pl.ds(at, size), :] = (
            v - part1[pl.ds(at + PAD - 1, size), :] - part2[pl.ds(at + PAD - 2, size), :]
        )

    def over(work, low, high):
        for at in range(low, high, step):
            work(at, min(step, high - at))

    def send(source, pad, k, low, high):
        copy = pltpu.make_async_copy(
            source.at[low + pad : high + pad, :], outs[k].at[low:high, :], sems.at[k]
        )
        copy.start()

    for c in range(chunks):
        last = c == chunks - 1
        low, high = c * chunk, (c + 1) * chunk
        over(gradients, low, high)
        send(diag, PAD, 1, low, high)
        low, high = max(low - TILE, 0), high if last else high - TILE
        over(bands, low, high)
        send(first, PAD, 2, low, high)
        send(second, PAD, 3, low, high)
        low, high = max(c * chunk - 2 * TILE, 0), high if last else high - TILE
        over(values, low, high)
        send(update, 0, 0, low, high)

    tops = [grad[PAD : PAD + TILE, :], diag[PAD : PAD + TILE, :], first[PAD : PAD + TILE, :]]
    tops.append(update[:TILE, :])
    tails = [r[end - TILE : end, :] for r in (grad, diag, first, second)]
    tails.append(update[rows - TILE :, :])
    tails += [r[end - TILE : end, :] for r in (part1, part2)]
    for k, tile in enumerate(tops + tails):
        edges[k * TILE : (k + 1) * TILE, :] = tile
    for k, (source, pad) in enumerate(((update, 0), (diag, PAD), (first, PAD), (second, PAD))):
        pltpu.make_async_copy(source.at[pad : pad + rows, :], outs[k], sems.at[k]).wait()


def border(rows, shards, scale, turn, *refs):
    chosen = lax.axis_index("fsdp") == 0
    if turn == 0:
        patch(rows, shards, scale, *refs)
    else:
        pl.when(chosen if turn == 1 else jnp.logical_not(chosen))(
            functools.partial(patch, rows, shards, scale, *refs)
        )


def patch(rows, shards, scale, *refs):
    edges, near, far, other = refs[:4]
    outs = refs[7:10]
    tiles, mixed, sem = refs[10:]
    tiles[0:8, :] = edges[3 * TILE : 4 * TILE, :]
    tiles[8:16, :] = edges[8 * TILE : 9 * TILE, :]
    tiles[16:24, :] = edges[6 * TILE : 7 * TILE, :]
    tiles[24:32, :] = edges[7 * TILE : 8 * TILE, :]
    rest = None
    if scale != 1.0:
        low = lax.axis_index("replica") == 0
        mine, theirs = far[...], other[...]
        mixed[0:8, :] = jnp.where(low, theirs, mine)
        mixed[8:16, :] = jnp.where(low, mine, theirs)
        far, rest = mixed.at[0:8, :], mixed.at[8:16, :]
    even = lax.rem(lax.axis_index("fsdp"), 2) == 0

    @pl.when(even)
    def _():
        lower(scale, edges, far, rest, tiles)
        upper(scale, shards, edges, near, None, tiles)

    @pl.when(jnp.logical_not(even))
    def _():
        lower(scale, edges, near, None, tiles)
        upper(scale, shards, edges, far, rest, tiles)

    targets = [outs[0].at[0:TILE, :]] + [out.at[rows - TILE : rows, :] for out in outs]
    for k, target in enumerate(targets):
        pltpu.make_async_copy(tiles.at[k * TILE : (k + 1) * TILE, :], target, sem).start()
    pltpu.make_async_copy(tiles, outs[0].at[0 : 4 * TILE, :], sem).wait()


def neighbour(scale, block, rest):
    g = [block[k : k + 1, :] for k in range(2)]
    if rest is not None:
        g = [(g[k] + rest[k : k + 1, :]) * scale for k in range(2)]
    d = [decay_rate * block[k + 2 : k + 3, :] + g[k] * g[k] + damping for k in range(2)]
    f = decay_rate * block[4:5, :] + g[0] * g[1]
    return g, d, f


def lower(scale, edges, block, rest, tiles):
    def edge(k, at):
        return edges[k * TILE + at : k * TILE + at + 1, :]

    (ga, gb), (da, db), fa = neighbour(scale, block, rest)
    g0, g1 = edge(0, 0), edge(0, 1)
    d0, d1 = edge(1, 0) + damping, edge(1, 1) + damping
    f0 = edge(2, 0)
    fb = decay_rate * block[5:6, :] + gb * g0
    sa = decay_rate * block[6:7, :] + ga * g0
    sb = decay_rate * block[7:8, :] + gb * g1
    _, _, far_a = solved(ga, gb, g0, da, db, d0, fa, fb, sa)
    _, near_b, far_b = solved(gb, g0, g1, db, d0, d1, fb, f0, sb)
    none = lax.axis_index("fsdp") == 0
    tiles[0:1, :] = edge(3, 0) - jnp.where(none, 0.0, near_b) - jnp.where(none, 0.0, far_a)
    tiles[1:2, :] = edge(3, 1) - jnp.where(none, 0.0, far_b)


def upper(scale, shards, edges, block, rest, tiles):
    def edge(k, at):
        return edges[k * TILE + at : k * TILE + at + 1, :]

    none = lax.axis_index("fsdp") == shards - 1
    (gp, gq), (dp, dq), fp = neighbour(scale, block, rest)
    gp, gq = jnp.where(none, 0.0, gp), jnp.where(none, 0.0, gq)
    dp, dq = jnp.where(none, 1.0, dp), jnp.where(none, 1.0, dq)
    fp = jnp.where(none, 0.0, fp)
    gx, gy = edge(4, 6), edge(4, 7)
    dx, dy = edge(5, 6) + damping, edge(5, 7) + damping
    fx = edge(6, 6)
    fy = jnp.where(none, 0.0, edge(6, 7) + gy * gp)
    sx = jnp.where(none, 0.0, edge(7, 6) + gx * gp)
    sy = jnp.where(none, 0.0, edge(7, 7) + gy * gq)
    vx, near_x, _ = solved(gx, gy, gp, dx, dy, dp, fx, fy, sx)
    vy, _, _ = solved(gy, gp, gq, dy, dp, dq, fy, fp, sy)
    tiles[14:15, :] = vx - edge(9, 5) - edge(10, 4)
    tiles[15:16, :] = vy - near_x - edge(10, 5)
    tiles[23:24, :] = fy
    tiles[30:31, :] = sx
    tiles[31:32, :] = sy


def trades(shards, low):
    partner = {}
    for i in range(low, shards - 1, 2):
        partner[i], partner[i + 1] = i + 1, i
    return [
        (2 * i + core, 2 * partner.get(i, i) + 1 - core) for i in range(shards) for core in range(2)
    ]


def body(partials, diag_stat, first_stat, second_stat):
    own = partials[0]
    rows, width = own.shape
    replicas = lax.axis_size("replica")
    shards = lax.axis_size("fsdp")
    scale = 1.0 / replicas
    axes = ("fsdp", "replica")
    paired = replicas == 2 and shards > 1

    shape = jax.ShapeDtypeStruct((rows, width), jnp.float32)
    vmem = pl.BlockSpec(memory_space=pltpu.VMEM)
    hbm = pl.BlockSpec(memory_space=pl.ANY)
    params = pltpu.CompilerParams(vmem_limit_bytes=24 * 2**20)

    def swap(block):
        return lax.ppermute(block, "replica", [(0, 1), (1, 0)])

    def stay(block):
        return pltpu.with_memory_space_constraint(block, pltpu.HBM)

    stats = (diag_stat, first_stat, second_stat)
    tile = pltpu.VMEM((TILE, width), jnp.float32)
    if paired:
        pieces = [own, swap(own)]
        far = pl.pallas_call(
            functools.partial(collect, rows),
            out_shape=tile,
            in_specs=[hbm] * 4,
            out_specs=vmem,
            scratch_shapes=[
                pltpu.VMEM((4 * TILE, width), jnp.float32),
                pltpu.SemaphoreType.DMA((4,)),
            ],
            compiler_params=params,
            name="collect",
        )(*[stay(x) for x in (own, *stats)])
        far = pl.pallas_call(
            functools.partial(choose, rows),
            out_shape=tile,
            in_specs=[vmem] * 2,
            out_specs=vmem,
            compiler_params=params,
            name="choose",
        )(far, pltpu.with_memory_space_constraint(own, pltpu.VMEM))
        far = lax.ppermute(far, axes, trades(shards, 1))
    else:
        pieces = [lax.psum(own, "replica") * scale]
        scale = 1.0
        tail = rows - 2
        unused = jnp.zeros((2, width), jnp.float32)
        last = jnp.concatenate([x[tail:] for x in (*pieces, *stats)])
        head = jnp.concatenate([x[:2] for x in (*pieces, *stats[:2])] + [unused])
        before = lax.ppermute(last, "fsdp", [(i, i + 1) for i in range(shards - 1)])
        after = lax.ppermute(head, "fsdp", [(i + 1, i) for i in range(shards - 1)])
        even = lax.axis_index("fsdp") % 2 == 0
        near, far = jnp.where(even, after, before), jnp.where(even, before, after)

    parts = len(pieces)
    whole = pltpu.VMEM((rows, width), jnp.float32)
    padded = pltpu.VMEM((rows + 2 * PAD, width), jnp.float32)
    chunk = 256 if rows % 256 == 0 else rows
    inner = [pltpu.with_memory_space_constraint(x, pltpu.VMEM) for x in (*pieces, *stats)]

    def inside(early, *done):
        return pl.pallas_call(
            functools.partial(interior, parts, early, scale, rows, chunk, 32),
            out_shape=(shape,) * 4 + (pltpu.VMEM((11 * TILE, width), jnp.float32),),
            in_specs=[vmem] * (parts + 3) + ([hbm] * 4 + [vmem] if done else []),
            out_specs=(hbm,) * 4 + (vmem,),
            input_output_aliases={parts + 3 + k: k for k in range(len(done[:4]))},
            scratch_shapes=[padded] * 6 + [whole, pltpu.SemaphoreType.DMA((4,))],
            compiler_params=params,
            cost_estimate=pl.CostEstimate(
                flops=45 * rows * width, bytes_accessed=36 * rows * width, transcendentals=0
            ),
            name="early" if early else "late",
        )(*inner, *done)

    done = inside(True)
    if paired:
        near = pl.pallas_call(
            functools.partial(ready, scale, rows),
            out_shape=tile,
            in_specs=[vmem] * 5,
            out_specs=vmem,
            compiler_params=params,
            name="ready",
        )(*inner)
        near, *done = lax.optimization_barrier((near, *done))
        near = lax.ppermute(near, axes, trades(shards, 0))
    update, diag_next, first_next, second_next, edges = inside(False, *done)
    other = far
    if paired:
        far, edges = lax.optimization_barrier((far, edges))
        other = swap(far)
    def patched(turn, other, *done):
        return pl.pallas_call(
            functools.partial(border, rows, shards, scale, turn),
            out_shape=(shape,) * 3,
            in_specs=[vmem] * 4 + [hbm] * 3,
            out_specs=(hbm,) * 3,
            input_output_aliases={4: 0, 5: 1, 6: 2},
            scratch_shapes=[
                pltpu.VMEM((4 * TILE, width), jnp.float32),
                pltpu.VMEM((2 * TILE, width), jnp.float32),
                pltpu.SemaphoreType.DMA,
            ],
            compiler_params=params,
            name="border",
        )(edges, near, far, other, *done)

    if paired:
        done = patched(1, far, update, first_next, second_next)
        update, first_next, second_next = patched(2, other, *done)
    else:
        update, first_next, second_next = patched(0, far, update, first_next, second_next)
    return update, diag_next, first_next, second_next


def solution(mesh):
    return jax.shard_map(
        body,
        mesh=mesh,
        in_specs=(P("replica", "fsdp", None), P("fsdp", None), P("fsdp", None), P("fsdp", None)),
        out_specs=(P("fsdp", None), P("fsdp", None), P("fsdp", None), P("fsdp", None)),
        check_vma=False,
    )
```

```python
import functools

import jax
import jax.numpy as jnp
from jax import lax
from jax.experimental import pallas as pl
from jax.experimental.pallas import tpu as pltpu
from jax.sharding import PartitionSpec as P

decay_rate = 0.95
damping = 0.01
PAD = 8
TILE = 8


def solved(g, g1, g2, d, upper, lower, f, c, s):
    det = upper * lower - c * c
    n1 = lower * f - c * s
    n2 = upper * s - c * f
    schur = d * det - f * n1 - s * n2
    top = g * det - n1 * g1 - n2 * g2
    w = top / (schur * det)
    return w * det, w * n1, w * n2


def collect(rows, own, diag, first, second, out, tiles, sems):
    even = lax.rem(lax.axis_index("fsdp"), 2) == 0
    low = lax.axis_index("replica") == 0

    @pl.when(low)
    def _():
        at = pl.multiple_of(jnp.where(even, 0, rows - TILE), TILE)
        copies = [
            pltpu.make_async_copy(
                source.at[pl.ds(at, TILE), :], tiles.at[k * TILE : (k + 1) * TILE, :], sems.at[k]
            )
            for k, source in enumerate((own, diag, first, second))
        ]
        for copy in copies:
            copy.start()
        for copy in copies:
            copy.wait()

    @pl.when(jnp.logical_and(low, even))
    def _():
        for k in range(3):
            out[2 * k : 2 * k + 2, :] = tiles[k * TILE : k * TILE + 2, :]
        out[6:8, :] = jnp.zeros((2, out.shape[1]), jnp.float32)

    @pl.when(jnp.logical_and(low, jnp.logical_not(even)))
    def _():
        for k in range(4):
            out[2 * k : 2 * k + 2, :] = tiles[(k + 1) * TILE - 2 : (k + 1) * TILE, :]


def choose(rows, block, own, out):
    even = lax.rem(lax.axis_index("fsdp"), 2) == 0
    low = lax.axis_index("replica") == 0

    @pl.when(low)
    def _():
        out[...] = block[...]

    @pl.when(jnp.logical_not(low))
    def _():
        out[2:8, :] = jnp.zeros((6, out.shape[1]), jnp.float32)
        out[0:2, :] = jnp.where(even, own[0:2, :], own[rows - 2 : rows, :])


def ready(scale, rows, own, other, diag, first, second, out):
    even = lax.rem(lax.axis_index("fsdp"), 2) == 0

    def fill(at, sources):
        out[0:2, :] = (own[at : at + 2, :] + other[at : at + 2, :]) * scale
        for k, source in enumerate(sources):
            out[2 * k + 2 : 2 * k + 4, :] = source[at : at + 2, :]

    @pl.when(even)
    def _():
        fill(rows - 2, (diag, first, second))

    @pl.when(jnp.logical_not(even))
    def _():
        fill(0, (diag, first))
        out[6:8, :] = jnp.zeros((2, out.shape[1]), jnp.float32)


def interior(parts, early, scale, rows, chunk, step, *refs):
    chosen = lax.axis_index("fsdp") == 0
    work = functools.partial(
        everything, parts, scale, rows, chunk, step, *refs[: parts + 3], *refs[-13:]
    )
    if early:
        pl.when(chosen)(work)
    else:
        pl.when(jnp.logical_not(chosen))(work)

        @pl.when(chosen)
        def _():
            refs[-9][...] = refs[parts + 7][...]


def everything(parts, scale, rows, chunk, step, *refs):
    pieces = refs[:parts]
    diag_in, first_in, second_in = refs[parts : parts + 3]
    outs = refs[parts + 3 : parts + 7]
    edges = refs[parts + 7]
    grad, diag, first, second, part1, part2, update, sems = refs[parts + 8 :]
    width = edges.shape[1]
    end = PAD + rows
    chunks = rows // chunk

    zeros = jnp.zeros((PAD, width), jnp.float32)
    grad[end:, :] = zeros
    diag[end:, :] = zeros + 1.0
    first[end:, :] = zeros
    part1[:PAD, :] = zeros
    part2[:PAD, :] = zeros

    def gradients(at, size):
        here, there = pl.ds(at, size), pl.ds(at + PAD, size)
        g = pieces[0][here, :]
        for piece in pieces[1:]:
            g = g + piece[here, :]
        g = g * scale
        grad[there, :] = g
        diag[there, :] = decay_rate * diag_in[here, :] + g * g

    def bands(at, size):
        here, there = pl.ds(at, size), pl.ds(at + PAD, size)
        g = grad[there, :]
        g1 = grad[pl.ds(at + PAD + 1, size), :]
        g2 = grad[pl.ds(at + PAD + 2, size), :]
        first[there, :] = decay_rate * first_in[here, :] + g * g1
        second[there, :] = decay_rate * second_in[here, :] + g * g2

    def values(at, size):
        there = pl.ds(at + PAD, size)
        after = pl.ds(at + PAD + 1, size)
        later = pl.ds(at + PAD + 2, size)
        v, p1, p2 = solved(
            grad[there, :],
            grad[after, :],
            grad[later, :],
            diag[there, :] + damping,
            diag[after, :] + damping,
            diag[later, :] + damping,
            first[there, :],
            first[after, :],
            second[there, :],
        )
        part1[there, :] = p1
        part2[there, :] = p2
        update[pl.ds(at, size), :] = (
            v - part1[pl.ds(at + PAD - 1, size), :] - part2[pl.ds(at + PAD - 2, size), :]
        )

    def over(work, low, high):
        for at in range(low, high, step):
            work(at, min(step, high - at))

    def send(source, pad, k, low, high):
        copy = pltpu.make_async_copy(
            source.at[low + pad : high + pad, :], outs[k].at[low:high, :], sems.at[k]
        )
        copy.start()

    for c in range(chunks):
        last = c == chunks - 1
        low, high = c * chunk, (c + 1) * chunk
        over(gradients, low, high)
        send(diag, PAD, 1, low, high)
        low, high = max(low - TILE, 0), high if last else high - TILE
        over(bands, low, high)
        send(first, PAD, 2, low, high)
        send(second, PAD, 3, low, high)
        low, high = max(c * chunk - 2 * TILE, 0), high if last else high - TILE
        over(values, low, high)
        send(update, 0, 0, low, high)

    tops = [grad[PAD : PAD + TILE, :], diag[PAD : PAD + TILE, :], first[PAD : PAD + TILE, :]]
    tops.append(update[:TILE, :])
    tails = [r[end - TILE : end, :] for r in (grad, diag, first, second)]
    tails.append(update[rows - TILE :, :])
    tails += [r[end - TILE : end, :] for r in (part1, part2)]
    for k, tile in enumerate(tops + tails):
        edges[k * TILE : (k + 1) * TILE, :] = tile
    for k, (source, pad) in enumerate(((update, 0), (diag, PAD), (first, PAD), (second, PAD))):
        pltpu.make_async_copy(source.at[pad : pad + rows, :], outs[k], sems.at[k]).wait()


def border(rows, shards, scale, turn, *refs):
    chosen = lax.axis_index("fsdp") == 0
    if turn == 0:
        patch(rows, shards, scale, *refs)
    else:
        pl.when(chosen if turn == 1 else jnp.logical_not(chosen))(
            functools.partial(patch, rows, shards, scale, *refs)
        )


def patch(rows, shards, scale, *refs):
    edges, near, far, other = refs[:4]
    outs = refs[7:10]
    tiles, sem = refs[10:]
    tiles[0:8, :] = edges[3 * TILE : 4 * TILE, :]
    tiles[8:16, :] = edges[8 * TILE : 9 * TILE, :]
    tiles[16:24, :] = edges[6 * TILE : 7 * TILE, :]
    tiles[24:32, :] = edges[7 * TILE : 8 * TILE, :]
    even = lax.rem(lax.axis_index("fsdp"), 2) == 0

    def edges_from(block, rest):
        @pl.when(even)
        def _():
            lower(scale, edges, block, rest, tiles)
            upper(scale, shards, edges, near, None, tiles)

        @pl.when(jnp.logical_not(even))
        def _():
            lower(scale, edges, near, None, tiles)
            upper(scale, shards, edges, block, rest, tiles)

    if scale == 1.0:
        edges_from(far, None)
    else:
        low = lax.axis_index("replica") == 0
        pl.when(low)(functools.partial(edges_from, other, far))
        pl.when(jnp.logical_not(low))(functools.partial(edges_from, far, other))

    targets = [outs[0].at[0:TILE, :]] + [out.at[rows - TILE : rows, :] for out in outs]
    for k, target in enumerate(targets):
        pltpu.make_async_copy(tiles.at[k * TILE : (k + 1) * TILE, :], target, sem).start()
    pltpu.make_async_copy(tiles, outs[0].at[0 : 4 * TILE, :], sem).wait()


def neighbour(scale, block, rest):
    g = [block[k : k + 1, :] for k in range(2)]
    if rest is not None:
        g = [(g[k] + rest[k : k + 1, :]) * scale for k in range(2)]
    d = [decay_rate * block[k + 2 : k + 3, :] + g[k] * g[k] + damping for k in range(2)]
    f = decay_rate * block[4:5, :] + g[0] * g[1]
    return g, d, f


def lower(scale, edges, block, rest, tiles):
    def edge(k, at):
        return edges[k * TILE + at : k * TILE + at + 1, :]

    (ga, gb), (da, db), fa = neighbour(scale, block, rest)
    g0, g1 = edge(0, 0), edge(0, 1)
    d0, d1 = edge(1, 0) + damping, edge(1, 1) + damping
    f0 = edge(2, 0)
    fb = decay_rate * block[5:6, :] + gb * g0
    sa = decay_rate * block[6:7, :] + ga * g0
    sb = decay_rate * block[7:8, :] + gb * g1
    _, _, far_a = solved(ga, gb, g0, da, db, d0, fa, fb, sa)
    _, near_b, far_b = solved(gb, g0, g1, db, d0, d1, fb, f0, sb)
    none = lax.axis_index("fsdp") == 0
    tiles[0:1, :] = edge(3, 0) - jnp.where(none, 0.0, near_b) - jnp.where(none, 0.0, far_a)
    tiles[1:2, :] = edge(3, 1) - jnp.where(none, 0.0, far_b)


def upper(scale, shards, edges, block, rest, tiles):
    def edge(k, at):
        return edges[k * TILE + at : k * TILE + at + 1, :]

    none = lax.axis_index("fsdp") == shards - 1
    (gp, gq), (dp, dq), fp = neighbour(scale, block, rest)
    gp, gq = jnp.where(none, 0.0, gp), jnp.where(none, 0.0, gq)
    dp, dq = jnp.where(none, 1.0, dp), jnp.where(none, 1.0, dq)
    fp = jnp.where(none, 0.0, fp)
    gx, gy = edge(4, 6), edge(4, 7)
    dx, dy = edge(5, 6) + damping, edge(5, 7) + damping
    fx = edge(6, 6)
    fy = jnp.where(none, 0.0, edge(6, 7) + gy * gp)
    sx = jnp.where(none, 0.0, edge(7, 6) + gx * gp)
    sy = jnp.where(none, 0.0, edge(7, 7) + gy * gq)
    vx, near_x, _ = solved(gx, gy, gp, dx, dy, dp, fx, fy, sx)
    vy, _, _ = solved(gy, gp, gq, dy, dp, dq, fy, fp, sy)
    tiles[14:15, :] = vx - edge(9, 5) - edge(10, 4)
    tiles[15:16, :] = vy - near_x - edge(10, 5)
    tiles[23:24, :] = fy
    tiles[30:31, :] = sx
    tiles[31:32, :] = sy


def trades(shards, low):
    partner = {}
    for i in range(low, shards - 1, 2):
        partner[i], partner[i + 1] = i + 1, i
    return [
        (2 * i + core, 2 * partner.get(i, i) + 1 - core) for i in range(shards) for core in range(2)
    ]


def body(partials, diag_stat, first_stat, second_stat):
    own = partials[0]
    rows, width = own.shape
    replicas = lax.axis_size("replica")
    shards = lax.axis_size("fsdp")
    scale = 1.0 / replicas
    axes = ("fsdp", "replica")
    paired = replicas == 2 and shards > 1

    shape = jax.ShapeDtypeStruct((rows, width), jnp.float32)
    vmem = pl.BlockSpec(memory_space=pltpu.VMEM)
    hbm = pl.BlockSpec(memory_space=pl.ANY)
    params = pltpu.CompilerParams(vmem_limit_bytes=24 * 2**20)

    def swap(block):
        return lax.ppermute(block, "replica", [(0, 1), (1, 0)])

    def stay(block):
        return pltpu.with_memory_space_constraint(block, pltpu.HBM)

    stats = (diag_stat, first_stat, second_stat)
    tile = pltpu.VMEM((TILE, width), jnp.float32)
    if paired:
        pieces = [own, swap(own)]
        far = pl.pallas_call(
            functools.partial(collect, rows),
            out_shape=tile,
            in_specs=[hbm] * 4,
            out_specs=vmem,
            scratch_shapes=[
                pltpu.VMEM((4 * TILE, width), jnp.float32),
                pltpu.SemaphoreType.DMA((4,)),
            ],
            compiler_params=params,
            name="collect",
        )(*[stay(x) for x in (own, *stats)])
        far = pl.pallas_call(
            functools.partial(choose, rows),
            out_shape=tile,
            in_specs=[vmem] * 2,
            out_specs=vmem,
            compiler_params=params,
            name="choose",
        )(far, pltpu.with_memory_space_constraint(own, pltpu.VMEM))
        far = lax.ppermute(far, axes, trades(shards, 1))
    else:
        pieces = [lax.psum(own, "replica") * scale]
        scale = 1.0
        tail = rows - 2
        unused = jnp.zeros((2, width), jnp.float32)
        last = jnp.concatenate([x[tail:] for x in (*pieces, *stats)])
        head = jnp.concatenate([x[:2] for x in (*pieces, *stats[:2])] + [unused])
        before = lax.ppermute(last, "fsdp", [(i, i + 1) for i in range(shards - 1)])
        after = lax.ppermute(head, "fsdp", [(i + 1, i) for i in range(shards - 1)])
        even = lax.axis_index("fsdp") % 2 == 0
        near, far = jnp.where(even, after, before), jnp.where(even, before, after)

    parts = len(pieces)
    whole = pltpu.VMEM((rows, width), jnp.float32)
    padded = pltpu.VMEM((rows + 2 * PAD, width), jnp.float32)
    chunk = 256 if rows % 256 == 0 else rows
    inner = [pltpu.with_memory_space_constraint(x, pltpu.VMEM) for x in (*pieces, *stats)]

    def inside(early, *done):
        return pl.pallas_call(
            functools.partial(interior, parts, early, scale, rows, chunk, 32),
            out_shape=(shape,) * 4 + (pltpu.VMEM((11 * TILE, width), jnp.float32),),
            in_specs=[vmem] * (parts + 3) + ([hbm] * 4 + [vmem] if done else []),
            out_specs=(hbm,) * 4 + (vmem,),
            input_output_aliases={parts + 3 + k: k for k in range(len(done[:4]))},
            scratch_shapes=[padded] * 6 + [whole, pltpu.SemaphoreType.DMA((4,))],
            compiler_params=params,
            cost_estimate=pl.CostEstimate(
                flops=45 * rows * width, bytes_accessed=36 * rows * width, transcendentals=0
            ),
            name="early" if early else "late",
        )(*inner, *done)

    done = inside(True)
    if paired:
        near = pl.pallas_call(
            functools.partial(ready, scale, rows),
            out_shape=tile,
            in_specs=[vmem] * 5,
            out_specs=vmem,
            compiler_params=params,
            name="ready",
        )(*inner)
        near, *done = lax.optimization_barrier((near, *done))
        near = lax.ppermute(near, axes, trades(shards, 0))
    update, diag_next, first_next, second_next, edges = inside(False, *done)
    other = far
    if paired:
        far, edges = lax.optimization_barrier((far, edges))
        other = swap(far)
    def patched(turn, other, *done):
        return pl.pallas_call(
            functools.partial(border, rows, shards, scale, turn),
            out_shape=(shape,) * 3,
            in_specs=[vmem] * 4 + [hbm] * 3,
            out_specs=(hbm,) * 3,
            input_output_aliases={4: 0, 5: 1, 6: 2},
            scratch_shapes=[
                pltpu.VMEM((4 * TILE, width), jnp.float32),
                pltpu.SemaphoreType.DMA,
            ],
            compiler_params=params,
            name="border",
        )(edges, near, far, other, *done)

    if paired:
        done = patched(1, far, update, first_next, second_next)
        update, first_next, second_next = patched(2, other, *done)
    else:
        update, first_next, second_next = patched(0, far, update, first_next, second_next)
    return update, diag_next, first_next, second_next


def solution(mesh):
    return jax.shard_map(
        body,
        mesh=mesh,
        in_specs=(P("replica", "fsdp", None), P("fsdp", None), P("fsdp", None), P("fsdp", None)),
        out_specs=(P("fsdp", None), P("fsdp", None), P("fsdp", None), P("fsdp", None)),
        check_vma=False,
    )
```

```python
import functools

import jax
import jax.numpy as jnp
from jax import lax
from jax.experimental import pallas as pl
from jax.experimental.pallas import tpu as pltpu
from jax.sharding import PartitionSpec as P

decay_rate = 0.95
damping = 0.01
PAD = 8
TILE = 8


def solved(g, g1, g2, d, upper, lower, f, c, s):
    det = upper * lower - c * c
    n1 = lower * f - c * s
    n2 = upper * s - c * f
    schur = d * det - f * n1 - s * n2
    top = g * det - n1 * g1 - n2 * g2
    w = top / (schur * det)
    return w * det, w * n1, w * n2


def collect(rows, own, diag, first, second, out, tiles, sems):
    even = lax.rem(lax.axis_index("fsdp"), 2) == 0
    low = lax.axis_index("replica") == 0

    @pl.when(low)
    def _():
        at = pl.multiple_of(jnp.where(even, 0, rows - TILE), TILE)
        copies = [
            pltpu.make_async_copy(
                source.at[pl.ds(at, TILE), :], tiles.at[k * TILE : (k + 1) * TILE, :], sems.at[k]
            )
            for k, source in enumerate((own, diag, first, second))
        ]
        for copy in copies[:3]:
            copy.start()

        @pl.when(jnp.logical_not(even))
        def _():
            copies[3].start()
            copies[3].wait()

        for copy in copies[:3]:
            copy.wait()

    @pl.when(jnp.logical_and(low, even))
    def _():
        for k in range(3):
            out[2 * k : 2 * k + 2, :] = tiles[k * TILE : k * TILE + 2, :]
        out[6:8, :] = jnp.zeros((2, out.shape[1]), jnp.float32)

    @pl.when(jnp.logical_and(low, jnp.logical_not(even)))
    def _():
        for k in range(4):
            out[2 * k : 2 * k + 2, :] = tiles[(k + 1) * TILE - 2 : (k + 1) * TILE, :]


def choose(rows, block, own, out):
    even = lax.rem(lax.axis_index("fsdp"), 2) == 0
    low = lax.axis_index("replica") == 0

    @pl.when(low)
    def _():
        out[...] = block[...]

    @pl.when(jnp.logical_not(low))
    def _():
        out[2:8, :] = jnp.zeros((6, out.shape[1]), jnp.float32)
        out[0:2, :] = jnp.where(even, own[0:2, :], own[rows - 2 : rows, :])


def ready(scale, rows, own, other, diag, first, second, out):
    even = lax.rem(lax.axis_index("fsdp"), 2) == 0

    def fill(at, sources):
        out[0:2, :] = (own[at : at + 2, :] + other[at : at + 2, :]) * scale
        for k, source in enumerate(sources):
            out[2 * k + 2 : 2 * k + 4, :] = source[at : at + 2, :]

    @pl.when(even)
    def _():
        fill(rows - 2, (diag, first, second))

    @pl.when(jnp.logical_not(even))
    def _():
        fill(0, (diag, first))
        out[6:8, :] = jnp.zeros((2, out.shape[1]), jnp.float32)


def interior(parts, early, scale, rows, chunk, step, *refs):
    chosen = lax.axis_index("fsdp") == 0
    work = functools.partial(
        everything, parts, scale, rows, chunk, step, *refs[: parts + 3], *refs[-13:]
    )
    if early:
        pl.when(chosen)(work)
    else:
        pl.when(jnp.logical_not(chosen))(work)

        @pl.when(chosen)
        def _():
            refs[-9][...] = refs[parts + 7][...]


def everything(parts, scale, rows, chunk, step, *refs):
    pieces = refs[:parts]
    diag_in, first_in, second_in = refs[parts : parts + 3]
    outs = refs[parts + 3 : parts + 7]
    edges = refs[parts + 7]
    grad, diag, first, second, part1, part2, update, sems = refs[parts + 8 :]
    width = edges.shape[1]
    end = PAD + rows
    chunks = rows // chunk

    zeros = jnp.zeros((PAD, width), jnp.float32)
    grad[end:, :] = zeros
    diag[end:, :] = zeros + 1.0
    first[end:, :] = zeros
    part1[:PAD, :] = zeros
    part2[:PAD, :] = zeros

    def gradients(at, size):
        here, there = pl.ds(at, size), pl.ds(at + PAD, size)
        g = pieces[0][here, :]
        for piece in pieces[1:]:
            g = g + piece[here, :]
        g = g * scale
        grad[there, :] = g
        diag[there, :] = decay_rate * diag_in[here, :] + g * g

    def bands(at, size):
        here, there = pl.ds(at, size), pl.ds(at + PAD, size)
        g = grad[there, :]
        g1 = grad[pl.ds(at + PAD + 1, size), :]
        g2 = grad[pl.ds(at + PAD + 2, size), :]
        first[there, :] = decay_rate * first_in[here, :] + g * g1
        second[there, :] = decay_rate * second_in[here, :] + g * g2

    def values(at, size):
        there = pl.ds(at + PAD, size)
        after = pl.ds(at + PAD + 1, size)
        later = pl.ds(at + PAD + 2, size)
        v, p1, p2 = solved(
            grad[there, :],
            grad[after, :],
            grad[later, :],
            diag[there, :] + damping,
            diag[after, :] + damping,
            diag[later, :] + damping,
            first[there, :],
            first[after, :],
            second[there, :],
        )
        part1[there, :] = p1
        part2[there, :] = p2
        update[pl.ds(at, size), :] = (
            v - part1[pl.ds(at + PAD - 1, size), :] - part2[pl.ds(at + PAD - 2, size), :]
        )

    def over(work, low, high):
        for at in range(low, high, step):
            work(at, min(step, high - at))

    def send(source, pad, k, low, high):
        copy = pltpu.make_async_copy(
            source.at[low + pad : high + pad, :], outs[k].at[low:high, :], sems.at[k]
        )
        copy.start()

    for c in range(chunks):
        last = c == chunks - 1
        low, high = c * chunk, (c + 1) * chunk
        over(gradients, low, high)
        send(diag, PAD, 1, low, high)
        low, high = max(low - TILE, 0), high if last else high - TILE
        over(bands, low, high)
        send(first, PAD, 2, low, high)
        send(second, PAD, 3, low, high)
        low, high = max(c * chunk - 2 * TILE, 0), high if last else high - TILE
        over(values, low, high)
        send(update, 0, 0, low, high)

    tops = [grad[PAD : PAD + TILE, :], diag[PAD : PAD + TILE, :], first[PAD : PAD + TILE, :]]
    tops.append(update[:TILE, :])
    tails = [r[end - TILE : end, :] for r in (grad, diag, first, second)]
    tails.append(update[rows - TILE :, :])
    tails += [r[end - TILE : end, :] for r in (part1, part2)]
    for k, tile in enumerate(tops + tails):
        edges[k * TILE : (k + 1) * TILE, :] = tile
    for k, (source, pad) in enumerate(((update, 0), (diag, PAD), (first, PAD), (second, PAD))):
        pltpu.make_async_copy(source.at[pad : pad + rows, :], outs[k], sems.at[k]).wait()


def border(rows, shards, scale, turn, *refs):
    chosen = lax.axis_index("fsdp") == 0
    if turn == 0:
        patch(rows, shards, scale, *refs)
    else:
        pl.when(chosen if turn == 1 else jnp.logical_not(chosen))(
            functools.partial(patch, rows, shards, scale, *refs)
        )


def patch(rows, shards, scale, *refs):
    edges, near, far, other = refs[:4]
    outs = refs[7:10]
    tiles, mixed, sem = refs[10:]
    tiles[0:8, :] = edges[3 * TILE : 4 * TILE, :]
    tiles[8:16, :] = edges[8 * TILE : 9 * TILE, :]
    tiles[16:24, :] = edges[6 * TILE : 7 * TILE, :]
    tiles[24:32, :] = edges[7 * TILE : 8 * TILE, :]
    rest = None
    if scale != 1.0:
        low = lax.axis_index("replica") == 0
        mine, theirs = far[...], other[...]
        mixed[0:8, :] = jnp.where(low, theirs, mine)
        mixed[8:16, :] = jnp.where(low, mine, theirs)
        far, rest = mixed.at[0:8, :], mixed.at[8:16, :]
    even = lax.rem(lax.axis_index("fsdp"), 2) == 0

    @pl.when(even)
    def _():
        lower(scale, edges, far, rest, tiles)
        upper(scale, shards, edges, near, None, tiles)

    @pl.when(jnp.logical_not(even))
    def _():
        lower(scale, edges, near, None, tiles)
        upper(scale, shards, edges, far, rest, tiles)

    targets = [outs[0].at[0:TILE, :]] + [out.at[rows - TILE : rows, :] for out in outs]
    for k, target in enumerate(targets):
        pltpu.make_async_copy(tiles.at[k * TILE : (k + 1) * TILE, :], target, sem).start()
    pltpu.make_async_copy(tiles, outs[0].at[0 : 4 * TILE, :], sem).wait()


def neighbour(scale, block, rest):
    g = [block[k : k + 1, :] for k in range(2)]
    if rest is not None:
        g = [(g[k] + rest[k : k + 1, :]) * scale for k in range(2)]
    d = [decay_rate * block[k + 2 : k + 3, :] + g[k] * g[k] + damping for k in range(2)]
    f = decay_rate * block[4:5, :] + g[0] * g[1]
    return g, d, f


def lower(scale, edges, block, rest, tiles):
    def edge(k, at):
        return edges[k * TILE + at : k * TILE + at + 1, :]

    (ga, gb), (da, db), fa = neighbour(scale, block, rest)
    g0, g1 = edge(0, 0), edge(0, 1)
    d0, d1 = edge(1, 0) + damping, edge(1, 1) + damping
    f0 = edge(2, 0)
    fb = decay_rate * block[5:6, :] + gb * g0
    sa = decay_rate * block[6:7, :] + ga * g0
    sb = decay_rate * block[7:8, :] + gb * g1
    _, _, far_a = solved(ga, gb, g0, da, db, d0, fa, fb, sa)
    _, near_b, far_b = solved(gb, g0, g1, db, d0, d1, fb, f0, sb)
    none = lax.axis_index("fsdp") == 0
    tiles[0:1, :] = edge(3, 0) - jnp.where(none, 0.0, near_b) - jnp.where(none, 0.0, far_a)
    tiles[1:2, :] = edge(3, 1) - jnp.where(none, 0.0, far_b)


def upper(scale, shards, edges, block, rest, tiles):
    def edge(k, at):
        return edges[k * TILE + at : k * TILE + at + 1, :]

    none = lax.axis_index("fsdp") == shards - 1
    (gp, gq), (dp, dq), fp = neighbour(scale, block, rest)
    gp, gq = jnp.where(none, 0.0, gp), jnp.where(none, 0.0, gq)
    dp, dq = jnp.where(none, 1.0, dp), jnp.where(none, 1.0, dq)
    fp = jnp.where(none, 0.0, fp)
    gx, gy = edge(4, 6), edge(4, 7)
    dx, dy = edge(5, 6) + damping, edge(5, 7) + damping
    fx = edge(6, 6)
    fy = jnp.where(none, 0.0, edge(6, 7) + gy * gp)
    sx = jnp.where(none, 0.0, edge(7, 6) + gx * gp)
    sy = jnp.where(none, 0.0, edge(7, 7) + gy * gq)
    vx, near_x, _ = solved(gx, gy, gp, dx, dy, dp, fx, fy, sx)
    vy, _, _ = solved(gy, gp, gq, dy, dp, dq, fy, fp, sy)
    tiles[14:15, :] = vx - edge(9, 5) - edge(10, 4)
    tiles[15:16, :] = vy - near_x - edge(10, 5)
    tiles[23:24, :] = fy
    tiles[30:31, :] = sx
    tiles[31:32, :] = sy


def trades(shards, low):
    partner = {}
    for i in range(low, shards - 1, 2):
        partner[i], partner[i + 1] = i + 1, i
    return [
        (2 * i + core, 2 * partner.get(i, i) + 1 - core) for i in range(shards) for core in range(2)
    ]


def body(partials, diag_stat, first_stat, second_stat):
    own = partials[0]
    rows, width = own.shape
    replicas = lax.axis_size("replica")
    shards = lax.axis_size("fsdp")
    scale = 1.0 / replicas
    axes = ("fsdp", "replica")
    paired = replicas == 2 and shards > 1

    shape = jax.ShapeDtypeStruct((rows, width), jnp.float32)
    vmem = pl.BlockSpec(memory_space=pltpu.VMEM)
    hbm = pl.BlockSpec(memory_space=pl.ANY)
    params = pltpu.CompilerParams(vmem_limit_bytes=24 * 2**20)

    def swap(block):
        return lax.ppermute(block, "replica", [(0, 1), (1, 0)])

    def stay(block):
        return pltpu.with_memory_space_constraint(block, pltpu.HBM)

    stats = (diag_stat, first_stat, second_stat)
    tile = pltpu.VMEM((TILE, width), jnp.float32)
    if paired:
        pieces = [own, swap(own)]
        far = pl.pallas_call(
            functools.partial(collect, rows),
            out_shape=tile,
            in_specs=[hbm] * 4,
            out_specs=vmem,
            scratch_shapes=[
                pltpu.VMEM((4 * TILE, width), jnp.float32),
                pltpu.SemaphoreType.DMA((4,)),
            ],
            compiler_params=params,
            name="collect",
        )(*[stay(x) for x in (own, *stats)])
        far = pl.pallas_call(
            functools.partial(choose, rows),
            out_shape=tile,
            in_specs=[vmem] * 2,
            out_specs=vmem,
            compiler_params=params,
            name="choose",
        )(far, pltpu.with_memory_space_constraint(own, pltpu.VMEM))
        far = lax.ppermute(far, axes, trades(shards, 1))
    else:
        pieces = [lax.psum(own, "replica") * scale]
        scale = 1.0
        tail = rows - 2
        unused = jnp.zeros((2, width), jnp.float32)
        last = jnp.concatenate([x[tail:] for x in (*pieces, *stats)])
        head = jnp.concatenate([x[:2] for x in (*pieces, *stats[:2])] + [unused])
        before = lax.ppermute(last, "fsdp", [(i, i + 1) for i in range(shards - 1)])
        after = lax.ppermute(head, "fsdp", [(i + 1, i) for i in range(shards - 1)])
        even = lax.axis_index("fsdp") % 2 == 0
        near, far = jnp.where(even, after, before), jnp.where(even, before, after)

    parts = len(pieces)
    whole = pltpu.VMEM((rows, width), jnp.float32)
    padded = pltpu.VMEM((rows + 2 * PAD, width), jnp.float32)
    chunk = 256 if rows % 256 == 0 else rows
    inner = [pltpu.with_memory_space_constraint(x, pltpu.VMEM) for x in (*pieces, *stats)]

    def inside(early, *done):
        return pl.pallas_call(
            functools.partial(interior, parts, early, scale, rows, chunk, 32),
            out_shape=(shape,) * 4 + (pltpu.VMEM((11 * TILE, width), jnp.float32),),
            in_specs=[vmem] * (parts + 3) + ([hbm] * 4 + [vmem] if done else []),
            out_specs=(hbm,) * 4 + (vmem,),
            input_output_aliases={parts + 3 + k: k for k in range(len(done[:4]))},
            scratch_shapes=[padded] * 6 + [whole, pltpu.SemaphoreType.DMA((4,))],
            compiler_params=params,
            cost_estimate=pl.CostEstimate(
                flops=45 * rows * width, bytes_accessed=36 * rows * width, transcendentals=0
            ),
            name="early" if early else "late",
        )(*inner, *done)

    done = inside(True)
    if paired:
        near = pl.pallas_call(
            functools.partial(ready, scale, rows),
            out_shape=tile,
            in_specs=[vmem] * 5,
            out_specs=vmem,
            compiler_params=params,
            name="ready",
        )(*inner)
        near, *done = lax.optimization_barrier((near, *done))
        near = lax.ppermute(near, axes, trades(shards, 0))
    update, diag_next, first_next, second_next, edges = inside(False, *done)
    other = far
    if paired:
        far, edges = lax.optimization_barrier((far, edges))
        other = swap(far)
    def patched(turn, other, *done):
        return pl.pallas_call(
            functools.partial(border, rows, shards, scale, turn),
            out_shape=(shape,) * 3,
            in_specs=[vmem] * 4 + [hbm] * 3,
            out_specs=(hbm,) * 3,
            input_output_aliases={4: 0, 5: 1, 6: 2},
            scratch_shapes=[
                pltpu.VMEM((4 * TILE, width), jnp.float32),
                pltpu.VMEM((2 * TILE, width), jnp.float32),
                pltpu.SemaphoreType.DMA,
            ],
            compiler_params=params,
            name="border",
        )(edges, near, far, other, *done)

    if paired:
        done = patched(1, far, update, first_next, second_next)
        update, first_next, second_next = patched(2, other, *done)
    else:
        update, first_next, second_next = patched(0, far, update, first_next, second_next)
    return update, diag_next, first_next, second_next


def solution(mesh):
    return jax.shard_map(
        body,
        mesh=mesh,
        in_specs=(P("replica", "fsdp", None), P("fsdp", None), P("fsdp", None), P("fsdp", None)),
        out_specs=(P("fsdp", None), P("fsdp", None), P("fsdp", None), P("fsdp", None)),
        check_vma=False,
    )
```

```python
import functools

import jax
import jax.numpy as jnp
from jax import lax
from jax.experimental import pallas as pl
from jax.experimental.pallas import tpu as pltpu
from jax.sharding import PartitionSpec as P

decay_rate = 0.95
damping = 0.01
PAD = 8
TILE = 8


def solved(g, g1, g2, d, upper, lower, f, c, s):
    det = upper * lower - c * c
    n1 = lower * f - c * s
    n2 = upper * s - c * f
    schur = d * det - f * n1 - s * n2
    top = g * det - n1 * g1 - n2 * g2
    w = top / (schur * det)
    return w * det, w * n1, w * n2


def collect(rows, own, diag, first, second, out, tiles, sems):
    even = lax.rem(lax.axis_index("fsdp"), 2) == 0
    low = lax.axis_index("replica") == 0

    @pl.when(low)
    def _():
        at = pl.multiple_of(jnp.where(even, 0, rows - TILE), TILE)
        copies = [
            pltpu.make_async_copy(
                source.at[pl.ds(at, TILE), :], tiles.at[k * TILE : (k + 1) * TILE, :], sems.at[k]
            )
            for k, source in enumerate((own, diag, first, second))
        ]
        for copy in copies:
            copy.start()
        for copy in copies:
            copy.wait()

    @pl.when(jnp.logical_and(low, even))
    def _():
        for k in range(3):
            out[2 * k : 2 * k + 2, :] = tiles[k * TILE : k * TILE + 2, :]
        out[6:8, :] = jnp.zeros((2, out.shape[1]), jnp.float32)

    @pl.when(jnp.logical_and(low, jnp.logical_not(even)))
    def _():
        for k in range(4):
            out[2 * k : 2 * k + 2, :] = tiles[(k + 1) * TILE - 2 : (k + 1) * TILE, :]


def choose(rows, block, own, out):
    even = lax.rem(lax.axis_index("fsdp"), 2) == 0
    low = lax.axis_index("replica") == 0

    @pl.when(low)
    def _():
        out[...] = block[...]

    @pl.when(jnp.logical_not(low))
    def _():
        out[2:8, :] = jnp.zeros((6, out.shape[1]), jnp.float32)
        out[0:2, :] = jnp.where(even, own[0:2, :], own[rows - 2 : rows, :])


def ready(scale, rows, own, other, diag, first, second, out):
    even = lax.rem(lax.axis_index("fsdp"), 2) == 0

    def fill(at, sources):
        out[0:2, :] = (own[at : at + 2, :] + other[at : at + 2, :]) * scale
        for k, source in enumerate(sources):
            out[2 * k + 2 : 2 * k + 4, :] = source[at : at + 2, :]

    @pl.when(even)
    def _():
        fill(rows - 2, (diag, first, second))

    @pl.when(jnp.logical_not(even))
    def _():
        fill(0, (diag, first))
        out[6:8, :] = jnp.zeros((2, out.shape[1]), jnp.float32)


def interior(parts, early, scale, rows, chunk, step, *refs):
    chosen = lax.axis_index("fsdp") == 0
    work = functools.partial(
        everything, parts, scale, rows, chunk, step, *refs[: parts + 3], *refs[-13:]
    )
    if early:
        pl.when(chosen)(work)
    else:
        pl.when(jnp.logical_not(chosen))(work)

        @pl.when(chosen)
        def _():
            refs[-9][...] = refs[parts + 7][...]


def everything(parts, scale, rows, chunk, step, *refs):
    pieces = refs[:parts]
    diag_in, first_in, second_in = refs[parts : parts + 3]
    outs = refs[parts + 3 : parts + 7]
    edges = refs[parts + 7]
    grad, diag, first, second, part1, part2, update, sems = refs[parts + 8 :]
    width = edges.shape[1]
    end = PAD + rows
    chunks = rows // chunk

    zeros = jnp.zeros((PAD, width), jnp.float32)
    grad[end:, :] = zeros
    diag[end:, :] = zeros + 1.0
    first[end:, :] = zeros
    part1[:PAD, :] = zeros
    part2[:PAD, :] = zeros

    def gradients(at, size):
        here, there = pl.ds(at, size), pl.ds(at + PAD, size)
        g = pieces[0][here, :]
        for piece in pieces[1:]:
            g = g + piece[here, :]
        g = g * scale
        grad[there, :] = g
        diag[there, :] = decay_rate * diag_in[here, :] + g * g

    def bands(at, size):
        here, there = pl.ds(at, size), pl.ds(at + PAD, size)
        g = grad[there, :]
        g1 = grad[pl.ds(at + PAD + 1, size), :]
        g2 = grad[pl.ds(at + PAD + 2, size), :]
        first[there, :] = decay_rate * first_in[here, :] + g * g1
        second[there, :] = decay_rate * second_in[here, :] + g * g2

    def values(at, size):
        there = pl.ds(at + PAD, size)
        after = pl.ds(at + PAD + 1, size)
        later = pl.ds(at + PAD + 2, size)
        v, p1, p2 = solved(
            grad[there, :],
            grad[after, :],
            grad[later, :],
            diag[there, :] + damping,
            diag[after, :] + damping,
            diag[later, :] + damping,
            first[there, :],
            first[after, :],
            second[there, :],
        )
        part1[there, :] = p1
        part2[there, :] = p2
        update[pl.ds(at, size), :] = (
            v - part1[pl.ds(at + PAD - 1, size), :] - part2[pl.ds(at + PAD - 2, size), :]
        )

    def over(work, low, high):
        for at in range(low, high, step):
            work(at, min(step, high - at))

    def send(source, pad, k, low, high):
        copy = pltpu.make_async_copy(
            source.at[low + pad : high + pad, :], outs[k].at[low:high, :], sems.at[k]
        )
        copy.start()

    for c in range(chunks):
        last = c == chunks - 1
        low, high = c * chunk, (c + 1) * chunk
        over(gradients, low, high)
        send(diag, PAD, 1, low, high)
        low, high = max(low - TILE, 0), high if last else high - TILE
        over(bands, low, high)
        send(first, PAD, 2, low, high)
        send(second, PAD, 3, low, high)
        low, high = max(c * chunk - 2 * TILE, 0), high if last else high - TILE
        over(values, low, high)
        send(update, 0, 0, low, high)

    tops = [grad[PAD : PAD + TILE, :], diag[PAD : PAD + TILE, :], first[PAD : PAD + TILE, :]]
    tops.append(update[:TILE, :])
    tails = [r[end - TILE : end, :] for r in (grad, diag, first, second)]
    tails.append(update[rows - TILE :, :])
    tails += [r[end - TILE : end, :] for r in (part1, part2)]
    for k, tile in enumerate(tops + tails):
        edges[k * TILE : (k + 1) * TILE, :] = tile
    for k, (source, pad) in enumerate(((update, 0), (diag, PAD), (first, PAD), (second, PAD))):
        pltpu.make_async_copy(source.at[pad : pad + rows, :], outs[k], sems.at[k]).wait()


def border(rows, shards, scale, turn, *refs):
    chosen = lax.axis_index("fsdp") == 0
    if turn == 0:
        patch(rows, shards, scale, *refs)
    else:
        pl.when(chosen if turn == 1 else jnp.logical_not(chosen))(
            functools.partial(patch, rows, shards, scale, *refs)
        )


def patch(rows, shards, scale, *refs):
    edges, near, far, other = refs[:4]
    outs = refs[7:10]
    tiles, mixed, sem = refs[10:]
    tiles[0:8, :] = edges[3 * TILE : 4 * TILE, :]
    tiles[8:16, :] = edges[8 * TILE : 9 * TILE, :]
    tiles[16:24, :] = edges[6 * TILE : 7 * TILE, :]
    tiles[24:32, :] = edges[7 * TILE : 8 * TILE, :]
    rest = None
    if scale != 1.0:
        low = lax.axis_index("replica") == 0
        mine, theirs = far[...], other[...]
        mixed[0:8, :] = jnp.where(low, theirs, mine)
        mixed[8:16, :] = jnp.where(low, mine, theirs)
        far, rest = mixed.at[0:8, :], mixed.at[8:16, :]
    even = lax.rem(lax.axis_index("fsdp"), 2) == 0

    @pl.when(even)
    def _():
        lower(scale, edges, far, rest, tiles)
        upper(scale, shards, edges, near, None, tiles)

    @pl.when(jnp.logical_not(even))
    def _():
        lower(scale, edges, near, None, tiles)
        upper(scale, shards, edges, far, rest, tiles)

    targets = [outs[0].at[0:TILE, :]] + [out.at[rows - TILE : rows, :] for out in outs]
    for k, target in enumerate(targets):
        pltpu.make_async_copy(tiles.at[k * TILE : (k + 1) * TILE, :], target, sem).start()
    pltpu.make_async_copy(tiles, outs[0].at[0 : 4 * TILE, :], sem).wait()


def neighbour(scale, block, rest):
    g = [block[k : k + 1, :] for k in range(2)]
    if rest is not None:
        g = [(g[k] + rest[k : k + 1, :]) * scale for k in range(2)]
    d = [decay_rate * block[k + 2 : k + 3, :] + g[k] * g[k] + damping for k in range(2)]
    f = decay_rate * block[4:5, :] + g[0] * g[1]
    return g, d, f


def lower(scale, edges, block, rest, tiles):
    def edge(k, at):
        return edges[k * TILE + at : k * TILE + at + 1, :]

    (ga, gb), (da, db), fa = neighbour(scale, block, rest)
    g0, g1 = edge(0, 0), edge(0, 1)
    d0, d1 = edge(1, 0) + damping, edge(1, 1) + damping
    f0 = edge(2, 0)
    fb = decay_rate * block[5:6, :] + gb * g0
    sa = decay_rate * block[6:7, :] + ga * g0
    sb = decay_rate * block[7:8, :] + gb * g1
    _, _, far_a = solved(ga, gb, g0, da, db, d0, fa, fb, sa)
    _, near_b, far_b = solved(gb, g0, g1, db, d0, d1, fb, f0, sb)
    none = lax.axis_index("fsdp") == 0
    tiles[0:1, :] = edge(3, 0) - jnp.where(none, 0.0, near_b) - jnp.where(none, 0.0, far_a)
    tiles[1:2, :] = edge(3, 1) - jnp.where(none, 0.0, far_b)


def upper(scale, shards, edges, block, rest, tiles):
    def edge(k, at):
        return edges[k * TILE + at : k * TILE + at + 1, :]

    none = lax.axis_index("fsdp") == shards - 1
    (gp, gq), (dp, dq), fp = neighbour(scale, block, rest)
    gp, gq = jnp.where(none, 0.0, gp), jnp.where(none, 0.0, gq)
    dp, dq = jnp.where(none, 1.0, dp), jnp.where(none, 1.0, dq)
    fp = jnp.where(none, 0.0, fp)
    gx, gy = edge(4, 6), edge(4, 7)
    dx, dy = edge(5, 6) + damping, edge(5, 7) + damping
    fx = edge(6, 6)
    fy = jnp.where(none, 0.0, edge(6, 7) + gy * gp)
    sx = jnp.where(none, 0.0, edge(7, 6) + gx * gp)
    sy = jnp.where(none, 0.0, edge(7, 7) + gy * gq)
    vx, near_x, _ = solved(gx, gy, gp, dx, dy, dp, fx, fy, sx)
    vy, _, _ = solved(gy, gp, gq, dy, dp, dq, fy, fp, sy)
    tiles[14:15, :] = vx - edge(9, 5) - edge(10, 4)
    tiles[15:16, :] = vy - near_x - edge(10, 5)
    tiles[23:24, :] = fy
    tiles[30:31, :] = sx
    tiles[31:32, :] = sy


def trades(shards, low):
    partner = {}
    for i in range(low, shards - 1, 2):
        partner[i], partner[i + 1] = i + 1, i
    return [
        (2 * i + core, 2 * partner.get(i, i) + 1 - core) for i in range(shards) for core in range(2)
    ]


def body(partials, diag_stat, first_stat, second_stat):
    own = partials[0]
    rows, width = own.shape
    replicas = lax.axis_size("replica")
    shards = lax.axis_size("fsdp")
    scale = 1.0 / replicas
    axes = ("fsdp", "replica")
    paired = replicas == 2 and shards > 1

    shape = jax.ShapeDtypeStruct((rows, width), jnp.float32)
    vmem = pl.BlockSpec(memory_space=pltpu.VMEM)
    hbm = pl.BlockSpec(memory_space=pl.ANY)
    params = pltpu.CompilerParams(vmem_limit_bytes=24 * 2**20)

    def swap(block):
        return lax.ppermute(block, "replica", [(0, 1), (1, 0)])

    def stay(block):
        return pltpu.with_memory_space_constraint(block, pltpu.HBM)

    stats = (diag_stat, first_stat, second_stat)
    tile = pltpu.VMEM((TILE, width), jnp.float32)
    if paired:
        pieces = [own, swap(own)]
        far = pl.pallas_call(
            functools.partial(collect, rows),
            out_shape=tile,
            in_specs=[hbm] * 4,
            out_specs=vmem,
            scratch_shapes=[
                pltpu.VMEM((4 * TILE, width), jnp.float32),
                pltpu.SemaphoreType.DMA((4,)),
            ],
            compiler_params=params,
            name="collect",
        )(*[stay(x) for x in (own, *stats)])
        far = pl.pallas_call(
            functools.partial(choose, rows),
            out_shape=tile,
            in_specs=[vmem] * 2,
            out_specs=vmem,
            compiler_params=params,
            name="choose",
        )(far, pltpu.with_memory_space_constraint(own, pltpu.VMEM))
        far = lax.ppermute(far, axes, trades(shards, 1))
    else:
        pieces = [lax.psum(own, "replica") * scale]
        scale = 1.0
        tail = rows - 2
        unused = jnp.zeros((2, width), jnp.float32)
        last = jnp.concatenate([x[tail:] for x in (*pieces, *stats)])
        head = jnp.concatenate([x[:2] for x in (*pieces, *stats[:2])] + [unused])
        before = lax.ppermute(last, "fsdp", [(i, i + 1) for i in range(shards - 1)])
        after = lax.ppermute(head, "fsdp", [(i + 1, i) for i in range(shards - 1)])
        even = lax.axis_index("fsdp") % 2 == 0
        near, far = jnp.where(even, after, before), jnp.where(even, before, after)

    parts = len(pieces)
    whole = pltpu.VMEM((rows, width), jnp.float32)
    padded = pltpu.VMEM((rows + 2 * PAD, width), jnp.float32)
    chunk = 256 if rows % 256 == 0 else rows
    inner = [pltpu.with_memory_space_constraint(x, pltpu.VMEM) for x in (*pieces, *stats)]

    def inside(early, *done):
        return pl.pallas_call(
            functools.partial(interior, parts, early, scale, rows, chunk, 16),
            out_shape=(shape,) * 4 + (pltpu.VMEM((11 * TILE, width), jnp.float32),),
            in_specs=[vmem] * (parts + 3) + ([hbm] * 4 + [vmem] if done else []),
            out_specs=(hbm,) * 4 + (vmem,),
            input_output_aliases={parts + 3 + k: k for k in range(len(done[:4]))},
            scratch_shapes=[padded] * 6 + [whole, pltpu.SemaphoreType.DMA((4,))],
            compiler_params=params,
            cost_estimate=pl.CostEstimate(
                flops=45 * rows * width, bytes_accessed=36 * rows * width, transcendentals=0
            ),
            name="early" if early else "late",
        )(*inner, *done)

    done = inside(True)
    if paired:
        near = pl.pallas_call(
            functools.partial(ready, scale, rows),
            out_shape=tile,
            in_specs=[vmem] * 5,
            out_specs=vmem,
            compiler_params=params,
            name="ready",
        )(*inner)
        near, *done = lax.optimization_barrier((near, *done))
        near = lax.ppermute(near, axes, trades(shards, 0))
    update, diag_next, first_next, second_next, edges = inside(False, *done)
    other = far
    if paired:
        far, edges = lax.optimization_barrier((far, edges))
        other = swap(far)
    def patched(turn, other, *done):
        return pl.pallas_call(
            functools.partial(border, rows, shards, scale, turn),
            out_shape=(shape,) * 3,
            in_specs=[vmem] * 4 + [hbm] * 3,
            out_specs=(hbm,) * 3,
            input_output_aliases={4: 0, 5: 1, 6: 2},
            scratch_shapes=[
                pltpu.VMEM((4 * TILE, width), jnp.float32),
                pltpu.VMEM((2 * TILE, width), jnp.float32),
                pltpu.SemaphoreType.DMA,
            ],
            compiler_params=params,
            name="border",
        )(edges, near, far, other, *done)

    if paired:
        done = patched(1, far, update, first_next, second_next)
        update, first_next, second_next = patched(2, other, *done)
    else:
        update, first_next, second_next = patched(0, far, update, first_next, second_next)
    return update, diag_next, first_next, second_next


def solution(mesh):
    return jax.shard_map(
        body,
        mesh=mesh,
        in_specs=(P("replica", "fsdp", None), P("fsdp", None), P("fsdp", None), P("fsdp", None)),
        out_specs=(P("fsdp", None), P("fsdp", None), P("fsdp", None), P("fsdp", None)),
        check_vma=False,
    )
```

```python
import functools

import jax
import jax.numpy as jnp
from jax import lax
from jax.experimental import pallas as pl
from jax.experimental.pallas import tpu as pltpu
from jax.sharding import PartitionSpec as P

decay_rate = 0.95
damping = 0.01
PAD = 8
TILE = 8


def solved(g, g1, g2, d, upper, lower, f, c, s):
    det = upper * lower - c * c
    n1 = lower * f - c * s
    n2 = upper * s - c * f
    schur = d * det - f * n1 - s * n2
    top = g * det - n1 * g1 - n2 * g2
    w = top / (schur * det)
    return w * det, w * n1, w * n2


def collect(rows, own, diag, first, second, out, tiles, sems):
    even = lax.rem(lax.axis_index("fsdp"), 2) == 0
    low = lax.axis_index("replica") == 0

    @pl.when(low)
    def _():
        at = pl.multiple_of(jnp.where(even, 0, rows - TILE), TILE)
        copies = [
            pltpu.make_async_copy(
                source.at[pl.ds(at, TILE), :], tiles.at[k * TILE : (k + 1) * TILE, :], sems.at[k]
            )
            for k, source in enumerate((own, diag, first, second))
        ]
        for copy in copies:
            copy.start()
        for copy in copies:
            copy.wait()

    @pl.when(jnp.logical_and(low, even))
    def _():
        for k in range(3):
            out[2 * k : 2 * k + 2, :] = tiles[k * TILE : k * TILE + 2, :]
        out[6:8, :] = jnp.zeros((2, out.shape[1]), jnp.float32)

    @pl.when(jnp.logical_and(low, jnp.logical_not(even)))
    def _():
        for k in range(4):
            out[2 * k : 2 * k + 2, :] = tiles[(k + 1) * TILE - 2 : (k + 1) * TILE, :]


def choose(rows, block, own, out):
    even = lax.rem(lax.axis_index("fsdp"), 2) == 0
    low = lax.axis_index("replica") == 0

    @pl.when(low)
    def _():
        out[...] = block[...]

    @pl.when(jnp.logical_not(low))
    def _():
        out[2:8, :] = jnp.zeros((6, out.shape[1]), jnp.float32)
        out[0:2, :] = jnp.where(even, own[0:2, :], own[rows - 2 : rows, :])


def ready(scale, rows, own, other, diag, first, second, out):
    even = lax.rem(lax.axis_index("fsdp"), 2) == 0

    def fill(at, sources):
        out[0:2, :] = (own[at : at + 2, :] + other[at : at + 2, :]) * scale
        for k, source in enumerate(sources):
            out[2 * k + 2 : 2 * k + 4, :] = source[at : at + 2, :]

    @pl.when(even)
    def _():
        fill(rows - 2, (diag, first, second))

    @pl.when(jnp.logical_not(even))
    def _():
        fill(0, (diag, first))
        out[6:8, :] = jnp.zeros((2, out.shape[1]), jnp.float32)


def interior(parts, early, scale, rows, chunk, step, *refs):
    chosen = lax.axis_index("fsdp") == 0
    work = functools.partial(
        everything, parts, scale, rows, chunk, step, *refs[: parts + 3], *refs[-13:]
    )
    if early:
        pl.when(chosen)(work)
    else:
        pl.when(jnp.logical_not(chosen))(work)

        @pl.when(chosen)
        def _():
            refs[-9][...] = refs[parts + 7][...]


def everything(parts, scale, rows, chunk, step, *refs):
    pieces = refs[:parts]
    diag_in, first_in, second_in = refs[parts : parts + 3]
    outs = refs[parts + 3 : parts + 7]
    edges = refs[parts + 7]
    grad, diag, first, second, part1, part2, update, sems = refs[parts + 8 :]
    width = edges.shape[1]
    end = PAD + rows
    chunks = rows // chunk

    zeros = jnp.zeros((PAD, width), jnp.float32)
    grad[end:, :] = zeros
    diag[end:, :] = zeros + 1.0
    first[end:, :] = zeros
    part1[:PAD, :] = zeros
    part2[:PAD, :] = zeros

    def gradients(at, size):
        here, there = pl.ds(at, size), pl.ds(at + PAD, size)
        g = pieces[0][here, :]
        for piece in pieces[1:]:
            g = g + piece[here, :]
        g = g * scale
        grad[there, :] = g
        diag[there, :] = decay_rate * diag_in[here, :] + g * g

    def bands(at, size):
        here, there = pl.ds(at, size), pl.ds(at + PAD, size)
        g = grad[there, :]
        g1 = grad[pl.ds(at + PAD + 1, size), :]
        g2 = grad[pl.ds(at + PAD + 2, size), :]
        first[there, :] = decay_rate * first_in[here, :] + g * g1
        second[there, :] = decay_rate * second_in[here, :] + g * g2

    def values(at, size):
        there = pl.ds(at + PAD, size)
        after = pl.ds(at + PAD + 1, size)
        later = pl.ds(at + PAD + 2, size)
        v, p1, p2 = solved(
            grad[there, :],
            grad[after, :],
            grad[later, :],
            diag[there, :] + damping,
            diag[after, :] + damping,
            diag[later, :] + damping,
            first[there, :],
            first[after, :],
            second[there, :],
        )
        part1[there, :] = p1
        part2[there, :] = p2
        update[pl.ds(at, size), :] = (
            v - part1[pl.ds(at + PAD - 1, size), :] - part2[pl.ds(at + PAD - 2, size), :]
        )

    def over(work, low, high):
        for at in range(low, high, step):
            work(at, min(step, high - at))

    def send(source, pad, k, low, high):
        copy = pltpu.make_async_copy(
            source.at[low + pad : high + pad, :], outs[k].at[low:high, :], sems.at[k]
        )
        copy.start()

    for c in range(chunks):
        last = c == chunks - 1
        low, high = c * chunk, (c + 1) * chunk
        over(gradients, low, high)
        send(diag, PAD, 1, low, high)
        low, high = max(low - TILE, 0), high if last else high - TILE
        over(bands, low, high)
        send(first, PAD, 2, low, high)
        send(second, PAD, 3, low, high)
        low, high = max(c * chunk - 2 * TILE, 0), high if last else high - TILE
        over(values, low, high)
        send(update, 0, 0, low, high)

    tops = [grad[PAD : PAD + TILE, :], diag[PAD : PAD + TILE, :], first[PAD : PAD + TILE, :]]
    tops.append(update[:TILE, :])
    tails = [r[end - TILE : end, :] for r in (grad, diag, first, second)]
    tails.append(update[rows - TILE :, :])
    tails += [r[end - TILE : end, :] for r in (part1, part2)]
    for k, tile in enumerate(tops + tails):
        edges[k * TILE : (k + 1) * TILE, :] = tile
    for k, (source, pad) in enumerate(((update, 0), (diag, PAD), (first, PAD), (second, PAD))):
        pltpu.make_async_copy(source.at[pad : pad + rows, :], outs[k], sems.at[k]).wait()


def border(rows, shards, scale, turn, *refs):
    chosen = lax.axis_index("fsdp") == 0
    if turn == 0:
        patch(rows, shards, scale, *refs)
    else:
        pl.when(chosen if turn == 1 else jnp.logical_not(chosen))(
            functools.partial(patch, rows, shards, scale, *refs)
        )


def patch(rows, shards, scale, *refs):
    edges, near, far, other = refs[:4]
    outs = refs[7:10]
    tiles, mixed, sem = refs[10:]
    tiles[0:8, :] = edges[3 * TILE : 4 * TILE, :]
    tiles[8:16, :] = edges[8 * TILE : 9 * TILE, :]
    tiles[16:24, :] = edges[6 * TILE : 7 * TILE, :]
    tiles[24:32, :] = edges[7 * TILE : 8 * TILE, :]
    rest = None
    if scale != 1.0:
        low = lax.axis_index("replica") == 0
        mine, theirs = far[...], other[...]
        mixed[0:8, :] = jnp.where(low, theirs, mine)
        mixed[8:16, :] = jnp.where(low, mine, theirs)
        far, rest = mixed.at[0:8, :], mixed.at[8:16, :]
    even = lax.rem(lax.axis_index("fsdp"), 2) == 0

    @pl.when(even)
    def _():
        lower(scale, edges, far, rest, tiles)
        upper(scale, shards, edges, near, None, tiles)

    @pl.when(jnp.logical_not(even))
    def _():
        lower(scale, edges, near, None, tiles)
        upper(scale, shards, edges, far, rest, tiles)

    targets = [outs[0].at[0:TILE, :]] + [out.at[rows - TILE : rows, :] for out in outs]
    for k, target in enumerate(targets):
        pltpu.make_async_copy(tiles.at[k * TILE : (k + 1) * TILE, :], target, sem).start()
    pltpu.make_async_copy(tiles, outs[0].at[0 : 4 * TILE, :], sem).wait()


def neighbour(scale, block, rest):
    g = [block[k : k + 1, :] for k in range(2)]
    if rest is not None:
        g = [(g[k] + rest[k : k + 1, :]) * scale for k in range(2)]
    d = [decay_rate * block[k + 2 : k + 3, :] + g[k] * g[k] + damping for k in range(2)]
    f = decay_rate * block[4:5, :] + g[0] * g[1]
    return g, d, f


def lower(scale, edges, block, rest, tiles):
    def edge(k, at):
        return edges[k * TILE + at : k * TILE + at + 1, :]

    (ga, gb), (da, db), fa = neighbour(scale, block, rest)
    g0, g1 = edge(0, 0), edge(0, 1)
    d0, d1 = edge(1, 0) + damping, edge(1, 1) + damping
    f0 = edge(2, 0)
    fb = decay_rate * block[5:6, :] + gb * g0
    sa = decay_rate * block[6:7, :] + ga * g0
    sb = decay_rate * block[7:8, :] + gb * g1
    _, _, far_a = solved(ga, gb, g0, da, db, d0, fa, fb, sa)
    _, near_b, far_b = solved(gb, g0, g1, db, d0, d1, fb, f0, sb)
    none = lax.axis_index("fsdp") == 0
    tiles[0:1, :] = edge(3, 0) - jnp.where(none, 0.0, near_b) - jnp.where(none, 0.0, far_a)
    tiles[1:2, :] = edge(3, 1) - jnp.where(none, 0.0, far_b)


def upper(scale, shards, edges, block, rest, tiles):
    def edge(k, at):
        return edges[k * TILE + at : k * TILE + at + 1, :]

    none = lax.axis_index("fsdp") == shards - 1
    (gp, gq), (dp, dq), fp = neighbour(scale, block, rest)
    gp, gq = jnp.where(none, 0.0, gp), jnp.where(none, 0.0, gq)
    dp, dq = jnp.where(none, 1.0, dp), jnp.where(none, 1.0, dq)
    fp = jnp.where(none, 0.0, fp)
    gx, gy = edge(4, 6), edge(4, 7)
    dx, dy = edge(5, 6) + damping, edge(5, 7) + damping
    fx = edge(6, 6)
    fy = jnp.where(none, 0.0, edge(6, 7) + gy * gp)
    sx = jnp.where(none, 0.0, edge(7, 6) + gx * gp)
    sy = jnp.where(none, 0.0, edge(7, 7) + gy * gq)
    vx, near_x, _ = solved(gx, gy, gp, dx, dy, dp, fx, fy, sx)
    vy, _, _ = solved(gy, gp, gq, dy, dp, dq, fy, fp, sy)
    tiles[14:15, :] = vx - edge(9, 5) - edge(10, 4)
    tiles[15:16, :] = vy - near_x - edge(10, 5)
    tiles[23:24, :] = fy
    tiles[30:31, :] = sx
    tiles[31:32, :] = sy


def trades(shards, low):
    partner = {}
    for i in range(low, shards - 1, 2):
        partner[i], partner[i + 1] = i + 1, i
    return [
        (2 * i + core, 2 * partner.get(i, i) + 1 - core) for i in range(shards) for core in range(2)
    ]


def body(partials, diag_stat, first_stat, second_stat):
    own = partials[0]
    rows, width = own.shape
    replicas = lax.axis_size("replica")
    shards = lax.axis_size("fsdp")
    scale = 1.0 / replicas
    axes = ("fsdp", "replica")
    paired = replicas == 2 and shards > 1

    shape = jax.ShapeDtypeStruct((rows, width), jnp.float32)
    vmem = pl.BlockSpec(memory_space=pltpu.VMEM)
    hbm = pl.BlockSpec(memory_space=pl.ANY)
    params = pltpu.CompilerParams(vmem_limit_bytes=24 * 2**20)

    def swap(block):
        return lax.ppermute(block, "replica", [(0, 1), (1, 0)])

    def stay(block):
        return pltpu.with_memory_space_constraint(block, pltpu.HBM)

    stats = (diag_stat, first_stat, second_stat)
    tile = pltpu.VMEM((TILE, width), jnp.float32)
    if paired:
        pieces = [own, swap(own)]
        far = pl.pallas_call(
            functools.partial(collect, rows),
            out_shape=tile,
            in_specs=[hbm] * 4,
            out_specs=vmem,
            scratch_shapes=[
                pltpu.VMEM((4 * TILE, width), jnp.float32),
                pltpu.SemaphoreType.DMA((4,)),
            ],
            compiler_params=params,
            name="collect",
        )(*[stay(x) for x in (own, *stats)])
        far = pl.pallas_call(
            functools.partial(choose, rows),
            out_shape=tile,
            in_specs=[vmem] * 2,
            out_specs=vmem,
            compiler_params=params,
            name="choose",
        )(far, pltpu.with_memory_space_constraint(own, pltpu.VMEM))
        far = lax.ppermute(far, axes, trades(shards, 1))
    else:
        pieces = [lax.psum(own, "replica") * scale]
        scale = 1.0
        tail = rows - 2
        unused = jnp.zeros((2, width), jnp.float32)
        last = jnp.concatenate([x[tail:] for x in (*pieces, *stats)])
        head = jnp.concatenate([x[:2] for x in (*pieces, *stats[:2])] + [unused])
        before = lax.ppermute(last, "fsdp", [(i, i + 1) for i in range(shards - 1)])
        after = lax.ppermute(head, "fsdp", [(i + 1, i) for i in range(shards - 1)])
        even = lax.axis_index("fsdp") % 2 == 0
        near, far = jnp.where(even, after, before), jnp.where(even, before, after)

    parts = len(pieces)
    whole = pltpu.VMEM((rows, width), jnp.float32)
    padded = pltpu.VMEM((rows + 2 * PAD, width), jnp.float32)
    chunk = 512 if rows % 512 == 0 else rows
    inner = [pltpu.with_memory_space_constraint(x, pltpu.VMEM) for x in (*pieces, *stats)]

    def inside(early, *done):
        return pl.pallas_call(
            functools.partial(interior, parts, early, scale, rows, chunk, 32),
            out_shape=(shape,) * 4 + (pltpu.VMEM((11 * TILE, width), jnp.float32),),
            in_specs=[vmem] * (parts + 3) + ([hbm] * 4 + [vmem] if done else []),
            out_specs=(hbm,) * 4 + (vmem,),
            input_output_aliases={parts + 3 + k: k for k in range(len(done[:4]))},
            scratch_shapes=[padded] * 6 + [whole, pltpu.SemaphoreType.DMA((4,))],
            compiler_params=params,
            cost_estimate=pl.CostEstimate(
                flops=45 * rows * width, bytes_accessed=36 * rows * width, transcendentals=0
            ),
            name="early" if early else "late",
        )(*inner, *done)

    done = inside(True)
    if paired:
        near = pl.pallas_call(
            functools.partial(ready, scale, rows),
            out_shape=tile,
            in_specs=[vmem] * 5,
            out_specs=vmem,
            compiler_params=params,
            name="ready",
        )(*inner)
        near, *done = lax.optimization_barrier((near, *done))
        near = lax.ppermute(near, axes, trades(shards, 0))
    update, diag_next, first_next, second_next, edges = inside(False, *done)
    other = far
    if paired:
        far, edges = lax.optimization_barrier((far, edges))
        other = swap(far)
    def patched(turn, other, *done):
        return pl.pallas_call(
            functools.partial(border, rows, shards, scale, turn),
            out_shape=(shape,) * 3,
            in_specs=[vmem] * 4 + [hbm] * 3,
            out_specs=(hbm,) * 3,
            input_output_aliases={4: 0, 5: 1, 6: 2},
            scratch_shapes=[
                pltpu.VMEM((4 * TILE, width), jnp.float32),
                pltpu.VMEM((2 * TILE, width), jnp.float32),
                pltpu.SemaphoreType.DMA,
            ],
            compiler_params=params,
            name="border",
        )(edges, near, far, other, *done)

    if paired:
        done = patched(1, far, update, first_next, second_next)
        update, first_next, second_next = patched(2, other, *done)
    else:
        update, first_next, second_next = patched(0, far, update, first_next, second_next)
    return update, diag_next, first_next, second_next


def solution(mesh):
    return jax.shard_map(
        body,
        mesh=mesh,
        in_specs=(P("replica", "fsdp", None), P("fsdp", None), P("fsdp", None), P("fsdp", None)),
        out_specs=(P("fsdp", None), P("fsdp", None), P("fsdp", None), P("fsdp", None)),
        check_vma=False,
    )
```
